32 devices in a mesh: seq: 8 (over y, x, core), rows: 4 (over z).
Axes of the slice: x: 2, y: 2, z: 4, core: 2. Of those that a mesh axis runs over, the one named last changes fastest.
Arguments:
- source: bfloat16 [2, 4, 1024, 1024], P(None, 'rows', 'seq'), may hold values from -6 to 6
- target: bfloat16 [2, 4, 1024, 1024], P(None, 'rows', 'seq'), may hold values from -6 to 6
- source_segments: int32 [2, 4, 1024], P(None, 'rows'), may hold values from 0 to 2, as said below
- target_segments: int32 [2, 4, 1024], P(None, 'rows'), may hold values from 0 to 2, as said below
- cotangent: bfloat16 [2, 4, 1024, 1024], P(None, 'rows', 'seq'), may hold values from -6 to 6
- encoder_qkv: bfloat16 [3, 1024, 1024], P(None, None, ('seq', 'rows')), may hold values from -0.1875 to 0.1875
- encoder_output: bfloat16 [1024, 1024], P(None, ('seq', 'rows')), may hold values from -1.5 to 1.5
- encoder_prefix: bfloat16 [2, 30, 1024], P(None, None, ('seq', 'rows')), may hold values from -4 to 4
- encoder_expand: bfloat16 [1024, 4096], P(None, ('seq', 'rows')), may hold values from -0.1875 to 0.1875
- encoder_contract: bfloat16 [4096, 1024], P(None, ('seq', 'rows')), may hold values from -0.09375 to 0.09375
- encoder_down: bfloat16 [1024, 512], P(None, ('seq', 'rows')), may hold values from -0.1875 to 0.1875
- encoder_up: bfloat16 [512, 1024], P(None, ('seq', 'rows')), may hold values from -0.0625 to 0.0625
- encoder_norms: bfloat16 [2, 2, 1024], P(None, None, ('seq', 'rows')), may hold values from -0.9 to 1.3
- decoder_qkv: bfloat16 [3, 1024, 1024], P(None, None, ('seq', 'rows')), may hold values from -0.1875 to 0.1875
- decoder_output: bfloat16 [1024, 1024], P(None, ('seq', 'rows')), may hold values from -1.5 to 1.5
- decoder_prefix: bfloat16 [2, 30, 1024], P(None, None, ('seq', 'rows')), may hold values from -4 to 4
- cross_query: bfloat16 [1024, 1024], P(None, ('seq', 'rows')), may hold values from -0.1875 to 0.1875
- cross_kv: bfloat16 [2, 1024, 1024], P(None, None, ('seq', 'rows')), may hold values from -0.1875 to 0.1875
- cross_output: bfloat16 [1024, 1024], P(None, ('seq', 'rows')), may hold values from -1.5 to 1.5
- cross_prefix: bfloat16 [2, 30, 1024], P(None, None, ('seq', 'rows')), may hold values from -4 to 4
- decoder_expand: bfloat16 [1024, 4096], P(None, ('seq', 'rows')), may hold values from -0.1875 to 0.1875
- decoder_contract: bfloat16 [4096, 1024], P(None, ('seq', 'rows')), may hold values from -0.09375 to 0.09375
- decoder_down: bfloat16 [1024, 512], P(None, ('seq', 'rows')), may hold values from -0.1875 to 0.1875
- decoder_up: bfloat16 [512, 1024], P(None, ('seq', 'rows')), may hold values from -0.0625 to 0.0625
- decoder_norms: bfloat16 [3, 2, 1024], P(None, None, ('seq', 'rows')), may hold values from -0.9 to 1.3
Outputs:
- result: bfloat16 [2, 4, 1024, 1024], P(None, 'rows', 'seq')
- source_grad: float32 [2, 4, 1024, 1024], P(None, 'rows', 'seq')
- target_grad: float32 [2, 4, 1024, 1024], P(None, 'rows', 'seq')
- encoder_qkv_grad: float32 [3, 1024, 1024], P(None, None, ('seq', 'rows'))
- encoder_output_grad: float32 [1024, 1024], P(None, ('seq', 'rows'))
- encoder_prefix_grad: float32 [2, 30, 1024], P(None, None, ('seq', 'rows'))
- encoder_expand_grad: float32 [1024, 4096], P(None, ('seq', 'rows'))
- encoder_contract_grad: float32 [4096, 1024], P(None, ('seq', 'rows'))
- encoder_down_grad: float32 [1024, 512], P(None, ('seq', 'rows'))
- encoder_up_grad: float32 [512, 1024], P(None, ('seq', 'rows'))
- encoder_norms_grad: float32 [2, 2, 1024], P(None, None, ('seq', 'rows'))
- decoder_qkv_grad: float32 [3, 1024, 1024], P(None, None, ('seq', 'rows'))
- decoder_output_grad: float32 [1024, 1024], P(None, ('seq', 'rows'))
- decoder_prefix_grad: float32 [2, 30, 1024], P(None, None, ('seq', 'rows'))
- cross_query_grad: float32 [1024, 1024], P(None, ('seq', 'rows'))
- cross_kv_grad: float32 [2, 1024, 1024], P(None, None, ('seq', 'rows'))
- cross_output_grad: float32 [1024, 1024], P(None, ('seq', 'rows'))
- cross_prefix_grad: float32 [2, 30, 1024], P(None, None, ('seq', 'rows'))
- decoder_expand_grad: float32 [1024, 4096], P(None, ('seq', 'rows'))
- decoder_contract_grad: float32 [4096, 1024], P(None, ('seq', 'rows'))
- decoder_down_grad: float32 [1024, 512], P(None, ('seq', 'rows'))
- decoder_up_grad: float32 [512, 1024], P(None, ('seq', 'rows'))
- decoder_norms_grad: float32 [3, 2, 1024], P(None, None, ('seq', 'rows'))
The draws below stay inside these ranges and needn't reach their ends.
Inputs may be any that keep to these rules, and one draw needn't show every extreme that they name: `source_segments`: ids never fall along a row; id 1 begins within the first 64 positions and ends within the last 64; ids 0 and 2 each cover at least one position. `target_segments`: ids never fall along a row; id 1 begins within the first 64 positions and ends within the last 64; ids 0 and 2 each cover at least one position.
All inputs are finite; a program needn't handle non-finite values.
Results may differ from the reference program's by a relative error of at most 0.024.
Values may be sent and summed in bfloat16 or wider, within the bound.
A program may use at most 448 MiB of HBM per device.

```python
import jax
import jax.numpy as jnp
from jax import lax

D = 1024
HEADS = 16
HEAD_DIM = 64
FF = 4096
ADAPT = 512
PREFIX = 30
LENGTH = 1024
MICRO = 2
BLOCK = 128
ROWS = 4


def segment_bounds(seed_key, salt_value):
    folded = jax.random.fold_in(seed_key, salt_value)
    first_key, last_key = jax.random.split(folded)
    starts = jax.random.randint(first_key, (MICRO, ROWS, 1), 1, BLOCK // 2 + 1)
    finishes = jax.random.randint(last_key, (MICRO, ROWS, 1), LENGTH - BLOCK // 2, LENGTH)
    places = jnp.arange(LENGTH, dtype=jnp.int32)[None, None, :]
    return (places >= starts).astype(jnp.int32) + (places >= finishes).astype(jnp.int32)


def draw_source_segments(key, part):
    return segment_bounds(key, 11)


def draw_target_segments(key, part):
    return segment_bounds(key, 23)


def norm_values(seed_key, layers):
    gain_key, shift_key = jax.random.split(seed_key)
    gains = 1.0 + 0.3 * jax.random.uniform(gain_key, (layers, 1, D), minval=-1.0, maxval=1.0)
    shifts = 0.3 * jax.random.truncated_normal(shift_key, -3.0, 3.0, (layers, 1, D))
    return jnp.concatenate([gains, shifts], axis=1).astype(jnp.bfloat16)


def draw_encoder_norms(key, part):
    return norm_values(jax.random.fold_in(key, 5), 2)


def draw_decoder_norms(key, part):
    return norm_values(jax.random.fold_in(key, 7), 3)


def shard_levels(key, dims, cuts, least, largest):
    level, own = 1.0, jax.random.fold_in(key, 6)
    for position, parts in cuts:
        draws = jnp.exp(jax.random.uniform(jax.random.fold_in(own, position), (parts,), jnp.float32, least / len(cuts), largest / len(cuts)))
        level = level * jnp.repeat(draws, dims[position] // parts).reshape([-1 if axis == position else 1 for axis in range(len(dims))])
    return level


def gaussian(key, extent, width, bound, cuts=(), held_as=jnp.bfloat16):
    array = jax.random.normal(key, extent, jnp.float32) * width
    if len(cuts) > 0:
        array = shard_levels(key, extent, cuts, -0.22, 0.18) * array
    return jnp.clip(array, min=-bound, max=bound).astype(held_as)


def setup_inputs(seed: int = 0) -> dict:
    seeds = jax.random.split(jax.random.key(seed), 26)
    return {
        "source": gaussian(seeds[0], (MICRO, ROWS, LENGTH, D), 1.0, 6.0, ((1, 4), (2, 8))),
        "target": gaussian(seeds[1], (MICRO, ROWS, LENGTH, D), 1.0, 6.0, ((1, 4), (2, 8))),
        "source_segments": draw_source_segments(jax.random.fold_in(seeds[25], 71), 0),
        "target_segments": draw_target_segments(jax.random.fold_in(seeds[25], 71), 0),
        "cotangent": gaussian(seeds[4], (MICRO, ROWS, LENGTH, D), 1.0, 6.0, ((1, 4), (2, 8))),
        "encoder_qkv": gaussian(seeds[5], (3, D, D), D ** -0.5, 0.1875, ((2, 32),)),
        "encoder_output": gaussian(seeds[6], (D, D), (HEAD_DIM // 4) ** -0.5, 1.5, ((1, 32),)),
        "encoder_prefix": gaussian(seeds[7], (2, PREFIX, D), 1.0, 4.0, ((2, 32),)),
        "encoder_expand": gaussian(seeds[8], (D, FF), D ** -0.5, 0.1875, ((1, 32),)),
        "encoder_contract": gaussian(seeds[9], (FF, D), FF ** -0.5, 0.09375, ((1, 32),)),
        "encoder_down": gaussian(seeds[10], (D, ADAPT), D ** -0.5, 0.1875, ((1, 32),)),
        "encoder_up": gaussian(seeds[11], (ADAPT, D), (16 * ADAPT) ** -0.5, 0.0625, ((1, 32),)),
        "encoder_norms": draw_encoder_norms(jax.random.fold_in(seeds[25], 71), 0),
        "decoder_qkv": gaussian(seeds[13], (3, D, D), D ** -0.5, 0.1875, ((2, 32),)),
        "decoder_output": gaussian(seeds[14], (D, D), (HEAD_DIM // 4) ** -0.5, 1.5, ((1, 32),)),
        "decoder_prefix": gaussian(seeds[15], (2, PREFIX, D), 1.0, 4.0, ((2, 32),)),
        "cross_query": gaussian(seeds[16], (D, D), D ** -0.5, 0.1875, ((1, 32),)),
        "cross_kv": gaussian(seeds[17], (2, D, D), D ** -0.5, 0.1875, ((2, 32),)),
        "cross_output": gaussian(seeds[18], (D, D), (HEAD_DIM // 4) ** -0.5, 1.5, ((1, 32),)),
        "cross_prefix": gaussian(seeds[19], (2, PREFIX, D), 1.0, 4.0, ((2, 32),)),
        "decoder_expand": gaussian(seeds[20], (D, FF), D ** -0.5, 0.1875, ((1, 32),)),
        "decoder_contract": gaussian(seeds[21], (FF, D), FF ** -0.5, 0.09375, ((1, 32),)),
        "decoder_down": gaussian(seeds[22], (D, ADAPT), D ** -0.5, 0.1875, ((1, 32),)),
        "decoder_up": gaussian(seeds[23], (ADAPT, D), (16 * ADAPT) ** -0.5, 0.0625, ((1, 32),)),
        "decoder_norms": draw_decoder_norms(jax.random.fold_in(seeds[25], 71), 0),
    }


@jax.custom_vjp
def low(v):
    return lax.optimization_barrier(v.astype(jnp.bfloat16)).astype(jnp.float32)

@jax.custom_vjp
def low_back(v):
    return v

def low_keep(v):
    return (low(v), None)

def low_pass(kept, grad):
    return (grad,)

def back_keep(v):
    return (v, None)

def back_low(kept, grad):
    return (low(grad),)
low.defvjp(low_keep, low_pass)
low_back.defvjp(back_keep, back_low)
epsilon = 1e-05
highest = lax.Precision.HIGHEST
adapter_scale = 4.0

def both_ways(tensor):
    return low_back(low(tensor))

def matmul(left, right):
    return jnp.matmul(left, right, precision=highest)

def normalize(tensor, params, index):
    average = lax.optimization_barrier(jnp.mean(tensor, axis=-1, keepdims=True))
    centered = tensor - average
    spread = lax.optimization_barrier(jnp.mean(centered * centered, axis=-1, keepdims=True))
    return centered * lax.rsqrt(spread + epsilon) * params[index, 0] + params[index, 1]

def attention(inputs, memory, w_query, w_key, w_value, w_output, prefix, allowed):
    queries = both_ways(matmul(inputs, w_query)).reshape(-1, HEADS, HEAD_DIM)
    keys_local = both_ways(matmul(memory, w_key)).reshape(-1, HEADS, HEAD_DIM)
    values_local = both_ways(matmul(memory, w_value)).reshape(-1, HEADS, HEAD_DIM)
    keys_all = jnp.concatenate([prefix[0].reshape(-1, HEADS, HEAD_DIM), keys_local], axis=0)
    values_all = jnp.concatenate([prefix[1].reshape(-1, HEADS, HEAD_DIM), values_local], axis=0)
    visible = jnp.concatenate([jnp.ones((allowed.shape[0], PREFIX), dtype=jnp.bool_), allowed], axis=1)
    scores = jnp.einsum('qhd,khd->hqk', queries, keys_all, precision=highest) * HEAD_DIM ** (-0.5)
    scores = low_back(scores)
    scores = jnp.where(visible[None], scores, -1e+30)
    weights = low(jax.nn.softmax(scores, axis=-1))
    context = jnp.einsum('hqk,khd->qhd', weights, values_all, precision=highest)
    context = both_ways(context.reshape(-1, HEADS * HEAD_DIM))
    return low_back(matmul(context, w_output))

def feed_forward(inputs, w_expand, w_contract, w_down, w_up):
    hidden = low(jax.nn.gelu(low_back(matmul(inputs, w_expand)), approximate=False))
    adapted = low(jax.nn.gelu(low_back(matmul(inputs, w_down)), approximate=False))
    return low_back(matmul(hidden, w_contract)) + adapter_scale * low_back(matmul(adapted, w_up))

def layer_pair(params, source, target, source_ids, target_ids):
    encoder_qkv, encoder_output, encoder_prefix, encoder_expand, encoder_contract, encoder_down, encoder_up, encoder_norms, decoder_qkv, decoder_output, decoder_prefix, cross_query, cross_kv, cross_output, cross_prefix, decoder_expand, decoder_contract, decoder_down, decoder_up, decoder_norms = params
    positions = jnp.arange(LENGTH, dtype=jnp.int32)
    encoder_allowed = source_ids[:, None] == source_ids[None, :]
    decoder_allowed = (target_ids[:, None] == target_ids[None, :]) & (positions[None, :] <= positions[:, None])
    cross_allowed = target_ids[:, None] == source_ids[None, :]
    encoder_in = low(source)
    attended = attention(encoder_in, encoder_in, encoder_qkv[0], encoder_qkv[1], encoder_qkv[2], encoder_output, encoder_prefix, encoder_allowed)
    middle = normalize(source + attended, encoder_norms, 0)
    branch = feed_forward(low(middle), encoder_expand, encoder_contract, encoder_down, encoder_up)
    memory = normalize(middle + branch, encoder_norms, 1)
    decoder_in = low(target)
    attended = attention(decoder_in, decoder_in, decoder_qkv[0], decoder_qkv[1], decoder_qkv[2], decoder_output, decoder_prefix, decoder_allowed)
    first_rows = normalize(target + attended, decoder_norms, 0)
    crossed = attention(low(first_rows), low(memory), cross_query, cross_kv[0], cross_kv[1], cross_output, cross_prefix, cross_allowed)
    second_rows = normalize(first_rows + crossed, decoder_norms, 1)
    branch = feed_forward(low(second_rows), decoder_expand, decoder_contract, decoder_down, decoder_up)
    return normalize(second_rows + branch, decoder_norms, 2)

def reference(source, target, source_segments, target_segments, cotangent, encoder_qkv, encoder_output, encoder_prefix, encoder_expand, encoder_contract, encoder_down, encoder_up, encoder_norms, decoder_qkv, decoder_output, decoder_prefix, cross_query, cross_kv, cross_output, cross_prefix, decoder_expand, decoder_contract, decoder_down, decoder_up, decoder_norms):
    params = tuple((tensor.astype(jnp.float32) for tensor in (encoder_qkv, encoder_output, encoder_prefix, encoder_expand, encoder_contract, encoder_down, encoder_up, encoder_norms, decoder_qkv, decoder_output, decoder_prefix, cross_query, cross_kv, cross_output, cross_prefix, decoder_expand, decoder_contract, decoder_down, decoder_up, decoder_norms)))
    row_count = MICRO * ROWS
    flat_source = source.reshape(row_count, LENGTH, D)
    flat_target = target.reshape(row_count, LENGTH, D)
    flat_cotangent = cotangent.reshape(row_count, LENGTH, D)
    flat_source_ids = source_segments.reshape(row_count, LENGTH)
    flat_target_ids = target_segments.reshape(row_count, LENGTH)

    def accumulate(totals, pieces):
        source_row, target_row, source_ids, target_ids, cotangent_row = pieces

        def forward(params_in, source_in, target_in):
            return layer_pair(params_in, source_in, target_in, source_ids, target_ids)
        output, pullback = jax.vjp(forward, params, source_row.astype(jnp.float32), target_row.astype(jnp.float32))
        gradients, source_back, target_back = pullback(cotangent_row.astype(jnp.float32))
        totals = jax.tree.map(jnp.add, totals, gradients)
        return (totals, (output.astype(jnp.bfloat16), source_back, target_back))
    initial = jax.tree.map(jnp.zeros_like, params)
    totals, (outputs, source_back, target_back) = lax.scan(accumulate, initial, (flat_source, flat_target, flat_source_ids, flat_target_ids, flat_cotangent))
    shape_out = (MICRO, ROWS, LENGTH, D)
    return (outputs.reshape(shape_out), source_back.reshape(shape_out), target_back.reshape(shape_out), totals[0], totals[1], totals[2], totals[3], totals[4], totals[5], totals[6], totals[7], totals[8], totals[9], totals[10], totals[11], totals[12], totals[13], totals[14], totals[15], totals[16], totals[17], totals[18], totals[19])
```

```python
import functools

import jax
import jax.numpy as jnp
from jax import lax
from jax.experimental import pallas as pl
from jax.experimental.pallas import tpu as pltpu
from jax.sharding import PartitionSpec as P

HEADS = 16
HEAD_DIM = 64
EPSILON = 1e-05
MASKED = -1e30
ADAPTER_SCALE = 4.0
SCALING = HEAD_DIM ** (-0.5)
PAD_PREFIX = 32
QUERY_BLOCK = 256

low = jnp.bfloat16
wide = jnp.float32


def dot(left, right, left_axis, right_axis):
    return lax.dot_general(
        left, right, (((left_axis,), (right_axis,)), ((), ())), preferred_element_type=wide
    )


def bit_list(count):
    bits = []
    value = 1
    while value < count:
        bits.append(value)
        value *= 2
    return bits


def swap_pairs(count, bit):
    return [(index, index ^ bit) for index in range(count)]


class Plane:
    def __init__(self, seq, block):
        self.seq = seq
        self.block = block
        bits = bit_list(seq)
        self.axes = bits[:1] + bits[1:][::-1]
        self.depth = len(bits)

    def order(self, micro):
        others = self.axes[1:]
        if micro % 2:
            others = others[::-1]
        return others + self.axes[:1]

    def gather(self, rows, micro):
        width = rows.shape[-1]
        value = rows.reshape((1,) * self.depth + rows.shape)
        for bit in self.order(micro):
            other = lax.ppermute(value, "seq", swap_pairs(self.seq, bit))
            value = jnp.concatenate([value, other], axis=self.axes.index(bit))
        return value.reshape(-1, width)

    def scatter(self, terms, micro):
        half = terms[0][0].shape[0] // 2
        width = terms[0][1].shape[1 - terms[0][2]]

        def part(start):
            total = None
            for left, right, axis in terms:
                value = dot(lax.slice_in_dim(left, start, start + half, axis=0), right, 1, axis)
                total = value if total is None else total + value
            return total

        order = self.order(micro)[::-1]
        sent = lax.ppermute(part(half).astype(low), "seq", swap_pairs(self.seq, order[0]))
        value = part(0) + sent.astype(wide)
        value = value.reshape((2,) * (self.depth - 1) + (self.block, width))
        for bit in order[1:]:
            axis = self.axes.index(bit) - 1
            keep = lax.slice_in_dim(value, 0, 1, axis=axis)
            send = lax.slice_in_dim(value, 1, 2, axis=axis).astype(low)
            sent = lax.ppermute(send, "seq", swap_pairs(self.seq, bit))
            value = keep + sent.astype(wide)
        return value.reshape(self.block, width)

    def relative(self, places, me):
        value = places.reshape((2,) * self.depth + (self.block,))
        for axis in range(self.depth):
            bit = 1 << (self.depth - 1 - axis)
            value = jnp.where((me & bit) != 0, jnp.flip(value, axis), value)
        value = jnp.moveaxis(value, self.depth - 1, 0)
        return value.reshape(-1)


def small_gather(value, axes):
    value = value[None]
    for name, count in axes[::-1]:
        me = lax.axis_index(name)
        for bit in bit_list(count):
            other = lax.ppermute(value, name, swap_pairs(count, bit))
            flip = (me & bit) != 0
            value = jnp.where(
                flip, jnp.concatenate([other, value]), jnp.concatenate([value, other])
            )
    return value


def small_scatter(value, axes):
    for name, count in axes:
        me = lax.axis_index(name)
        for bit in bit_list(count)[::-1]:
            half = value.shape[0] // 2
            flip = (me & bit) != 0
            lower, upper = value[:half], value[half:]
            sent = lax.ppermute(jnp.where(flip, lower, upper), name, swap_pairs(count, bit))
            value = jnp.where(flip, upper, lower) + sent
    return value[0]


def masked_scores(keys, queries, key_ids, query_ids, key_places, query_places, causal):
    scores = dot(keys, queries, 1, 1)
    allowed = key_ids == query_ids
    if causal:
        allowed = allowed & (key_places <= query_places)
    return jnp.where(allowed, scores, MASKED)


def prefix_scores(keys, queries, count):
    scores = dot(keys, queries, 1, 1)
    rows = lax.broadcasted_iota(jnp.int32, scores.shape, 0)
    return jnp.where(rows < count, scores, MASKED)


def attend_kernel(
    heads, offsets, count, causal, q_ref, kv_ref, prefix_ref, kid_ref, qid_ref, kpos_ref, qpos_ref,
    context_ref, logs_ref,
):
    q_at, k_at, v_at = offsets
    step = pl.program_id(0)
    block = context_ref.shape[0]
    rows = pl.ds(pl.multiple_of(step * block, block), block)
    for head in range(heads):
        lanes = slice(head * HEAD_DIM, (head + 1) * HEAD_DIM)
        at = head * HEAD_DIM
        queries = q_ref[rows, q_at + at : q_at + at + HEAD_DIM] * jnp.asarray(SCALING, low)
        keys = kv_ref[:, k_at + at : k_at + at + HEAD_DIM]
        values = kv_ref[:, v_at + at : v_at + at + HEAD_DIM]
        scores = masked_scores(
            keys, queries, kid_ref[...], qid_ref[...], kpos_ref[...], qpos_ref[...], causal
        )
        extra = prefix_scores(prefix_ref[0, :, lanes], queries, count)
        peak = jnp.maximum(
            jnp.max(scores, axis=0, keepdims=True), jnp.max(extra, axis=0, keepdims=True)
        )
        scores = jnp.exp(scores - peak)
        extra = jnp.exp(extra - peak)
        total = jnp.sum(scores, axis=0, keepdims=True) + jnp.sum(extra, axis=0, keepdims=True)
        context = dot(values, scores.astype(low), 0, 0)
        context = context + dot(prefix_ref[1, :, lanes], extra.astype(low), 0, 0)
        context = context / total
        context_ref[:, lanes] = context.T.astype(low)
        logs_ref[head : head + 1, :] = peak + jnp.log(total)


def attend_back_kernel(
    heads, offsets, count, causal, q_ref, kv_ref, prefix_ref, kid_ref, qid_ref, kpos_ref, qpos_ref,
    logs_ref, up_ref, grad_ref, prefix_grad_ref, k_sum, v_sum,
):
    q_at, k_at, v_at = offsets
    step = pl.program_id(0)
    width = heads * HEAD_DIM
    block = up_ref.shape[0]
    rows = pl.ds(pl.multiple_of(step * block, block), block)

    @pl.when(step == 0)
    def _():
        k_sum[...] = jnp.zeros_like(k_sum)
        v_sum[...] = jnp.zeros_like(v_sum)
        prefix_grad_ref[...] = jnp.zeros_like(prefix_grad_ref)

    for head in range(heads):
        lanes = slice(head * HEAD_DIM, (head + 1) * HEAD_DIM)
        at = head * HEAD_DIM
        queries = q_ref[rows, q_at + at : q_at + at + HEAD_DIM] * jnp.asarray(SCALING, low)
        keys = kv_ref[:, k_at + at : k_at + at + HEAD_DIM]
        values = kv_ref[:, v_at + at : v_at + at + HEAD_DIM]
        logs = logs_ref[head : head + 1, :]
        scores = masked_scores(
            keys, queries, kid_ref[...], qid_ref[...], kpos_ref[...], qpos_ref[...], causal
        )
        weights = jnp.exp(scores - logs)
        extra = jnp.exp(prefix_scores(prefix_ref[0, :, lanes], queries, count) - logs)
        up = up_ref[:, lanes]
        dots = dot(values, up, 1, 1)
        extra_dots = dot(prefix_ref[1, :, lanes], up, 1, 1)
        centre = jnp.sum(weights * dots, axis=0, keepdims=True) + jnp.sum(
            extra * extra_dots, axis=0, keepdims=True
        )
        slope = (weights * (dots - centre)).astype(low)
        extra_slope = (extra * (extra_dots - centre)).astype(low)
        query_grad = dot(keys, slope, 0, 0) + dot(prefix_ref[0, :, lanes], extra_slope, 0, 0)
        grad_ref[rows, lanes] = (query_grad * SCALING).T.astype(low)
        k_sum[:, lanes] += dot(slope, queries, 1, 0)
        v_sum[:, lanes] += dot(weights.astype(low), up, 1, 0)
        prefix_grad_ref[0, :, lanes] += dot(extra_slope, queries, 1, 0)
        prefix_grad_ref[1, :, lanes] += dot(extra.astype(low), up, 1, 0)

    @pl.when(step == pl.num_programs(0) - 1)
    def _():
        grad_ref[:, width : 2 * width] = k_sum[...].astype(low)
        grad_ref[:, 2 * width : 3 * width] = v_sum[...].astype(low)


def whole_spec(array):
    rank = len(array.shape)
    return pl.BlockSpec(array.shape, lambda step: (0,) * rank)


def attend_forward(queries, keyvalues, offsets, prefix, count, ids, causal):
    key_ids, query_ids, key_places, query_places = ids
    length = queries.shape[0]
    width = prefix.shape[2]
    heads = width // HEAD_DIM
    block = min(QUERY_BLOCK, length)
    row_spec = pl.BlockSpec((1, block), lambda step: (0, step))
    pairs = length * (keyvalues.shape[0] + PAD_PREFIX) * heads
    return pl.pallas_call(
        functools.partial(attend_kernel, heads, offsets, count, causal),
        grid=(length // block,),
        out_shape=(
            jax.ShapeDtypeStruct((length, width), low),
            jax.ShapeDtypeStruct((heads, length), wide),
        ),
        in_specs=[
            whole_spec(queries),
            whole_spec(keyvalues),
            whole_spec(prefix),
            whole_spec(key_ids),
            row_spec,
            whole_spec(key_places),
            row_spec,
        ],
        out_specs=(
            pl.BlockSpec((block, width), lambda step: (step, 0)),
            pl.BlockSpec((heads, block), lambda step: (0, step)),
        ),
        compiler_params=pltpu.CompilerParams(vmem_limit_bytes=40 * 1024 * 1024),
        cost_estimate=pl.CostEstimate(
            flops=pairs * HEAD_DIM * 4 * 4, bytes_accessed=4 * 2 * length * width, transcendentals=pairs
        ),
    )(queries, keyvalues, prefix, key_ids, query_ids, key_places, query_places)


def attend_backward(queries, keyvalues, offsets, prefix, count, ids, causal, logs, upstream):
    key_ids, query_ids, key_places, query_places = ids
    length = queries.shape[0]
    width = prefix.shape[2]
    heads = width // HEAD_DIM
    block = min(QUERY_BLOCK, length)
    row_spec = pl.BlockSpec((1, block), lambda step: (0, step))
    pairs = length * (keyvalues.shape[0] + PAD_PREFIX) * heads
    return pl.pallas_call(
        functools.partial(attend_back_kernel, heads, offsets, count, causal),
        grid=(length // block,),
        out_shape=(
            jax.ShapeDtypeStruct((length, 3 * width), low),
            jax.ShapeDtypeStruct((2, PAD_PREFIX, width), wide),
        ),
        in_specs=[
            whole_spec(queries),
            whole_spec(keyvalues),
            whole_spec(prefix),
            whole_spec(key_ids),
            row_spec,
            whole_spec(key_places),
            row_spec,
            pl.BlockSpec((heads, block), lambda step: (0, step)),
            pl.BlockSpec((block, width), lambda step: (step, 0)),
        ],
        out_specs=(
            pl.BlockSpec((length, 3 * width), lambda step: (0, 0)),
            pl.BlockSpec((2, PAD_PREFIX, width), lambda step: (0, 0, 0)),
        ),
        scratch_shapes=[
            pltpu.VMEM((length, width), wide),
            pltpu.VMEM((length, width), wide),
        ],
        compiler_params=pltpu.CompilerParams(vmem_limit_bytes=40 * 1024 * 1024),
        cost_estimate=pl.CostEstimate(
            flops=pairs * HEAD_DIM * 10 * 4, bytes_accessed=8 * 2 * length * width, transcendentals=pairs
        ),
    )(queries, keyvalues, prefix, key_ids, query_ids, key_places, query_places, logs, upstream)


def normalized(tensor):
    average = jnp.mean(tensor, axis=-1, keepdims=True)
    centered = tensor - average
    spread = jnp.mean(centered * centered, axis=-1, keepdims=True)
    inverse = lax.rsqrt(spread + EPSILON)
    return centered * inverse, inverse


def layer_norm(tensor, scales):
    return normalized(tensor)[0] * scales[0] + scales[1]


def norm_back(upstream, tensor, scales):
    unit, inverse = normalized(tensor)
    slope = upstream * scales[0]
    grad = inverse * (
        slope
        - jnp.mean(slope, axis=-1, keepdims=True)
        - unit * jnp.mean(slope * unit, axis=-1, keepdims=True)
    )
    return grad, jnp.stack([jnp.sum(upstream * unit, axis=0), jnp.sum(upstream, axis=0)])


def gelu_exact(tensor):
    return jax.nn.gelu(tensor, approximate=False)


def gelu_slope(tensor):
    _, pullback = jax.vjp(gelu_exact, tensor)
    return pullback(jnp.ones_like(tensor))[0]


def outer_sum(lefts, rights):
    total = None
    for left, right in zip(lefts, rights):
        value = dot(left, right, 0, 0)
        total = value if total is None else total + value
    return total


def local(
    seq, ranks,
    source, target, source_segments, target_segments, cotangent,
    encoder_qkv, encoder_output, encoder_prefix, encoder_expand, encoder_contract, encoder_down,
    encoder_up, encoder_norms, decoder_qkv, decoder_output, decoder_prefix, cross_query, cross_kv,
    cross_output, cross_prefix, decoder_expand, decoder_contract, decoder_down, decoder_up,
    decoder_norms,
):
    micro_count, batch_rows, block, width = source.shape
    length = source_segments.shape[2]
    me = lax.axis_index("seq")
    plane = Plane(seq, block)
    stacked = micro_count * batch_rows
    every = range(stacked)
    head_width = width // seq
    slice_cols = encoder_output.shape[1]
    count = encoder_prefix.shape[1]
    hidden = encoder_contract.shape[0] // seq
    adapt = encoder_up.shape[0] // seq
    both = hidden + adapt

    sources = [row for row in source.reshape(stacked, block, width)]
    targets = [row for row in target.reshape(stacked, block, width)]
    upstreams = [row for row in cotangent.reshape(stacked, block, width)]

    places = plane.relative(jnp.arange(length, dtype=jnp.int32), me)
    place_pair = (places[:, None], places[None, :])
    source_ids = [plane.relative(row, me) for row in source_segments.reshape(stacked, length)]
    target_ids = [plane.relative(row, me) for row in target_segments.reshape(stacked, length)]

    def id_set(keys, queries):
        return (keys[:, None], queries[None, :]) + place_pair

    encoder_ids = [id_set(source_ids[m], source_ids[m]) for m in every]
    decoder_ids = [id_set(target_ids[m], target_ids[m]) for m in every]
    cross_ids = [id_set(source_ids[m], target_ids[m]) for m in every]

    def columns(weight):
        return jnp.swapaxes(weight, -1, -2)

    def gather_rows(value):
        return lax.all_gather(value, "rows", axis=0, tiled=False)

    def stack_columns(pieces):
        gathered = gather_rows(jnp.concatenate(pieces, axis=0))
        outs = []
        start = 0
        for piece in pieces:
            size = piece.shape[0]
            outs.append(gathered[:, start : start + size])
            start += size
        return outs

    def flat_columns(gathered, parts):
        value = gathered.reshape(ranks, parts, slice_cols, width)
        return jnp.swapaxes(value, 0, 1).reshape(parts * ranks * slice_cols, width)

    def split_rows(weight):
        value = columns(weight)
        return value.reshape(slice_cols, seq, -1)

    def exchange(value):
        return lax.all_to_all(value, "seq", 1, 1, tiled=False)

    row_pieces = jnp.concatenate(
        [
            split_rows(encoder_output),
            split_rows(decoder_output),
            split_rows(cross_output),
            split_rows(encoder_contract),
            split_rows(encoder_up) * jnp.asarray(ADAPTER_SCALE, low),
            split_rows(decoder_contract),
            split_rows(decoder_up) * jnp.asarray(ADAPTER_SCALE, low),
        ],
        axis=2,
    )
    row_pieces = lax.all_to_all(row_pieces, "seq", 1, 0, tiled=False).reshape(
        seq, slice_cols, -1
    )

    def row_weight(start, size):
        gathered = gather_rows(row_pieces[:, :, start : start + size])
        return jnp.swapaxes(gathered, 0, 1).reshape(width, size)

    qkv_parts = gather_rows(
        jnp.concatenate(
            [
                columns(encoder_qkv).reshape(-1, width),
                columns(decoder_qkv).reshape(-1, width),
            ]
        )
    )
    encoder_in = flat_columns(qkv_parts[:, : 3 * slice_cols], 3)
    decoder_in = flat_columns(qkv_parts[:, 3 * slice_cols :], 3)
    outputs_low = row_weight(0, 3 * head_width)
    encoder_out = outputs_low[:, :head_width]
    decoder_out = outputs_low[:, head_width : 2 * head_width]
    cross_out = outputs_low[:, 2 * head_width :]

    def ffn_in(expand, down):
        gathered = gather_rows(jnp.concatenate([columns(expand), columns(down)]))
        cut = expand.shape[1]
        return jnp.concatenate(
            [gathered[:, :cut].reshape(-1, width), gathered[:, cut:].reshape(-1, width)]
        )

    encoder_one = ffn_in(encoder_expand, encoder_down)
    encoder_two = row_weight(3 * head_width, both)
    cross_parts = gather_rows(
        jnp.concatenate([columns(cross_query), columns(cross_kv).reshape(-1, width)])
    )
    cross_in = flat_columns(cross_parts, 3)
    cross_q_in, cross_kv_in = cross_in[:head_width], cross_in[head_width:]
    decoder_one = ffn_in(decoder_expand, decoder_down)
    decoder_two = row_weight(3 * head_width + both, both)

    prefixes = small_gather(
        jnp.concatenate([encoder_prefix, decoder_prefix, cross_prefix]), [("rows", ranks)]
    )
    prefixes = jnp.moveaxis(prefixes, 0, 2).reshape(6, count, head_width)
    prefixes = jnp.pad(prefixes, ((0, 0), (0, PAD_PREFIX - count), (0, 0)))
    encoder_pre, decoder_pre, cross_pre = prefixes[0:2], prefixes[2:4], prefixes[4:6]

    norm_axes = [("seq", seq), ("rows", ranks)]
    scales = small_gather(
        jnp.concatenate([encoder_norms, decoder_norms]), norm_axes
    )
    scales = jnp.moveaxis(scales, 0, 2).reshape(-1, 2, width).astype(wide)
    norm_count = encoder_norms.shape[0]

    self_offsets = (0, head_width, 2 * head_width)
    cross_offsets = (0, 0, head_width)

    def ffn_forward(rows, weight_one):
        before = dot(rows, weight_one, 1, 1)
        return before, gelu_exact(before).astype(low)

    source_all = [plane.gather(sources[m], m) for m in every]
    target_all = [plane.gather(targets[m], m) for m in every]
    encoder_qkvs = [dot(source_all[m], encoder_in, 1, 1).astype(low) for m in every]
    decoder_qkvs = [dot(target_all[m], decoder_in, 1, 1).astype(low) for m in every]
    encoder_ctx, encoder_logs, resid_one, middle, middle_all = [], [], [], [], []
    decoder_ctx, decoder_logs, resid_three, first, first_all = [], [], [], [], []
    for m in every:
        context, logs = attend_forward(
            encoder_qkvs[m], encoder_qkvs[m], self_offsets, encoder_pre, count, encoder_ids[m], False
        )
        encoder_ctx.append(context)
        encoder_logs.append(logs)
        attended = plane.scatter([(context, encoder_out, 1)], m)
        resid_one.append(sources[m].astype(wide) + attended)
        middle.append(layer_norm(resid_one[m], scales[0]))
        middle_all.append(plane.gather(middle[m].astype(low), m))
    for m in every:
        context, logs = attend_forward(
            decoder_qkvs[m], decoder_qkvs[m], self_offsets, decoder_pre, count, decoder_ids[m], True
        )
        decoder_ctx.append(context)
        decoder_logs.append(logs)
        attended = plane.scatter([(context, decoder_out, 1)], m)
        resid_three.append(targets[m].astype(wide) + attended)
        first.append(layer_norm(resid_three[m], scales[norm_count]))
        first_all.append(plane.gather(first[m].astype(low), m))
    encoder_before, encoder_hidden, resid_two, memory_all = [], [], [], []
    for m in every:
        before, after = ffn_forward(middle_all[m], encoder_one)
        encoder_before.append(before)
        encoder_hidden.append(after)
        branch = plane.scatter([(after, encoder_two, 1)], m)
        resid_two.append(middle[m] + branch)
        memory = layer_norm(resid_two[m], scales[1])
        memory_all.append(plane.gather(memory.astype(low), m))
    cross_q = [dot(first_all[m], cross_q_in, 1, 1).astype(low) for m in every]
    cross_kvs = [dot(memory_all[m], cross_kv_in, 1, 1).astype(low) for m in every]
    cross_ctx, cross_logs, resid_four, second, second_all = [], [], [], [], []
    for m in every:
        context, logs = attend_forward(
            cross_q[m], cross_kvs[m], cross_offsets, cross_pre, count, cross_ids[m], False
        )
        cross_ctx.append(context)
        cross_logs.append(logs)
        crossed = plane.scatter([(context, cross_out, 1)], m)
        resid_four.append(first[m] + crossed)
        second.append(layer_norm(resid_four[m], scales[norm_count + 1]))
        second_all.append(plane.gather(second[m].astype(low), m))
    decoder_before, decoder_hidden, resid_five, results = [], [], [], []
    for m in every:
        before, after = ffn_forward(second_all[m], decoder_one)
        decoder_before.append(before)
        decoder_hidden.append(after)
        branch = plane.scatter([(after, decoder_two, 1)], m)
        resid_five.append(second[m] + branch)
        results.append(layer_norm(resid_five[m], scales[norm_count + 2]).astype(low))

    def scatter_ranks(value):
        return lax.psum_scatter(value.astype(low), "rows", scatter_dimension=0, tiled=False)

    def reduce_columns(grad, parts):
        value = grad.reshape(parts, ranks, slice_cols, width)
        return scatter_ranks(jnp.swapaxes(value, 0, 1))

    def reduce_rows(grad):
        value = grad.reshape(seq, ranks, slice_cols, -1)
        return scatter_ranks(jnp.swapaxes(value, 0, 1))

    def reduce_ffn_in(grad):
        value = jnp.concatenate(
            [grad[:hidden].reshape(ranks, -1, width), grad[hidden:].reshape(ranks, -1, width)],
            axis=1,
        )
        return scatter_ranks(value)

    def ffn_backward(low_all, befores, weight_one, weight_two, m):
        slope = dot(low_all, weight_two, 1, 0) * gelu_slope(befores[m])
        slope = slope.astype(low)
        return slope, plane.scatter([(slope, weight_one, 0)], m)

    norm_grads = {}

    def norm_step(index, upstream_rows, residuals):
        grads, sums = [], None
        for m in every:
            grad, pair = norm_back(upstream_rows[m], residuals[m], scales[index])
            grads.append(grad)
            sums = pair if sums is None else sums + pair
        norm_grads[index] = sums
        return grads

    third_in = norm_step(norm_count + 2, [u.astype(wide) for u in upstreams], resid_five)
    third_all = [plane.gather(third_in[m].astype(low), m) for m in every]
    slopes, second_up = [], []
    for m in every:
        slope, from_ffn = ffn_backward(third_all[m], decoder_before, decoder_one, decoder_two, m)
        slopes.append(slope)
        second_up.append(third_in[m] + from_ffn)
    decoder_two_grad = reduce_rows(outer_sum(third_all, decoder_hidden))
    decoder_one_grad = reduce_ffn_in(outer_sum(slopes, second_all))

    second_in = norm_step(norm_count + 1, second_up, resid_four)
    second_low = [plane.gather(second_in[m].astype(low), m) for m in every]
    cross_grads, cross_pre_grad, first_up, memory_up = [], None, [], []
    for m in every:
        context_grad = dot(second_low[m], cross_out, 1, 0).astype(low)
        grads, pre = attend_backward(
            cross_q[m], cross_kvs[m], cross_offsets, cross_pre, count, cross_ids[m], False,
            cross_logs[m], context_grad,
        )
        cross_grads.append(grads)
        cross_pre_grad = pre if cross_pre_grad is None else cross_pre_grad + pre
        memory_up.append(plane.scatter([(grads[:, head_width:], cross_kv_in, 0)], m))
        first_up.append(
            second_in[m] + plane.scatter([(grads[:, :head_width], cross_q_in, 0)], m)
        )
    cross_out_grad = reduce_rows(outer_sum(second_low, cross_ctx))
    cross_in_grad = reduce_columns(
        jnp.concatenate(
            [
                outer_sum([g[:, :head_width] for g in cross_grads], first_all),
                outer_sum([g[:, head_width:] for g in cross_grads], memory_all),
            ]
        ),
        3,
    )

    memory_in = norm_step(1, memory_up, resid_two)
    first_in = norm_step(norm_count, first_up, resid_three)
    memory_low = [plane.gather(memory_in[m].astype(low), m) for m in every]
    first_low = [plane.gather(first_in[m].astype(low), m) for m in every]

    slopes, middle_up = [], []
    for m in every:
        slope, from_ffn = ffn_backward(memory_low[m], encoder_before, encoder_one, encoder_two, m)
        slopes.append(slope)
        middle_up.append(memory_in[m] + from_ffn)
    encoder_two_grad = reduce_rows(outer_sum(memory_low, encoder_hidden))
    encoder_one_grad = reduce_ffn_in(outer_sum(slopes, middle_all))

    def self_backward(low_all, out_weight, in_weight, qkvs, prefix, ids, causal, logs, rows_in):
        grads_all, prefix_sum, totals = [], None, []
        for m in every:
            context_grad = dot(low_all[m], out_weight, 1, 0).astype(low)
            grads, pre = attend_backward(
                qkvs[m], qkvs[m], self_offsets, prefix, count, ids[m], causal, logs[m], context_grad
            )
            grads_all.append(grads)
            prefix_sum = pre if prefix_sum is None else prefix_sum + pre
            totals.append(rows_in[m] + plane.scatter([(grads, in_weight, 0)], m))
        return grads_all, prefix_sum, totals

    decoder_grads, decoder_pre_grad, target_grads = self_backward(
        first_low, decoder_out, decoder_in, decoder_qkvs, decoder_pre, decoder_ids, True,
        decoder_logs, first_in,
    )
    decoder_out_grad = reduce_rows(outer_sum(first_low, decoder_ctx))
    decoder_in_grad = reduce_columns(outer_sum(decoder_grads, target_all), 3)

    middle_in = norm_step(0, middle_up, resid_one)
    middle_low = [plane.gather(middle_in[m].astype(low), m) for m in every]
    encoder_grads, encoder_pre_grad, source_grads = self_backward(
        middle_low, encoder_out, encoder_in, encoder_qkvs, encoder_pre, encoder_ids, False,
        encoder_logs, middle_in,
    )
    encoder_out_grad = reduce_rows(outer_sum(middle_low, encoder_ctx))
    encoder_in_grad = reduce_columns(outer_sum(encoder_grads, source_all), 3)

    def give_back(pieces):
        value = jnp.concatenate(pieces, axis=2)
        return lax.all_to_all(value, "seq", 0, 1, tiled=False)

    decoder_rows = give_back([decoder_two_grad, cross_out_grad, decoder_out_grad])
    encoder_rows = give_back([encoder_two_grad, encoder_out_grad])

    def row_grad(value, start, size, scale=None):
        piece = value[:, :, start : start + size].astype(wide)
        if scale is not None:
            piece = piece * scale
        return piece.reshape(slice_cols, -1).T

    def column_grad(value):
        return jnp.swapaxes(value.astype(wide), -1, -2)

    prefix_total = jnp.concatenate([encoder_pre_grad, decoder_pre_grad, cross_pre_grad])[:, :count]
    prefix_total = jnp.moveaxis(prefix_total.reshape(6, count, ranks, slice_cols), 2, 0)
    prefix_total = small_scatter(prefix_total, [("rows", ranks)])
    norm_total = jnp.stack([norm_grads[index] for index in sorted(norm_grads)])
    norm_total = jnp.moveaxis(norm_total.reshape(-1, 2, seq * ranks, slice_cols), 2, 0)
    norm_total = small_scatter(norm_total, norm_axes)

    cut = encoder_expand.shape[1]
    shape_out = source.shape
    return (
        jnp.stack(results).reshape(shape_out),
        jnp.stack(source_grads).reshape(shape_out),
        jnp.stack(target_grads).reshape(shape_out),
        column_grad(encoder_in_grad),
        row_grad(encoder_rows, both, head_width),
        prefix_total[0:2],
        column_grad(encoder_one_grad[:cut]),
        row_grad(encoder_rows, 0, hidden),
        column_grad(encoder_one_grad[cut:]),
        row_grad(encoder_rows, hidden, adapt, ADAPTER_SCALE),
        norm_total[:norm_count],
        column_grad(decoder_in_grad),
        row_grad(decoder_rows, both + head_width, head_width),
        prefix_total[2:4],
        column_grad(cross_in_grad[0]),
        column_grad(cross_in_grad[1:]),
        row_grad(decoder_rows, both, head_width),
        prefix_total[4:6],
        column_grad(decoder_one_grad[:cut]),
        row_grad(decoder_rows, 0, hidden),
        column_grad(decoder_one_grad[cut:]),
        row_grad(decoder_rows, hidden, adapt, ADAPTER_SCALE),
        norm_total[norm_count:],
    )


def solution(mesh):
    rows = P(None, "rows", "seq", None)
    ids = P(None, "rows", None)
    flat = P(None, ("seq", "rows"))
    deep = P(None, None, ("seq", "rows"))
    weights = (
        deep, flat, deep, flat, flat, flat, flat, deep, deep, flat, deep, flat, deep, flat, deep,
        flat, flat, flat, flat, deep,
    )
    body = functools.partial(local, mesh.shape["seq"], mesh.shape["rows"])
    return jax.shard_map(
        body,
        mesh=mesh,
        in_specs=(rows, rows, ids, ids, rows) + weights,
        out_specs=(rows, rows, rows) + weights,
        check_vma=False,
    )
```

```python
import functools

import jax
import jax.numpy as jnp
from jax import lax
from jax.experimental import pallas as pl
from jax.experimental.layout import Layout, with_layout_constraint
from jax.experimental.pallas import tpu as pltpu
from jax.sharding import PartitionSpec as P

HEADS = 16
HEAD_DIM = 64
EPSILON = 1e-05
MASKED = -1e30
ADAPTER_SCALE = 4.0
SCALING = HEAD_DIM ** (-0.5)
PAD_PREFIX = 32
QUERY_BLOCK = 256
CHUNK = 256
LANES = 128
VMEM_LIMIT = 56 * 1024 * 1024
HALF_ROOT = 0.7071067811865476
DENSITY = 0.3989422804014327

low = jnp.bfloat16
wide = jnp.float32


def dot(left, right, left_axis, right_axis):
    return lax.dot_general(
        left, right, (((left_axis,), (right_axis,)), ((), ())), preferred_element_type=wide
    )


def bit_list(count):
    bits = []
    value = 1
    while value < count:
        bits.append(value)
        value *= 2
    return bits


def swap_pairs(count, bit):
    return [(index, index ^ bit) for index in range(count)]


class Plane:
    def __init__(self, seq, block):
        self.seq = seq
        self.block = block
        bits = bit_list(seq)
        self.axes = bits[:1] + bits[1:][::-1]
        self.depth = len(bits)

    def order(self, micro):
        others = self.axes[1:]
        if micro % 2:
            others = others[::-1]
        return others + self.axes[:1]

    def gather(self, rows, micro):
        width = rows.shape[-1]
        value = rows.reshape((1,) * self.depth + rows.shape)
        for bit in self.order(micro):
            other = lax.ppermute(value, "seq", swap_pairs(self.seq, bit))
            value = jnp.concatenate([value, other], axis=self.axes.index(bit))
        return value.reshape(-1, width)

    def scatter(self, terms, micro):
        half = terms[0][0].shape[0] // 2
        width = terms[0][1].shape[1 - terms[0][2]]

        def part(start):
            total = None
            for left, right, axis in terms:
                value = dot(lax.slice_in_dim(left, start, start + half, axis=0), right, 1, axis)
                total = value if total is None else total + value
            return total

        order = self.order(micro)[::-1]
        sent = lax.ppermute(part(half).astype(low), "seq", swap_pairs(self.seq, order[0]))
        value = part(0) + sent.astype(wide)
        value = value.reshape((2,) * (self.depth - 1) + (self.block, width))
        for bit in order[1:]:
            axis = self.axes.index(bit) - 1
            keep = lax.slice_in_dim(value, 0, 1, axis=axis)
            send = lax.slice_in_dim(value, 1, 2, axis=axis).astype(low)
            sent = lax.ppermute(send, "seq", swap_pairs(self.seq, bit))
            value = keep + sent.astype(wide)
        return value.reshape(self.block, width)

    def relative(self, places, me):
        value = places.reshape((2,) * self.depth + (self.block,))
        for axis in range(self.depth):
            bit = 1 << (self.depth - 1 - axis)
            value = jnp.where((me & bit) != 0, jnp.flip(value, axis), value)
        value = jnp.moveaxis(value, self.depth - 1, 0)
        return value.reshape(-1)


def small_gather(value, axes):
    value = value[None]
    for name, count in axes[::-1]:
        me = lax.axis_index(name)
        for bit in bit_list(count):
            other = lax.ppermute(value, name, swap_pairs(count, bit))
            flip = (me & bit) != 0
            value = jnp.where(
                flip, jnp.concatenate([other, value]), jnp.concatenate([value, other])
            )
    return value


def small_scatter(value, axes):
    for name, count in axes:
        me = lax.axis_index(name)
        for bit in bit_list(count)[::-1]:
            half = value.shape[0] // 2
            flip = (me & bit) != 0
            lower, upper = value[:half], value[half:]
            sent = lax.ppermute(jnp.where(flip, lower, upper), name, swap_pairs(count, bit))
            value = jnp.where(flip, upper, lower) + sent
    return value[0]


def masked_scores(keys, queries, key_ids, query_ids, key_places, query_places, causal):
    scores = dot(keys, queries, 1, 1)
    allowed = key_ids == query_ids
    if causal:
        allowed = allowed & (key_places <= query_places)
    return jnp.where(allowed, scores, MASKED)


def prefix_scores(keys, queries, count):
    scores = dot(keys, queries, 1, 1)
    rows = lax.broadcasted_iota(jnp.int32, scores.shape, 0)
    return jnp.where(rows < count, scores, MASKED)


def attend_kernel(
    heads, offsets, count, causal, q_ref, kv_ref, prefix_ref, kid_ref, qid_ref, kpos_ref, qpos_ref,
    context_ref, logs_ref,
):
    q_at, k_at, v_at = offsets
    step = pl.program_id(0)
    block = context_ref.shape[0]
    rows = pl.ds(pl.multiple_of(step * block, block), block)
    for head in range(heads):
        lanes = slice(head * HEAD_DIM, (head + 1) * HEAD_DIM)
        at = head * HEAD_DIM
        queries = q_ref[rows, q_at + at : q_at + at + HEAD_DIM] * jnp.asarray(SCALING, low)
        keys = kv_ref[:, k_at + at : k_at + at + HEAD_DIM]
        values = kv_ref[:, v_at + at : v_at + at + HEAD_DIM]
        scores = masked_scores(
            keys, queries, kid_ref[...], qid_ref[...], kpos_ref[...], qpos_ref[...], causal
        )
        extra = prefix_scores(prefix_ref[0, :, lanes], queries, count)
        peak = jnp.maximum(
            jnp.max(scores, axis=0, keepdims=True), jnp.max(extra, axis=0, keepdims=True)
        )
        scores = jnp.exp(scores - peak)
        extra = jnp.exp(extra - peak)
        total = jnp.sum(scores, axis=0, keepdims=True) + jnp.sum(extra, axis=0, keepdims=True)
        context = dot(values, scores.astype(low), 0, 0)
        context = context + dot(prefix_ref[1, :, lanes], extra.astype(low), 0, 0)
        context = context / total
        context_ref[:, lanes] = context.T.astype(low)
        logs_ref[head : head + 1, :] = peak + jnp.log(total)


def attend_back_kernel(
    heads, offsets, count, causal, q_ref, kv_ref, prefix_ref, kid_ref, qid_ref, kpos_ref, qpos_ref,
    logs_ref, up_ref, grad_ref, prefix_grad_ref, k_sum, v_sum,
):
    q_at, k_at, v_at = offsets
    step = pl.program_id(0)
    width = heads * HEAD_DIM
    block = up_ref.shape[0]
    rows = pl.ds(pl.multiple_of(step * block, block), block)

    @pl.when(step == 0)
    def _():
        k_sum[...] = jnp.zeros_like(k_sum)
        v_sum[...] = jnp.zeros_like(v_sum)
        prefix_grad_ref[...] = jnp.zeros_like(prefix_grad_ref)

    for head in range(heads):
        lanes = slice(head * HEAD_DIM, (head + 1) * HEAD_DIM)
        at = head * HEAD_DIM
        queries = q_ref[rows, q_at + at : q_at + at + HEAD_DIM] * jnp.asarray(SCALING, low)
        keys = kv_ref[:, k_at + at : k_at + at + HEAD_DIM]
        values = kv_ref[:, v_at + at : v_at + at + HEAD_DIM]
        logs = logs_ref[head : head + 1, :]
        scores = masked_scores(
            keys, queries, kid_ref[...], qid_ref[...], kpos_ref[...], qpos_ref[...], causal
        )
        weights = jnp.exp(scores - logs)
        extra = jnp.exp(prefix_scores(prefix_ref[0, :, lanes], queries, count) - logs)
        up = up_ref[:, lanes]
        dots = dot(values, up, 1, 1)
        extra_dots = dot(prefix_ref[1, :, lanes], up, 1, 1)
        centre = jnp.sum(weights * dots, axis=0, keepdims=True) + jnp.sum(
            extra * extra_dots, axis=0, keepdims=True
        )
        slope = (weights * (dots - centre)).astype(low)
        extra_slope = (extra * (extra_dots - centre)).astype(low)
        query_grad = dot(keys, slope, 0, 0) + dot(prefix_ref[0, :, lanes], extra_slope, 0, 0)
        grad_ref[rows, lanes] = (query_grad * SCALING).T.astype(low)
        k_sum[:, lanes] += dot(slope, queries, 1, 0)
        v_sum[:, lanes] += dot(weights.astype(low), up, 1, 0)
        prefix_grad_ref[0, :, lanes] += dot(extra_slope, queries, 1, 0)
        prefix_grad_ref[1, :, lanes] += dot(extra.astype(low), up, 1, 0)

    @pl.when(step == pl.num_programs(0) - 1)
    def _():
        grad_ref[:, width : 2 * width] = k_sum[...].astype(low)
        grad_ref[:, 2 * width : 3 * width] = v_sum[...].astype(low)


def whole_spec(array):
    rank = len(array.shape)
    return pl.BlockSpec(array.shape, lambda step: (0,) * rank)


def attend_forward(queries, keyvalues, offsets, prefix, count, ids, causal):
    key_ids, query_ids, key_places, query_places = ids
    length = queries.shape[0]
    width = prefix.shape[2]
    heads = width // HEAD_DIM
    block = min(QUERY_BLOCK, length)
    row_spec = pl.BlockSpec((1, block), lambda step: (0, step))
    pairs = length * (keyvalues.shape[0] + PAD_PREFIX) * heads
    return pl.pallas_call(
        functools.partial(attend_kernel, heads, offsets, count, causal),
        grid=(length // block,),
        out_shape=(
            jax.ShapeDtypeStruct((length, width), low),
            jax.ShapeDtypeStruct((heads, length), wide),
        ),
        in_specs=[
            whole_spec(queries),
            whole_spec(keyvalues),
            whole_spec(prefix),
            whole_spec(key_ids),
            row_spec,
            whole_spec(key_places),
            row_spec,
        ],
        out_specs=(
            pl.BlockSpec((block, width), lambda step: (step, 0)),
            pl.BlockSpec((heads, block), lambda step: (0, step)),
        ),
        compiler_params=pltpu.CompilerParams(vmem_limit_bytes=40 * 1024 * 1024),
        cost_estimate=pl.CostEstimate(
            flops=pairs * HEAD_DIM * 4 * 4, bytes_accessed=4 * 2 * length * width, transcendentals=pairs
        ),
    )(queries, keyvalues, prefix, key_ids, query_ids, key_places, query_places)


def attend_backward(queries, keyvalues, offsets, prefix, count, ids, causal, logs, upstream):
    key_ids, query_ids, key_places, query_places = ids
    length = queries.shape[0]
    width = prefix.shape[2]
    heads = width // HEAD_DIM
    block = min(QUERY_BLOCK, length)
    row_spec = pl.BlockSpec((1, block), lambda step: (0, step))
    pairs = length * (keyvalues.shape[0] + PAD_PREFIX) * heads
    return pl.pallas_call(
        functools.partial(attend_back_kernel, heads, offsets, count, causal),
        grid=(length // block,),
        out_shape=(
            jax.ShapeDtypeStruct((length, 3 * width), low),
            jax.ShapeDtypeStruct((2, PAD_PREFIX, width), wide),
        ),
        in_specs=[
            whole_spec(queries),
            whole_spec(keyvalues),
            whole_spec(prefix),
            whole_spec(key_ids),
            row_spec,
            whole_spec(key_places),
            row_spec,
            pl.BlockSpec((heads, block), lambda step: (0, step)),
            pl.BlockSpec((block, width), lambda step: (step, 0)),
        ],
        out_specs=(
            pl.BlockSpec((length, 3 * width), lambda step: (0, 0)),
            pl.BlockSpec((2, PAD_PREFIX, width), lambda step: (0, 0, 0)),
        ),
        scratch_shapes=[
            pltpu.VMEM((length, width), wide),
            pltpu.VMEM((length, width), wide),
        ],
        compiler_params=pltpu.CompilerParams(vmem_limit_bytes=40 * 1024 * 1024),
        cost_estimate=pl.CostEstimate(
            flops=pairs * HEAD_DIM * 10 * 4, bytes_accessed=8 * 2 * length * width, transcendentals=pairs
        ),
    )(queries, keyvalues, prefix, key_ids, query_ids, key_places, query_places, logs, upstream)


def normalized(tensor):
    average = jnp.mean(tensor, axis=-1, keepdims=True)
    centered = tensor - average
    spread = jnp.mean(centered * centered, axis=-1, keepdims=True)
    inverse = lax.rsqrt(spread + EPSILON)
    return centered * inverse, inverse


def layer_norm(tensor, scales):
    return normalized(tensor)[0] * scales[0] + scales[1]


def norm_back(upstream, tensor, scales):
    unit, inverse = normalized(tensor)
    slope = upstream * scales[0]
    grad = inverse * (
        slope
        - jnp.mean(slope, axis=-1, keepdims=True)
        - unit * jnp.mean(slope * unit, axis=-1, keepdims=True)
    )
    return (
        grad,
        jnp.sum(upstream * unit, axis=0, keepdims=True),
        jnp.sum(upstream, axis=0, keepdims=True),
    )


def gelu_exact(tensor):
    return tensor * (0.5 + 0.5 * lax.erf(tensor * HALF_ROOT))


def gelu_slope(tensor):
    density = jnp.exp(-0.5 * tensor * tensor) * DENSITY
    return 0.5 + 0.5 * lax.erf(tensor * HALF_ROOT) + tensor * density


class Links:
    def __init__(self, seq):
        self.seq = seq
        self.far = [bit for bit in bit_list(seq) if bit > 1]
        self.orders = [self.far, self.far[::-1]]
        self.half = seq // 2
        self.me = lax.axis_index("seq")

    def place(self, mask):
        return (mask & 1) * self.half + (mask >> 1)

    def device(self, bit):
        return {"seq": jnp.bitwise_xor(self.me, bit)}

    def enter(self):
        barrier = pltpu.get_barrier_semaphore()
        bits = bit_list(self.seq)
        for bit in bits:
            pl.semaphore_signal(
                barrier, inc=1, device_id=self.device(bit), device_id_type=pl.DeviceIdType.MESH
            )
        pl.semaphore_wait(barrier, len(bits))

    def copy(self, source, target, send_sem, recv_sem, bit):
        return pltpu.make_async_remote_copy(
            src_ref=source,
            dst_ref=target,
            send_sem=send_sem,
            recv_sem=recv_sem,
            device_id=self.device(bit),
            device_id_type=pl.DeviceIdType.MESH,
        )


def span(bits):
    masks = [0]
    for bit in bits:
        masks = masks + [mask | bit for mask in masks]
    return masks


class Gather:
    def __init__(self, links, own_ref, all_ref, sends, recvs, local_sem):
        self.links, self.own, self.all = links, own_ref, all_ref
        self.sends, self.recvs, self.local = sends, recvs, local_sem
        self.rows = own_ref.shape[1]
        self.cut = self.rows // 2

    def at(self, micro, mask, part):
        start = self.links.place(mask) * self.rows + part * self.cut
        return self.all.at[micro, start : start + self.cut]

    def piece(self, micro, mask, part):
        if mask & 1:
            return 1
        seen = 0
        for bit in self.links.orders[part]:
            if mask & bit:
                seen = bit
        return seen

    def send(self, micro, mask, part, bit):
        there = mask ^ bit
        source = self.at(micro, mask, part)
        if mask == 0:
            source = self.own.at[micro, part * self.cut : (part + 1) * self.cut]
        self.links.copy(
            source,
            self.at(micro, there, part),
            self.sends.at[micro, self.links.place(there), part],
            self.recvs.at[micro, self.links.place(there), part],
            bit,
        ).start()

    def descriptor(self, micro, mask, part):
        bit = self.piece(micro, mask, part)
        source = self.at(micro, mask ^ bit, part)
        if mask ^ bit == 0:
            source = self.own.at[micro, part * self.cut : (part + 1) * self.cut]
        place = self.links.place(mask)
        return self.links.copy(
            source,
            self.at(micro, mask, part),
            self.sends.at[micro, place, part],
            self.recvs.at[micro, place, part],
            bit,
        )

    def keep_own(self, micro):
        return pltpu.make_async_copy(
            self.own.at[micro], self.all.at[micro, 0 : self.rows], self.local.at[micro]
        )

    def start(self, micro):
        for part in range(2):
            self.send(micro, 0, part, self.links.orders[part][0])
        for part in range(2):
            self.send(micro, 0, part, 1)
        self.keep_own(micro).start()

    def advance(self, micro, phase):
        count = len(self.links.far)
        for part in range(2):
            order = self.links.orders[part]
            fresh = [mask | order[phase] for mask in span(order[:phase])]
            for mask in fresh:
                self.descriptor(micro, mask, part).wait_recv()
            if phase + 1 < count:
                for mask in span(order[: phase + 1]):
                    self.send(micro, mask, part, order[phase + 1])
            for mask in fresh:
                self.send(micro, mask, part, 1)

    def phases(self):
        return len(self.links.far)

    def near(self, micro):
        for part in range(2):
            for mask in span(self.links.far):
                self.descriptor(micro, mask | 1, part).wait_recv()
        self.keep_own(micro).wait()

    def drain(self, micro):
        for part in range(2):
            for mask in range(1, self.links.seq):
                self.descriptor(micro, mask, part).wait_send()


class Scatter:
    def __init__(self, links, rows, sum_ref, near_send, near_recv, far_send, far_recv, sems):
        self.links, self.rows, self.cut = links, rows, rows // 2
        self.sum, self.near_send, self.near_recv = sum_ref, near_send, near_recv
        self.far_send, self.far_recv = far_send, far_recv
        self.near_sems, self.far_sems = sems

    def near_copy(self, micro, index):
        view = slice(index * self.rows, (index + 1) * self.rows)
        return self.links.copy(
            self.near_send.at[micro, view],
            self.near_recv.at[micro, view],
            self.near_sems.at[0, micro, index],
            self.near_sems.at[1, micro, index],
            1,
        )

    def start(self, micro, indexes):
        for index in indexes:
            self.near_copy(micro, index).start()

    def far_view(self, index, part):
        start = index * self.rows + part * self.cut
        return slice(start, start + self.cut)

    def bit_of(self, index, part):
        last = 0
        for bit in self.links.orders[part]:
            if (index * 2) & bit:
                last = bit
        return last

    def far_copy(self, micro, index, part):
        view = self.far_view(index, part)
        return self.links.copy(
            self.far_send.at[micro, view],
            self.far_recv.at[micro, view],
            self.far_sems.at[0, micro, index, part],
            self.far_sems.at[1, micro, index, part],
            self.bit_of(index, part),
        )

    def send_far(self, micro, index, part, value):
        self.far_send[micro, self.far_view(index, part)] = value.astype(low)
        self.far_copy(micro, index, part).start()

    def near_sum(self, micro):
        count = len(self.links.far)
        first = {}
        for part in range(2):
            bit = self.links.orders[part][count - 1]
            first[part] = [mask | bit for mask in span(self.links.orders[part][: count - 1])]
        ordered = sorted(range(self.links.half), key=lambda index: index == 0)
        for index in ordered:
            self.near_copy(micro, index).wait_recv()
            for part in range(2):
                view = self.far_view(index, part)
                value = self.sum[micro, view] + self.near_recv[micro, view].astype(wide)
                if index * 2 in first[part]:
                    self.send_far(micro, index, part, value)
                else:
                    self.sum[micro, view] = value

    def far_sum(self, micro, phase):
        count = len(self.links.far)
        for part in range(2):
            order = self.links.orders[part]
            bit = order[count - 1 - phase]
            remain = span(order[: count - 1 - phase])
            following = order[count - 2 - phase] if phase + 1 < count else 0
            for mask in sorted(remain, key=lambda mask: (mask & following) == 0):
                index, came = mask // 2, (mask | bit) // 2
                self.far_copy(micro, came, part).wait_recv()
                view = self.far_view(index, part)
                value = self.sum[micro, view] + self.far_recv[
                    micro, self.far_view(came, part)
                ].astype(wide)
                if mask & following:
                    self.send_far(micro, index, part, value)
                else:
                    self.sum[micro, view] = value

    def total(self, micro):
        return self.sum[micro, 0 : self.rows]

    def phases(self):
        return len(self.links.far)

    def drain(self, micro):
        for index in range(self.links.half):
            self.near_copy(micro, index).wait_send()
        for part in range(2):
            for index in range(1, self.links.half):
                self.far_copy(micro, index, part).wait_send()


def gather_scratch(seq, micros):
    return [
        pltpu.SemaphoreType.DMA((micros, seq, 2)),
        pltpu.SemaphoreType.DMA((micros, seq, 2)),
        pltpu.SemaphoreType.DMA((micros,)),
    ]


def scatter_scratch(seq, micros, rows, width):
    half = seq // 2
    part = pltpu.VMEM((micros, half * rows, width), low)
    return [
        pltpu.VMEM((micros, half * rows, width), wide),
        part,
        part,
        part,
        part,
        pltpu.SemaphoreType.DMA((2, micros, half)),
        pltpu.SemaphoreType.DMA((2, micros, half, 2)),
    ]


def merged(first, second):
    steps = []
    for index in range(max(len(first), len(second))):
        steps += first[index : index + 1] + second[index : index + 1]
    return steps


def run_stage(micros, arrive, compute, leave):
    for step in arrive(0):
        step()
    for micro in range(micros):
        other = (leave(micro - 1) if micro > 0 else []) + (
            arrive(micro + 1) if micro + 1 < micros else []
        )
        for step in merged(compute(micro), other):
            step()
    for step in leave(micros - 1):
        step()


def arrive_steps(gathers, micro):
    steps = []
    for gather in gathers:
        for phase in range(gather.phases()):
            steps.append(functools.partial(gather.advance, micro, phase))
    return steps + [functools.partial(gather.near, micro) for gather in gathers]


def leave_steps(scatters, finish, micro):
    steps = [functools.partial(scatter.near_sum, micro) for scatter in scatters]
    for phase in range(scatters[0].phases()):
        for scatter in scatters:
            steps.append(functools.partial(scatter.far_sum, micro, phase))
    return steps + [functools.partial(finish, micro)]


def half_steps(scatter, micro, length, chunk):
    half = length // 2
    size = min(CHUNK, half)

    def odd():
        def body(index, carry):
            start = pl.multiple_of(half + index * size, size)
            place = pl.ds(pl.multiple_of(index * size, size), size)
            scatter.near_send[micro, place] = chunk(start, size).astype(low)
            return carry

        lax.fori_loop(0, half // size, body, 0)
        scatter.start(micro, range(scatter.links.half))

    def even():
        def body(index, carry):
            start = pl.multiple_of(index * size, size)
            scatter.sum[micro, pl.ds(start, size)] = chunk(start, size)
            return carry

        lax.fori_loop(0, half // size, body, 0)

    return [odd, even]


def ffn_kernel(
    seq, own_ref, resid_ref, one_ref, two_ref, pair_ref, all_ref, before_ref, hidden_ref, sum_ref,
    norm_ref, *scratch,
):
    links = Links(seq)
    micros, rows, _ = own_ref.shape
    length = all_ref.shape[1]
    gather = Gather(links, own_ref, all_ref, *scratch[:3])
    scatter = Scatter(links, rows, *scratch[3:8], scratch[8:])
    links.enter()
    for micro in range(micros):
        gather.start(micro)

    def compute(micro):
        def chunk(start, size):
            place = pl.ds(start, size)
            before = dot(all_ref[micro, place], one_ref[...], 1, 1)
            before_ref[micro, place] = before
            after = gelu_exact(before).astype(low)
            hidden_ref[micro, place] = after
            return dot(after, two_ref[...], 1, 1)

        return half_steps(scatter, micro, length, chunk)

    def finish(micro):
        total = resid_ref[micro] + scatter.total(micro)
        sum_ref[micro] = total
        norm_ref[micro] = layer_norm(total, (pair_ref[0:1], pair_ref[1:2]))

    run_stage(
        micros,
        functools.partial(arrive_steps, [gather]),
        compute,
        functools.partial(leave_steps, [scatter], finish),
    )
    for micro in range(micros):
        gather.drain(micro)
        scatter.drain(micro)


def stage_call(kernel, name_id, outs, scratch, args, flops):
    return pl.pallas_call(
        kernel,
        out_shape=outs,
        in_specs=[pl.BlockSpec(memory_space=pltpu.VMEM)] * len(args),
        out_specs=tuple(pl.BlockSpec(memory_space=pltpu.VMEM) for _ in outs),
        scratch_shapes=scratch,
        compiler_params=pltpu.CompilerParams(
            collective_id=name_id, has_side_effects=True, vmem_limit_bytes=VMEM_LIMIT
        ),
        cost_estimate=pl.CostEstimate(flops=flops, bytes_accessed=1 << 24, transcendentals=0),
    )(*args)


def ffn_stage(seq, name_id, own, resid, one, two, pair):
    micros, rows, width = own.shape
    hidden = one.shape[0]
    length = rows * seq
    outs = (
        jax.ShapeDtypeStruct((micros, length, width), low),
        jax.ShapeDtypeStruct((micros, length, hidden), wide),
        jax.ShapeDtypeStruct((micros, length, hidden), low),
        jax.ShapeDtypeStruct((micros, rows, width), wide),
        jax.ShapeDtypeStruct((micros, rows, width), wide),
    )
    scratch = gather_scratch(seq, micros) + scatter_scratch(seq, micros, rows, width)
    return stage_call(
        functools.partial(ffn_kernel, seq), name_id, outs, scratch,
        (own, resid, one, two, pair), 4 * micros * length * width * hidden,
    )


def prologue(micro, up_ref, resid_ref, pair_ref, own_ref, kept_ref, pair_grad_ref):
    gains = (pair_ref[0:1], pair_ref[1:2])
    grad, gain_grad, shift_grad = norm_back(up_ref[micro].astype(wide), resid_ref[micro], gains)
    kept_ref[micro] = grad
    own_ref[micro] = grad.astype(low)
    if micro == 0:
        pair_grad_ref[0:1] = gain_grad
        pair_grad_ref[1:2] = shift_grad
    else:
        pair_grad_ref[0:1] += gain_grad
        pair_grad_ref[1:2] += shift_grad


def ffn_back_kernel(
    seq, up_ref, resid_ref, pair_ref, before_ref, one_ref, two_ref, all_ref, slope_ref, out_ref,
    pair_grad_ref, own_ref, kept_ref, *scratch,
):
    links = Links(seq)
    micros, rows, _ = own_ref.shape
    length = all_ref.shape[1]
    gather = Gather(links, own_ref, all_ref, *scratch[:3])
    scatter = Scatter(links, rows, *scratch[3:8], scratch[8:])
    links.enter()
    for micro in range(micros):
        prologue(micro, up_ref, resid_ref, pair_ref, own_ref, kept_ref, pair_grad_ref)
        gather.start(micro)

    def compute(micro):
        def chunk(start, size):
            place = pl.ds(start, size)
            slope = dot(all_ref[micro, place], two_ref[...], 1, 0)
            slope = (slope * gelu_slope(before_ref[micro, place])).astype(low)
            slope_ref[micro, place] = slope
            return dot(slope, one_ref[...], 1, 0)

        return half_steps(scatter, micro, length, chunk)

    def finish(micro):
        out_ref[micro] = kept_ref[micro] + scatter.total(micro)

    run_stage(
        micros,
        functools.partial(arrive_steps, [gather]),
        compute,
        functools.partial(leave_steps, [scatter], finish),
    )
    for micro in range(micros):
        gather.drain(micro)
        scatter.drain(micro)


def ffn_back_stage(seq, name_id, up, resid, pair, before, one, two):
    micros, rows, width = up.shape
    hidden = one.shape[0]
    length = rows * seq
    outs = (
        jax.ShapeDtypeStruct((micros, length, width), low),
        jax.ShapeDtypeStruct((micros, length, hidden), low),
        jax.ShapeDtypeStruct((micros, rows, width), wide),
        jax.ShapeDtypeStruct((2, width), wide),
    )
    scratch = (
        [pltpu.VMEM((micros, rows, width), low), pltpu.VMEM((micros, rows, width), wide)]
        + gather_scratch(seq, micros)
        + scatter_scratch(seq, micros, rows, width)
    )
    return stage_call(
        functools.partial(ffn_back_kernel, seq), name_id, outs, scratch,
        (up, resid, pair, before, one, two), 4 * micros * length * width * hidden,
    )


def outer_sum(lefts, rights):
    total = None
    for left, right in zip(lefts, rights):
        value = dot(left, right, 0, 0)
        total = value if total is None else total + value
    return total


def local(
    seq, ranks,
    source, target, source_segments, target_segments, cotangent,
    encoder_qkv, encoder_output, encoder_prefix, encoder_expand, encoder_contract, encoder_down,
    encoder_up, encoder_norms, decoder_qkv, decoder_output, decoder_prefix, cross_query, cross_kv,
    cross_output, cross_prefix, decoder_expand, decoder_contract, decoder_down, decoder_up,
    decoder_norms,
):
    micro_count, batch_rows, block, width = source.shape
    length = source_segments.shape[2]
    me = lax.axis_index("seq")
    plane = Plane(seq, block)
    stacked = micro_count * batch_rows
    every = range(stacked)
    head_width = width // seq
    slice_cols = encoder_output.shape[1]
    count = encoder_prefix.shape[1]
    hidden = encoder_contract.shape[0] // seq
    adapt = encoder_up.shape[0] // seq
    both = hidden + adapt
    padded = (both + LANES - 1) // LANES * LANES

    sources = [row for row in source.reshape(stacked, block, width)]
    targets = [row for row in target.reshape(stacked, block, width)]

    places = plane.relative(jnp.arange(length, dtype=jnp.int32), me)
    place_pair = (places[:, None], places[None, :])
    source_ids = [plane.relative(row, me) for row in source_segments.reshape(stacked, length)]
    target_ids = [plane.relative(row, me) for row in target_segments.reshape(stacked, length)]

    def id_set(keys, queries):
        return (keys[:, None], queries[None, :]) + place_pair

    encoder_ids = [id_set(source_ids[m], source_ids[m]) for m in every]
    decoder_ids = [id_set(target_ids[m], target_ids[m]) for m in every]
    cross_ids = [id_set(source_ids[m], target_ids[m]) for m in every]

    def columns(weight):
        return jnp.swapaxes(weight, -1, -2)

    def gather_rows(value):
        return lax.all_gather(value, "rows", axis=0, tiled=False)

    def stack_columns(pieces):
        gathered = gather_rows(jnp.concatenate(pieces, axis=0))
        outs = []
        start = 0
        for piece in pieces:
            size = piece.shape[0]
            outs.append(gathered[:, start : start + size])
            start += size
        return outs

    def flat_columns(gathered, parts):
        value = gathered.reshape(ranks, parts, slice_cols, width)
        return jnp.swapaxes(value, 0, 1).reshape(parts * ranks * slice_cols, width)

    def split_rows(weight):
        value = columns(weight)
        return value.reshape(slice_cols, seq, -1)

    def exchange(value):
        return lax.all_to_all(value, "seq", 1, 1, tiled=False)

    def ffn_rows(contract, up):
        pieces = [split_rows(contract), split_rows(up) * jnp.asarray(ADAPTER_SCALE, low)]
        if padded > both:
            pieces.append(jnp.zeros((slice_cols, seq, padded - both), low))
        return pieces

    row_pieces = jnp.concatenate(
        [split_rows(encoder_output), split_rows(decoder_output), split_rows(cross_output)]
        + ffn_rows(encoder_contract, encoder_up)
        + ffn_rows(decoder_contract, decoder_up),
        axis=2,
    )
    row_pieces = lax.all_to_all(row_pieces, "seq", 1, 0, tiled=False).reshape(seq, slice_cols, -1)

    def row_weight(start, size):
        gathered = gather_rows(row_pieces[:, :, start : start + size])
        return jnp.swapaxes(gathered, 0, 1).reshape(width, size)

    qkv_parts = gather_rows(
        jnp.concatenate(
            [
                columns(encoder_qkv).reshape(-1, width),
                columns(decoder_qkv).reshape(-1, width),
            ]
        )
    )
    encoder_in = flat_columns(qkv_parts[:, : 3 * slice_cols], 3)
    decoder_in = flat_columns(qkv_parts[:, 3 * slice_cols :], 3)
    first_rows = row_weight(0, 3 * head_width + padded)
    encoder_out = first_rows[:, :head_width]
    decoder_out = first_rows[:, head_width : 2 * head_width]
    cross_out = first_rows[:, 2 * head_width : 3 * head_width]
    encoder_two = first_rows[:, 3 * head_width :]
    cut = encoder_expand.shape[1]

    def ffn_in(gathered):
        pieces = [gathered[:, :cut].reshape(-1, width), gathered[:, cut:].reshape(-1, width)]
        if padded > both:
            pieces.append(jnp.zeros((padded - both, width), low))
        return jnp.concatenate(pieces)

    second_parts = gather_rows(
        jnp.concatenate(
            [
                columns(encoder_expand),
                columns(encoder_down),
                columns(cross_query),
                columns(cross_kv).reshape(-1, width),
            ]
        )
    )
    ffn_cut = cut + encoder_down.shape[1]
    encoder_one = ffn_in(second_parts[:, :ffn_cut])
    cross_in = flat_columns(second_parts[:, ffn_cut:], 3)
    cross_q_in, cross_kv_in = cross_in[:head_width], cross_in[head_width:]
    decoder_one = ffn_in(
        gather_rows(jnp.concatenate([columns(decoder_expand), columns(decoder_down)]))
    )
    decoder_two = row_weight(3 * head_width + padded, padded)

    prefixes = small_gather(
        jnp.concatenate([encoder_prefix, decoder_prefix, cross_prefix]), [("rows", ranks)]
    )
    prefixes = jnp.moveaxis(prefixes, 0, 2).reshape(6, count, head_width)
    prefixes = jnp.pad(prefixes, ((0, 0), (0, PAD_PREFIX - count), (0, 0)))
    encoder_pre, decoder_pre, cross_pre = prefixes[0:2], prefixes[2:4], prefixes[4:6]

    norm_axes = [("seq", seq), ("rows", ranks)]
    scales = small_gather(
        jnp.concatenate([encoder_norms, decoder_norms]), norm_axes
    )
    scales = jnp.moveaxis(scales, 0, 2).reshape(-1, 2, width).astype(wide)
    norm_count = encoder_norms.shape[0]

    self_offsets = (0, head_width, 2 * head_width)
    cross_offsets = (0, 0, head_width)

    source_all = [plane.gather(sources[m], m) for m in every]
    target_all = [plane.gather(targets[m], m) for m in every]
    encoder_qkvs = [dot(source_all[m], encoder_in, 1, 1).astype(low) for m in every]
    decoder_qkvs = [dot(target_all[m], decoder_in, 1, 1).astype(low) for m in every]
    encoder_ctx, encoder_logs, resid_one, middle = [], [], [], []
    decoder_ctx, decoder_logs, resid_three, first, first_all = [], [], [], [], []
    for m in every:
        context, logs = attend_forward(
            encoder_qkvs[m], encoder_qkvs[m], self_offsets, encoder_pre, count, encoder_ids[m], False
        )
        encoder_ctx.append(context)
        encoder_logs.append(logs)
        attended = plane.scatter([(context, encoder_out, 1)], m)
        resid_one.append(sources[m].astype(wide) + attended)
        middle.append(layer_norm(resid_one[m], scales[0]))
    for m in every:
        context, logs = attend_forward(
            decoder_qkvs[m], decoder_qkvs[m], self_offsets, decoder_pre, count, decoder_ids[m], True
        )
        decoder_ctx.append(context)
        decoder_logs.append(logs)
        attended = plane.scatter([(context, decoder_out, 1)], m)
        resid_three.append(targets[m].astype(wide) + attended)
        first.append(layer_norm(resid_three[m], scales[norm_count]))
        first_all.append(plane.gather(first[m].astype(low), m))
    middle_low = jnp.stack(middle).astype(low)
    middle_all, encoder_before, encoder_hidden, resid_two, memory = ffn_stage(
        seq, 1, middle_low, jnp.stack(middle), encoder_one, encoder_two, scales[1]
    )
    memory_low = memory.astype(low)
    memory_all = [plane.gather(memory_low[m], m) for m in every]
    cross_q = [dot(first_all[m], cross_q_in, 1, 1).astype(low) for m in every]
    cross_kvs = [dot(memory_all[m], cross_kv_in, 1, 1).astype(low) for m in every]
    cross_ctx, cross_logs, resid_four, second = [], [], [], []
    for m in every:
        context, logs = attend_forward(
            cross_q[m], cross_kvs[m], cross_offsets, cross_pre, count, cross_ids[m], False
        )
        cross_ctx.append(context)
        cross_logs.append(logs)
        crossed = plane.scatter([(context, cross_out, 1)], m)
        resid_four.append(first[m] + crossed)
        second.append(layer_norm(resid_four[m], scales[norm_count + 1]))
    second_low = jnp.stack(second).astype(low)
    second_all, decoder_before, decoder_hidden, resid_five, third = ffn_stage(
        seq, 2, second_low, jnp.stack(second), decoder_one, decoder_two, scales[norm_count + 2]
    )
    result = third.astype(low)

    def scatter_ranks(value):
        value = with_layout_constraint(value.astype(low), Layout(tuple(range(value.ndim))))
        return lax.psum_scatter(value, "rows", scatter_dimension=0, tiled=False)

    def reduce_columns(grad, parts):
        value = grad.reshape(parts, ranks, slice_cols, width)
        return scatter_ranks(jnp.swapaxes(value, 0, 1))

    def reduce_rows(grad):
        value = grad.reshape(seq, ranks, slice_cols, -1)
        return scatter_ranks(jnp.swapaxes(value, 0, 1))

    def reduce_ffn_in(grad):
        value = jnp.concatenate(
            [
                grad[:hidden].reshape(ranks, -1, width),
                grad[hidden:both].reshape(ranks, -1, width),
            ],
            axis=1,
        )
        return scatter_ranks(value)

    def flat(value):
        return value.reshape(-1, value.shape[-1])

    norm_grads = {}

    def norm_step(index, upstream_rows, residuals):
        grads, gain_sum, shift_sum = [], 0.0, 0.0
        for m in every:
            grad, gain_grad, shift_grad = norm_back(upstream_rows[m], residuals[m], scales[index])
            grads.append(grad)
            gain_sum = gain_sum + gain_grad
            shift_sum = shift_sum + shift_grad
        norm_grads[index] = (gain_sum, shift_sum)
        return grads

    def ffn_back(name_id, index, up, resid, before, hidden_low, rows_all, one, two):
        up_all, slope, out, pair = ffn_back_stage(
            seq, name_id, up, resid, scales[index], before, one, two
        )
        norm_grads[index] = (pair[0:1], pair[1:2])
        two_grad = reduce_rows(dot(flat(up_all), flat(hidden_low), 0, 0))
        one_grad = reduce_ffn_in(dot(flat(slope), flat(rows_all), 0, 0))
        return out, one_grad, two_grad

    second_up, decoder_one_grad, decoder_two_grad = ffn_back(
        3, norm_count + 2, cotangent.reshape(stacked, block, width), resid_five, decoder_before,
        decoder_hidden, second_all, decoder_one, decoder_two,
    )

    second_in = norm_step(norm_count + 1, second_up, resid_four)
    second_low = [plane.gather(second_in[m].astype(low), m) for m in every]
    cross_grads, cross_pre_grad, first_up, memory_up = [], None, [], []
    for m in every:
        context_grad = dot(second_low[m], cross_out, 1, 0).astype(low)
        grads, pre = attend_backward(
            cross_q[m], cross_kvs[m], cross_offsets, cross_pre, count, cross_ids[m], False,
            cross_logs[m], context_grad,
        )
        cross_grads.append(grads)
        cross_pre_grad = pre if cross_pre_grad is None else cross_pre_grad + pre
        memory_up.append(plane.scatter([(grads[:, head_width:], cross_kv_in, 0)], m))
        first_up.append(
            second_in[m] + plane.scatter([(grads[:, :head_width], cross_q_in, 0)], m)
        )
    cross_out_grad = reduce_rows(outer_sum(second_low, cross_ctx))
    cross_in_grad = reduce_columns(
        jnp.concatenate(
            [
                outer_sum([g[:, :head_width] for g in cross_grads], first_all),
                outer_sum([g[:, head_width:] for g in cross_grads], memory_all),
            ]
        ),
        3,
    )

    middle_up, encoder_one_grad, encoder_two_grad = ffn_back(
        4, 1, jnp.stack(memory_up), resid_two, encoder_before, encoder_hidden, middle_all,
        encoder_one, encoder_two,
    )
    first_in = norm_step(norm_count, first_up, resid_three)
    first_low = [plane.gather(first_in[m].astype(low), m) for m in every]

    def self_backward(low_all, out_weight, in_weight, qkvs, prefix, ids, causal, logs, rows_in):
        grads_all, prefix_sum, totals = [], None, []
        for m in every:
            context_grad = dot(low_all[m], out_weight, 1, 0).astype(low)
            grads, pre = attend_backward(
                qkvs[m], qkvs[m], self_offsets, prefix, count, ids[m], causal, logs[m], context_grad
            )
            grads_all.append(grads)
            prefix_sum = pre if prefix_sum is None else prefix_sum + pre
            totals.append(rows_in[m] + plane.scatter([(grads, in_weight, 0)], m))
        return grads_all, prefix_sum, totals

    decoder_grads, decoder_pre_grad, target_grads = self_backward(
        first_low, decoder_out, decoder_in, decoder_qkvs, decoder_pre, decoder_ids, True,
        decoder_logs, first_in,
    )
    decoder_out_grad = reduce_rows(outer_sum(first_low, decoder_ctx))
    decoder_in_grad = reduce_columns(outer_sum(decoder_grads, target_all), 3)

    middle_in = norm_step(0, middle_up, resid_one)
    middle_low = [plane.gather(middle_in[m].astype(low), m) for m in every]
    encoder_grads, encoder_pre_grad, source_grads = self_backward(
        middle_low, encoder_out, encoder_in, encoder_qkvs, encoder_pre, encoder_ids, False,
        encoder_logs, middle_in,
    )
    encoder_out_grad = reduce_rows(outer_sum(middle_low, encoder_ctx))
    encoder_in_grad = reduce_columns(outer_sum(encoder_grads, source_all), 3)

    def give_back(pieces):
        value = jnp.concatenate(pieces, axis=2)
        return lax.all_to_all(value, "seq", 0, 1, tiled=False)

    decoder_rows = give_back([decoder_two_grad, cross_out_grad, decoder_out_grad])
    encoder_rows = give_back([encoder_two_grad, encoder_out_grad])

    def row_grad(value, start, size, scale=None):
        piece = value[:, :, start : start + size].astype(wide)
        if scale is not None:
            piece = piece * scale
        return piece.reshape(slice_cols, -1).T

    def column_grad(value):
        return jnp.swapaxes(value.astype(wide), -1, -2)

    prefix_total = jnp.concatenate([encoder_pre_grad, decoder_pre_grad, cross_pre_grad])[:, :count]
    prefix_total = jnp.moveaxis(prefix_total.reshape(6, count, ranks, slice_cols), 2, 0)
    prefix_total = small_scatter(prefix_total, [("rows", ranks)])
    norm_rows = [row for index in sorted(norm_grads) for row in norm_grads[index]]
    which = lax.broadcasted_iota(jnp.int32, (len(norm_rows), width), 0)
    norm_total = sum(jnp.where(which == k, row, 0.0) for k, row in enumerate(norm_rows))
    norm_total = jnp.moveaxis(norm_total.reshape(-1, 2, seq * ranks, slice_cols), 2, 0)
    norm_total = small_scatter(norm_total, norm_axes)

    shape_out = source.shape
    return (
        result.reshape(shape_out),
        jnp.stack(source_grads).reshape(shape_out),
        jnp.stack(target_grads).reshape(shape_out),
        column_grad(encoder_in_grad),
        row_grad(encoder_rows, padded, head_width),
        prefix_total[0:2],
        column_grad(encoder_one_grad[:cut]),
        row_grad(encoder_rows, 0, hidden),
        column_grad(encoder_one_grad[cut:]),
        row_grad(encoder_rows, hidden, adapt, ADAPTER_SCALE),
        norm_total[:norm_count],
        column_grad(decoder_in_grad),
        row_grad(decoder_rows, padded + head_width, head_width),
        prefix_total[2:4],
        column_grad(cross_in_grad[0]),
        column_grad(cross_in_grad[1:]),
        row_grad(decoder_rows, padded, head_width),
        prefix_total[4:6],
        column_grad(decoder_one_grad[:cut]),
        row_grad(decoder_rows, 0, hidden),
        column_grad(decoder_one_grad[cut:]),
        row_grad(decoder_rows, hidden, adapt, ADAPTER_SCALE),
        norm_total[norm_count:],
    )


def solution(mesh):
    rows = P(None, "rows", "seq", None)
    ids = P(None, "rows", None)
    flat = P(None, ("seq", "rows"))
    deep = P(None, None, ("seq", "rows"))
    weights = (
        deep, flat, deep, flat, flat, flat, flat, deep, deep, flat, deep, flat, deep, flat, deep,
        flat, flat, flat, flat, deep,
    )
    body = functools.partial(local, mesh.shape["seq"], mesh.shape["rows"])
    return jax.shard_map(
        body,
        mesh=mesh,
        in_specs=(rows, rows, ids, ids, rows) + weights,
        out_specs=(rows, rows, rows) + weights,
        check_vma=False,
    )
```

```python
import functools

import jax
import jax.numpy as jnp
from jax import lax
from jax.experimental import pallas as pl
from jax.experimental.layout import Layout, with_layout_constraint
from jax.experimental.pallas import tpu as pltpu
from jax.sharding import PartitionSpec as P

HEADS = 16
HEAD_DIM = 64
EPSILON = 1e-05
MASKED = -1e30
ADAPTER_SCALE = 4.0
SCALING = HEAD_DIM ** (-0.5)
PAD_PREFIX = 32
CHUNK = 256
LANES = 128
VMEM_LIMIT = 60 * 1024 * 1024
HALF_ROOT = 0.7071067811865476
DENSITY = 0.3989422804014327

low = jnp.bfloat16
wide = jnp.float32


def dot(left, right, left_axis, right_axis):
    return lax.dot_general(
        left, right, (((left_axis,), (right_axis,)), ((), ())), preferred_element_type=wide
    )


def bit_list(count):
    bits = []
    value = 1
    while value < count:
        bits.append(value)
        value *= 2
    return bits


def swap_pairs(count, bit):
    return [(index, index ^ bit) for index in range(count)]


def relative(places, seq, me):
    depth = len(bit_list(seq))
    value = places.reshape((2,) * depth + (-1,))
    for axis in range(depth):
        bit = 1 << (depth - 1 - axis)
        value = jnp.where((me & bit) != 0, jnp.flip(value, axis), value)
    return jnp.moveaxis(value, depth - 1, 0).reshape(-1)


def small_gather(value, axes):
    value = value[None]
    for name, count in axes[::-1]:
        me = lax.axis_index(name)
        for bit in bit_list(count):
            other = lax.ppermute(value, name, swap_pairs(count, bit))
            flip = (me & bit) != 0
            value = jnp.where(
                flip, jnp.concatenate([other, value]), jnp.concatenate([value, other])
            )
    return value


def small_scatter(value, axes):
    for name, count in axes:
        me = lax.axis_index(name)
        for bit in bit_list(count)[::-1]:
            half = value.shape[0] // 2
            flip = (me & bit) != 0
            lower, upper = value[:half], value[half:]
            sent = lax.ppermute(jnp.where(flip, lower, upper), name, swap_pairs(count, bit))
            value = jnp.where(flip, upper, lower) + sent
    return value[0]


def normalized(tensor):
    average = jnp.mean(tensor, axis=-1, keepdims=True)
    centered = tensor - average
    spread = jnp.mean(centered * centered, axis=-1, keepdims=True)
    inverse = lax.rsqrt(spread + EPSILON)
    return centered * inverse, inverse


def layer_norm(tensor, scales):
    return normalized(tensor)[0] * scales[0] + scales[1]


def norm_back(upstream, tensor, scales):
    unit, inverse = normalized(tensor)
    slope = upstream * scales[0]
    grad = inverse * (
        slope
        - jnp.mean(slope, axis=-1, keepdims=True)
        - unit * jnp.mean(slope * unit, axis=-1, keepdims=True)
    )
    return (
        grad,
        jnp.sum(upstream * unit, axis=0, keepdims=True),
        jnp.sum(upstream, axis=0, keepdims=True),
    )


def gelu_exact(tensor):
    return tensor * (0.5 + 0.5 * lax.erf(tensor * HALF_ROOT))


def gelu_slope(tensor):
    density = jnp.exp(-0.5 * tensor * tensor) * DENSITY
    return 0.5 + 0.5 * lax.erf(tensor * HALF_ROOT) + tensor * density


class Links:
    def __init__(self, seq):
        self.seq = seq
        self.far = [bit for bit in bit_list(seq) if bit > 1]
        self.orders = [self.far, self.far[::-1]]
        self.half = seq // 2
        self.me = lax.axis_index("seq")

    def place(self, mask):
        return (mask & 1) * self.half + (mask >> 1)

    def device(self, bit):
        return {"seq": jnp.bitwise_xor(self.me, bit)}

    def enter(self):
        barrier = pltpu.get_barrier_semaphore()
        bits = bit_list(self.seq)
        for bit in bits:
            pl.semaphore_signal(
                barrier, inc=1, device_id=self.device(bit), device_id_type=pl.DeviceIdType.MESH
            )
        pl.semaphore_wait(barrier, len(bits))

    def copy(self, source, target, send_sem, recv_sem, bit):
        return pltpu.make_async_remote_copy(
            src_ref=source,
            dst_ref=target,
            send_sem=send_sem,
            recv_sem=recv_sem,
            device_id=self.device(bit),
            device_id_type=pl.DeviceIdType.MESH,
        )


def span(bits):
    masks = [0]
    for bit in bits:
        masks = masks + [mask | bit for mask in masks]
    return masks


class Gather:
    def __init__(self, links, own_ref, all_ref, sends, recvs, local_sem):
        self.links, self.own, self.all = links, own_ref, all_ref
        self.sends, self.recvs, self.local = sends, recvs, local_sem
        self.rows = own_ref.shape[1]
        self.cut = self.rows // 2

    def at(self, micro, mask, part):
        start = self.links.place(mask) * self.rows + part * self.cut
        return self.all.at[micro, start : start + self.cut]

    def piece(self, micro, mask, part):
        if mask & 1:
            return 1
        seen = 0
        for bit in self.links.orders[part]:
            if mask & bit:
                seen = bit
        return seen

    def send(self, micro, mask, part, bit):
        there = mask ^ bit
        source = self.at(micro, mask, part)
        if mask == 0:
            source = self.own.at[micro, part * self.cut : (part + 1) * self.cut]
        self.links.copy(
            source,
            self.at(micro, there, part),
            self.sends.at[micro, self.links.place(there), part],
            self.recvs.at[micro, self.links.place(there), part],
            bit,
        ).start()

    def descriptor(self, micro, mask, part):
        bit = self.piece(micro, mask, part)
        source = self.at(micro, mask ^ bit, part)
        if mask ^ bit == 0:
            source = self.own.at[micro, part * self.cut : (part + 1) * self.cut]
        place = self.links.place(mask)
        return self.links.copy(
            source,
            self.at(micro, mask, part),
            self.sends.at[micro, place, part],
            self.recvs.at[micro, place, part],
            bit,
        )

    def keep_own(self, micro):
        return pltpu.make_async_copy(
            self.own.at[micro], self.all.at[micro, 0 : self.rows], self.local.at[micro]
        )

    def start(self, micro):
        for part in range(2):
            self.send(micro, 0, part, self.links.orders[part][0])
        for part in range(2):
            self.send(micro, 0, part, 1)
        self.keep_own(micro).start()

    def advance(self, micro, phase):
        count = len(self.links.far)
        for part in range(2):
            order = self.links.orders[part]
            fresh = [mask | order[phase] for mask in span(order[:phase])]
            for mask in fresh:
                self.descriptor(micro, mask, part).wait_recv()
            if phase + 1 < count:
                for mask in span(order[: phase + 1]):
                    self.send(micro, mask, part, order[phase + 1])
            for mask in fresh:
                self.send(micro, mask, part, 1)

    def phases(self):
        return len(self.links.far)

    def near(self, micro):
        for part in range(2):
            for mask in span(self.links.far):
                self.descriptor(micro, mask | 1, part).wait_recv()
        self.keep_own(micro).wait()

    def drain(self, micro):
        for part in range(2):
            for mask in range(1, self.links.seq):
                self.descriptor(micro, mask, part).wait_send()


class Scatter:
    def __init__(self, links, rows, sum_ref, near_send, near_recv, far_send, far_recv, sems):
        self.links, self.rows, self.cut = links, rows, rows // 2
        self.sum, self.near_send, self.near_recv = sum_ref, near_send, near_recv
        self.far_send, self.far_recv = far_send, far_recv
        self.near_sems, self.far_sems = sems

    def near_copy(self, micro, index):
        view = slice(index * self.rows, (index + 1) * self.rows)
        return self.links.copy(
            self.near_send.at[micro, view],
            self.near_recv.at[micro, view],
            self.near_sems.at[0, micro, index],
            self.near_sems.at[1, micro, index],
            1,
        )

    def start(self, micro, indexes):
        for index in indexes:
            self.near_copy(micro, index).start()

    def far_view(self, index, part):
        start = index * self.rows + part * self.cut
        return slice(start, start + self.cut)

    def bit_of(self, index, part):
        last = 0
        for bit in self.links.orders[part]:
            if (index * 2) & bit:
                last = bit
        return last

    def far_copy(self, micro, index, part):
        view = self.far_view(index, part)
        return self.links.copy(
            self.far_send.at[micro, view],
            self.far_recv.at[micro, view],
            self.far_sems.at[0, micro, index, part],
            self.far_sems.at[1, micro, index, part],
            self.bit_of(index, part),
        )

    def send_far(self, micro, index, part, value):
        self.far_send[micro, self.far_view(index, part)] = value.astype(low)
        self.far_copy(micro, index, part).start()

    def near_sum(self, micro):
        count = len(self.links.far)
        first = {}
        for part in range(2):
            bit = self.links.orders[part][count - 1]
            first[part] = [mask | bit for mask in span(self.links.orders[part][: count - 1])]
        ordered = sorted(range(self.links.half), key=lambda index: index == 0)
        for index in ordered:
            self.near_copy(micro, index).wait_recv()
            for part in range(2):
                view = self.far_view(index, part)
                value = self.sum[micro, view] + self.near_recv[micro, view].astype(wide)
                if index * 2 in first[part]:
                    self.send_far(micro, index, part, value)
                else:
                    self.sum[micro, view] = value

    def far_sum(self, micro, phase):
        count = len(self.links.far)
        for part in range(2):
            order = self.links.orders[part]
            bit = order[count - 1 - phase]
            remain = span(order[: count - 1 - phase])
            following = order[count - 2 - phase] if phase + 1 < count else 0
            for mask in sorted(remain, key=lambda mask: (mask & following) == 0):
                index, came = mask // 2, (mask | bit) // 2
                self.far_copy(micro, came, part).wait_recv()
                view = self.far_view(index, part)
                value = self.sum[micro, view] + self.far_recv[
                    micro, self.far_view(came, part)
                ].astype(wide)
                if mask & following:
                    self.send_far(micro, index, part, value)
                else:
                    self.sum[micro, view] = value

    def total(self, micro):
        return self.sum[micro, 0 : self.rows]

    def phases(self):
        return len(self.links.far)

    def drain(self, micro):
        for index in range(self.links.half):
            self.near_copy(micro, index).wait_send()
        for part in range(2):
            for index in range(1, self.links.half):
                self.far_copy(micro, index, part).wait_send()


def gather_scratch(seq, micros):
    return [
        pltpu.SemaphoreType.DMA((micros, seq, 2)),
        pltpu.SemaphoreType.DMA((micros, seq, 2)),
        pltpu.SemaphoreType.DMA((micros,)),
    ]


def scatter_scratch(seq, micros, rows, width):
    half = seq // 2
    part = pltpu.VMEM((micros, half * rows, width), low)
    return [
        pltpu.VMEM((micros, half * rows, width), wide),
        part,
        part,
        part,
        part,
        pltpu.SemaphoreType.DMA((2, micros, half)),
        pltpu.SemaphoreType.DMA((2, micros, half, 2)),
    ]


def merged(first, second):
    steps = []
    for index in range(max(len(first), len(second))):
        steps += first[index : index + 1] + second[index : index + 1]
    return steps


def run_stage(micros, arrive, compute, leave):
    for step in arrive(0):
        step()
    for micro in range(micros):
        other = (leave(micro - 1) if micro > 0 else []) + (
            arrive(micro + 1) if micro + 1 < micros else []
        )
        for step in merged(compute(micro), other):
            step()
    for step in leave(micros - 1):
        step()


def arrive_steps(gathers, micro):
    steps = []
    for gather in gathers:
        for phase in range(gather.phases()):
            steps.append(functools.partial(gather.advance, micro, phase))
    return steps + [functools.partial(gather.near, micro) for gather in gathers]


def leave_steps(scatters, finish, micro):
    steps = [functools.partial(scatter.near_sum, micro) for scatter in scatters]
    for phase in range(scatters[0].phases()):
        for scatter in scatters:
            steps.append(functools.partial(scatter.far_sum, micro, phase))
    return steps + [functools.partial(finish, micro)]


def half_steps(scatter, micro, length, chunk):
    half = length // 2
    size = min(CHUNK, half)

    def odd():
        def body(index, carry):
            start = pl.multiple_of(half + index * size, size)
            place = pl.ds(pl.multiple_of(index * size, size), size)
            scatter.near_send[micro, place] = chunk(start, size).astype(low)
            return carry

        lax.fori_loop(0, half // size, body, 0)
        scatter.start(micro, range(scatter.links.half))

    def even():
        def body(index, carry):
            start = pl.multiple_of(index * size, size)
            scatter.sum[micro, pl.ds(start, size)] = chunk(start, size)
            return carry

        lax.fori_loop(0, half // size, body, 0)

    return [odd, even]


def ffn_kernel(
    seq, own_ref, resid_ref, one_ref, two_ref, pair_ref, all_ref, before_ref, hidden_ref, sum_ref,
    norm_ref, *scratch,
):
    links = Links(seq)
    micros, rows, _ = own_ref.shape
    length = all_ref.shape[1]
    gather = Gather(links, own_ref, all_ref, *scratch[:3])
    scatter = Scatter(links, rows, *scratch[3:8], scratch[8:])
    links.enter()
    for micro in range(micros):
        gather.start(micro)

    def compute(micro):
        def chunk(start, size):
            place = pl.ds(start, size)
            before = dot(all_ref[micro, place], one_ref[...], 1, 1)
            before_ref[micro, place] = before
            after = gelu_exact(before).astype(low)
            hidden_ref[micro, place] = after
            return dot(after, two_ref[...], 1, 1)

        return half_steps(scatter, micro, length, chunk)

    def finish(micro):
        total = resid_ref[micro] + scatter.total(micro)
        sum_ref[micro] = total
        norm_ref[micro] = layer_norm(total, (pair_ref[0:1], pair_ref[1:2]))

    run_stage(
        micros,
        functools.partial(arrive_steps, [gather]),
        compute,
        functools.partial(leave_steps, [scatter], finish),
    )
    for micro in range(micros):
        gather.drain(micro)
        scatter.drain(micro)


def stage_call(kernel, name_id, outs, scratch, args, micros):
    return pl.pallas_call(
        kernel,
        out_shape=outs,
        in_specs=[pl.BlockSpec(memory_space=pltpu.VMEM)] * len(args),
        out_specs=tuple(pl.BlockSpec(memory_space=pltpu.VMEM) for _ in outs),
        scratch_shapes=scratch,
        compiler_params=pltpu.CompilerParams(
            collective_id=name_id, has_side_effects=True, vmem_limit_bytes=VMEM_LIMIT
        ),
        cost_estimate=pl.CostEstimate(
            flops=micros * 2_500_000_000, bytes_accessed=1 << 24, transcendentals=0
        ),
    )(*args)


def ffn_stage(seq, name_id, own, resid, one, two, pair):
    micros, rows, width = own.shape
    hidden = one.shape[0]
    length = rows * seq
    outs = (
        jax.ShapeDtypeStruct((micros, length, width), low),
        jax.ShapeDtypeStruct((micros, length, hidden), wide),
        jax.ShapeDtypeStruct((micros, length, hidden), low),
        jax.ShapeDtypeStruct((micros, rows, width), wide),
        jax.ShapeDtypeStruct((micros, rows, width), wide),
    )
    scratch = gather_scratch(seq, micros) + scatter_scratch(seq, micros, rows, width)
    return stage_call(
        functools.partial(ffn_kernel, seq), name_id, outs, scratch,
        (own, resid, one, two, pair), 60,
    )


def prologue(micro, up_ref, resid_ref, pair_ref, own_ref, kept_ref, pair_grad_ref):
    gains = (pair_ref[0:1], pair_ref[1:2])
    grad, gain_grad, shift_grad = norm_back(up_ref[micro].astype(wide), resid_ref[micro], gains)
    kept_ref[micro] = grad
    own_ref[micro] = grad.astype(low)
    if micro == 0:
        pair_grad_ref[0:1] = gain_grad
        pair_grad_ref[1:2] = shift_grad
    else:
        pair_grad_ref[0:1] += gain_grad
        pair_grad_ref[1:2] += shift_grad


def ffn_back_kernel(
    seq, up_ref, resid_ref, pair_ref, before_ref, one_ref, two_ref, all_ref, slope_ref, out_ref,
    pair_grad_ref, own_ref, kept_ref, *scratch,
):
    links = Links(seq)
    micros, rows, _ = own_ref.shape
    length = all_ref.shape[1]
    gather = Gather(links, own_ref, all_ref, *scratch[:3])
    scatter = Scatter(links, rows, *scratch[3:8], scratch[8:])
    links.enter()
    for micro in range(micros):
        prologue(micro, up_ref, resid_ref, pair_ref, own_ref, kept_ref, pair_grad_ref)
        gather.start(micro)

    def compute(micro):
        def chunk(start, size):
            place = pl.ds(start, size)
            slope = dot(all_ref[micro, place], two_ref[...], 1, 0)
            slope = (slope * gelu_slope(before_ref[micro, place])).astype(low)
            slope_ref[micro, place] = slope
            return dot(slope, one_ref[...], 1, 0)

        return half_steps(scatter, micro, length, chunk)

    def finish(micro):
        out_ref[micro] = kept_ref[micro] + scatter.total(micro)

    run_stage(
        micros,
        functools.partial(arrive_steps, [gather]),
        compute,
        functools.partial(leave_steps, [scatter], finish),
    )
    for micro in range(micros):
        gather.drain(micro)
        scatter.drain(micro)


def ffn_back_stage(seq, name_id, up, resid, pair, before, one, two):
    micros, rows, width = up.shape
    hidden = one.shape[0]
    length = rows * seq
    outs = (
        jax.ShapeDtypeStruct((micros, length, width), low),
        jax.ShapeDtypeStruct((micros, length, hidden), low),
        jax.ShapeDtypeStruct((micros, rows, width), wide),
        jax.ShapeDtypeStruct((2, width), wide),
    )
    scratch = (
        [pltpu.VMEM((micros, rows, width), low), pltpu.VMEM((micros, rows, width), wide)]
        + gather_scratch(seq, micros)
        + scatter_scratch(seq, micros, rows, width)
    )
    return stage_call(
        functools.partial(ffn_back_kernel, seq), name_id, outs, scratch,
        (up, resid, pair, before, one, two), 60,
    )


class Task:
    def __init__(self, begin, arrive, compute, leave, drain):
        self.begin, self.arrive, self.compute = begin, arrive, compute
        self.leave, self.drain = leave, drain


def spread(first, second):
    steps, done = [], 0
    for index, step in enumerate(first):
        steps.append(step)
        upto = len(second) * (index + 1) // len(first)
        steps += second[done:upto]
        done = upto
    return steps + second[done:]


def run_tasks(tasks):
    for task in tasks[:2]:
        task.begin()
    for step in tasks[0].arrive:
        step()
    for index, task in enumerate(tasks):
        other = []
        if index > 0:
            other += tasks[index - 1].leave
        if index + 1 < len(tasks):
            other += tasks[index + 1].arrive
        if index + 2 < len(tasks):
            other.append(tasks[index + 2].begin)
        for step in spread(task.compute, other):
            step()
    for step in tasks[-1].leave:
        step()
    for task in tasks:
        task.drain()


def make_task(micro, gathers, scatters, compute, finish, before=None):
    def begin():
        if before is not None:
            before(micro)
        for gather in gathers:
            gather.start(micro)

    def drain():
        for item in gathers + scatters:
            item.drain(micro)

    arrive = arrive_steps(gathers, micro)
    leave = leave_steps(scatters, finish, micro) if scatters else []
    return Task(begin, arrive, compute(micro), leave, drain)


def gather_kernel(seq, count, *refs):
    links = Links(seq)
    owns, alls, scratch = refs[:count], refs[count : 2 * count], refs[2 * count :]
    gathers = [
        Gather(links, owns[k], alls[k], *scratch[3 * k : 3 * k + 3]) for k in range(count)
    ]
    links.enter()
    tasks = []
    for gather in gathers:
        for micro in range(owns[0].shape[0]):
            tasks.append(make_task(micro, [gather], [], lambda micro: [], None))
    for task in tasks:
        task.begin()
    for phase in range(len(tasks[0].arrive)):
        for task in tasks:
            task.arrive[phase]()
    for task in tasks:
        task.drain()


def gather_stage(seq, name_id, owns):
    micros, rows, width = owns[0].shape
    outs = tuple(jax.ShapeDtypeStruct((micros, seq * rows, width), low) for _ in owns)
    scratch = gather_scratch(seq, micros) * len(owns)
    return stage_call(
        functools.partial(gather_kernel, seq, len(owns)), name_id, outs, scratch, owns, 45
    )


class Attention:
    def __init__(self, q_ref, kv_ref, offsets, prefix_ref, ids, count, causal):
        self.q, self.kv, self.offsets, self.prefix = q_ref, kv_ref, offsets, prefix_ref
        self.key_ids, self.query_ids, self.key_places, self.query_places = ids
        self.count, self.causal = count, causal
        self.heads = prefix_ref.shape[2] // HEAD_DIM

    def load(self, micro, head, place):
        q_at, k_at, v_at = (at + head * HEAD_DIM for at in self.offsets)
        queries = self.q[micro, place, q_at : q_at + HEAD_DIM] * jnp.asarray(SCALING, low)
        keys = self.kv[micro, :, k_at : k_at + HEAD_DIM]
        values = self.kv[micro, :, v_at : v_at + HEAD_DIM]
        return queries, keys, values

    def scores(self, micro, keys, queries, lanes, place):
        scores = dot(keys, queries, 1, 1)
        allowed = self.key_ids[micro] == self.query_ids[micro, :, place]
        if self.causal:
            allowed = allowed & (self.key_places[...] <= self.query_places[:, place])
        scores = jnp.where(allowed, scores, MASKED)
        extra = dot(self.prefix[0, :, lanes], queries, 1, 1)
        rows = lax.broadcasted_iota(jnp.int32, extra.shape, 0)
        return scores, jnp.where(rows < self.count, extra, MASKED)

    def forward(self, micro, start, size, context_ref, logs_ref):
        place = pl.ds(start, size)
        for head in range(self.heads):
            lanes = slice(head * HEAD_DIM, (head + 1) * HEAD_DIM)
            queries, keys, values = self.load(micro, head, place)
            scores, extra = self.scores(micro, keys, queries, lanes, place)
            peak = jnp.maximum(
                jnp.max(scores, axis=0, keepdims=True), jnp.max(extra, axis=0, keepdims=True)
            )
            scores = jnp.exp(scores - peak)
            extra = jnp.exp(extra - peak)
            total = jnp.sum(scores, axis=0, keepdims=True) + jnp.sum(extra, axis=0, keepdims=True)
            context = dot(values, scores.astype(low), 0, 0)
            context = context + dot(self.prefix[1, :, lanes], extra.astype(low), 0, 0)
            context_ref[micro, place, lanes] = (context / total).T.astype(low)
            logs_ref[micro, head : head + 1, place] = peak + jnp.log(total)

    def backward(self, micro, start, size, up_ref, logs_ref, grad_ref, k_sum, v_sum, pre_ref):
        place = pl.ds(start, size)
        for head in range(self.heads):
            lanes = slice(head * HEAD_DIM, (head + 1) * HEAD_DIM)
            queries, keys, values = self.load(micro, head, place)
            scores, extra = self.scores(micro, keys, queries, lanes, place)
            logs = logs_ref[micro, head : head + 1, place]
            weights = jnp.exp(scores - logs)
            extra = jnp.exp(extra - logs)
            up = up_ref[:, lanes]
            dots = dot(values, up, 1, 1)
            extra_dots = dot(self.prefix[1, :, lanes], up, 1, 1)
            centre = jnp.sum(weights * dots, axis=0, keepdims=True) + jnp.sum(
                extra * extra_dots, axis=0, keepdims=True
            )
            slope = (weights * (dots - centre)).astype(low)
            extra_slope = (extra * (extra_dots - centre)).astype(low)
            query_grad = dot(keys, slope, 0, 0) + dot(self.prefix[0, :, lanes], extra_slope, 0, 0)
            grad_ref[micro, place, lanes] = (query_grad * SCALING).T.astype(low)
            k_sum[:, lanes] += dot(slope, queries, 1, 0)
            v_sum[:, lanes] += dot(weights.astype(low), up, 1, 0)
            pre_ref[0, :, lanes] += dot(extra_slope, queries, 1, 0)
            pre_ref[1, :, lanes] += dot(extra.astype(low), up, 1, 0)


def loop(first, count, size, body):
    def step(index, carry):
        body(pl.multiple_of(first + index * size, size), index)
        return carry

    lax.fori_loop(0, count, step, 0)


def project_steps(micro, rows_ref, weight_ref, out_ref):
    length = rows_ref.shape[1]
    size = min(CHUNK, length)

    def body(start, index):
        place = pl.ds(start, size)
        out_ref[micro, place] = dot(rows_ref[micro, place], weight_ref[...], 1, 1).astype(low)

    return [lambda: loop(0, length // size, size, body)]


def self_kernel(seq, count, *refs):
    kinds = 2
    scratch = refs[-kinds * 7 :]
    refs = refs[: -kinds * 7]
    places = refs[:2]
    links = Links(seq)
    links.enter()
    tasks = []
    for kind in range(kinds):
        (all_ref, own_ref, in_ref, out_ref, prefix_ref, kid_ref, qid_ref, pair_ref) = refs[
            2 + 8 * kind : 10 + 8 * kind
        ]
        (qkv_ref, context_ref, logs_ref, sum_ref, norm_ref, low_ref) = refs[
            2 + 8 * kinds + 6 * kind : 8 + 8 * kinds + 6 * kind
        ]
        micros, rows, _ = own_ref.shape
        length = all_ref.shape[1]
        head_width = prefix_ref.shape[2]
        piece = scratch[7 * kind : 7 * kind + 7]
        scatter = Scatter(links, rows, *piece[:5], piece[5:])
        ids = (kid_ref, qid_ref) + tuple(places)
        attention = Attention(
            qkv_ref, qkv_ref, (0, head_width, 2 * head_width), prefix_ref, ids, count, kind == 1
        )

        def compute(
            micro, attention=attention, context_ref=context_ref, logs_ref=logs_ref,
            out_ref=out_ref, all_ref=all_ref, in_ref=in_ref, qkv_ref=qkv_ref, scatter=scatter,
        ):
            def chunk(start, size):
                attention.forward(micro, start, size, context_ref, logs_ref)
                return dot(context_ref[micro, pl.ds(start, size)], out_ref[...], 1, 1)

            return project_steps(micro, all_ref, in_ref, qkv_ref) + half_steps(
                scatter, micro, length, chunk
            )

        def finish(
            micro, own_ref=own_ref, scatter=scatter, sum_ref=sum_ref, norm_ref=norm_ref,
            low_ref=low_ref, pair_ref=pair_ref,
        ):
            total = own_ref[micro].astype(wide) + scatter.total(micro)
            sum_ref[micro] = total
            value = layer_norm(total, (pair_ref[0:1], pair_ref[1:2]))
            norm_ref[micro] = value
            low_ref[micro] = value.astype(low)

        for micro in range(micros):
            tasks.append(make_task(micro, [], [scatter], compute, finish))
    run_tasks(tasks)


def self_stage(seq, name_id, count, places, sides):
    micros, rows, width = sides[0][1].shape
    length = rows * seq
    head_width = sides[0][4].shape[2]
    heads = head_width // HEAD_DIM
    side_outs = (
        jax.ShapeDtypeStruct((micros, length, 3 * head_width), low),
        jax.ShapeDtypeStruct((micros, length, head_width), low),
        jax.ShapeDtypeStruct((micros, heads, length), wide),
        jax.ShapeDtypeStruct((micros, rows, width), wide),
        jax.ShapeDtypeStruct((micros, rows, width), wide),
        jax.ShapeDtypeStruct((micros, rows, width), low),
    )
    scratch = scatter_scratch(seq, micros, rows, width) * 2
    args = tuple(places) + sides[0] + sides[1]
    outs = stage_call(
        functools.partial(self_kernel, seq, count), name_id, side_outs * 2, scratch, args, 75
    )
    return outs[:6], outs[6:]


def cross_kernel(
    seq, count, kpos_ref, qpos_ref, first_ref, first_low_ref, memory_ref, q_in_ref, kv_in_ref,
    out_ref, prefix_ref, kid_ref, qid_ref, pair_ref, first_all, memory_all, q_ref, kv_ref,
    context_ref, logs_ref, sum_ref, norm_ref, low_ref, *scratch,
):
    links = Links(seq)
    micros, rows, _ = first_ref.shape
    length = first_all.shape[1]
    head_width = prefix_ref.shape[2]
    gathers = [
        Gather(links, memory_ref, memory_all, *scratch[:3]),
        Gather(links, first_low_ref, first_all, *scratch[3:6]),
    ]
    scatter = Scatter(links, rows, *scratch[6:11], scratch[11:])
    ids = (kid_ref, qid_ref, kpos_ref, qpos_ref)
    attention = Attention(q_ref, kv_ref, (0, 0, head_width), prefix_ref, ids, count, False)
    links.enter()

    def compute(micro):
        def chunk(start, size):
            attention.forward(micro, start, size, context_ref, logs_ref)
            return dot(context_ref[micro, pl.ds(start, size)], out_ref[...], 1, 1)

        return (
            project_steps(micro, memory_all, kv_in_ref, kv_ref)
            + project_steps(micro, first_all, q_in_ref, q_ref)
            + half_steps(scatter, micro, length, chunk)
        )

    def finish(micro):
        total = first_ref[micro] + scatter.total(micro)
        sum_ref[micro] = total
        value = layer_norm(total, (pair_ref[0:1], pair_ref[1:2]))
        norm_ref[micro] = value
        low_ref[micro] = value.astype(low)

    run_tasks(
        [make_task(micro, gathers, [scatter], compute, finish) for micro in range(micros)]
    )


def cross_stage(seq, name_id, count, places, args):
    micros, rows, width = args[0].shape
    length = rows * seq
    head_width = args[6].shape[2]
    heads = head_width // HEAD_DIM
    whole = jax.ShapeDtypeStruct((micros, length, width), low)
    outs = (
        whole,
        whole,
        jax.ShapeDtypeStruct((micros, length, head_width), low),
        jax.ShapeDtypeStruct((micros, length, 2 * head_width), low),
        jax.ShapeDtypeStruct((micros, length, head_width), low),
        jax.ShapeDtypeStruct((micros, heads, length), wide),
        jax.ShapeDtypeStruct((micros, rows, width), wide),
        jax.ShapeDtypeStruct((micros, rows, width), wide),
        jax.ShapeDtypeStruct((micros, rows, width), low),
    )
    scratch = gather_scratch(seq, micros) * 2 + scatter_scratch(seq, micros, rows, width)
    return stage_call(
        functools.partial(cross_kernel, seq, count), name_id, outs, scratch,
        tuple(places) + args, 85,
    )


def attend_back_steps(
    attention, micro, length, up_all, out_ref, logs_ref, grad_ref, k_sum, v_sum, pre_ref, up_ref,
    emit=None,
):
    head_width = up_ref.shape[1]
    half = length // 2
    size = min(CHUNK, half)

    def run(first, zero):
        if zero:
            k_sum[...] = jnp.zeros_like(k_sum)
            v_sum[...] = jnp.zeros_like(v_sum)
            if micro == 0:
                pre_ref[...] = jnp.zeros_like(pre_ref)

        def body(start, index):
            place = pl.ds(start, size)
            up_ref[...] = dot(up_all[micro, place], out_ref[...], 1, 0).astype(low)
            attention.backward(
                micro, start, size, up_ref, logs_ref, grad_ref, k_sum, v_sum, pre_ref
            )
            if emit is not None:
                emit(start, index, size)

        loop(first, half // size, size, body)

    def keys():
        grad_ref[micro, :, head_width : 2 * head_width] = k_sum[...].astype(low)
        grad_ref[micro, :, 2 * head_width : 3 * head_width] = v_sum[...].astype(low)

    return [lambda: run(half, True), lambda: run(0, False), keys]


def cross_back_kernel(
    seq, count, kpos_ref, qpos_ref, up_ref, resid_ref, pair_ref, q_ref, kv_ref, logs_ref, q_in_ref,
    kv_in_ref, out_ref, prefix_ref, kid_ref, qid_ref, up_all, grad_ref, pre_ref, first_out,
    memory_out, pair_grad_ref, own_ref, kept_ref, k_sum, v_sum, up_chunk, *scratch,
):
    links = Links(seq)
    micros, rows, _ = own_ref.shape
    length = up_all.shape[1]
    head_width = prefix_ref.shape[2]
    gather = Gather(links, own_ref, up_all, *scratch[:3])
    first_sum = Scatter(links, rows, *scratch[3:8], scratch[8:10])
    memory_sum = Scatter(links, rows, *scratch[10:15], scratch[15:17])
    ids = (kid_ref, qid_ref, kpos_ref, qpos_ref)
    attention = Attention(q_ref, kv_ref, (0, 0, head_width), prefix_ref, ids, count, False)
    links.enter()

    def before(micro):
        prologue(micro, up_ref, resid_ref, pair_ref, own_ref, kept_ref, pair_grad_ref)

    def compute(micro):
        def first_chunk(start, size):
            return dot(
                grad_ref[micro, pl.ds(start, size), 0:head_width], q_in_ref[...], 1, 0
            )

        def memory_chunk(start, size):
            return dot(
                grad_ref[micro, pl.ds(start, size), head_width : 3 * head_width],
                kv_in_ref[...],
                1,
                0,
            )

        attend = attend_back_steps(
            attention, micro, length, up_all, out_ref, logs_ref, grad_ref, k_sum, v_sum, pre_ref,
            up_chunk,
        )
        sums = half_steps(first_sum, micro, length, first_chunk)
        return (
            [attend[0], sums[0], attend[1], sums[1], attend[2]]
            + half_steps(memory_sum, micro, length, memory_chunk)
        )

    def finish(micro):
        first_out[micro] = kept_ref[micro] + first_sum.total(micro)
        memory_out[micro] = memory_sum.total(micro)

    run_tasks(
        [
            make_task(micro, [gather], [first_sum, memory_sum], compute, finish, before)
            for micro in range(micros)
        ]
    )


def cross_back_stage(seq, name_id, count, places, args):
    micros, rows, width = args[0].shape
    length = rows * seq
    head_width = args[9].shape[2]
    own = jax.ShapeDtypeStruct((micros, rows, width), wide)
    outs = (
        jax.ShapeDtypeStruct((micros, length, width), low),
        jax.ShapeDtypeStruct((micros, length, 3 * head_width), low),
        jax.ShapeDtypeStruct((2, PAD_PREFIX, head_width), wide),
        own,
        own,
        jax.ShapeDtypeStruct((2, width), wide),
    )
    scratch = (
        back_scratch(micros, rows, width)
        + sum_scratch(length, head_width)
        + gather_scratch(seq, micros)
        + scatter_scratch(seq, micros, rows, width) * 2
    )
    return stage_call(
        functools.partial(cross_back_kernel, seq, count), name_id, outs, scratch,
        tuple(places) + args, 85,
    )


def back_scratch(micros, rows, width):
    return [pltpu.VMEM((micros, rows, width), low), pltpu.VMEM((micros, rows, width), wide)]


def sum_scratch(length, head_width):
    return [
        pltpu.VMEM((length, head_width), wide),
        pltpu.VMEM((length, head_width), wide),
        pltpu.VMEM((min(CHUNK, length // 2), head_width), low),
    ]


def self_back_kernel(seq, count, causals, *refs):
    kinds = len(causals)
    size = 2 + 3 + 7
    scratch = refs[-(3 + kinds * size) :]
    refs = refs[: -(3 + kinds * size)]
    k_sum, v_sum, up_chunk = scratch[:3]
    places = refs[:2]
    links = Links(seq)
    links.enter()
    tasks = []
    for kind in range(kinds):
        (
            up_ref, resid_ref, pair_ref, qkv_ref, logs_ref, in_ref, out_ref, prefix_ref, kid_ref,
            qid_ref,
        ) = refs[2 + 10 * kind : 12 + 10 * kind]
        up_all, grad_ref, pre_ref, grad_out, pair_grad_ref = refs[
            2 + 10 * kinds + 5 * kind : 7 + 10 * kinds + 5 * kind
        ]
        piece = scratch[3 + size * kind : 3 + size * kind + size]
        own_ref, kept_ref = piece[:2]
        micros, rows, _ = own_ref.shape
        length = up_all.shape[1]
        head_width = prefix_ref.shape[2]
        gather = Gather(links, own_ref, up_all, *piece[2:5])
        scatter = Scatter(links, rows, *piece[5:10], piece[10:12])
        ids = (kid_ref, qid_ref) + tuple(places)
        attention = Attention(
            qkv_ref, qkv_ref, (0, head_width, 2 * head_width), prefix_ref, ids, count, causals[kind]
        )

        def before(
            micro, args=(up_ref, resid_ref, pair_ref, own_ref, kept_ref, pair_grad_ref)
        ):
            prologue(micro, *args)

        def compute(
            micro, attention=attention, up_all=up_all, out_ref=out_ref, logs_ref=logs_ref,
            grad_ref=grad_ref, pre_ref=pre_ref, in_ref=in_ref, scatter=scatter,
        ):
            def chunk(start, size):
                return dot(grad_ref[micro, pl.ds(start, size)], in_ref[...], 1, 0)

            return attend_back_steps(
                attention, micro, length, up_all, out_ref, logs_ref, grad_ref, k_sum, v_sum,
                pre_ref, up_chunk,
            ) + half_steps(scatter, micro, length, chunk)

        def finish(micro, grad_out=grad_out, kept_ref=kept_ref, scatter=scatter):
            grad_out[micro] = kept_ref[micro] + scatter.total(micro)

        for micro in range(micros):
            tasks.append(make_task(micro, [gather], [scatter], compute, finish, before))
    run_tasks(tasks)


def self_back_stage(seq, name_id, count, places, causal, side):
    micros, rows, width = side[0].shape
    length = rows * seq
    head_width = side[7].shape[2]
    outs = (
        jax.ShapeDtypeStruct((micros, length, width), low),
        jax.ShapeDtypeStruct((micros, length, 3 * head_width), low),
        jax.ShapeDtypeStruct((2, PAD_PREFIX, head_width), wide),
        jax.ShapeDtypeStruct((micros, rows, width), wide),
        jax.ShapeDtypeStruct((2, width), wide),
    )
    scratch = sum_scratch(length, head_width) + (
        back_scratch(micros, rows, width)
        + gather_scratch(seq, micros)
        + scatter_scratch(seq, micros, rows, width)
    )
    return stage_call(
        functools.partial(self_back_kernel, seq, count, (causal,)), name_id, outs, scratch,
        tuple(places) + side, 75,
    )


def local(
    seq, ranks,
    source, target, source_segments, target_segments, cotangent,
    encoder_qkv, encoder_output, encoder_prefix, encoder_expand, encoder_contract, encoder_down,
    encoder_up, encoder_norms, decoder_qkv, decoder_output, decoder_prefix, cross_query, cross_kv,
    cross_output, cross_prefix, decoder_expand, decoder_contract, decoder_down, decoder_up,
    decoder_norms,
):
    micro_count, batch_rows, block, width = source.shape
    length = source_segments.shape[2]
    me = lax.axis_index("seq")
    stacked = micro_count * batch_rows
    head_width = width // seq
    slice_cols = encoder_output.shape[1]
    count = encoder_prefix.shape[1]
    hidden = encoder_contract.shape[0] // seq
    adapt = encoder_up.shape[0] // seq
    both = hidden + adapt
    padded = (both + LANES - 1) // LANES * LANES

    sources = source.reshape(stacked, block, width)
    targets = target.reshape(stacked, block, width)

    order = relative(jnp.arange(length, dtype=jnp.int32), seq, me)
    places = (order[:, None], order[None, :])

    def relative_ids(ids):
        rows = [relative(row, seq, me) for row in ids.reshape(stacked, length)]
        value = jnp.stack(rows)
        return value[:, :, None], value[:, None, :]

    source_keys, source_queries = relative_ids(source_segments)
    target_keys, target_queries = relative_ids(target_segments)

    def columns(weight):
        return jnp.swapaxes(weight, -1, -2)

    def gather_rows(value):
        return lax.all_gather(value, "rows", axis=0, tiled=False)

    def stack_columns(pieces):
        gathered = gather_rows(jnp.concatenate(pieces, axis=0))
        outs = []
        start = 0
        for piece in pieces:
            size = piece.shape[0]
            outs.append(gathered[:, start : start + size])
            start += size
        return outs

    def flat_columns(gathered, parts):
        value = gathered.reshape(ranks, parts, slice_cols, width)
        return jnp.swapaxes(value, 0, 1).reshape(parts * ranks * slice_cols, width)

    def split_rows(weight):
        value = columns(weight)
        return value.reshape(slice_cols, seq, -1)

    def exchange(value):
        return lax.all_to_all(value, "seq", 1, 1, tiled=False)

    def ffn_rows(contract, up):
        pieces = [split_rows(contract), split_rows(up) * jnp.asarray(ADAPTER_SCALE, low)]
        if padded > both:
            pieces.append(jnp.zeros((slice_cols, seq, padded - both), low))
        return pieces

    row_pieces = jnp.concatenate(
        [split_rows(encoder_output), split_rows(decoder_output), split_rows(cross_output)]
        + ffn_rows(encoder_contract, encoder_up)
        + ffn_rows(decoder_contract, decoder_up),
        axis=2,
    )
    row_pieces = lax.all_to_all(row_pieces, "seq", 1, 0, tiled=False).reshape(seq, slice_cols, -1)

    qkv_parts = gather_rows(
        jnp.concatenate(
            [
                columns(encoder_qkv).reshape(-1, width),
                columns(decoder_qkv).reshape(-1, width),
            ]
        )
    )
    lead = 512 if 3 * head_width < 512 else 3 * head_width
    front = gather_rows(row_pieces[:, :, :lead])
    late = [
        jnp.concatenate(
            [
                columns(encoder_expand),
                columns(encoder_down),
                columns(cross_query),
                columns(cross_kv).reshape(-1, width),
            ]
        ),
        row_pieces[:, :, lead : 3 * head_width + padded],
        jnp.concatenate([columns(decoder_expand), columns(decoder_down)]),
        row_pieces[:, :, 3 * head_width + padded :],
    ]
    source_all, target_all = gather_stage(seq, 1, (sources, targets))
    source_all, qkv_parts, front, late = lax.optimization_barrier(
        (source_all, qkv_parts, front, late)
    )
    encoder_in = flat_columns(qkv_parts[:, : 3 * slice_cols], 3)
    decoder_in = flat_columns(qkv_parts[:, 3 * slice_cols :], 3)
    front_rows = jnp.swapaxes(front[..., : 3 * head_width], 0, 1).reshape(width, -1)
    encoder_out = front_rows[:, :head_width]
    decoder_out = front_rows[:, head_width : 2 * head_width]
    cross_out = front_rows[:, 2 * head_width :]
    cut = encoder_expand.shape[1]

    def ffn_in(gathered):
        pieces = [gathered[:, :cut].reshape(-1, width), gathered[:, cut:].reshape(-1, width)]
        if padded > both:
            pieces.append(jnp.zeros((padded - both, width), low))
        return jnp.concatenate(pieces)

    def row_order(gathered):
        return jnp.swapaxes(gathered, 0, 1).reshape(width, -1)

    second_parts = gather_rows(late[0])
    rest = gather_rows(late[1])
    prefixes = small_gather(
        jnp.concatenate([encoder_prefix, decoder_prefix, cross_prefix]), [("rows", ranks)]
    )
    prefixes = jnp.moveaxis(prefixes, 0, 2).reshape(6, count, head_width)
    prefixes = jnp.pad(prefixes, ((0, 0), (0, PAD_PREFIX - count), (0, 0)))
    encoder_pre, decoder_pre, cross_pre = prefixes[0:2], prefixes[2:4], prefixes[4:6]

    norm_axes = [("seq", seq), ("rows", ranks)]
    scales = small_gather(
        jnp.concatenate([encoder_norms, decoder_norms]), norm_axes
    )
    scales = jnp.moveaxis(scales, 0, 2).reshape(-1, 2, width).astype(wide)
    norm_count = encoder_norms.shape[0]

    encoder_side, decoder_side = self_stage(
        seq, 2, count, places,
        (
            (
                source_all, sources, encoder_in, encoder_out, encoder_pre, source_keys,
                source_queries, scales[0],
            ),
            (
                target_all, targets, decoder_in, decoder_out, decoder_pre, target_keys,
                target_queries, scales[norm_count],
            ),
        ),
    )
    encoder_qkvs, encoder_ctx, encoder_logs, resid_one, middle, middle_low = encoder_side
    middle_low, second_parts, rest, last = lax.optimization_barrier(
        (middle_low, second_parts, rest, late[2:])
    )
    encoder_two = row_order(jnp.concatenate([front[..., 3 * head_width :], rest], axis=3))
    ffn_cut = cut + encoder_down.shape[1]
    encoder_one = ffn_in(second_parts[:, :ffn_cut])
    cross_in = flat_columns(second_parts[:, ffn_cut:], 3)
    cross_q_in, cross_kv_in = cross_in[:head_width], cross_in[head_width:]
    decoder_one = ffn_in(gather_rows(last[0]))
    decoder_two = row_order(gather_rows(last[1]))

    decoder_qkvs, decoder_ctx, decoder_logs, resid_three, first, first_low = decoder_side
    middle_all, encoder_before, encoder_hidden, resid_two, memory = ffn_stage(
        seq, 3, middle_low, middle, encoder_one, encoder_two, scales[1]
    )
    (
        first_all, memory_all, cross_q, cross_kvs, cross_ctx, cross_logs, resid_four, second,
        second_low,
    ) = cross_stage(
        seq, 4, count, places,
        (
            first, first_low, memory.astype(low), cross_q_in, cross_kv_in, cross_out, cross_pre,
            source_keys, target_queries, scales[norm_count + 1],
        ),
    )
    second_all, decoder_before, decoder_hidden, resid_five, third = ffn_stage(
        seq, 5, second_low, second, decoder_one, decoder_two, scales[norm_count + 2]
    )
    result = third.astype(low)

    def scatter_ranks(value):
        return lax.psum_scatter(value, "rows", scatter_dimension=0, tiled=False)

    def laid(value):
        return with_layout_constraint(value.astype(low), Layout(tuple(range(value.ndim))))

    def column_terms(grad, parts):
        value = grad.reshape(parts, ranks, slice_cols, width)
        return laid(jnp.swapaxes(value, 0, 1))

    def row_terms(grad):
        value = grad.astype(low).T.reshape(seq, ranks, slice_cols, -1)
        return laid(jnp.swapaxes(value, 0, 1))

    def ffn_in_terms(grad):
        return laid(
            jnp.concatenate(
                [
                    grad[:hidden].reshape(ranks, -1, width),
                    grad[hidden:both].reshape(ranks, -1, width),
                ],
                axis=1,
            )
        )

    def flat(value):
        return value.reshape(-1, value.shape[-1])

    norm_grads = {}

    def ffn_back(name_id, index, up, resid, before, hidden_low, rows_all, one, two):
        up_all, slope, out, pair = ffn_back_stage(
            seq, name_id, up, resid, scales[index], before, one, two
        )
        norm_grads[index] = (pair[0:1], pair[1:2])
        two_terms = row_terms(dot(flat(hidden_low), flat(up_all), 0, 0))
        one_terms = ffn_in_terms(dot(flat(slope), flat(rows_all), 0, 0))
        return out, one_terms, two_terms

    def hold(value, terms, sums):
        value, terms, sums = lax.optimization_barrier((value, terms, sums))
        return value, [scatter_ranks(term) for term in terms], sums

    second_up, one_terms, two_terms = ffn_back(
        6, norm_count + 2, cotangent.reshape(stacked, block, width), resid_five, decoder_before,
        decoder_hidden, second_all, decoder_one, decoder_two,
    )
    second_up, ffn_sums, _ = hold(second_up, [two_terms, one_terms], [])

    def keep_pair(index, pair):
        norm_grads[index] = (pair[0:1], pair[1:2])

    second_grad_all, cross_grads, cross_pre_grad, first_up, memory_up, pair = cross_back_stage(
        seq, 7, count, places,
        (
            second_up, resid_four, scales[norm_count + 1], cross_q, cross_kvs, cross_logs,
            cross_q_in, cross_kv_in, cross_out, cross_pre, source_keys, target_queries,
        ),
    )
    keep_pair(norm_count + 1, pair)
    cross_terms = [
        row_terms(dot(flat(cross_ctx), flat(second_grad_all), 0, 0)),
        column_terms(
            jnp.concatenate(
                [
                    dot(flat(cross_grads[:, :, :head_width]), flat(first_all), 0, 0),
                    dot(flat(cross_grads[:, :, head_width:]), flat(memory_all), 0, 0),
                ]
            ),
            3,
        ),
    ]
    first_up, cross_sums, ffn_sums = hold(first_up, cross_terms, ffn_sums)
    decoder_two_grad, decoder_one_grad = ffn_sums

    def self_back(name_id, index, causal, side, context, rows_all, sums):
        grad_all, grads, pre_grad, out, pair = self_back_stage(
            seq, name_id, count, places, causal, side
        )
        grad_all, grads, pre_grad, out, pair, sums = lax.optimization_barrier(
            (grad_all, grads, pre_grad, out, pair, sums)
        )
        keep_pair(index, pair)
        return (
            out,
            pre_grad,
            sums,
            [
                row_terms(dot(flat(context), flat(grad_all), 0, 0)),
                column_terms(dot(flat(grads), flat(rows_all), 0, 0), 3),
            ],
        )

    target_grad, decoder_pre_grad, cross_sums, self_terms = self_back(
        9, norm_count, True,
        (
            first_up, resid_three, scales[norm_count], decoder_qkvs, decoder_logs, decoder_in,
            decoder_out, decoder_pre, target_keys, target_queries,
        ),
        decoder_ctx, target_all, cross_sums,
    )
    memory_up, self_sums, _ = hold(memory_up, self_terms, [])
    cross_out_grad, cross_in_grad = cross_sums

    middle_up, one_terms, two_terms = ffn_back(
        8, 1, memory_up, resid_two, encoder_before, encoder_hidden, middle_all,
        encoder_one, encoder_two,
    )
    middle_up, ffn_sums, self_sums = hold(middle_up, [two_terms, one_terms], self_sums)
    decoder_out_grad, decoder_in_grad = self_sums

    def give_back(pieces):
        value = jnp.concatenate(pieces, axis=2) if len(pieces) > 1 else pieces[0]
        return lax.all_to_all(value, "seq", 0, 1, tiled=False)

    decoder_rows = give_back([decoder_two_grad, cross_out_grad, decoder_out_grad])

    source_grad, encoder_pre_grad, ffn_sums, self_terms = self_back(
        10, 0, False,
        (
            middle_up, resid_one, scales[0], encoder_qkvs, encoder_logs, encoder_in,
            encoder_out, encoder_pre, source_keys, source_queries,
        ),
        encoder_ctx, source_all, ffn_sums,
    )
    source_grad, self_sums, _ = hold(source_grad, self_terms, [])
    encoder_two_grad, encoder_one_grad = ffn_sums
    encoder_out_grad, encoder_in_grad = self_sums
    encoder_rows = give_back([encoder_two_grad])
    encoder_out_rows = give_back([encoder_out_grad])

    def row_grad(value, start, size, scale=None):
        piece = value[:, :, start : start + size].astype(wide)
        if scale is not None:
            piece = piece * scale
        return piece.reshape(slice_cols, -1).T

    def column_grad(value):
        return jnp.swapaxes(value.astype(wide), -1, -2)

    prefix_total = jnp.concatenate([encoder_pre_grad, decoder_pre_grad, cross_pre_grad])[:, :count]
    prefix_total = jnp.moveaxis(prefix_total.reshape(6, count, ranks, slice_cols), 2, 0)
    prefix_total = small_scatter(prefix_total, [("rows", ranks)])
    norm_rows = [row for index in sorted(norm_grads) for row in norm_grads[index]]
    which = lax.broadcasted_iota(jnp.int32, (len(norm_rows), width), 0)
    norm_total = sum(jnp.where(which == k, row, 0.0) for k, row in enumerate(norm_rows))
    norm_total = jnp.moveaxis(norm_total.reshape(-1, 2, seq * ranks, slice_cols), 2, 0)
    norm_total = small_scatter(norm_total, norm_axes)

    shape_out = source.shape
    return (
        result.reshape(shape_out),
        source_grad.reshape(shape_out),
        target_grad.reshape(shape_out),
        column_grad(encoder_in_grad),
        row_grad(encoder_out_rows, 0, head_width),
        prefix_total[0:2],
        column_grad(encoder_one_grad[:cut]),
        row_grad(encoder_rows, 0, hidden),
        column_grad(encoder_one_grad[cut:]),
        row_grad(encoder_rows, hidden, adapt, ADAPTER_SCALE),
        norm_total[:norm_count],
        column_grad(decoder_in_grad),
        row_grad(decoder_rows, padded + head_width, head_width),
        prefix_total[2:4],
        column_grad(cross_in_grad[0]),
        column_grad(cross_in_grad[1:]),
        row_grad(decoder_rows, padded, head_width),
        prefix_total[4:6],
        column_grad(decoder_one_grad[:cut]),
        row_grad(decoder_rows, 0, hidden),
        column_grad(decoder_one_grad[cut:]),
        row_grad(decoder_rows, hidden, adapt, ADAPTER_SCALE),
        norm_total[norm_count:],
    )


def solution(mesh):
    rows = P(None, "rows", "seq", None)
    ids = P(None, "rows", None)
    flat = P(None, ("seq", "rows"))
    deep = P(None, None, ("seq", "rows"))
    weights = (
        deep, flat, deep, flat, flat, flat, flat, deep, deep, flat, deep, flat, deep, flat, deep,
        flat, flat, flat, flat, deep,
    )
    body = functools.partial(local, mesh.shape["seq"], mesh.shape["rows"])
    return jax.shard_map(
        body,
        mesh=mesh,
        in_specs=(rows, rows, ids, ids, rows) + weights,
        out_specs=(rows, rows, rows) + weights,
        check_vma=False,
    )
```

```python
import functools

import jax
import jax.numpy as jnp
from jax import lax
from jax.experimental import pallas as pl
from jax.experimental.layout import Layout, with_layout_constraint
from jax.experimental.pallas import tpu as pltpu
from jax.sharding import PartitionSpec as P

HEADS = 16
HEAD_DIM = 64
EPSILON = 1e-05
MASKED = -1e30
ADAPTER_SCALE = 4.0
SCALING = HEAD_DIM ** (-0.5)
PAD_PREFIX = 32
CHUNK = 256
LANES = 128
VMEM_LIMIT = 60 * 1024 * 1024
HALF_ROOT = 0.7071067811865476
DENSITY = 0.3989422804014327

low = jnp.bfloat16
wide = jnp.float32


def dot(left, right, left_axis, right_axis):
    return lax.dot_general(
        left, right, (((left_axis,), (right_axis,)), ((), ())), preferred_element_type=wide
    )


def bit_list(count):
    bits = []
    value = 1
    while value < count:
        bits.append(value)
        value *= 2
    return bits


def swap_pairs(count, bit):
    return [(index, index ^ bit) for index in range(count)]


def relative(places, seq, me):
    depth = len(bit_list(seq))
    value = places.reshape((2,) * depth + (-1,))
    for axis in range(depth):
        bit = 1 << (depth - 1 - axis)
        value = jnp.where((me & bit) != 0, jnp.flip(value, axis), value)
    return jnp.moveaxis(value, depth - 1, 0).reshape(-1)


def small_gather(value, axes):
    value = value[None]
    for name, count in axes[::-1]:
        me = lax.axis_index(name)
        for bit in bit_list(count):
            other = lax.ppermute(value, name, swap_pairs(count, bit))
            flip = (me & bit) != 0
            value = jnp.where(
                flip, jnp.concatenate([other, value]), jnp.concatenate([value, other])
            )
    return value


def small_scatter(value, axes):
    for name, count in axes:
        me = lax.axis_index(name)
        for bit in bit_list(count)[::-1]:
            half = value.shape[0] // 2
            flip = (me & bit) != 0
            lower, upper = value[:half], value[half:]
            sent = lax.ppermute(jnp.where(flip, lower, upper), name, swap_pairs(count, bit))
            value = jnp.where(flip, upper, lower) + sent
    return value[0]


def normalized(tensor):
    average = jnp.mean(tensor, axis=-1, keepdims=True)
    centered = tensor - average
    spread = jnp.mean(centered * centered, axis=-1, keepdims=True)
    inverse = lax.rsqrt(spread + EPSILON)
    return centered * inverse, inverse


def layer_norm(tensor, scales):
    return normalized(tensor)[0] * scales[0] + scales[1]


def norm_back(upstream, tensor, scales):
    unit, inverse = normalized(tensor)
    slope = upstream * scales[0]
    grad = inverse * (
        slope
        - jnp.mean(slope, axis=-1, keepdims=True)
        - unit * jnp.mean(slope * unit, axis=-1, keepdims=True)
    )
    return (
        grad,
        jnp.sum(upstream * unit, axis=0, keepdims=True),
        jnp.sum(upstream, axis=0, keepdims=True),
    )


def gelu_exact(tensor):
    return tensor * (0.5 + 0.5 * lax.erf(tensor * HALF_ROOT))


def gelu_slope(tensor):
    density = jnp.exp(-0.5 * tensor * tensor) * DENSITY
    return 0.5 + 0.5 * lax.erf(tensor * HALF_ROOT) + tensor * density


class Links:
    def __init__(self, seq):
        self.seq = seq
        self.far = [bit for bit in bit_list(seq) if bit > 1]
        self.orders = [self.far, self.far[::-1]]
        self.half = seq // 2
        self.me = lax.axis_index("seq")

    def place(self, mask):
        return (mask & 1) * self.half + (mask >> 1)

    def device(self, bit):
        return {"seq": jnp.bitwise_xor(self.me, bit)}

    def enter(self):
        barrier = pltpu.get_barrier_semaphore()
        bits = bit_list(self.seq)
        for bit in bits:
            pl.semaphore_signal(
                barrier, inc=1, device_id=self.device(bit), device_id_type=pl.DeviceIdType.MESH
            )
        pl.semaphore_wait(barrier, len(bits))

    def copy(self, source, target, send_sem, recv_sem, bit):
        return pltpu.make_async_remote_copy(
            src_ref=source,
            dst_ref=target,
            send_sem=send_sem,
            recv_sem=recv_sem,
            device_id=self.device(bit),
            device_id_type=pl.DeviceIdType.MESH,
        )


def span(bits):
    masks = [0]
    for bit in bits:
        masks = masks + [mask | bit for mask in masks]
    return masks


class Gather:
    def __init__(self, links, own_ref, all_ref, sends, recvs, local_sem):
        self.links, self.own, self.all = links, own_ref, all_ref
        self.sends, self.recvs, self.local = sends, recvs, local_sem
        self.rows = own_ref.shape[1]
        self.cut = self.rows // 2

    def at(self, micro, mask, part):
        start = self.links.place(mask) * self.rows + part * self.cut
        return self.all.at[micro, start : start + self.cut]

    def piece(self, micro, mask, part):
        if mask & 1:
            return 1
        seen = 0
        for bit in self.links.orders[part]:
            if mask & bit:
                seen = bit
        return seen

    def send(self, micro, mask, part, bit):
        there = mask ^ bit
        source = self.at(micro, mask, part)
        if mask == 0:
            source = self.own.at[micro, part * self.cut : (part + 1) * self.cut]
        self.links.copy(
            source,
            self.at(micro, there, part),
            self.sends.at[micro, self.links.place(there), part],
            self.recvs.at[micro, self.links.place(there), part],
            bit,
        ).start()

    def descriptor(self, micro, mask, part):
        bit = self.piece(micro, mask, part)
        source = self.at(micro, mask ^ bit, part)
        if mask ^ bit == 0:
            source = self.own.at[micro, part * self.cut : (part + 1) * self.cut]
        place = self.links.place(mask)
        return self.links.copy(
            source,
            self.at(micro, mask, part),
            self.sends.at[micro, place, part],
            self.recvs.at[micro, place, part],
            bit,
        )

    def keep_own(self, micro):
        return pltpu.make_async_copy(
            self.own.at[micro], self.all.at[micro, 0 : self.rows], self.local.at[micro]
        )

    def start(self, micro):
        for part in range(2):
            self.send(micro, 0, part, self.links.orders[part][0])
        for part in range(2):
            self.send(micro, 0, part, 1)
        self.keep_own(micro).start()

    def advance(self, micro, phase):
        count = len(self.links.far)
        for part in range(2):
            order = self.links.orders[part]
            fresh = [mask | order[phase] for mask in span(order[:phase])]
            for mask in fresh:
                self.descriptor(micro, mask, part).wait_recv()
            if phase + 1 < count:
                for mask in span(order[: phase + 1]):
                    self.send(micro, mask, part, order[phase + 1])
            for mask in fresh:
                self.send(micro, mask, part, 1)

    def phases(self):
        return len(self.links.far)

    def near(self, micro):
        for part in range(2):
            for mask in span(self.links.far):
                self.descriptor(micro, mask | 1, part).wait_recv()
        self.keep_own(micro).wait()

    def drain(self, micro):
        for part in range(2):
            for mask in range(1, self.links.seq):
                self.descriptor(micro, mask, part).wait_send()


class Scatter:
    def __init__(self, links, rows, sum_ref, near_send, near_recv, far_send, far_recv, sems):
        self.links, self.rows, self.cut = links, rows, rows // 2
        self.sum, self.near_send, self.near_recv = sum_ref, near_send, near_recv
        self.far_send, self.far_recv = far_send, far_recv
        self.near_sems, self.far_sems = sems

    def near_copy(self, micro, index):
        view = slice(index * self.rows, (index + 1) * self.rows)
        return self.links.copy(
            self.near_send.at[micro, view],
            self.near_recv.at[micro, view],
            self.near_sems.at[0, micro, index],
            self.near_sems.at[1, micro, index],
            1,
        )

    def start(self, micro, indexes):
        for index in indexes:
            self.near_copy(micro, index).start()

    def far_view(self, index, part):
        start = index * self.rows + part * self.cut
        return slice(start, start + self.cut)

    def bit_of(self, index, part):
        last = 0
        for bit in self.links.orders[part]:
            if (index * 2) & bit:
                last = bit
        return last

    def far_copy(self, micro, index, part):
        view = self.far_view(index, part)
        return self.links.copy(
            self.far_send.at[micro, view],
            self.far_recv.at[micro, view],
            self.far_sems.at[0, micro, index, part],
            self.far_sems.at[1, micro, index, part],
            self.bit_of(index, part),
        )

    def send_far(self, micro, index, part, value):
        self.far_send[micro, self.far_view(index, part)] = value.astype(low)
        self.far_copy(micro, index, part).start()

    def near_sum(self, micro):
        count = len(self.links.far)
        first = {}
        for part in range(2):
            bit = self.links.orders[part][count - 1]
            first[part] = [mask | bit for mask in span(self.links.orders[part][: count - 1])]
        ordered = sorted(range(self.links.half), key=lambda index: index == 0)
        for index in ordered:
            self.near_copy(micro, index).wait_recv()
            for part in range(2):
                view = self.far_view(index, part)
                value = self.sum[micro, view] + self.near_recv[micro, view].astype(wide)
                if index * 2 in first[part]:
                    self.send_far(micro, index, part, value)
                else:
                    self.sum[micro, view] = value

    def far_sum(self, micro, phase):
        count = len(self.links.far)
        for part in range(2):
            order = self.links.orders[part]
            bit = order[count - 1 - phase]
            remain = span(order[: count - 1 - phase])
            following = order[count - 2 - phase] if phase + 1 < count else 0
            for mask in sorted(remain, key=lambda mask: (mask & following) == 0):
                index, came = mask // 2, (mask | bit) // 2
                self.far_copy(micro, came, part).wait_recv()
                view = self.far_view(index, part)
                value = self.sum[micro, view] + self.far_recv[
                    micro, self.far_view(came, part)
                ].astype(wide)
                if mask & following:
                    self.send_far(micro, index, part, value)
                else:
                    self.sum[micro, view] = value

    def total(self, micro):
        return self.sum[micro, 0 : self.rows]

    def phases(self):
        return len(self.links.far)

    def drain(self, micro):
        for index in range(self.links.half):
            self.near_copy(micro, index).wait_send()
        for part in range(2):
            for index in range(1, self.links.half):
                self.far_copy(micro, index, part).wait_send()


def gather_scratch(seq, micros):
    return [
        pltpu.SemaphoreType.DMA((micros, seq, 2)),
        pltpu.SemaphoreType.DMA((micros, seq, 2)),
        pltpu.SemaphoreType.DMA((micros,)),
    ]


def scatter_scratch(seq, micros, rows, width):
    half = seq // 2
    part = pltpu.VMEM((micros, half * rows, width), low)
    return [
        pltpu.VMEM((micros, half * rows, width), wide),
        part,
        part,
        part,
        part,
        pltpu.SemaphoreType.DMA((2, micros, half)),
        pltpu.SemaphoreType.DMA((2, micros, half, 2)),
    ]


NEAR_GAP, FAR_GAP, SHORT_GAP = 3.0, 6.0, 0.1


def arrive_steps(gathers, micro):
    steps = []
    for phase in range(gathers[0].phases() if gathers else 0):
        for index, gather in enumerate(gathers):
            gap = SHORT_GAP if index else FAR_GAP
            steps.append((functools.partial(gather.advance, micro, phase), gap))
    for index, gather in enumerate(gathers):
        gap = SHORT_GAP if index else NEAR_GAP
        steps.append((functools.partial(gather.near, micro), gap))
    return steps


def leave_steps(scatters, finish, micro):
    steps = []
    for index, scatter in enumerate(scatters):
        gap = SHORT_GAP if index else NEAR_GAP
        steps.append((functools.partial(scatter.near_sum, micro), gap))
    for phase in range(scatters[0].phases()):
        for index, scatter in enumerate(scatters):
            gap = SHORT_GAP if index else FAR_GAP
            steps.append((functools.partial(scatter.far_sum, micro, phase), gap))
    return steps + [(functools.partial(finish, micro), SHORT_GAP)]


def half_steps(scatter, micro, length, chunk, cost):
    half = length // 2
    size = min(CHUNK, half)

    def odd():
        def body(index, carry):
            start = pl.multiple_of(half + index * size, size)
            place = pl.ds(pl.multiple_of(index * size, size), size)
            scatter.near_send[micro, place] = chunk(start, size).astype(low)
            return carry

        lax.fori_loop(0, half // size, body, 0)
        scatter.start(micro, range(scatter.links.half))

    def even():
        def body(index, carry):
            start = pl.multiple_of(index * size, size)
            scatter.sum[micro, pl.ds(start, size)] = chunk(start, size)
            return carry

        lax.fori_loop(0, half // size, body, 0)

    return [(odd, cost), (even, cost)]


def prologue(micro, up_ref, resid_ref, pair_ref, own_ref, kept_ref, pair_grad_ref):
    gains = (pair_ref[0:1], pair_ref[1:2])
    grad, gain_grad, shift_grad = norm_back(up_ref[micro].astype(wide), resid_ref[micro], gains)
    kept_ref[micro] = grad
    own_ref[micro] = grad.astype(low)
    if micro == 0:
        pair_grad_ref[0:1] = gain_grad
        pair_grad_ref[1:2] = shift_grad
    else:
        pair_grad_ref[0:1] += gain_grad
        pair_grad_ref[1:2] += shift_grad


class Task:
    def __init__(self, begin, arrive, compute, leave, drain, load=None, store=None):
        self.begin, self.arrive, self.compute = begin, arrive, compute
        self.leave, self.drain, self.load, self.store = leave, drain, load, store


class Waits:
    def __init__(self):
        self.time, self.queues = 0.0, []

    def add(self, steps):
        if steps:
            self.queues.append([list(steps), self.time + steps[0][1]])

    def take(self, entry):
        queue = entry[0]
        queue.pop(0)[0]()
        self.time += 0.4
        if queue:
            entry[1] = self.time + queue[0][1]
        else:
            self.queues.remove(entry)

    def run(self, step, cost):
        step()
        self.time += cost
        ready = [entry for entry in self.queues if entry[1] <= self.time]
        while ready:
            self.take(ready[0])
            ready = [entry for entry in self.queues if entry[1] <= self.time]

    def finish(self, steps):
        while any(entry[0] and entry[0][-1] is steps[-1] for entry in self.queues):
            entry = min(self.queues, key=lambda entry: entry[1])
            self.time = max(self.time, entry[1])
            self.take(entry)


def run_tasks(tasks, io, fill=(), fill_load=None):
    waits = Waits()
    for task in tasks[:2]:
        task.begin()
        waits.add(task.arrive)
    for index, task in enumerate(tasks):
        if task.arrive:
            waits.finish(task.arrive)
        io.load(task.load)
        for step, cost in task.compute:
            waits.run(step, cost)
        io.store(task.store)
        waits.add(task.leave)
        if index + 2 < len(tasks):
            tasks[index + 2].begin()
            waits.add(tasks[index + 2].arrive)
    if fill:
        io.load(fill_load)
        for step, cost in fill:
            waits.run(step, cost)
    while waits.queues:
        waits.take(min(waits.queues, key=lambda entry: entry[1]))
    for task in tasks:
        task.drain()
    io.close()


def make_task(micro, gathers, scatters, compute, finish, before=None, load=None, store=None):
    def begin():
        if before is not None:
            before(micro)
        for gather in gathers:
            gather.start(micro)

    def drain():
        for item in gathers + scatters:
            item.drain(micro)

    arrive = arrive_steps(gathers, micro)
    leave = leave_steps(scatters, finish, micro) if scatters else []
    return Task(begin, arrive, compute(micro), leave, drain, load, store)


class Operands:
    def __init__(self, ins, outs, in_sems, out_sems):
        self.ins, self.outs, self.in_sems, self.out_sems = ins, outs, in_sems, out_sems
        self.open = []

    def start(self):
        for index, (_, source, target) in enumerate(self.ins):
            pltpu.make_async_copy(source, target, self.in_sems.at[index]).start()

    def load(self, key):
        for index, (name, source, target) in enumerate(self.ins):
            if key is not None and name == key:
                pltpu.make_async_copy(source, target, self.in_sems.at[index]).wait()

    def copy_out(self, index, micro):
        _, source, target = self.outs[index]
        return pltpu.make_async_copy(
            source.at[micro], target.at[micro], self.out_sems.at[index, micro]
        )

    def store(self, key):
        if key is None:
            return
        name, micro = key
        for index, (group, _, _) in enumerate(self.outs):
            if group == name:
                self.copy_out(index, micro).start()
                self.open.append((index, micro))

    def close(self):
        for index, micro in self.open:
            self.copy_out(index, micro).wait()


def stage_call(kernel, name_id, outs, scratch, args, micros, lazy=None, early=None):
    lazy, early = lazy or {}, early or {}
    count, given, own = len(args), len(outs), len(scratch)
    lazy_places, early_places = sorted(lazy), sorted(early)
    parts = max([outs[place].shape[0] for place in early_places] + [1])

    def body(*refs):
        ins, results = list(refs[:count]), list(refs[count : count + given])
        own_scratch = refs[count + given : count + given + own]
        extra = refs[count + given + own :]
        loads, stores = [], []
        for index, place in enumerate(lazy_places):
            loads.append((lazy[place], ins[place], extra[index]))
            ins[place] = extra[index]
        for index, place in enumerate(early_places):
            buffer = extra[len(lazy_places) + index]
            stores.append((early[place], buffer, results[place]))
            results[place] = buffer
        io = Operands(loads, stores, extra[-2], extra[-1])
        io.start()
        kernel(io, *ins, *results, *own_scratch)

    held = [pltpu.VMEM(args[place].shape, args[place].dtype) for place in lazy_places]
    held += [pltpu.VMEM(outs[place].shape, outs[place].dtype) for place in early_places]
    sems = [
        pltpu.SemaphoreType.DMA((max(len(lazy_places), 1),)),
        pltpu.SemaphoreType.DMA((max(len(early_places), 1), parts)),
    ]
    near, far = pl.BlockSpec(memory_space=pltpu.VMEM), pl.BlockSpec(memory_space=pl.ANY)
    return pl.pallas_call(
        body,
        out_shape=tuple(outs),
        in_specs=[far if place in lazy else near for place in range(count)],
        out_specs=tuple(far if place in early else near for place in range(given)),
        scratch_shapes=list(scratch) + held + sems,
        compiler_params=pltpu.CompilerParams(
            collective_id=name_id, has_side_effects=True, vmem_limit_bytes=VMEM_LIMIT
        ),
        cost_estimate=pl.CostEstimate(
            flops=micros * 2_500_000_000, bytes_accessed=1 << 24, transcendentals=0
        ),
    )(*args)


def ffn_kernel(
    seq, io, own_ref, resid_ref, one_ref, two_ref, pair_ref, all_ref, before_ref, hidden_ref,
    sum_ref, norm_ref, low_ref, *scratch,
):
    links = Links(seq)
    micros, rows, _ = own_ref.shape
    length = all_ref.shape[1]
    gather = Gather(links, own_ref, all_ref, *scratch[:3])
    scatter = Scatter(links, rows, *scratch[3:8], scratch[8:])
    links.enter()

    def compute(micro):
        def chunk(start, size):
            place = pl.ds(start, size)
            before = dot(all_ref[micro, place], one_ref[...], 1, 1)
            before_ref[micro, place] = before
            after = gelu_exact(before).astype(low)
            hidden_ref[micro, place] = after
            return dot(after, two_ref[...], 1, 1)

        return half_steps(scatter, micro, length, chunk, 2.5)

    def finish(micro):
        total = resid_ref[micro] + scatter.total(micro)
        sum_ref[micro] = total
        value = layer_norm(total, (pair_ref[0:1], pair_ref[1:2]))
        norm_ref[micro] = value
        low_ref[micro] = value.astype(low)

    tasks = [
        make_task(
            micro, [gather], [scatter], compute, finish, None, 0 if micro == 0 else None, (0, micro)
        )
        for micro in range(micros)
    ]
    run_tasks(tasks, io)


def ffn_stage(seq, name_id, own, resid, one, two, pair):
    micros, rows, width = own.shape
    hidden = one.shape[0]
    length = rows * seq
    outs = (
        jax.ShapeDtypeStruct((micros, length, width), low),
        jax.ShapeDtypeStruct((micros, length, hidden), wide),
        jax.ShapeDtypeStruct((micros, length, hidden), low),
        jax.ShapeDtypeStruct((micros, rows, width), wide),
        jax.ShapeDtypeStruct((micros, rows, width), wide),
        jax.ShapeDtypeStruct((micros, rows, width), low),
    )
    scratch = gather_scratch(seq, micros) + scatter_scratch(seq, micros, rows, width)
    return stage_call(
        functools.partial(ffn_kernel, seq), name_id, outs, scratch,
        (own, resid, one, two, pair), 60, {1: 0, 2: 0, 3: 0, 4: 0}, {0: 0, 1: 0, 2: 0},
    )


def token_sum(left_ref, lanes, right_ref, micros):
    total = None
    for micro in range(micros):
        value = dot(left_ref[micro, :, lanes], right_ref[micro], 0, 0)
        total = value if total is None else total + value
    return total


def ffn_back_kernel(
    seq, ranks, hidden, io, up_ref, resid_ref, pair_ref, before_ref, one_ref, two_ref, rows_ref,
    hidden_ref, out_ref, pair_grad_ref, expand_ref, down_ref, two_terms_ref, all_ref, slope_ref,
    own_ref, kept_ref, *scratch,
):
    links = Links(seq)
    micros, rows, width = own_ref.shape
    length = all_ref.shape[1]
    adapt = down_ref.shape[0] * down_ref.shape[1]
    gather = Gather(links, own_ref, all_ref, *scratch[:3])
    scatter = Scatter(links, rows, *scratch[3:8], scratch[8:])
    links.enter()

    def before(micro):
        prologue(micro, up_ref, resid_ref, pair_ref, own_ref, kept_ref, pair_grad_ref)

    def compute(micro):
        def chunk(start, size):
            place = pl.ds(start, size)
            slope = dot(all_ref[micro, place], two_ref[...], 1, 0)
            slope = (slope * gelu_slope(before_ref[micro, place])).astype(low)
            slope_ref[micro, place] = slope
            return dot(slope, one_ref[...], 1, 0)

        return half_steps(scatter, micro, length, chunk, 2.5)

    def finish(micro):
        out_ref[micro] = kept_ref[micro] + scatter.total(micro)

    cut = hidden // ranks

    def one_tile(start):
        value = token_sum(slope_ref, slice(start, start + LANES), rows_ref, micros)
        if start < hidden:
            for part in range(0, LANES, cut):
                rank = (start + part) // cut
                expand_ref[rank] = value[part : part + cut].astype(low)
        else:
            down_ref[...] = value[:adapt].reshape(ranks, adapt // ranks, width).astype(low)

    def two_tile(start):
        value = token_sum(hidden_ref, slice(start, start + LANES), all_ref, micros).T
        value = value.reshape(seq, ranks, width // (seq * ranks), LANES)
        for rank in range(ranks):
            two_terms_ref[rank, :, :, start : start + LANES] = value[:, rank].astype(low)

    starts = range(0, slope_ref.shape[2], LANES)
    fill = [
        (functools.partial(tile, start), 1.2) for tile in (two_tile, one_tile) for start in starts
    ]
    tasks = [
        make_task(
            micro, [gather], [scatter], compute, finish, before, 0 if micro == 0 else None
        )
        for micro in range(micros)
    ]
    run_tasks(tasks, io, fill, 1)


def ffn_back_stage(seq, ranks, hidden, adapt, name_id, up, resid, pair, before, one, two, rows_all,
                   hidden_low):
    micros, rows, width = up.shape
    padded = one.shape[0]
    length = rows * seq
    outs = (
        jax.ShapeDtypeStruct((micros, rows, width), wide),
        jax.ShapeDtypeStruct((2, width), wide),
        jax.ShapeDtypeStruct((ranks, hidden // ranks, width), low),
        jax.ShapeDtypeStruct((ranks, adapt // ranks, width), low),
        jax.ShapeDtypeStruct((ranks, seq, width // (seq * ranks), padded), low),
    )
    scratch = (
        [pltpu.VMEM((micros, length, width), low), pltpu.VMEM((micros, length, padded), low)]
        + back_scratch(micros, rows, width)
        + gather_scratch(seq, micros)
        + scatter_scratch(seq, micros, rows, width)
    )
    return stage_call(
        functools.partial(ffn_back_kernel, seq, ranks, hidden), name_id, outs, scratch,
        (up, resid, pair, before, one, two, rows_all, hidden_low), 65,
        {3: 0, 4: 0, 5: 0, 6: 1, 7: 1},
    )


def gather_kernel(seq, count, io, *refs):
    links = Links(seq)
    owns, alls, scratch = refs[:count], refs[count : 2 * count], refs[2 * count :]
    gathers = [
        Gather(links, owns[k], alls[k], *scratch[3 * k : 3 * k + 3]) for k in range(count)
    ]
    links.enter()
    tasks = []
    for gather in gathers:
        for micro in range(owns[0].shape[0]):
            tasks.append(make_task(micro, [gather], [], lambda micro: [], None))
    for task in tasks:
        task.begin()
    for phase in range(len(tasks[0].arrive)):
        for task in tasks:
            task.arrive[phase][0]()
    for task in tasks:
        task.drain()


def gather_stage(seq, name_id, owns):
    micros, rows, width = owns[0].shape
    outs = tuple(jax.ShapeDtypeStruct((micros, seq * rows, width), low) for _ in owns)
    scratch = gather_scratch(seq, micros) * len(owns)
    return stage_call(
        functools.partial(gather_kernel, seq, len(owns)), name_id, outs, scratch, owns, 45
    )


class Attention:
    def __init__(self, q_ref, kv_ref, offsets, prefix_ref, ids, count, causal):
        self.q, self.kv, self.offsets, self.prefix = q_ref, kv_ref, offsets, prefix_ref
        self.key_ids, self.query_ids, self.key_places, self.query_places = ids
        self.count, self.causal = count, causal
        self.heads = prefix_ref.shape[2] // HEAD_DIM

    def load(self, micro, head, place):
        q_at, k_at, v_at = (at + head * HEAD_DIM for at in self.offsets)
        queries = self.q[micro, place, q_at : q_at + HEAD_DIM] * jnp.asarray(SCALING, low)
        keys = self.kv[micro, :, k_at : k_at + HEAD_DIM]
        values = self.kv[micro, :, v_at : v_at + HEAD_DIM]
        return queries, keys, values

    def scores(self, micro, keys, queries, lanes, place):
        scores = dot(keys, queries, 1, 1)
        allowed = self.key_ids[micro] == self.query_ids[micro, :, place]
        if self.causal:
            allowed = allowed & (self.key_places[...] <= self.query_places[:, place])
        scores = jnp.where(allowed, scores, MASKED)
        extra = dot(self.prefix[0, :, lanes], queries, 1, 1)
        rows = lax.broadcasted_iota(jnp.int32, extra.shape, 0)
        return scores, jnp.where(rows < self.count, extra, MASKED)

    def forward(self, micro, start, size, context_ref, logs_ref):
        place = pl.ds(start, size)
        for head in range(self.heads):
            lanes = slice(head * HEAD_DIM, (head + 1) * HEAD_DIM)
            queries, keys, values = self.load(micro, head, place)
            scores, extra = self.scores(micro, keys, queries, lanes, place)
            peak = jnp.maximum(
                jnp.max(scores, axis=0, keepdims=True), jnp.max(extra, axis=0, keepdims=True)
            )
            scores = jnp.exp(scores - peak)
            extra = jnp.exp(extra - peak)
            total = jnp.sum(scores, axis=0, keepdims=True) + jnp.sum(extra, axis=0, keepdims=True)
            context = dot(values, scores.astype(low), 0, 0)
            context = context + dot(self.prefix[1, :, lanes], extra.astype(low), 0, 0)
            context_ref[micro, place, lanes] = (context / total).T.astype(low)
            logs_ref[micro, head : head + 1, place] = peak + jnp.log(total)

    def backward(self, micro, start, size, up_ref, logs_ref, grad_ref, k_sum, v_sum, pre_ref):
        place = pl.ds(start, size)
        for head in range(self.heads):
            lanes = slice(head * HEAD_DIM, (head + 1) * HEAD_DIM)
            queries, keys, values = self.load(micro, head, place)
            scores, extra = self.scores(micro, keys, queries, lanes, place)
            logs = logs_ref[micro, head : head + 1, place]
            weights = jnp.exp(scores - logs)
            extra = jnp.exp(extra - logs)
            up = up_ref[:, lanes]
            dots = dot(values, up, 1, 1)
            extra_dots = dot(self.prefix[1, :, lanes], up, 1, 1)
            centre = jnp.sum(weights * dots, axis=0, keepdims=True) + jnp.sum(
                extra * extra_dots, axis=0, keepdims=True
            )
            slope = (weights * (dots - centre)).astype(low)
            extra_slope = (extra * (extra_dots - centre)).astype(low)
            query_grad = dot(keys, slope, 0, 0) + dot(self.prefix[0, :, lanes], extra_slope, 0, 0)
            grad_ref[micro, place, lanes] = (query_grad * SCALING).T.astype(low)
            k_sum[:, lanes] += dot(slope, queries, 1, 0)
            v_sum[:, lanes] += dot(weights.astype(low), up, 1, 0)
            pre_ref[0, :, lanes] += dot(extra_slope, queries, 1, 0)
            pre_ref[1, :, lanes] += dot(extra.astype(low), up, 1, 0)


def loop(first, count, size, body):
    def step(index, carry):
        body(pl.multiple_of(first + index * size, size), index)
        return carry

    lax.fori_loop(0, count, step, 0)


def project_steps(micro, rows_ref, weight_ref, out_ref):
    length = rows_ref.shape[1]
    size = min(CHUNK, length)

    def body(start, index):
        place = pl.ds(start, size)
        out_ref[micro, place] = dot(rows_ref[micro, place], weight_ref[...], 1, 1).astype(low)

    return [(lambda: loop(0, length // size, size, body), 1.3)]


def self_kernel(seq, count, io, *refs):
    kinds = 2
    scratch = refs[-kinds * 7 :]
    refs = refs[: -kinds * 7]
    places = refs[:2]
    links = Links(seq)
    links.enter()
    tasks = []
    for kind in range(kinds):
        (all_ref, own_ref, in_ref, out_ref, prefix_ref, kid_ref, qid_ref, pair_ref) = refs[
            2 + 8 * kind : 10 + 8 * kind
        ]
        (qkv_ref, context_ref, logs_ref, sum_ref, norm_ref, low_ref) = refs[
            2 + 8 * kinds + 6 * kind : 8 + 8 * kinds + 6 * kind
        ]
        micros, rows, _ = own_ref.shape
        length = all_ref.shape[1]
        head_width = prefix_ref.shape[2]
        piece = scratch[7 * kind : 7 * kind + 7]
        scatter = Scatter(links, rows, *piece[:5], piece[5:])
        ids = (kid_ref, qid_ref) + tuple(places)
        attention = Attention(
            qkv_ref, qkv_ref, (0, head_width, 2 * head_width), prefix_ref, ids, count, kind == 1
        )

        def compute(
            micro, attention=attention, context_ref=context_ref, logs_ref=logs_ref,
            out_ref=out_ref, all_ref=all_ref, in_ref=in_ref, qkv_ref=qkv_ref, scatter=scatter,
        ):
            def chunk(start, size):
                attention.forward(micro, start, size, context_ref, logs_ref)
                return dot(context_ref[micro, pl.ds(start, size)], out_ref[...], 1, 1)

            return project_steps(micro, all_ref, in_ref, qkv_ref) + half_steps(
                scatter, micro, length, chunk, 4.2
            )

        def finish(
            micro, own_ref=own_ref, scatter=scatter, sum_ref=sum_ref, norm_ref=norm_ref,
            low_ref=low_ref, pair_ref=pair_ref,
        ):
            total = own_ref[micro].astype(wide) + scatter.total(micro)
            sum_ref[micro] = total
            value = layer_norm(total, (pair_ref[0:1], pair_ref[1:2]))
            norm_ref[micro] = value
            low_ref[micro] = value.astype(low)

        for micro in range(micros):
            load = kind if micro == 0 else None
            tasks.append(
                make_task(micro, [], [scatter], compute, finish, None, load, (kind, micro))
            )
    run_tasks(tasks, io)


def self_stage(seq, name_id, count, places, sides):
    micros, rows, width = sides[0][1].shape
    length = rows * seq
    head_width = sides[0][4].shape[2]
    heads = head_width // HEAD_DIM
    side_outs = (
        jax.ShapeDtypeStruct((micros, length, 3 * head_width), low),
        jax.ShapeDtypeStruct((micros, length, head_width), low),
        jax.ShapeDtypeStruct((micros, heads, length), wide),
        jax.ShapeDtypeStruct((micros, rows, width), wide),
        jax.ShapeDtypeStruct((micros, rows, width), wide),
        jax.ShapeDtypeStruct((micros, rows, width), low),
    )
    scratch = scatter_scratch(seq, micros, rows, width) * 2
    args = tuple(places) + sides[0] + sides[1]
    outs = stage_call(
        functools.partial(self_kernel, seq, count), name_id, side_outs * 2, scratch, args, 75,
        {10: 1, 11: 1, 12: 1, 13: 1, 15: 1}, {0: 0, 1: 0, 6: 1, 7: 1},
    )
    return outs[:6], outs[6:]


def cross_kernel(
    seq, count, io, kpos_ref, qpos_ref, first_ref, first_low_ref, memory_ref, q_in_ref, kv_in_ref,
    out_ref, prefix_ref, kid_ref, qid_ref, pair_ref, first_all, memory_all, q_ref, kv_ref,
    context_ref, logs_ref, sum_ref, norm_ref, low_ref, *scratch,
):
    links = Links(seq)
    micros, rows, _ = first_ref.shape
    length = first_all.shape[1]
    head_width = prefix_ref.shape[2]
    gathers = [
        Gather(links, memory_ref, memory_all, *scratch[:3]),
        Gather(links, first_low_ref, first_all, *scratch[3:6]),
    ]
    scatter = Scatter(links, rows, *scratch[6:11], scratch[11:])
    ids = (kid_ref, qid_ref, kpos_ref, qpos_ref)
    attention = Attention(q_ref, kv_ref, (0, 0, head_width), prefix_ref, ids, count, False)
    links.enter()

    def compute(micro):
        def chunk(start, size):
            attention.forward(micro, start, size, context_ref, logs_ref)
            return dot(context_ref[micro, pl.ds(start, size)], out_ref[...], 1, 1)

        return (
            project_steps(micro, memory_all, kv_in_ref, kv_ref)
            + project_steps(micro, first_all, q_in_ref, q_ref)
            + half_steps(scatter, micro, length, chunk, 4.2)
        )

    def finish(micro):
        total = first_ref[micro] + scatter.total(micro)
        sum_ref[micro] = total
        value = layer_norm(total, (pair_ref[0:1], pair_ref[1:2]))
        norm_ref[micro] = value
        low_ref[micro] = value.astype(low)

    tasks = [
        make_task(
            micro, gathers, [scatter], compute, finish, None, 0 if micro == 0 else None, (0, micro)
        )
        for micro in range(micros)
    ]
    run_tasks(tasks, io)


def cross_stage(seq, name_id, count, places, args):
    micros, rows, width = args[0].shape
    length = rows * seq
    head_width = args[6].shape[2]
    heads = head_width // HEAD_DIM
    whole = jax.ShapeDtypeStruct((micros, length, width), low)
    outs = (
        whole,
        whole,
        jax.ShapeDtypeStruct((micros, length, head_width), low),
        jax.ShapeDtypeStruct((micros, length, 2 * head_width), low),
        jax.ShapeDtypeStruct((micros, length, head_width), low),
        jax.ShapeDtypeStruct((micros, heads, length), wide),
        jax.ShapeDtypeStruct((micros, rows, width), wide),
        jax.ShapeDtypeStruct((micros, rows, width), wide),
        jax.ShapeDtypeStruct((micros, rows, width), low),
    )
    scratch = gather_scratch(seq, micros) * 2 + scatter_scratch(seq, micros, rows, width)
    return stage_call(
        functools.partial(cross_kernel, seq, count), name_id, outs, scratch,
        tuple(places) + args, 85, {place: 0 for place in (2, 5, 6, 7, 8, 9, 10)},
        {place: 0 for place in range(5)},
    )


def attend_back_steps(
    attention, micro, length, up_all, out_ref, logs_ref, grad_ref, k_sum, v_sum, pre_ref, up_ref,
    emit=None,
):
    head_width = up_ref.shape[1]
    half = length // 2
    size = min(CHUNK, half)

    def run(first, zero):
        if zero:
            k_sum[...] = jnp.zeros_like(k_sum)
            v_sum[...] = jnp.zeros_like(v_sum)
            if micro == 0:
                pre_ref[...] = jnp.zeros_like(pre_ref)

        def body(start, index):
            place = pl.ds(start, size)
            up_ref[...] = dot(up_all[micro, place], out_ref[...], 1, 0).astype(low)
            attention.backward(
                micro, start, size, up_ref, logs_ref, grad_ref, k_sum, v_sum, pre_ref
            )
            if emit is not None:
                emit(start, index, size)

        loop(first, half // size, size, body)

    def keys():
        grad_ref[micro, :, head_width : 2 * head_width] = k_sum[...].astype(low)
        grad_ref[micro, :, 2 * head_width : 3 * head_width] = v_sum[...].astype(low)

    return [(lambda: run(half, True), 5.0), (lambda: run(0, False), 5.0), (keys, 0.5)]


def term_steps(context_ref, up_all, grad_ref, sources, in_terms_ref, out_terms_ref):
    micros = grad_ref.shape[0]
    ranks, seq, cols, head_width = out_terms_ref.shape
    width = up_all.shape[2]

    def out_tile():
        value = token_sum(context_ref, slice(0, head_width), up_all, micros).T
        value = value.reshape(seq, ranks, cols, head_width)
        for rank in range(ranks):
            out_terms_ref[rank] = value[:, rank].astype(low)

    def in_tile(part):
        lanes = slice(part * head_width, (part + 1) * head_width)
        value = token_sum(grad_ref, lanes, sources[part], micros)
        in_terms_ref[:, part] = value.reshape(ranks, cols, width).astype(low)

    return [(out_tile, 1.5)] + [(functools.partial(in_tile, part), 1.0) for part in range(3)]


def term_shapes(seq, ranks, width, head_width):
    cols = width // (seq * ranks)
    return (
        jax.ShapeDtypeStruct((ranks, 3, cols, width), low),
        jax.ShapeDtypeStruct((ranks, seq, cols, head_width), low),
    )


def cross_back_kernel(
    seq, count, io, kpos_ref, qpos_ref, up_ref, resid_ref, pair_ref, q_ref, kv_ref, logs_ref,
    q_in_ref, kv_in_ref, out_ref, prefix_ref, kid_ref, qid_ref, first_all, memory_all, context_ref,
    pre_ref, first_out, memory_out, pair_grad_ref, in_terms_ref, out_terms_ref, up_all, grad_ref,
    own_ref, kept_ref, k_sum, v_sum, up_chunk, *scratch,
):
    links = Links(seq)
    micros, rows, _ = own_ref.shape
    length = up_all.shape[1]
    head_width = prefix_ref.shape[2]
    gather = Gather(links, own_ref, up_all, *scratch[:3])
    first_sum = Scatter(links, rows, *scratch[3:8], scratch[8:10])
    memory_sum = Scatter(links, rows, *scratch[10:15], scratch[15:17])
    ids = (kid_ref, qid_ref, kpos_ref, qpos_ref)
    attention = Attention(q_ref, kv_ref, (0, 0, head_width), prefix_ref, ids, count, False)
    links.enter()

    def before(micro):
        prologue(micro, up_ref, resid_ref, pair_ref, own_ref, kept_ref, pair_grad_ref)

    def compute(micro):
        def first_chunk(start, size):
            return dot(
                grad_ref[micro, pl.ds(start, size), 0:head_width], q_in_ref[...], 1, 0
            )

        def memory_chunk(start, size):
            return dot(
                grad_ref[micro, pl.ds(start, size), head_width : 3 * head_width],
                kv_in_ref[...],
                1,
                0,
            )

        attend = attend_back_steps(
            attention, micro, length, up_all, out_ref, logs_ref, grad_ref, k_sum, v_sum, pre_ref,
            up_chunk,
        )
        sums = half_steps(first_sum, micro, length, first_chunk, 0.6)
        return (
            [attend[0], sums[0], attend[1], sums[1], attend[2]]
            + half_steps(memory_sum, micro, length, memory_chunk, 0.8)
        )

    def finish(micro):
        first_out[micro] = kept_ref[micro] + first_sum.total(micro)
        memory_out[micro] = memory_sum.total(micro)

    tasks = [
        make_task(
            micro, [gather], [first_sum, memory_sum], compute, finish, before,
            0 if micro == 0 else None,
        )
        for micro in range(micros)
    ]
    fill = term_steps(
        context_ref, up_all, grad_ref, (first_all, memory_all, memory_all), in_terms_ref,
        out_terms_ref,
    )
    run_tasks(tasks, io, fill, 1)


def cross_back_stage(seq, ranks, name_id, count, places, args):
    micros, rows, width = args[0].shape
    length = rows * seq
    head_width = args[9].shape[2]
    own = jax.ShapeDtypeStruct((micros, rows, width), wide)
    outs = (
        jax.ShapeDtypeStruct((2, PAD_PREFIX, head_width), wide),
        own,
        own,
        jax.ShapeDtypeStruct((2, width), wide),
    ) + term_shapes(seq, ranks, width, head_width)
    scratch = (
        [
            pltpu.VMEM((micros, length, width), low),
            pltpu.VMEM((micros, length, 3 * head_width), low),
        ]
        + back_scratch(micros, rows, width)
        + sum_scratch(length, head_width)
        + gather_scratch(seq, micros)
        + scatter_scratch(seq, micros, rows, width) * 2
    )
    lazy = {place: 0 for place in range(5, 14)}
    lazy.update({14: 1, 15: 1, 16: 1})
    return stage_call(
        functools.partial(cross_back_kernel, seq, count), name_id, outs, scratch,
        tuple(places) + args, 85, lazy,
    )


def back_scratch(micros, rows, width):
    return [pltpu.VMEM((micros, rows, width), low), pltpu.VMEM((micros, rows, width), wide)]


def sum_scratch(length, head_width):
    return [
        pltpu.VMEM((length, head_width), wide),
        pltpu.VMEM((length, head_width), wide),
        pltpu.VMEM((min(CHUNK, length // 2), head_width), low),
    ]


def self_back_kernel(
    seq, count, causal, io, kpos_ref, qpos_ref, up_ref, resid_ref, pair_ref, qkv_ref, logs_ref,
    in_ref, out_ref, prefix_ref, kid_ref, qid_ref, context_ref, rows_ref, pre_ref, grad_out,
    pair_grad_ref, in_terms_ref, out_terms_ref, up_all, grad_ref, own_ref, kept_ref, k_sum, v_sum,
    up_chunk, *scratch,
):
    links = Links(seq)
    micros, rows, _ = own_ref.shape
    length = up_all.shape[1]
    head_width = prefix_ref.shape[2]
    gather = Gather(links, own_ref, up_all, *scratch[:3])
    scatter = Scatter(links, rows, *scratch[3:8], scratch[8:10])
    ids = (kid_ref, qid_ref, kpos_ref, qpos_ref)
    attention = Attention(
        qkv_ref, qkv_ref, (0, head_width, 2 * head_width), prefix_ref, ids, count, causal
    )
    links.enter()

    def before(micro):
        prologue(micro, up_ref, resid_ref, pair_ref, own_ref, kept_ref, pair_grad_ref)

    def compute(micro):
        def chunk(start, size):
            return dot(grad_ref[micro, pl.ds(start, size)], in_ref[...], 1, 0)

        return attend_back_steps(
            attention, micro, length, up_all, out_ref, logs_ref, grad_ref, k_sum, v_sum,
            pre_ref, up_chunk,
        ) + half_steps(scatter, micro, length, chunk, 0.9)

    def finish(micro):
        grad_out[micro] = kept_ref[micro] + scatter.total(micro)

    tasks = [
        make_task(
            micro, [gather], [scatter], compute, finish, before, 0 if micro == 0 else None
        )
        for micro in range(micros)
    ]
    fill = term_steps(
        context_ref, up_all, grad_ref, (rows_ref,) * 3, in_terms_ref, out_terms_ref
    )
    run_tasks(tasks, io, fill, 1)


def self_back_stage(seq, ranks, name_id, count, places, causal, side):
    micros, rows, width = side[0].shape
    length = rows * seq
    head_width = side[7].shape[2]
    outs = (
        jax.ShapeDtypeStruct((2, PAD_PREFIX, head_width), wide),
        jax.ShapeDtypeStruct((micros, rows, width), wide),
        jax.ShapeDtypeStruct((2, width), wide),
    ) + term_shapes(seq, ranks, width, head_width)
    scratch = (
        [
            pltpu.VMEM((micros, length, width), low),
            pltpu.VMEM((micros, length, 3 * head_width), low),
        ]
        + back_scratch(micros, rows, width)
        + sum_scratch(length, head_width)
        + gather_scratch(seq, micros)
        + scatter_scratch(seq, micros, rows, width)
    )
    lazy = {place: 0 for place in range(5, 12)}
    lazy.update({12: 1, 13: 1})
    return stage_call(
        functools.partial(self_back_kernel, seq, count, causal), name_id, outs, scratch,
        tuple(places) + side, 75, lazy,
    )


def local(
    seq, ranks,
    source, target, source_segments, target_segments, cotangent,
    encoder_qkv, encoder_output, encoder_prefix, encoder_expand, encoder_contract, encoder_down,
    encoder_up, encoder_norms, decoder_qkv, decoder_output, decoder_prefix, cross_query, cross_kv,
    cross_output, cross_prefix, decoder_expand, decoder_contract, decoder_down, decoder_up,
    decoder_norms,
):
    micro_count, batch_rows, block, width = source.shape
    length = source_segments.shape[2]
    me = lax.axis_index("seq")
    stacked = micro_count * batch_rows
    head_width = width // seq
    slice_cols = encoder_output.shape[1]
    count = encoder_prefix.shape[1]
    hidden = encoder_contract.shape[0] // seq
    adapt = encoder_up.shape[0] // seq
    both = hidden + adapt
    padded = (both + LANES - 1) // LANES * LANES

    sources = source.reshape(stacked, block, width)
    targets = target.reshape(stacked, block, width)

    order = relative(jnp.arange(length, dtype=jnp.int32), seq, me)
    places = (order[:, None], order[None, :])

    def relative_ids(ids):
        rows = [relative(row, seq, me) for row in ids.reshape(stacked, length)]
        value = jnp.stack(rows)
        return value[:, :, None], value[:, None, :]

    source_keys, source_queries = relative_ids(source_segments)
    target_keys, target_queries = relative_ids(target_segments)

    def columns(weight):
        return jnp.swapaxes(weight, -1, -2)

    def gather_rows(value):
        return lax.all_gather(value, "rows", axis=0, tiled=False)

    def stack_columns(pieces):
        gathered = gather_rows(jnp.concatenate(pieces, axis=0))
        outs = []
        start = 0
        for piece in pieces:
            size = piece.shape[0]
            outs.append(gathered[:, start : start + size])
            start += size
        return outs

    def flat_columns(gathered, parts):
        value = gathered.reshape(ranks, parts, slice_cols, width)
        return jnp.swapaxes(value, 0, 1).reshape(parts * ranks * slice_cols, width)

    def split_rows(weight):
        value = columns(weight)
        return value.reshape(slice_cols, seq, -1)

    def exchange(value):
        return lax.all_to_all(value, "seq", 1, 1, tiled=False)

    def ffn_rows(contract, up):
        pieces = [split_rows(contract), split_rows(up) * jnp.asarray(ADAPTER_SCALE, low)]
        if padded > both:
            pieces.append(jnp.zeros((slice_cols, seq, padded - both), low))
        return pieces

    row_pieces = jnp.concatenate(
        [split_rows(encoder_output), split_rows(decoder_output), split_rows(cross_output)]
        + ffn_rows(encoder_contract, encoder_up)
        + ffn_rows(decoder_contract, decoder_up),
        axis=2,
    )
    row_pieces = lax.all_to_all(row_pieces, "seq", 1, 0, tiled=False).reshape(seq, slice_cols, -1)

    qkv_parts = gather_rows(
        jnp.concatenate(
            [
                columns(encoder_qkv).reshape(-1, width),
                columns(decoder_qkv).reshape(-1, width),
            ]
        )
    )
    lead = 512 if 3 * head_width < 512 else 3 * head_width
    front = gather_rows(row_pieces[:, :, :lead])
    late = [
        jnp.concatenate(
            [
                columns(encoder_expand),
                columns(encoder_down),
                columns(cross_query),
                columns(cross_kv).reshape(-1, width),
            ]
        ),
        row_pieces[:, :, lead : 3 * head_width + padded],
        jnp.concatenate([columns(decoder_expand), columns(decoder_down)]),
        row_pieces[:, :, 3 * head_width + padded :],
    ]
    source_all, target_all = gather_stage(seq, 1, (sources, targets))
    source_all, qkv_parts, front, late = lax.optimization_barrier(
        (source_all, qkv_parts, front, late)
    )
    encoder_in = flat_columns(qkv_parts[:, : 3 * slice_cols], 3)
    decoder_in = flat_columns(qkv_parts[:, 3 * slice_cols :], 3)
    front_rows = jnp.swapaxes(front[..., : 3 * head_width], 0, 1).reshape(width, -1)
    encoder_out = front_rows[:, :head_width]
    decoder_out = front_rows[:, head_width : 2 * head_width]
    cross_out = front_rows[:, 2 * head_width :]
    cut = encoder_expand.shape[1]

    def ffn_in(gathered):
        pieces = [gathered[:, :cut].reshape(-1, width), gathered[:, cut:].reshape(-1, width)]
        if padded > both:
            pieces.append(jnp.zeros((padded - both, width), low))
        return jnp.concatenate(pieces)

    def row_order(gathered):
        return jnp.swapaxes(gathered, 0, 1).reshape(width, -1)

    second_parts = gather_rows(late[0])
    rest = gather_rows(late[1])
    prefixes = small_gather(
        jnp.concatenate([encoder_prefix, decoder_prefix, cross_prefix]), [("rows", ranks)]
    )
    prefixes = jnp.moveaxis(prefixes, 0, 2).reshape(6, count, head_width)
    prefixes = jnp.pad(prefixes, ((0, 0), (0, PAD_PREFIX - count), (0, 0)))
    encoder_pre, decoder_pre, cross_pre = prefixes[0:2], prefixes[2:4], prefixes[4:6]

    norm_axes = [("seq", seq), ("rows", ranks)]
    scales = small_gather(
        jnp.concatenate([encoder_norms, decoder_norms]), norm_axes
    )
    scales = jnp.moveaxis(scales, 0, 2).reshape(-1, 2, width).astype(wide)
    norm_count = encoder_norms.shape[0]

    encoder_side, decoder_side = self_stage(
        seq, 2, count, places,
        (
            (
                source_all, sources, encoder_in, encoder_out, encoder_pre, source_keys,
                source_queries, scales[0],
            ),
            (
                target_all, targets, decoder_in, decoder_out, decoder_pre, target_keys,
                target_queries, scales[norm_count],
            ),
        ),
    )
    encoder_qkvs, encoder_ctx, encoder_logs, resid_one, middle, middle_low = encoder_side
    middle_low, second_parts, rest, last = lax.optimization_barrier(
        (middle_low, second_parts, rest, late[2:])
    )
    encoder_two = row_order(jnp.concatenate([front[..., 3 * head_width :], rest], axis=3))
    ffn_cut = cut + encoder_down.shape[1]
    encoder_one = ffn_in(second_parts[:, :ffn_cut])
    cross_in = flat_columns(second_parts[:, ffn_cut:], 3)
    cross_q_in, cross_kv_in = cross_in[:head_width], cross_in[head_width:]
    decoder_one = ffn_in(gather_rows(last[0]))
    decoder_two = row_order(gather_rows(last[1]))

    decoder_qkvs, decoder_ctx, decoder_logs, resid_three, first, first_low = decoder_side
    middle_all, encoder_before, encoder_hidden, resid_two, _, memory_low = ffn_stage(
        seq, 3, middle_low, middle, encoder_one, encoder_two, scales[1]
    )
    (
        first_all, memory_all, cross_q, cross_kvs, cross_ctx, cross_logs, resid_four, second,
        second_low,
    ) = cross_stage(
        seq, 4, count, places,
        (
            first, first_low, memory_low, cross_q_in, cross_kv_in, cross_out, cross_pre,
            source_keys, target_queries, scales[norm_count + 1],
        ),
    )
    second_all, decoder_before, decoder_hidden, resid_five, _, result = ffn_stage(
        seq, 5, second_low, second, decoder_one, decoder_two, scales[norm_count + 2]
    )

    def scatter_ranks(value):
        return lax.psum_scatter(value, "rows", scatter_dimension=0, tiled=False)

    norm_grads = {}

    def ffn_back(name_id, index, up, resid, before, hidden_low, rows_all, one, two):
        out, pair, expand, down, two_terms = ffn_back_stage(
            seq, ranks, hidden, adapt, name_id, up, resid, scales[index], before, one, two,
            rows_all, hidden_low,
        )
        keep_pair(index, pair)
        return out, [two_terms, jnp.concatenate([expand, down], axis=1)]

    def hold(value, terms, sums):
        value, terms, sums = lax.optimization_barrier((value, terms, sums))
        return value, [scatter_ranks(term) for term in terms], sums

    def keep_pair(index, pair):
        norm_grads[index] = (pair[0:1], pair[1:2])

    second_up, terms = ffn_back(
        6, norm_count + 2, cotangent.reshape(stacked, block, width), resid_five, decoder_before,
        decoder_hidden, second_all, decoder_one, decoder_two,
    )
    second_up, ffn_sums, _ = hold(second_up, terms, [])

    cross_pre_grad, first_up, memory_up, pair, in_terms, out_terms = cross_back_stage(
        seq, ranks, 7, count, places,
        (
            second_up, resid_four, scales[norm_count + 1], cross_q, cross_kvs, cross_logs,
            cross_q_in, cross_kv_in, cross_out, cross_pre, source_keys, target_queries,
            first_all, memory_all, cross_ctx,
        ),
    )
    keep_pair(norm_count + 1, pair)
    first_up, cross_sums, ffn_sums = hold(first_up, [out_terms, in_terms], ffn_sums)
    decoder_two_grad, decoder_one_grad = ffn_sums

    def self_back(name_id, index, causal, side, sums):
        held = self_back_stage(seq, ranks, name_id, count, places, causal, side)
        held, sums = lax.optimization_barrier((held, sums))
        pre_grad, out, pair, in_terms, out_terms = held
        keep_pair(index, pair)
        return out, pre_grad, sums, [out_terms, in_terms]

    target_grad, decoder_pre_grad, cross_sums, self_terms = self_back(
        9, norm_count, True,
        (
            first_up, resid_three, scales[norm_count], decoder_qkvs, decoder_logs, decoder_in,
            decoder_out, decoder_pre, target_keys, target_queries, decoder_ctx, target_all,
        ),
        cross_sums,
    )
    memory_up, self_sums, _ = hold(memory_up, self_terms, [])
    cross_out_grad, cross_in_grad = cross_sums

    middle_up, terms = ffn_back(
        8, 1, memory_up, resid_two, encoder_before, encoder_hidden, middle_all,
        encoder_one, encoder_two,
    )
    middle_up, ffn_sums, self_sums = hold(middle_up, terms, self_sums)
    decoder_out_grad, decoder_in_grad = self_sums

    def give_back(pieces):
        value = jnp.concatenate(pieces, axis=2) if len(pieces) > 1 else pieces[0]
        return lax.all_to_all(value, "seq", 0, 1, tiled=False)

    decoder_rows = give_back([decoder_two_grad, cross_out_grad, decoder_out_grad])

    source_grad, encoder_pre_grad, ffn_sums, self_terms = self_back(
        10, 0, False,
        (
            middle_up, resid_one, scales[0], encoder_qkvs, encoder_logs, encoder_in,
            encoder_out, encoder_pre, source_keys, source_queries, encoder_ctx, source_all,
        ),
        ffn_sums,
    )
    source_grad, self_sums, _ = hold(source_grad, self_terms, [])
    encoder_two_grad, encoder_one_grad = ffn_sums
    encoder_out_grad, encoder_in_grad = self_sums
    encoder_rows = give_back([encoder_two_grad])
    encoder_out_rows = give_back([encoder_out_grad])

    def row_grad(value, start, size, scale=None):
        piece = value[:, :, start : start + size].astype(wide)
        if scale is not None:
            piece = piece * scale
        return piece.reshape(slice_cols, -1).T

    def column_grad(value):
        return jnp.swapaxes(value.astype(wide), -1, -2)

    prefix_total = jnp.concatenate([encoder_pre_grad, decoder_pre_grad, cross_pre_grad])[:, :count]
    prefix_total = jnp.moveaxis(prefix_total.reshape(6, count, ranks, slice_cols), 2, 0)
    prefix_total = small_scatter(prefix_total, [("rows", ranks)])
    norm_rows = [row for index in sorted(norm_grads) for row in norm_grads[index]]
    which = lax.broadcasted_iota(jnp.int32, (len(norm_rows), width), 0)
    norm_total = sum(jnp.where(which == k, row, 0.0) for k, row in enumerate(norm_rows))
    norm_total = jnp.moveaxis(norm_total.reshape(-1, 2, seq * ranks, slice_cols), 2, 0)
    norm_total = small_scatter(norm_total, norm_axes)

    shape_out = source.shape
    return (
        result.reshape(shape_out),
        source_grad.reshape(shape_out),
        target_grad.reshape(shape_out),
        column_grad(encoder_in_grad),
        row_grad(encoder_out_rows, 0, head_width),
        prefix_total[0:2],
        column_grad(encoder_one_grad[:cut]),
        row_grad(encoder_rows, 0, hidden),
        column_grad(encoder_one_grad[cut:]),
        row_grad(encoder_rows, hidden, adapt, ADAPTER_SCALE),
        norm_total[:norm_count],
        column_grad(decoder_in_grad),
        row_grad(decoder_rows, padded + head_width, head_width),
        prefix_total[2:4],
        column_grad(cross_in_grad[0]),
        column_grad(cross_in_grad[1:]),
        row_grad(decoder_rows, padded, head_width),
        prefix_total[4:6],
        column_grad(decoder_one_grad[:cut]),
        row_grad(decoder_rows, 0, hidden),
        column_grad(decoder_one_grad[cut:]),
        row_grad(decoder_rows, hidden, adapt, ADAPTER_SCALE),
        norm_total[norm_count:],
    )


def solution(mesh):
    rows = P(None, "rows", "seq", None)
    ids = P(None, "rows", None)
    flat = P(None, ("seq", "rows"))
    deep = P(None, None, ("seq", "rows"))
    weights = (
        deep, flat, deep, flat, flat, flat, flat, deep, deep, flat, deep, flat, deep, flat, deep,
        flat, flat, flat, flat, deep,
    )
    body = functools.partial(local, mesh.shape["seq"], mesh.shape["rows"])
    return jax.shard_map(
        body,
        mesh=mesh,
        in_specs=(rows, rows, ids, ids, rows) + weights,
        out_specs=(rows, rows, rows) + weights,
        check_vma=False,
    )
```

```python
import functools

import jax
import jax.numpy as jnp
from jax import lax
from jax.experimental import pallas as pl
from jax.experimental.layout import Layout, with_layout_constraint
from jax.experimental.pallas import tpu as pltpu
from jax.sharding import PartitionSpec as P

HEADS = 16
HEAD_DIM = 64
EPSILON = 1e-05
MASKED = -1e30
ADAPTER_SCALE = 4.0
SCALING = HEAD_DIM ** (-0.5)
PAD_PREFIX = 32
CHUNK = 256
LANES = 128
VMEM_LIMIT = 60 * 1024 * 1024
HALF_ROOT = 0.7071067811865476
DENSITY = 0.3989422804014327

low = jnp.bfloat16
wide = jnp.float32


def dot(left, right, left_axis, right_axis):
    return lax.dot_general(
        left, right, (((left_axis,), (right_axis,)), ((), ())), preferred_element_type=wide
    )


def bit_list(count):
    bits = []
    value = 1
    while value < count:
        bits.append(value)
        value *= 2
    return bits


def swap_pairs(count, bit):
    return [(index, index ^ bit) for index in range(count)]


def relative(places, seq, me):
    depth = len(bit_list(seq))
    value = places.reshape((2,) * depth + (-1,))
    for axis in range(depth):
        bit = 1 << (depth - 1 - axis)
        value = jnp.where((me & bit) != 0, jnp.flip(value, axis), value)
    return jnp.moveaxis(value, depth - 1, 0).reshape(-1)


def small_scatter(value, axes):
    for name, count in axes:
        me = lax.axis_index(name)
        for bit in bit_list(count)[::-1]:
            half = value.shape[0] // 2
            flip = (me & bit) != 0
            lower, upper = value[:half], value[half:]
            sent = lax.ppermute(jnp.where(flip, lower, upper), name, swap_pairs(count, bit))
            value = jnp.where(flip, upper, lower) + sent
    return value[0]


def normalized(tensor):
    average = jnp.mean(tensor, axis=-1, keepdims=True)
    centered = tensor - average
    spread = jnp.mean(centered * centered, axis=-1, keepdims=True)
    inverse = lax.rsqrt(spread + EPSILON)
    return centered * inverse, inverse


def layer_norm(tensor, scales):
    return normalized(tensor)[0] * scales[0] + scales[1]


def norm_back(upstream, tensor, scales):
    unit, inverse = normalized(tensor)
    slope = upstream * scales[0]
    grad = inverse * (
        slope
        - jnp.mean(slope, axis=-1, keepdims=True)
        - unit * jnp.mean(slope * unit, axis=-1, keepdims=True)
    )
    return (
        grad,
        jnp.sum(upstream * unit, axis=0, keepdims=True),
        jnp.sum(upstream, axis=0, keepdims=True),
    )


def gelu_exact(tensor):
    return tensor * (0.5 + 0.5 * lax.erf(tensor * HALF_ROOT))


def gelu_slope(tensor):
    density = jnp.exp(-0.5 * tensor * tensor) * DENSITY
    return 0.5 + 0.5 * lax.erf(tensor * HALF_ROOT) + tensor * density


class Links:
    def __init__(self, seq):
        self.seq = seq
        self.far = [bit for bit in bit_list(seq) if bit > 1]
        self.orders = [self.far, self.far[::-1]]
        self.half = seq // 2
        self.me = lax.axis_index("seq")

    def place(self, mask):
        return (mask & 1) * self.half + (mask >> 1)

    def device(self, bit):
        return {"seq": jnp.bitwise_xor(self.me, bit)}

    def enter(self, others=()):
        barrier = pltpu.get_barrier_semaphore()
        bits = bit_list(self.seq)
        for bit in bits:
            pl.semaphore_signal(
                barrier, inc=1, device_id=self.device(bit), device_id_type=pl.DeviceIdType.MESH
            )
        count = len(bits)
        for other in others:
            count += other.greet(barrier)
        pl.semaphore_wait(barrier, count)

    def copy(self, source, target, send_sem, recv_sem, bit):
        return pltpu.make_async_remote_copy(
            src_ref=source,
            dst_ref=target,
            send_sem=send_sem,
            recv_sem=recv_sem,
            device_id=self.device(bit),
            device_id_type=pl.DeviceIdType.MESH,
        )


def span(bits):
    masks = [0]
    for bit in bits:
        masks = masks + [mask | bit for mask in masks]
    return masks


class Gather:
    def __init__(self, links, own_ref, all_ref, sends, recvs, local_sem):
        self.links, self.own, self.all = links, own_ref, all_ref
        self.sends, self.recvs, self.local = sends, recvs, local_sem
        self.rows = own_ref.shape[1]
        self.cut = self.rows // 2

    def at(self, micro, mask, part):
        start = self.links.place(mask) * self.rows + part * self.cut
        return self.all.at[micro, start : start + self.cut]

    def piece(self, micro, mask, part):
        if mask & 1:
            return 1
        seen = 0
        for bit in self.links.orders[part]:
            if mask & bit:
                seen = bit
        return seen

    def send(self, micro, mask, part, bit):
        there = mask ^ bit
        source = self.at(micro, mask, part)
        if mask == 0:
            source = self.own.at[micro, part * self.cut : (part + 1) * self.cut]
        self.links.copy(
            source,
            self.at(micro, there, part),
            self.sends.at[micro, self.links.place(there), part],
            self.recvs.at[micro, self.links.place(there), part],
            bit,
        ).start()

    def descriptor(self, micro, mask, part):
        bit = self.piece(micro, mask, part)
        source = self.at(micro, mask ^ bit, part)
        if mask ^ bit == 0:
            source = self.own.at[micro, part * self.cut : (part + 1) * self.cut]
        place = self.links.place(mask)
        return self.links.copy(
            source,
            self.at(micro, mask, part),
            self.sends.at[micro, place, part],
            self.recvs.at[micro, place, part],
            bit,
        )

    def keep_own(self, micro):
        return pltpu.make_async_copy(
            self.own.at[micro], self.all.at[micro, 0 : self.rows], self.local.at[micro]
        )

    def start(self, micro):
        for part in range(2):
            self.send(micro, 0, part, self.links.orders[part][0])
        for part in range(2):
            self.send(micro, 0, part, 1)
        self.keep_own(micro).start()

    def advance(self, micro, phase):
        count = len(self.links.far)
        for part in range(2):
            order = self.links.orders[part]
            fresh = [mask | order[phase] for mask in span(order[:phase])]
            for mask in fresh:
                self.descriptor(micro, mask, part).wait_recv()
            if phase + 1 < count:
                for mask in span(order[: phase + 1]):
                    self.send(micro, mask, part, order[phase + 1])
            for mask in fresh:
                self.send(micro, mask, part, 1)

    def phases(self):
        return len(self.links.far)

    def near(self, micro):
        for part in range(2):
            for mask in span(self.links.far):
                self.descriptor(micro, mask | 1, part).wait_recv()
        self.keep_own(micro).wait()

    def drain(self, micro):
        for part in range(2):
            for mask in range(1, self.links.seq):
                self.descriptor(micro, mask, part).wait_send()


class Scatter:
    def __init__(self, links, rows, sum_ref, near_send, near_recv, far_send, far_recv, sems):
        self.links, self.rows, self.cut = links, rows, rows // 2
        self.sum, self.near_send, self.near_recv = sum_ref, near_send, near_recv
        self.far_send, self.far_recv = far_send, far_recv
        self.near_sems, self.far_sems = sems

    def near_copy(self, micro, index):
        view = slice(index * self.rows, (index + 1) * self.rows)
        return self.links.copy(
            self.near_send.at[micro, view],
            self.near_recv.at[micro, view],
            self.near_sems.at[0, micro, index],
            self.near_sems.at[1, micro, index],
            1,
        )

    def start(self, micro, indexes):
        for index in indexes:
            self.near_copy(micro, index).start()

    def far_view(self, index, part):
        start = index * self.rows + part * self.cut
        return slice(start, start + self.cut)

    def bit_of(self, index, part):
        last = 0
        for bit in self.links.orders[part]:
            if (index * 2) & bit:
                last = bit
        return last

    def far_copy(self, micro, index, part):
        view = self.far_view(index, part)
        return self.links.copy(
            self.far_send.at[micro, view],
            self.far_recv.at[micro, view],
            self.far_sems.at[0, micro, index, part],
            self.far_sems.at[1, micro, index, part],
            self.bit_of(index, part),
        )

    def send_far(self, micro, index, part, value):
        self.far_send[micro, self.far_view(index, part)] = value.astype(low)
        self.far_copy(micro, index, part).start()

    def near_sum(self, micro):
        count = len(self.links.far)
        first = {}
        for part in range(2):
            bit = self.links.orders[part][count - 1]
            first[part] = [mask | bit for mask in span(self.links.orders[part][: count - 1])]
        ordered = sorted(range(self.links.half), key=lambda index: index == 0)
        for index in ordered:
            self.near_copy(micro, index).wait_recv()
            for part in range(2):
                view = self.far_view(index, part)
                value = self.sum[micro, view] + self.near_recv[micro, view].astype(wide)
                if index * 2 in first[part]:
                    self.send_far(micro, index, part, value)
                else:
                    self.sum[micro, view] = value

    def far_sum(self, micro, phase):
        count = len(self.links.far)
        for part in range(2):
            order = self.links.orders[part]
            bit = order[count - 1 - phase]
            remain = span(order[: count - 1 - phase])
            following = order[count - 2 - phase] if phase + 1 < count else 0
            for mask in sorted(remain, key=lambda mask: (mask & following) == 0):
                index, came = mask // 2, (mask | bit) // 2
                self.far_copy(micro, came, part).wait_recv()
                view = self.far_view(index, part)
                value = self.sum[micro, view] + self.far_recv[
                    micro, self.far_view(came, part)
                ].astype(wide)
                if mask & following:
                    self.send_far(micro, index, part, value)
                else:
                    self.sum[micro, view] = value

    def total(self, micro):
        return self.sum[micro, 0 : self.rows]

    def phases(self):
        return len(self.links.far)

    def drain(self, micro):
        for index in range(self.links.half):
            self.near_copy(micro, index).wait_send()
        for part in range(2):
            for index in range(1, self.links.half):
                self.far_copy(micro, index, part).wait_send()


def gather_scratch(seq, micros):
    return [
        pltpu.SemaphoreType.DMA((micros, seq, 2)),
        pltpu.SemaphoreType.DMA((micros, seq, 2)),
        pltpu.SemaphoreType.DMA((micros,)),
    ]


def scatter_scratch(seq, micros, rows, width):
    half = seq // 2
    part = pltpu.VMEM((micros, half * rows, width), low)
    return [
        pltpu.VMEM((micros, half * rows, width), wide),
        part,
        part,
        part,
        part,
        pltpu.SemaphoreType.DMA((2, micros, half)),
        pltpu.SemaphoreType.DMA((2, micros, half, 2)),
    ]


NEAR_GAP, FAR_GAP, SHORT_GAP = 3.0, 6.0, 0.1


def arrive_steps(gathers, micro):
    steps = []
    for phase in range(gathers[0].phases() if gathers else 0):
        for index, gather in enumerate(gathers):
            gap = SHORT_GAP if index else FAR_GAP
            steps.append((functools.partial(gather.advance, micro, phase), gap))
    for index, gather in enumerate(gathers):
        gap = SHORT_GAP if index else NEAR_GAP
        steps.append((functools.partial(gather.near, micro), gap))
    return steps


def leave_steps(scatters, finish, micro):
    steps = []
    for index, scatter in enumerate(scatters):
        gap = SHORT_GAP if index else NEAR_GAP
        steps.append((functools.partial(scatter.near_sum, micro), gap))
    for phase in range(scatters[0].phases()):
        for index, scatter in enumerate(scatters):
            gap = SHORT_GAP if index else FAR_GAP
            steps.append((functools.partial(scatter.far_sum, micro, phase), gap))
    return steps + [(functools.partial(finish, micro), SHORT_GAP)]


def half_steps(scatter, micro, length, chunk, cost):
    half = length // 2
    size = min(CHUNK, half)

    def odd():
        def body(index, carry):
            start = pl.multiple_of(half + index * size, size)
            place = pl.ds(pl.multiple_of(index * size, size), size)
            scatter.near_send[micro, place] = chunk(start, size).astype(low)
            return carry

        lax.fori_loop(0, half // size, body, 0)
        scatter.start(micro, range(scatter.links.half))

    def even():
        def body(index, carry):
            start = pl.multiple_of(index * size, size)
            scatter.sum[micro, pl.ds(start, size)] = chunk(start, size)
            return carry

        lax.fori_loop(0, half // size, body, 0)

    return [(odd, cost), (even, cost)]


def prologue(micro, up_ref, resid_ref, pair_ref, own_ref, kept_ref, pair_grad_ref):
    gains = (pair_ref[0:1], pair_ref[1:2])
    grad, gain_grad, shift_grad = norm_back(up_ref[micro].astype(wide), resid_ref[micro], gains)
    kept_ref[micro] = grad
    own_ref[micro] = grad.astype(low)
    if micro == 0:
        pair_grad_ref[0:1] = gain_grad
        pair_grad_ref[1:2] = shift_grad
    else:
        pair_grad_ref[0:1] += gain_grad
        pair_grad_ref[1:2] += shift_grad


class Task:
    def __init__(self, begin, arrive, compute, leave, drain, load=None, store=None):
        self.begin, self.arrive, self.compute = begin, arrive, compute
        self.leave, self.drain, self.load, self.store = leave, drain, load, store


class Waits:
    def __init__(self):
        self.time, self.queues = 0.0, []

    def add(self, steps):
        if steps:
            self.queues.append([list(steps), self.time + steps[0][1]])

    def take(self, entry):
        queue = entry[0]
        queue.pop(0)[0]()
        self.time += 0.4
        if queue:
            entry[1] = self.time + queue[0][1]
        else:
            self.queues.remove(entry)

    def run(self, step, cost):
        step()
        self.time += cost
        ready = [entry for entry in self.queues if entry[1] <= self.time]
        while ready:
            self.take(ready[0])
            ready = [entry for entry in self.queues if entry[1] <= self.time]

    def finish(self, steps):
        while any(entry[0] and entry[0][-1] is steps[-1] for entry in self.queues):
            entry = min(self.queues, key=lambda entry: entry[1])
            self.time = max(self.time, entry[1])
            self.take(entry)


def run_tasks(tasks, io, fill=(), fill_load=None):
    waits = Waits()
    for task in tasks[:2]:
        task.begin()
        waits.add(task.arrive)
    for index, task in enumerate(tasks):
        if task.arrive:
            waits.finish(task.arrive)
        io.load(task.load)
        for step, cost in task.compute:
            waits.run(step, cost)
        io.store(task.store)
        waits.add(task.leave)
        if index + 2 < len(tasks):
            tasks[index + 2].begin()
            waits.add(tasks[index + 2].arrive)
    if fill:
        io.load(fill_load)
        for step, cost in fill:
            waits.run(step, cost)
    while waits.queues:
        waits.take(min(waits.queues, key=lambda entry: entry[1]))
    for task in tasks:
        task.drain()
    io.close()


def make_task(micro, gathers, scatters, compute, finish, before=None, load=None, store=None):
    def begin():
        if before is not None:
            before(micro)
        for gather in gathers:
            gather.start(micro)

    def drain():
        for item in gathers + scatters:
            item.drain(micro)

    arrive = arrive_steps(gathers, micro)
    leave = leave_steps(scatters, finish, micro) if scatters else []
    return Task(begin, arrive, compute(micro), leave, drain, load, store)


class Operands:
    def __init__(self, ins, outs, in_sems, out_sems):
        self.ins, self.outs, self.in_sems, self.out_sems = ins, outs, in_sems, out_sems
        self.open = []

    def start(self):
        for index, (_, source, target) in enumerate(self.ins):
            pltpu.make_async_copy(source, target, self.in_sems.at[index]).start()

    def load(self, key):
        for index, (name, source, target) in enumerate(self.ins):
            if key is not None and name == key:
                pltpu.make_async_copy(source, target, self.in_sems.at[index]).wait()

    def copy_out(self, index, micro):
        _, source, target = self.outs[index]
        return pltpu.make_async_copy(
            source.at[micro], target.at[micro], self.out_sems.at[index, micro]
        )

    def store(self, key):
        if key is None:
            return
        name, micro = key
        for index, (group, _, _) in enumerate(self.outs):
            if group == name:
                self.copy_out(index, micro).start()
                self.open.append((index, micro))

    def close(self):
        for index, micro in self.open:
            self.copy_out(index, micro).wait()


def stage_call(kernel, name_id, outs, scratch, args, micros, lazy=None, early=None):
    lazy, early = lazy or {}, early or {}
    count, given, own = len(args), len(outs), len(scratch)
    lazy_places, early_places = sorted(lazy), sorted(early)
    parts = max([outs[place].shape[0] for place in early_places] + [1])

    def body(*refs):
        ins, results = list(refs[:count]), list(refs[count : count + given])
        own_scratch = refs[count + given : count + given + own]
        extra = refs[count + given + own :]
        loads, stores = [], []
        for index, place in enumerate(lazy_places):
            loads.append((lazy[place], ins[place], extra[index]))
            ins[place] = extra[index]
        for index, place in enumerate(early_places):
            buffer = extra[len(lazy_places) + index]
            stores.append((early[place], buffer, results[place]))
            results[place] = buffer
        io = Operands(loads, stores, extra[-2], extra[-1])
        io.start()
        kernel(io, *ins, *results, *own_scratch)

    held = [pltpu.VMEM(args[place].shape, args[place].dtype) for place in lazy_places]
    held += [pltpu.VMEM(outs[place].shape, outs[place].dtype) for place in early_places]
    sems = [
        pltpu.SemaphoreType.DMA((max(len(lazy_places), 1),)),
        pltpu.SemaphoreType.DMA((max(len(early_places), 1), parts)),
    ]
    near, far = pl.BlockSpec(memory_space=pltpu.VMEM), pl.BlockSpec(memory_space=pl.ANY)
    return pl.pallas_call(
        body,
        out_shape=tuple(outs),
        in_specs=[far if place in lazy else near for place in range(count)],
        out_specs=tuple(far if place in early else near for place in range(given)),
        scratch_shapes=list(scratch) + held + sems,
        compiler_params=pltpu.CompilerParams(
            collective_id=name_id, has_side_effects=True, vmem_limit_bytes=VMEM_LIMIT
        ),
        cost_estimate=pl.CostEstimate(
            flops=micros * 2_500_000_000, bytes_accessed=1 << 24, transcendentals=0
        ),
    )(*args)


def ffn_kernel(
    seq, io, own_ref, resid_ref, one_ref, two_ref, pair_ref, all_ref, before_ref, hidden_ref,
    sum_ref, norm_ref, low_ref, *scratch,
):
    links = Links(seq)
    micros, rows, _ = own_ref.shape
    length = all_ref.shape[1]
    gather = Gather(links, own_ref, all_ref, *scratch[:3])
    scatter = Scatter(links, rows, *scratch[3:8], scratch[8:])
    links.enter()

    def compute(micro):
        def chunk(start, size):
            place = pl.ds(start, size)
            before = dot(all_ref[micro, place], one_ref[...], 1, 1)
            before_ref[micro, place] = before
            after = gelu_exact(before).astype(low)
            hidden_ref[micro, place] = after
            return dot(after, two_ref[...], 1, 1)

        return half_steps(scatter, micro, length, chunk, 2.5)

    def finish(micro):
        total = resid_ref[micro] + scatter.total(micro)
        sum_ref[micro] = total
        value = layer_norm(total, (pair_ref[0:1], pair_ref[1:2]))
        norm_ref[micro] = value
        low_ref[micro] = value.astype(low)

    tasks = [
        make_task(
            micro, [gather], [scatter], compute, finish, None, 0 if micro == 0 else None, (0, micro)
        )
        for micro in range(micros)
    ]
    run_tasks(tasks, io)


def ffn_stage(seq, name_id, own, resid, one, two, pair):
    micros, rows, width = own.shape
    hidden = one.shape[0]
    length = rows * seq
    outs = (
        jax.ShapeDtypeStruct((micros, length, width), low),
        jax.ShapeDtypeStruct((micros, length, hidden), wide),
        jax.ShapeDtypeStruct((micros, length, hidden), low),
        jax.ShapeDtypeStruct((micros, rows, width), wide),
        jax.ShapeDtypeStruct((micros, rows, width), wide),
        jax.ShapeDtypeStruct((micros, rows, width), low),
    )
    scratch = gather_scratch(seq, micros) + scatter_scratch(seq, micros, rows, width)
    return stage_call(
        functools.partial(ffn_kernel, seq), name_id, outs, scratch,
        (own, resid, one, two, pair), 60, {1: 0, 2: 0, 3: 0, 4: 0}, {0: 0, 1: 0, 2: 0},
    )


def token_sum(left_ref, lanes, right_ref, micros):
    total = None
    for micro in range(micros):
        value = dot(left_ref[micro, :, lanes], right_ref[micro], 0, 0)
        total = value if total is None else total + value
    return total


def ffn_back_kernel(
    seq, ranks, hidden, io, up_ref, resid_ref, pair_ref, before_ref, one_ref, two_ref, rows_ref,
    hidden_ref, out_ref, pair_grad_ref, expand_ref, down_ref, two_terms_ref, all_ref, slope_ref,
    own_ref, kept_ref, *scratch,
):
    links = Links(seq)
    micros, rows, width = own_ref.shape
    length = all_ref.shape[1]
    adapt = down_ref.shape[0] * down_ref.shape[1]
    gather = Gather(links, own_ref, all_ref, *scratch[:3])
    scatter = Scatter(links, rows, *scratch[3:8], scratch[8:])
    links.enter()

    def before(micro):
        prologue(micro, up_ref, resid_ref, pair_ref, own_ref, kept_ref, pair_grad_ref)

    def compute(micro):
        def chunk(start, size):
            place = pl.ds(start, size)
            slope = dot(all_ref[micro, place], two_ref[...], 1, 0)
            slope = (slope * gelu_slope(before_ref[micro, place])).astype(low)
            slope_ref[micro, place] = slope
            return dot(slope, one_ref[...], 1, 0)

        return half_steps(scatter, micro, length, chunk, 2.5)

    def finish(micro):
        out_ref[micro] = kept_ref[micro] + scatter.total(micro)

    cut = hidden // ranks

    def one_tile(start):
        value = token_sum(slope_ref, slice(start, start + LANES), rows_ref, micros)
        if start < hidden:
            for part in range(0, LANES, cut):
                rank = (start + part) // cut
                expand_ref[rank] = value[part : part + cut].astype(low)
        else:
            down_ref[...] = value[:adapt].reshape(ranks, adapt // ranks, width).astype(low)

    def two_tile(start):
        value = token_sum(hidden_ref, slice(start, start + LANES), all_ref, micros).T
        value = value.reshape(seq, ranks, width // (seq * ranks), LANES)
        for rank in range(ranks):
            two_terms_ref[rank, :, :, start : start + LANES] = value[:, rank].astype(low)

    starts = range(0, slope_ref.shape[2], LANES)
    fill = [
        (functools.partial(tile, start), 1.2) for tile in (two_tile, one_tile) for start in starts
    ]
    tasks = [
        make_task(
            micro, [gather], [scatter], compute, finish, before, 0 if micro == 0 else None
        )
        for micro in range(micros)
    ]
    run_tasks(tasks, io, fill, 1)


def ffn_back_stage(seq, ranks, hidden, adapt, name_id, up, resid, pair, before, one, two, rows_all,
                   hidden_low):
    micros, rows, width = up.shape
    padded = one.shape[0]
    length = rows * seq
    outs = (
        jax.ShapeDtypeStruct((micros, rows, width), wide),
        jax.ShapeDtypeStruct((2, width), wide),
        jax.ShapeDtypeStruct((ranks, hidden // ranks, width), low),
        jax.ShapeDtypeStruct((ranks, adapt // ranks, width), low),
        jax.ShapeDtypeStruct((ranks, seq, width // (seq * ranks), padded), low),
    )
    scratch = (
        [pltpu.VMEM((micros, length, width), low), pltpu.VMEM((micros, length, padded), low)]
        + back_scratch(micros, rows, width)
        + gather_scratch(seq, micros)
        + scatter_scratch(seq, micros, rows, width)
    )
    return stage_call(
        functools.partial(ffn_back_kernel, seq, ranks, hidden), name_id, outs, scratch,
        (up, resid, pair, before, one, two, rows_all, hidden_low), 65,
        {3: 0, 4: 0, 5: 0, 6: 1, 7: 1},
    )


def opening_kernel(
    seq, ranks, io, source_ref, target_ref, out_ref, ffn_ref, small_ref, source_all, target_all,
    out_all, ffn_all, small_all, norm_all, *scratch,
):
    links = Links(seq)
    me, row = lax.axis_index("seq"), lax.axis_index("rows")
    gathers = [
        Gather(links, source_ref, source_all, *scratch[0:3]),
        Gather(links, target_ref, target_all, *scratch[3:6]),
    ]
    out_sems, ffn_sems, norm_sems, out_row_sems, small_row_sems, local_sems = scratch[6:]
    masks = range(1, seq)
    row_bits = bit_list(ranks)
    norm_rows = norm_all.shape[2]

    def remote(source, target, sems, index, device):
        return pltpu.make_async_remote_copy(
            src_ref=source,
            dst_ref=target,
            send_sem=sems.at[0, index],
            recv_sem=sems.at[1, index],
            device_id=device,
            device_id_type=pl.DeviceIdType.MESH,
        )

    def plane(mask):
        return {"seq": jnp.bitwise_xor(me, mask)}

    def other(mask):
        return jnp.bitwise_xor(me, mask)

    barrier = pltpu.get_barrier_semaphore()
    for mask in masks:
        pl.semaphore_signal(
            barrier, inc=1, device_id=plane(mask), device_id_type=pl.DeviceIdType.MESH
        )
    for bit in row_bits:
        pl.semaphore_signal(
            barrier,
            inc=1,
            device_id={"rows": jnp.bitwise_xor(row, bit)},
            device_id_type=pl.DeviceIdType.MESH,
        )
    pl.semaphore_wait(barrier, seq - 1 + len(row_bits))

    locals_ = [
        pltpu.make_async_copy(out_ref.at[me], out_all.at[row, me], local_sems.at[0]),
        pltpu.make_async_copy(ffn_ref.at[me], ffn_all.at[me], local_sems.at[1]),
        pltpu.make_async_copy(small_ref, small_all.at[row], local_sems.at[2]),
    ]
    for copy in locals_:
        copy.start()

    def out_send(mask):
        return remote(
            out_ref.at[other(mask)], out_all.at[row, me], out_sems, mask, plane(mask)
        )

    def out_wait(mask):
        return remote(
            out_ref.at[other(mask)], out_all.at[row, other(mask)], out_sems, mask, plane(mask)
        )

    def ffn_send(mask):
        return remote(ffn_ref.at[other(mask)], ffn_all.at[me], ffn_sems, mask, plane(mask))

    def ffn_wait(mask):
        return remote(
            ffn_ref.at[other(mask)], ffn_all.at[other(mask)], ffn_sems, mask, plane(mask)
        )

    def norm_send(mask):
        return remote(
            small_all.at[:, 0:norm_rows], norm_all.at[me], norm_sems, mask, plane(mask)
        )

    def norm_wait(mask):
        return remote(
            small_all.at[:, 0:norm_rows], norm_all.at[other(mask)], norm_sems, mask, plane(mask)
        )

    def row_copy(array, sems, mask, bit, there):
        at = jnp.bitwise_xor(row, mask)
        place = jnp.bitwise_xor(at, bit) if there else at
        return remote(
            array.at[at],
            array.at[place],
            sems,
            mask | bit,
            {"rows": jnp.bitwise_xor(row, bit)},
        )

    def row_phase(array, sems, phase):
        bit = row_bits[phase]
        for mask in span(row_bits[:phase]):
            row_copy(array, sems, mask, bit, False).start()

    def row_done(array, sems, phase):
        bit = row_bits[phase]
        for mask in span(row_bits[:phase]):
            row_copy(array, sems, mask, bit, True).wait_recv()

    for mask in masks:
        out_send(mask).start()
    tasks = [
        make_task(micro, [gather], [], lambda micro: [], None)
        for gather in gathers
        for micro in range(source_ref.shape[0])
    ]
    locals_[2].wait()
    row_phase(small_all, small_row_sems, 0)
    for task in tasks:
        task.begin()
    for mask in masks:
        ffn_send(mask).start()
    locals_[0].wait()
    for mask in masks:
        out_wait(mask).wait_recv()
    row_phase(out_all, out_row_sems, 0)
    steps = [
        functools.partial(task.arrive[phase][0])
        for phase in range(len(tasks[0].arrive))
        for task in tasks
    ]
    for phase in range(len(row_bits)):
        row_done(small_all, small_row_sems, phase)
        if phase + 1 < len(row_bits):
            row_phase(small_all, small_row_sems, phase + 1)
    norm_all[me] = small_all[:, 0:norm_rows]
    for mask in masks:
        norm_send(mask).start()
    cuts = [len(steps) * part // len(row_bits) for part in range(len(row_bits) + 1)]
    for phase in range(len(row_bits)):
        for step in steps[cuts[phase] : cuts[phase + 1]]:
            step()
        row_done(out_all, out_row_sems, phase)
        if phase + 1 < len(row_bits):
            row_phase(out_all, out_row_sems, phase + 1)
    for mask in masks:
        norm_wait(mask).wait_recv()
        ffn_wait(mask).wait_recv()
    locals_[1].wait()
    for mask in masks:
        out_send(mask).wait_send()
        ffn_send(mask).wait_send()
        norm_send(mask).wait_send()
    for phase, bit in enumerate(row_bits):
        for mask in span(row_bits[:phase]):
            row_copy(out_all, out_row_sems, mask, bit, False).wait_send()
            row_copy(small_all, small_row_sems, mask, bit, False).wait_send()
    for task in tasks:
        task.drain()


def opening_stage(seq, ranks, name_id, norm_rows, args):
    source, _, out_pieces, ffn_pieces, small = args
    micros, rows, width = source.shape
    whole = jax.ShapeDtypeStruct((micros, seq * rows, width), low)
    outs = (
        whole,
        whole,
        jax.ShapeDtypeStruct((ranks,) + out_pieces.shape, low),
        jax.ShapeDtypeStruct(ffn_pieces.shape, low),
        jax.ShapeDtypeStruct((ranks,) + small.shape, low),
        jax.ShapeDtypeStruct((seq, ranks, norm_rows, small.shape[1]), low),
    )
    scratch = gather_scratch(seq, micros) * 2 + [
        pltpu.SemaphoreType.DMA((2, seq)),
        pltpu.SemaphoreType.DMA((2, seq)),
        pltpu.SemaphoreType.DMA((2, seq)),
        pltpu.SemaphoreType.DMA((2, ranks)),
        pltpu.SemaphoreType.DMA((2, ranks)),
        pltpu.SemaphoreType.DMA((3,)),
    ]
    return stage_call(
        functools.partial(opening_kernel, seq, ranks), name_id, outs, scratch, args, 55
    )


class Attention:
    def __init__(self, q_ref, kv_ref, offsets, prefix_ref, ids, count, causal):
        self.q, self.kv, self.offsets, self.prefix = q_ref, kv_ref, offsets, prefix_ref
        self.key_ids, self.query_ids, self.key_places, self.query_places = ids
        self.count, self.causal = count, causal
        self.heads = prefix_ref.shape[2] // HEAD_DIM

    def load(self, micro, head, place):
        q_at, k_at, v_at = (at + head * HEAD_DIM for at in self.offsets)
        queries = self.q[micro, place, q_at : q_at + HEAD_DIM] * jnp.asarray(SCALING, low)
        keys = self.kv[micro, :, k_at : k_at + HEAD_DIM]
        values = self.kv[micro, :, v_at : v_at + HEAD_DIM]
        return queries, keys, values

    def scores(self, micro, keys, queries, lanes, place):
        scores = dot(keys, queries, 1, 1)
        allowed = self.key_ids[micro] == self.query_ids[micro, :, place]
        if self.causal:
            allowed = allowed & (self.key_places[...] <= self.query_places[:, place])
        scores = jnp.where(allowed, scores, MASKED)
        extra = dot(self.prefix[0, :, lanes], queries, 1, 1)
        rows = lax.broadcasted_iota(jnp.int32, extra.shape, 0)
        return scores, jnp.where(rows < self.count, extra, MASKED)

    def forward(self, micro, start, size, context_ref, logs_ref):
        place = pl.ds(start, size)
        for head in range(self.heads):
            lanes = slice(head * HEAD_DIM, (head + 1) * HEAD_DIM)
            queries, keys, values = self.load(micro, head, place)
            scores, extra = self.scores(micro, keys, queries, lanes, place)
            peak = jnp.maximum(
                jnp.max(scores, axis=0, keepdims=True), jnp.max(extra, axis=0, keepdims=True)
            )
            scores = jnp.exp(scores - peak)
            extra = jnp.exp(extra - peak)
            total = jnp.sum(scores, axis=0, keepdims=True) + jnp.sum(extra, axis=0, keepdims=True)
            context = dot(values, scores.astype(low), 0, 0)
            context = context + dot(self.prefix[1, :, lanes], extra.astype(low), 0, 0)
            context_ref[micro, place, lanes] = (context / total).T.astype(low)
            logs_ref[micro, head : head + 1, place] = peak + jnp.log(total)

    def backward(self, micro, start, size, up_ref, logs_ref, grad_ref, k_sum, v_sum, pre_ref):
        place = pl.ds(start, size)
        for head in range(self.heads):
            lanes = slice(head * HEAD_DIM, (head + 1) * HEAD_DIM)
            queries, keys, values = self.load(micro, head, place)
            scores, extra = self.scores(micro, keys, queries, lanes, place)
            logs = logs_ref[micro, head : head + 1, place]
            weights = jnp.exp(scores - logs)
            extra = jnp.exp(extra - logs)
            up = up_ref[:, lanes]
            dots = dot(values, up, 1, 1)
            extra_dots = dot(self.prefix[1, :, lanes], up, 1, 1)
            centre = jnp.sum(weights * dots, axis=0, keepdims=True) + jnp.sum(
                extra * extra_dots, axis=0, keepdims=True
            )
            slope = (weights * (dots - centre)).astype(low)
            extra_slope = (extra * (extra_dots - centre)).astype(low)
            query_grad = dot(keys, slope, 0, 0) + dot(self.prefix[0, :, lanes], extra_slope, 0, 0)
            grad_ref[micro, place, lanes] = (query_grad * SCALING).T.astype(low)
            k_sum[:, lanes] += dot(slope, queries, 1, 0)
            v_sum[:, lanes] += dot(weights.astype(low), up, 1, 0)
            pre_ref[0, :, lanes] += dot(extra_slope, queries, 1, 0)
            pre_ref[1, :, lanes] += dot(extra.astype(low), up, 1, 0)


def loop(first, count, size, body):
    def step(index, carry):
        body(pl.multiple_of(first + index * size, size), index)
        return carry

    lax.fori_loop(0, count, step, 0)


def project_steps(micro, rows_ref, weight_ref, out_ref):
    length = rows_ref.shape[1]
    size = min(CHUNK, length)

    def body(start, index):
        place = pl.ds(start, size)
        out_ref[micro, place] = dot(rows_ref[micro, place], weight_ref[...], 1, 1).astype(low)

    return [(lambda: loop(0, length // size, size, body), 1.3)]


def self_kernel(seq, count, io, *refs):
    kinds = 2
    scratch = refs[-kinds * 7 :]
    refs = refs[: -kinds * 7]
    places = refs[:2]
    links = Links(seq)
    links.enter()
    tasks = []
    for kind in range(kinds):
        (all_ref, own_ref, in_ref, out_ref, prefix_ref, kid_ref, qid_ref, pair_ref) = refs[
            2 + 8 * kind : 10 + 8 * kind
        ]
        (qkv_ref, context_ref, logs_ref, sum_ref, norm_ref, low_ref) = refs[
            2 + 8 * kinds + 6 * kind : 8 + 8 * kinds + 6 * kind
        ]
        micros, rows, _ = own_ref.shape
        length = all_ref.shape[1]
        head_width = prefix_ref.shape[2]
        piece = scratch[7 * kind : 7 * kind + 7]
        scatter = Scatter(links, rows, *piece[:5], piece[5:])
        ids = (kid_ref, qid_ref) + tuple(places)
        attention = Attention(
            qkv_ref, qkv_ref, (0, head_width, 2 * head_width), prefix_ref, ids, count, kind == 1
        )

        def compute(
            micro, attention=attention, context_ref=context_ref, logs_ref=logs_ref,
            out_ref=out_ref, all_ref=all_ref, in_ref=in_ref, qkv_ref=qkv_ref, scatter=scatter,
        ):
            def chunk(start, size):
                attention.forward(micro, start, size, context_ref, logs_ref)
                return dot(context_ref[micro, pl.ds(start, size)], out_ref[...], 1, 1)

            return project_steps(micro, all_ref, in_ref, qkv_ref) + half_steps(
                scatter, micro, length, chunk, 4.2
            )

        def finish(
            micro, own_ref=own_ref, scatter=scatter, sum_ref=sum_ref, norm_ref=norm_ref,
            low_ref=low_ref, pair_ref=pair_ref,
        ):
            total = own_ref[micro].astype(wide) + scatter.total(micro)
            sum_ref[micro] = total
            value = layer_norm(total, (pair_ref[0:1], pair_ref[1:2]))
            norm_ref[micro] = value
            low_ref[micro] = value.astype(low)

        for micro in range(micros):
            load = kind if micro == 0 else None
            tasks.append(
                make_task(micro, [], [scatter], compute, finish, None, load, (kind, micro))
            )
    run_tasks(tasks, io)


def self_stage(seq, name_id, count, places, sides):
    micros, rows, width = sides[0][1].shape
    length = rows * seq
    head_width = sides[0][4].shape[2]
    heads = head_width // HEAD_DIM
    side_outs = (
        jax.ShapeDtypeStruct((micros, length, 3 * head_width), low),
        jax.ShapeDtypeStruct((micros, length, head_width), low),
        jax.ShapeDtypeStruct((micros, heads, length), wide),
        jax.ShapeDtypeStruct((micros, rows, width), wide),
        jax.ShapeDtypeStruct((micros, rows, width), wide),
        jax.ShapeDtypeStruct((micros, rows, width), low),
    )
    scratch = scatter_scratch(seq, micros, rows, width) * 2
    args = tuple(places) + sides[0] + sides[1]
    outs = stage_call(
        functools.partial(self_kernel, seq, count), name_id, side_outs * 2, scratch, args, 75,
        {10: 1, 11: 1, 12: 1, 13: 1, 15: 1}, {0: 0, 1: 0, 6: 1, 7: 1},
    )
    return outs[:6], outs[6:]


def cross_kernel(
    seq, count, io, kpos_ref, qpos_ref, first_ref, first_low_ref, memory_ref, q_in_ref, kv_in_ref,
    out_ref, prefix_ref, kid_ref, qid_ref, pair_ref, first_all, memory_all, q_ref, kv_ref,
    context_ref, logs_ref, sum_ref, norm_ref, low_ref, *scratch,
):
    links = Links(seq)
    micros, rows, _ = first_ref.shape
    length = first_all.shape[1]
    head_width = prefix_ref.shape[2]
    gathers = [
        Gather(links, memory_ref, memory_all, *scratch[:3]),
        Gather(links, first_low_ref, first_all, *scratch[3:6]),
    ]
    scatter = Scatter(links, rows, *scratch[6:11], scratch[11:])
    ids = (kid_ref, qid_ref, kpos_ref, qpos_ref)
    attention = Attention(q_ref, kv_ref, (0, 0, head_width), prefix_ref, ids, count, False)
    links.enter()

    def compute(micro):
        def chunk(start, size):
            attention.forward(micro, start, size, context_ref, logs_ref)
            return dot(context_ref[micro, pl.ds(start, size)], out_ref[...], 1, 1)

        return (
            project_steps(micro, memory_all, kv_in_ref, kv_ref)
            + project_steps(micro, first_all, q_in_ref, q_ref)
            + half_steps(scatter, micro, length, chunk, 4.2)
        )

    def finish(micro):
        total = first_ref[micro] + scatter.total(micro)
        sum_ref[micro] = total
        value = layer_norm(total, (pair_ref[0:1], pair_ref[1:2]))
        norm_ref[micro] = value
        low_ref[micro] = value.astype(low)

    tasks = [
        make_task(
            micro, gathers, [scatter], compute, finish, None, 0 if micro == 0 else None, (0, micro)
        )
        for micro in range(micros)
    ]
    run_tasks(tasks, io)


def cross_stage(seq, name_id, count, places, args):
    micros, rows, width = args[0].shape
    length = rows * seq
    head_width = args[6].shape[2]
    heads = head_width // HEAD_DIM
    whole = jax.ShapeDtypeStruct((micros, length, width), low)
    outs = (
        whole,
        whole,
        jax.ShapeDtypeStruct((micros, length, head_width), low),
        jax.ShapeDtypeStruct((micros, length, 2 * head_width), low),
        jax.ShapeDtypeStruct((micros, length, head_width), low),
        jax.ShapeDtypeStruct((micros, heads, length), wide),
        jax.ShapeDtypeStruct((micros, rows, width), wide),
        jax.ShapeDtypeStruct((micros, rows, width), wide),
        jax.ShapeDtypeStruct((micros, rows, width), low),
    )
    scratch = gather_scratch(seq, micros) * 2 + scatter_scratch(seq, micros, rows, width)
    return stage_call(
        functools.partial(cross_kernel, seq, count), name_id, outs, scratch,
        tuple(places) + args, 85, {place: 0 for place in (2, 5, 6, 7, 8, 9, 10)},
        {place: 0 for place in range(5)},
    )


def attend_back_steps(
    attention, micro, length, up_all, out_ref, logs_ref, grad_ref, k_sum, v_sum, pre_ref, up_ref,
    emit=None,
):
    head_width = up_ref.shape[1]
    half = length // 2
    size = min(CHUNK, half)

    def run(first, zero):
        if zero:
            k_sum[...] = jnp.zeros_like(k_sum)
            v_sum[...] = jnp.zeros_like(v_sum)
            if micro == 0:
                pre_ref[...] = jnp.zeros_like(pre_ref)

        def body(start, index):
            place = pl.ds(start, size)
            up_ref[...] = dot(up_all[micro, place], out_ref[...], 1, 0).astype(low)
            attention.backward(
                micro, start, size, up_ref, logs_ref, grad_ref, k_sum, v_sum, pre_ref
            )
            if emit is not None:
                emit(start, index, size)

        loop(first, half // size, size, body)

    def keys():
        grad_ref[micro, :, head_width : 2 * head_width] = k_sum[...].astype(low)
        grad_ref[micro, :, 2 * head_width : 3 * head_width] = v_sum[...].astype(low)

    return [(lambda: run(half, True), 5.0), (lambda: run(0, False), 5.0), (keys, 0.5)]


def term_steps(context_ref, up_all, grad_ref, sources, terms_ref, seq, send=None):
    micros = grad_ref.shape[0]
    ranks, _, cols, width = terms_ref.shape
    head_width = context_ref.shape[2]

    def tile(part):
        if part == 3:
            value = token_sum(context_ref, slice(0, head_width), up_all, micros).T
            value = value.reshape(seq, ranks, cols, head_width)
            for owner in range(seq):
                lanes = slice(owner * head_width, (owner + 1) * head_width)
                terms_ref[:, 3, :, lanes] = value[owner].astype(low)
        else:
            lanes = slice(part * head_width, (part + 1) * head_width)
            value = token_sum(grad_ref, lanes, sources[part], micros)
            terms_ref[:, part] = value.reshape(ranks, cols, width).astype(low)
        if send is not None:
            send(part)

    return [(functools.partial(tile, part), 1.2) for part in (3, 0, 1, 2)]


def term_shape(seq, ranks, width):
    return jax.ShapeDtypeStruct((ranks, 4, width // (seq * ranks), width), low)


class RankSum:
    def __init__(self, ranks, terms_ref, recv_ref, total_ref, sems):
        self.ranks, self.terms, self.recv = ranks, terms_ref, recv_ref
        self.total, self.sems, self.row = total_ref, sems, lax.axis_index("rows")

    def greet(self, barrier):
        for mask in range(1, self.ranks):
            pl.semaphore_signal(
                barrier,
                inc=1,
                device_id={"rows": jnp.bitwise_xor(self.row, mask)},
                device_id_type=pl.DeviceIdType.MESH,
            )
        return self.ranks - 1

    def copy(self, part, mask):
        owner = jnp.bitwise_xor(self.row, mask)
        return pltpu.make_async_remote_copy(
            src_ref=self.terms.at[owner, part],
            dst_ref=self.recv.at[mask, part],
            send_sem=self.sems.at[0, mask, part],
            recv_sem=self.sems.at[1, mask, part],
            device_id={"rows": owner},
            device_id_type=pl.DeviceIdType.MESH,
        )

    def send(self, part):
        for mask in range(1, self.ranks):
            self.copy(part, mask).start()

    def finish(self):
        for part in (3, 0, 1, 2):
            value = self.terms[self.row, part].astype(wide)
            for mask in range(1, self.ranks):
                self.copy(part, mask).wait_recv()
                value = value + self.recv[mask, part].astype(wide)
            self.total[part] = value
        for part in range(4):
            for mask in range(1, self.ranks):
                self.copy(part, mask).wait_send()


def cross_back_kernel(
    seq, count, io, kpos_ref, qpos_ref, up_ref, resid_ref, pair_ref, q_ref, kv_ref, logs_ref,
    q_in_ref, kv_in_ref, out_ref, prefix_ref, kid_ref, qid_ref, first_all, memory_all, context_ref,
    pre_ref, first_out, memory_out, pair_grad_ref, terms_ref, up_all, grad_ref, own_ref, kept_ref, k_sum, v_sum, up_chunk, *scratch,
):
    links = Links(seq)
    micros, rows, _ = own_ref.shape
    length = up_all.shape[1]
    head_width = prefix_ref.shape[2]
    gather = Gather(links, own_ref, up_all, *scratch[:3])
    first_sum = Scatter(links, rows, *scratch[3:8], scratch[8:10])
    memory_sum = Scatter(links, rows, *scratch[10:15], scratch[15:17])
    ids = (kid_ref, qid_ref, kpos_ref, qpos_ref)
    attention = Attention(q_ref, kv_ref, (0, 0, head_width), prefix_ref, ids, count, False)
    links.enter()

    def before(micro):
        prologue(micro, up_ref, resid_ref, pair_ref, own_ref, kept_ref, pair_grad_ref)

    def compute(micro):
        def first_chunk(start, size):
            return dot(
                grad_ref[micro, pl.ds(start, size), 0:head_width], q_in_ref[...], 1, 0
            )

        def memory_chunk(start, size):
            return dot(
                grad_ref[micro, pl.ds(start, size), head_width : 3 * head_width],
                kv_in_ref[...],
                1,
                0,
            )

        attend = attend_back_steps(
            attention, micro, length, up_all, out_ref, logs_ref, grad_ref, k_sum, v_sum, pre_ref,
            up_chunk,
        )
        sums = half_steps(first_sum, micro, length, first_chunk, 0.6)
        return (
            [attend[0], sums[0], attend[1], sums[1], attend[2]]
            + half_steps(memory_sum, micro, length, memory_chunk, 0.8)
        )

    def finish(micro):
        first_out[micro] = kept_ref[micro] + first_sum.total(micro)
        memory_out[micro] = memory_sum.total(micro)

    tasks = [
        make_task(
            micro, [gather], [first_sum, memory_sum], compute, finish, before,
            0 if micro == 0 else None,
        )
        for micro in range(micros)
    ]
    fill = term_steps(
        context_ref, up_all, grad_ref, (first_all, memory_all, memory_all), terms_ref, seq
    )
    run_tasks(tasks, io, fill, 1)


def cross_back_stage(seq, ranks, name_id, count, places, args):
    micros, rows, width = args[0].shape
    length = rows * seq
    head_width = args[9].shape[2]
    own = jax.ShapeDtypeStruct((micros, rows, width), wide)
    outs = (
        jax.ShapeDtypeStruct((2, PAD_PREFIX, head_width), wide),
        own,
        own,
        jax.ShapeDtypeStruct((2, width), wide),
        term_shape(seq, ranks, width),
    )
    scratch = (
        [
            pltpu.VMEM((micros, length, width), low),
            pltpu.VMEM((micros, length, 3 * head_width), low),
        ]
        + back_scratch(micros, rows, width)
        + sum_scratch(length, head_width)
        + gather_scratch(seq, micros)
        + scatter_scratch(seq, micros, rows, width) * 2
    )
    lazy = {place: 0 for place in range(5, 14)}
    lazy.update({14: 1, 15: 1, 16: 1})
    return stage_call(
        functools.partial(cross_back_kernel, seq, count), name_id, outs, scratch,
        tuple(places) + args, 85, lazy,
    )


def back_scratch(micros, rows, width):
    return [pltpu.VMEM((micros, rows, width), low), pltpu.VMEM((micros, rows, width), wide)]


def sum_scratch(length, head_width):
    return [
        pltpu.VMEM((length, head_width), wide),
        pltpu.VMEM((length, head_width), wide),
        pltpu.VMEM((min(CHUNK, length // 2), head_width), low),
    ]


def self_back_kernel(
    seq, count, causal, reduce, io, kpos_ref, qpos_ref, up_ref, resid_ref, pair_ref, qkv_ref,
    logs_ref, in_ref, out_ref, prefix_ref, kid_ref, qid_ref, context_ref, rows_ref, pre_ref,
    grad_out, pair_grad_ref, result_ref, up_all, grad_ref, own_ref, kept_ref, k_sum, v_sum,
    up_chunk, *scratch,
):
    links = Links(seq)
    micros, rows, _ = own_ref.shape
    length = up_all.shape[1]
    head_width = prefix_ref.shape[2]
    gather = Gather(links, own_ref, up_all, *scratch[:3])
    scatter = Scatter(links, rows, *scratch[3:8], scratch[8:10])
    terms_ref, rank_sum = result_ref, None
    if reduce:
        terms_ref, recv_ref, rank_sems = scratch[10:]
        rank_sum = RankSum(terms_ref.shape[0], terms_ref, recv_ref, result_ref, rank_sems)
    ids = (kid_ref, qid_ref, kpos_ref, qpos_ref)
    attention = Attention(
        qkv_ref, qkv_ref, (0, head_width, 2 * head_width), prefix_ref, ids, count, causal
    )
    links.enter([rank_sum] if reduce else [])

    def before(micro):
        prologue(micro, up_ref, resid_ref, pair_ref, own_ref, kept_ref, pair_grad_ref)

    def compute(micro):
        def chunk(start, size):
            return dot(grad_ref[micro, pl.ds(start, size)], in_ref[...], 1, 0)

        return attend_back_steps(
            attention, micro, length, up_all, out_ref, logs_ref, grad_ref, k_sum, v_sum,
            pre_ref, up_chunk,
        ) + half_steps(scatter, micro, length, chunk, 0.9)

    def finish(micro):
        grad_out[micro] = kept_ref[micro] + scatter.total(micro)

    tasks = [
        make_task(
            micro, [gather], [scatter], compute, finish, before, 0 if micro == 0 else None
        )
        for micro in range(micros)
    ]
    fill = term_steps(
        context_ref, up_all, grad_ref, (rows_ref,) * 3, terms_ref, seq,
        rank_sum.send if reduce else None,
    )
    run_tasks(tasks, io, fill, 1)
    if reduce:
        rank_sum.finish()


def self_back_stage(seq, ranks, name_id, count, places, causal, reduce, side):
    micros, rows, width = side[0].shape
    length = rows * seq
    head_width = side[7].shape[2]
    outs = (
        jax.ShapeDtypeStruct((2, PAD_PREFIX, head_width), wide),
        jax.ShapeDtypeStruct((micros, rows, width), wide),
        jax.ShapeDtypeStruct((2, width), wide),
        term_shape(seq, ranks, width),
    )
    terms = outs[3]
    if reduce:
        outs = outs[:3] + (jax.ShapeDtypeStruct(terms.shape[1:], wide),)
    scratch = (
        [
            pltpu.VMEM((micros, length, width), low),
            pltpu.VMEM((micros, length, 3 * head_width), low),
        ]
        + back_scratch(micros, rows, width)
        + sum_scratch(length, head_width)
        + gather_scratch(seq, micros)
        + scatter_scratch(seq, micros, rows, width)
    )
    if reduce:
        scratch += [
            pltpu.VMEM(terms.shape, low),
            pltpu.VMEM(terms.shape, low),
            pltpu.SemaphoreType.DMA((2, ranks, 4)),
        ]
    lazy = {place: 0 for place in range(5, 12)}
    lazy.update({12: 1, 13: 1})
    return stage_call(
        functools.partial(self_back_kernel, seq, count, causal, reduce), name_id, outs, scratch,
        tuple(places) + side, 75, lazy,
    )


def local(
    seq, ranks,
    source, target, source_segments, target_segments, cotangent,
    encoder_qkv, encoder_output, encoder_prefix, encoder_expand, encoder_contract, encoder_down,
    encoder_up, encoder_norms, decoder_qkv, decoder_output, decoder_prefix, cross_query, cross_kv,
    cross_output, cross_prefix, decoder_expand, decoder_contract, decoder_down, decoder_up,
    decoder_norms,
):
    micro_count, batch_rows, block, width = source.shape
    length = source_segments.shape[2]
    me = lax.axis_index("seq")
    stacked = micro_count * batch_rows
    head_width = width // seq
    slice_cols = encoder_output.shape[1]
    count = encoder_prefix.shape[1]
    hidden = encoder_contract.shape[0] // seq
    adapt = encoder_up.shape[0] // seq
    both = hidden + adapt
    padded = (both + LANES - 1) // LANES * LANES

    sources = source.reshape(stacked, block, width)
    targets = target.reshape(stacked, block, width)

    order = relative(jnp.arange(length, dtype=jnp.int32), seq, me)
    places = (order[:, None], order[None, :])

    def relative_ids(ids):
        rows = [relative(row, seq, me) for row in ids.reshape(stacked, length)]
        value = jnp.stack(rows)
        return value[:, :, None], value[:, None, :]

    source_keys, source_queries = relative_ids(source_segments)
    target_keys, target_queries = relative_ids(target_segments)

    def columns(weight):
        return jnp.swapaxes(weight, -1, -2)

    def gather_rows(value):
        return lax.all_gather(value, "rows", axis=0, tiled=False)

    def stack_columns(pieces):
        gathered = gather_rows(jnp.concatenate(pieces, axis=0))
        outs = []
        start = 0
        for piece in pieces:
            size = piece.shape[0]
            outs.append(gathered[:, start : start + size])
            start += size
        return outs

    def flat_columns(gathered, parts):
        value = gathered.reshape(ranks, parts, slice_cols, width)
        return jnp.swapaxes(value, 0, 1).reshape(parts * ranks * slice_cols, width)

    def split_rows(weight):
        return columns(weight).reshape(slice_cols, seq, -1)

    def ffn_rows(contract, up):
        pieces = [split_rows(contract), split_rows(up) * jnp.asarray(ADAPTER_SCALE, low)]
        if padded > both:
            pieces.append(jnp.zeros((slice_cols, seq, padded - both), low))
        return pieces

    def by_target(pieces):
        return jnp.swapaxes(jnp.concatenate(pieces, axis=2), 0, 1)

    out_pieces = by_target([split_rows(encoder_output), split_rows(decoder_output)])
    ffn_pieces = by_target(
        [split_rows(cross_output)]
        + ffn_rows(encoder_contract, encoder_up)
        + ffn_rows(decoder_contract, decoder_up)
    )
    qkv_parts = gather_rows(
        jnp.concatenate(
            [
                columns(encoder_qkv).reshape(-1, width),
                columns(decoder_qkv).reshape(-1, width),
            ]
        )
    )
    norm_count = encoder_norms.shape[0]
    norms = jnp.concatenate([encoder_norms, decoder_norms]).reshape(-1, slice_cols)
    prefixes = jnp.concatenate([encoder_prefix, decoder_prefix, cross_prefix])
    prefixes = prefixes.reshape(-1, slice_cols)
    norm_rows = (norms.shape[0] + 15) // 16 * 16
    small = jnp.concatenate(
        [jnp.pad(norms, ((0, norm_rows - norms.shape[0]), (0, 0))), prefixes]
    )
    small = jnp.pad(small, ((0, -small.shape[0] % 16), (0, 0)))
    source_all, target_all, front, row_pieces, small_all, norm_all = opening_stage(
        seq, ranks, 1, norm_rows, (sources, targets, out_pieces, ffn_pieces, small)
    )
    scales = norm_all[:, :, : norms.shape[0]].reshape(seq * ranks, -1, slice_cols)
    scales = jnp.moveaxis(scales, 0, 1).reshape(-1, 2, width).astype(wide)
    prefixes = small_all[:, norm_rows : norm_rows + 6 * count]
    prefixes = jnp.moveaxis(prefixes.reshape(ranks, 6, count, slice_cols), 0, 2)
    prefixes = prefixes.reshape(6, count, head_width)
    prefixes = jnp.pad(prefixes, ((0, 0), (0, PAD_PREFIX - count), (0, 0)))
    encoder_pre, decoder_pre, cross_pre = prefixes[0:2], prefixes[2:4], prefixes[4:6]
    norm_axes = [("seq", seq), ("rows", ranks)]

    late = [
        jnp.concatenate(
            [
                columns(encoder_expand),
                columns(encoder_down),
                columns(cross_query),
                columns(cross_kv).reshape(-1, width),
            ]
        ),
        row_pieces[:, :, : head_width + padded],
        jnp.concatenate([columns(decoder_expand), columns(decoder_down)]),
        row_pieces[:, :, head_width + padded :],
    ]
    source_all, late = lax.optimization_barrier((source_all, late))
    encoder_in = flat_columns(qkv_parts[:, : 3 * slice_cols], 3)
    decoder_in = flat_columns(qkv_parts[:, 3 * slice_cols :], 3)
    front_rows = jnp.swapaxes(front, 0, 1).reshape(width, -1)
    encoder_out = front_rows[:, :head_width]
    decoder_out = front_rows[:, head_width:]
    cut = encoder_expand.shape[1]

    def ffn_in(gathered):
        pieces = [gathered[:, :cut].reshape(-1, width), gathered[:, cut:].reshape(-1, width)]
        if padded > both:
            pieces.append(jnp.zeros((padded - both, width), low))
        return jnp.concatenate(pieces)

    def row_order(gathered):
        return jnp.swapaxes(gathered, 0, 1).reshape(width, -1)

    second_parts = gather_rows(late[0])
    rest = gather_rows(late[1])
    encoder_side, decoder_side = self_stage(
        seq, 2, count, places,
        (
            (
                source_all, sources, encoder_in, encoder_out, encoder_pre, source_keys,
                source_queries, scales[0],
            ),
            (
                target_all, targets, decoder_in, decoder_out, decoder_pre, target_keys,
                target_queries, scales[norm_count],
            ),
        ),
    )
    encoder_qkvs, encoder_ctx, encoder_logs, resid_one, middle, middle_low = encoder_side
    middle_low, second_parts, rest, last = lax.optimization_barrier(
        (middle_low, second_parts, rest, late[2:])
    )
    rest = row_order(rest)
    cross_out, encoder_two = rest[:, :head_width], rest[:, head_width:]
    ffn_cut = cut + encoder_down.shape[1]
    encoder_one = ffn_in(second_parts[:, :ffn_cut])
    cross_in = flat_columns(second_parts[:, ffn_cut:], 3)
    cross_q_in, cross_kv_in = cross_in[:head_width], cross_in[head_width:]
    decoder_qkvs, decoder_ctx, decoder_logs, resid_three, first, first_low = decoder_side
    middle_all, encoder_before, encoder_hidden, resid_two, _, memory_low = ffn_stage(
        seq, 3, middle_low, middle, encoder_one, encoder_two, scales[1]
    )
    memory_low, last = lax.optimization_barrier(
        (memory_low, [gather_rows(piece) for piece in last])
    )
    decoder_one, decoder_two = ffn_in(last[0]), row_order(last[1])
    (
        first_all, memory_all, cross_q, cross_kvs, cross_ctx, cross_logs, resid_four, second,
        second_low,
    ) = cross_stage(
        seq, 4, count, places,
        (
            first, first_low, memory_low, cross_q_in, cross_kv_in, cross_out, cross_pre,
            source_keys, target_queries, scales[norm_count + 1],
        ),
    )
    second_all, decoder_before, decoder_hidden, resid_five, _, result = ffn_stage(
        seq, 5, second_low, second, decoder_one, decoder_two, scales[norm_count + 2]
    )

    def scatter_ranks(value):
        return lax.psum_scatter(value, "rows", scatter_dimension=0, tiled=False)

    norm_grads = {}

    def ffn_back(name_id, index, up, resid, before, hidden_low, rows_all, one, two):
        out, pair, expand, down, two_terms = ffn_back_stage(
            seq, ranks, hidden, adapt, name_id, up, resid, scales[index], before, one, two,
            rows_all, hidden_low,
        )
        keep_pair(index, pair)
        return out, [two_terms, jnp.concatenate([expand, down], axis=1)]

    def hold(value, terms, sums):
        value, terms, sums = lax.optimization_barrier((value, terms, sums))
        return value, [scatter_ranks(term) for term in terms], sums

    def keep_pair(index, pair):
        norm_grads[index] = (pair[0:1], pair[1:2])

    second_up, terms = ffn_back(
        6, norm_count + 2, cotangent.reshape(stacked, block, width), resid_five, decoder_before,
        decoder_hidden, second_all, decoder_one, decoder_two,
    )
    second_up, ffn_sums, _ = hold(second_up, terms, [])

    cross_pre_grad, first_up, memory_up, pair, terms = cross_back_stage(
        seq, ranks, 7, count, places,
        (
            second_up, resid_four, scales[norm_count + 1], cross_q, cross_kvs, cross_logs,
            cross_q_in, cross_kv_in, cross_out, cross_pre, source_keys, target_queries,
            first_all, memory_all, cross_ctx,
        ),
    )
    keep_pair(norm_count + 1, pair)
    first_up, cross_sums, ffn_sums = hold(first_up, [terms], ffn_sums)
    decoder_two_grad, decoder_one_grad = ffn_sums

    def self_back(name_id, index, causal, reduce, side, sums):
        held = self_back_stage(seq, ranks, name_id, count, places, causal, reduce, side)
        held, sums = lax.optimization_barrier((held, sums))
        pre_grad, out, pair, terms = held
        keep_pair(index, pair)
        return out, pre_grad, sums, terms

    def owner_parts(value):
        out_part = value[3].reshape(slice_cols, seq, head_width)
        return jnp.swapaxes(out_part, 0, 1), value[:3]

    target_grad, decoder_pre_grad, cross_sums, self_terms = self_back(
        9, norm_count, True, False,
        (
            first_up, resid_three, scales[norm_count], decoder_qkvs, decoder_logs, decoder_in,
            decoder_out, decoder_pre, target_keys, target_queries, decoder_ctx, target_all,
        ),
        cross_sums,
    )
    memory_up, self_sums, _ = hold(memory_up, [self_terms], [])
    cross_out_grad, cross_in_grad = owner_parts(cross_sums[0])

    middle_up, terms = ffn_back(
        8, 1, memory_up, resid_two, encoder_before, encoder_hidden, middle_all,
        encoder_one, encoder_two,
    )
    middle_up, ffn_sums, self_sums = hold(middle_up, terms, self_sums)
    decoder_out_grad, decoder_in_grad = owner_parts(self_sums[0])

    def give_back(pieces):
        value = jnp.concatenate(pieces, axis=2) if len(pieces) > 1 else pieces[0]
        return lax.all_to_all(value, "seq", 0, 1, tiled=False)

    decoder_rows = give_back([decoder_two_grad, cross_out_grad, decoder_out_grad])

    source_grad, encoder_pre_grad, ffn_sums, self_terms = self_back(
        10, 0, False, True,
        (
            middle_up, resid_one, scales[0], encoder_qkvs, encoder_logs, encoder_in,
            encoder_out, encoder_pre, source_keys, source_queries, encoder_ctx, source_all,
        ),
        ffn_sums,
    )
    encoder_two_grad, encoder_one_grad = ffn_sums
    encoder_out_grad, encoder_in_grad = owner_parts(self_terms)
    encoder_rows = give_back([encoder_two_grad])
    encoder_out_rows = give_back([encoder_out_grad.astype(low)])

    def row_grad(value, start, size, scale=None):
        piece = value[:, :, start : start + size].astype(wide)
        if scale is not None:
            piece = piece * scale
        return piece.reshape(slice_cols, -1).T

    def column_grad(value):
        return jnp.swapaxes(value.astype(wide), -1, -2)

    prefix_total = jnp.concatenate([encoder_pre_grad, decoder_pre_grad, cross_pre_grad])[:, :count]
    prefix_total = jnp.moveaxis(prefix_total.reshape(6, count, ranks, slice_cols), 2, 0)
    prefix_total = small_scatter(prefix_total, [("rows", ranks)])
    norm_rows = [row for index in sorted(norm_grads) for row in norm_grads[index]]
    which = lax.broadcasted_iota(jnp.int32, (len(norm_rows), width), 0)
    norm_total = sum(jnp.where(which == k, row, 0.0) for k, row in enumerate(norm_rows))
    norm_total = jnp.moveaxis(norm_total.reshape(-1, 2, seq * ranks, slice_cols), 2, 0)
    norm_total = small_scatter(norm_total, norm_axes)

    shape_out = source.shape
    return (
        result.reshape(shape_out),
        source_grad.reshape(shape_out),
        target_grad.reshape(shape_out),
        column_grad(encoder_in_grad),
        row_grad(encoder_out_rows, 0, head_width),
        prefix_total[0:2],
        column_grad(encoder_one_grad[:cut]),
        row_grad(encoder_rows, 0, hidden),
        column_grad(encoder_one_grad[cut:]),
        row_grad(encoder_rows, hidden, adapt, ADAPTER_SCALE),
        norm_total[:norm_count],
        column_grad(decoder_in_grad),
        row_grad(decoder_rows, padded + head_width, head_width),
        prefix_total[2:4],
        column_grad(cross_in_grad[0]),
        column_grad(cross_in_grad[1:]),
        row_grad(decoder_rows, padded, head_width),
        prefix_total[4:6],
        column_grad(decoder_one_grad[:cut]),
        row_grad(decoder_rows, 0, hidden),
        column_grad(decoder_one_grad[cut:]),
        row_grad(decoder_rows, hidden, adapt, ADAPTER_SCALE),
        norm_total[norm_count:],
    )


def solution(mesh):
    rows = P(None, "rows", "seq", None)
    ids = P(None, "rows", None)
    flat = P(None, ("seq", "rows"))
    deep = P(None, None, ("seq", "rows"))
    weights = (
        deep, flat, deep, flat, flat, flat, flat, deep, deep, flat, deep, flat, deep, flat, deep,
        flat, flat, flat, flat, deep,
    )
    body = functools.partial(local, mesh.shape["seq"], mesh.shape["rows"])
    return jax.shard_map(
        body,
        mesh=mesh,
        in_specs=(rows, rows, ids, ids, rows) + weights,
        out_specs=(rows, rows, rows) + weights,
        check_vma=False,
    )
```

```python
import functools

import jax
import jax.numpy as jnp
from jax import lax
from jax.experimental import pallas as pl
from jax.experimental.layout import Layout, with_layout_constraint
from jax.experimental.pallas import tpu as pltpu
from jax.sharding import PartitionSpec as P

HEADS = 16
HEAD_DIM = 64
EPSILON = 1e-05
MASKED = -1e30
ADAPTER_SCALE = 4.0
SCALING = HEAD_DIM ** (-0.5)
PAD_PREFIX = 32
CHUNK = 256
LANES = 128
VMEM_LIMIT = 60 * 1024 * 1024
HALF_ROOT = 0.7071067811865476
DENSITY = 0.3989422804014327

low = jnp.bfloat16
wide = jnp.float32


def dot(left, right, left_axis, right_axis):
    return lax.dot_general(
        left, right, (((left_axis,), (right_axis,)), ((), ())), preferred_element_type=wide
    )


def bit_list(count):
    bits = []
    value = 1
    while value < count:
        bits.append(value)
        value *= 2
    return bits


def swap_pairs(count, bit):
    return [(index, index ^ bit) for index in range(count)]


def relative(places, seq, me):
    depth = len(bit_list(seq))
    value = places.reshape((2,) * depth + (-1,))
    for axis in range(depth):
        bit = 1 << (depth - 1 - axis)
        value = jnp.where((me & bit) != 0, jnp.flip(value, axis), value)
    return jnp.moveaxis(value, depth - 1, 0).reshape(-1)


def normalized(tensor):
    average = jnp.mean(tensor, axis=-1, keepdims=True)
    centered = tensor - average
    spread = jnp.mean(centered * centered, axis=-1, keepdims=True)
    inverse = lax.rsqrt(spread + EPSILON)
    return centered * inverse, inverse


def layer_norm(tensor, scales):
    return normalized(tensor)[0] * scales[0] + scales[1]


def norm_back(upstream, tensor, scales):
    unit, inverse = normalized(tensor)
    slope = upstream * scales[0]
    grad = inverse * (
        slope
        - jnp.mean(slope, axis=-1, keepdims=True)
        - unit * jnp.mean(slope * unit, axis=-1, keepdims=True)
    )
    return (
        grad,
        jnp.sum(upstream * unit, axis=0, keepdims=True),
        jnp.sum(upstream, axis=0, keepdims=True),
    )


def gelu_exact(tensor):
    return tensor * (0.5 + 0.5 * lax.erf(tensor * HALF_ROOT))


def gelu_slope(tensor):
    density = jnp.exp(-0.5 * tensor * tensor) * DENSITY
    return 0.5 + 0.5 * lax.erf(tensor * HALF_ROOT) + tensor * density


class Links:
    def __init__(self, seq):
        self.seq = seq
        self.far = [bit for bit in bit_list(seq) if bit > 1]
        self.orders = [self.far, self.far[::-1]]
        self.half = seq // 2
        self.me = lax.axis_index("seq")

    def place(self, mask):
        return (mask & 1) * self.half + (mask >> 1)

    def device(self, bit):
        return {"seq": jnp.bitwise_xor(self.me, bit)}

    def enter(self, others=()):
        barrier = pltpu.get_barrier_semaphore()
        bits = bit_list(self.seq)
        for bit in bits:
            pl.semaphore_signal(
                barrier, inc=1, device_id=self.device(bit), device_id_type=pl.DeviceIdType.MESH
            )
        count = len(bits)
        for other in others:
            count += other.greet(barrier)
        pl.semaphore_wait(barrier, count)

    def copy(self, source, target, send_sem, recv_sem, bit):
        return pltpu.make_async_remote_copy(
            src_ref=source,
            dst_ref=target,
            send_sem=send_sem,
            recv_sem=recv_sem,
            device_id=self.device(bit),
            device_id_type=pl.DeviceIdType.MESH,
        )


def span(bits):
    masks = [0]
    for bit in bits:
        masks = masks + [mask | bit for mask in masks]
    return masks


class Gather:
    def __init__(self, links, own_ref, all_ref, sends, recvs, local_sem):
        self.links, self.own, self.all = links, own_ref, all_ref
        self.sends, self.recvs, self.local = sends, recvs, local_sem
        self.rows = own_ref.shape[1]
        self.cut = self.rows // 2

    def at(self, micro, mask, part):
        start = self.links.place(mask) * self.rows + part * self.cut
        return self.all.at[micro, start : start + self.cut]

    def piece(self, micro, mask, part):
        if mask & 1:
            return 1
        seen = 0
        for bit in self.links.orders[part]:
            if mask & bit:
                seen = bit
        return seen

    def send(self, micro, mask, part, bit):
        there = mask ^ bit
        source = self.at(micro, mask, part)
        if mask == 0:
            source = self.own.at[micro, part * self.cut : (part + 1) * self.cut]
        self.links.copy(
            source,
            self.at(micro, there, part),
            self.sends.at[micro, self.links.place(there), part],
            self.recvs.at[micro, self.links.place(there), part],
            bit,
        ).start()

    def descriptor(self, micro, mask, part):
        bit = self.piece(micro, mask, part)
        source = self.at(micro, mask ^ bit, part)
        if mask ^ bit == 0:
            source = self.own.at[micro, part * self.cut : (part + 1) * self.cut]
        place = self.links.place(mask)
        return self.links.copy(
            source,
            self.at(micro, mask, part),
            self.sends.at[micro, place, part],
            self.recvs.at[micro, place, part],
            bit,
        )

    def keep_own(self, micro):
        return pltpu.make_async_copy(
            self.own.at[micro], self.all.at[micro, 0 : self.rows], self.local.at[micro]
        )

    def start(self, micro):
        for part in range(2):
            self.send(micro, 0, part, self.links.orders[part][0])
        for part in range(2):
            self.send(micro, 0, part, 1)
        self.keep_own(micro).start()

    def advance(self, micro, phase):
        count = len(self.links.far)
        for part in range(2):
            order = self.links.orders[part]
            fresh = [mask | order[phase] for mask in span(order[:phase])]
            for mask in fresh:
                self.descriptor(micro, mask, part).wait_recv()
            if phase + 1 < count:
                for mask in span(order[: phase + 1]):
                    self.send(micro, mask, part, order[phase + 1])
            for mask in fresh:
                self.send(micro, mask, part, 1)

    def phases(self):
        return len(self.links.far)

    def near(self, micro):
        for part in range(2):
            for mask in span(self.links.far):
                self.descriptor(micro, mask | 1, part).wait_recv()
        self.keep_own(micro).wait()

    def drain(self, micro):
        for part in range(2):
            for mask in range(1, self.links.seq):
                self.descriptor(micro, mask, part).wait_send()


class Scatter:
    def __init__(self, links, rows, sum_ref, near_send, near_recv, far_send, far_recv, sems):
        self.links, self.rows, self.cut = links, rows, rows // 2
        self.sum, self.near_send, self.near_recv = sum_ref, near_send, near_recv
        self.far_send, self.far_recv = far_send, far_recv
        self.near_sems, self.far_sems = sems

    def near_copy(self, micro, index):
        view = slice(index * self.rows, (index + 1) * self.rows)
        return self.links.copy(
            self.near_send.at[micro, view],
            self.near_recv.at[micro, view],
            self.near_sems.at[0, micro, index],
            self.near_sems.at[1, micro, index],
            1,
        )

    def start(self, micro, indexes):
        for index in indexes:
            self.near_copy(micro, index).start()

    def far_view(self, index, part):
        start = index * self.rows + part * self.cut
        return slice(start, start + self.cut)

    def bit_of(self, index, part):
        last = 0
        for bit in self.links.orders[part]:
            if (index * 2) & bit:
                last = bit
        return last

    def far_copy(self, micro, index, part):
        view = self.far_view(index, part)
        return self.links.copy(
            self.far_send.at[micro, view],
            self.far_recv.at[micro, view],
            self.far_sems.at[0, micro, index, part],
            self.far_sems.at[1, micro, index, part],
            self.bit_of(index, part),
        )

    def send_far(self, micro, index, part, value):
        self.far_send[micro, self.far_view(index, part)] = value.astype(low)
        self.far_copy(micro, index, part).start()

    def near_sum(self, micro):
        count = len(self.links.far)
        first = {}
        for part in range(2):
            bit = self.links.orders[part][count - 1]
            first[part] = [mask | bit for mask in span(self.links.orders[part][: count - 1])]
        ordered = sorted(range(self.links.half), key=lambda index: index == 0)
        for index in ordered:
            self.near_copy(micro, index).wait_recv()
            for part in range(2):
                view = self.far_view(index, part)
                value = self.sum[micro, view] + self.near_recv[micro, view].astype(wide)
                if index * 2 in first[part]:
                    self.send_far(micro, index, part, value)
                else:
                    self.sum[micro, view] = value

    def far_sum(self, micro, phase):
        count = len(self.links.far)
        for part in range(2):
            order = self.links.orders[part]
            bit = order[count - 1 - phase]
            remain = span(order[: count - 1 - phase])
            following = order[count - 2 - phase] if phase + 1 < count else 0
            for mask in sorted(remain, key=lambda mask: (mask & following) == 0):
                index, came = mask // 2, (mask | bit) // 2
                self.far_copy(micro, came, part).wait_recv()
                view = self.far_view(index, part)
                value = self.sum[micro, view] + self.far_recv[
                    micro, self.far_view(came, part)
                ].astype(wide)
                if mask & following:
                    self.send_far(micro, index, part, value)
                else:
                    self.sum[micro, view] = value

    def total(self, micro):
        return self.sum[micro, 0 : self.rows]

    def phases(self):
        return len(self.links.far)

    def drain(self, micro):
        for index in range(self.links.half):
            self.near_copy(micro, index).wait_send()
        for part in range(2):
            for index in range(1, self.links.half):
                self.far_copy(micro, index, part).wait_send()


def gather_scratch(seq, micros):
    return [
        pltpu.SemaphoreType.DMA((micros, seq, 2)),
        pltpu.SemaphoreType.DMA((micros, seq, 2)),
        pltpu.SemaphoreType.DMA((micros,)),
    ]


def scatter_scratch(seq, micros, rows, width):
    half = seq // 2
    part = pltpu.VMEM((micros, half * rows, width), low)
    return [
        pltpu.VMEM((micros, half * rows, width), wide),
        part,
        part,
        part,
        part,
        pltpu.SemaphoreType.DMA((2, micros, half)),
        pltpu.SemaphoreType.DMA((2, micros, half, 2)),
    ]


NEAR_GAP, FAR_GAP, SHORT_GAP = 3.0, 6.0, 0.1


def arrive_steps(gathers, micro):
    steps = []
    for phase in range(gathers[0].phases() if gathers else 0):
        for index, gather in enumerate(gathers):
            gap = SHORT_GAP if index else FAR_GAP
            steps.append((functools.partial(gather.advance, micro, phase), gap))
    for index, gather in enumerate(gathers):
        gap = SHORT_GAP if index else NEAR_GAP
        steps.append((functools.partial(gather.near, micro), gap))
    return steps


def leave_steps(scatters, finish, micro):
    steps = []
    for index, scatter in enumerate(scatters):
        gap = SHORT_GAP if index else NEAR_GAP
        steps.append((functools.partial(scatter.near_sum, micro), gap))
    for phase in range(scatters[0].phases()):
        for index, scatter in enumerate(scatters):
            gap = SHORT_GAP if index else FAR_GAP
            steps.append((functools.partial(scatter.far_sum, micro, phase), gap))
    return steps + [(functools.partial(finish, micro), SHORT_GAP)]


def half_steps(scatter, micro, length, chunk, cost):
    half = length // 2
    size = min(CHUNK, half)

    def odd():
        def body(index, carry):
            start = pl.multiple_of(half + index * size, size)
            place = pl.ds(pl.multiple_of(index * size, size), size)
            scatter.near_send[micro, place] = chunk(start, size).astype(low)
            return carry

        lax.fori_loop(0, half // size, body, 0)
        scatter.start(micro, range(scatter.links.half))

    def even():
        def body(index, carry):
            start = pl.multiple_of(index * size, size)
            scatter.sum[micro, pl.ds(start, size)] = chunk(start, size)
            return carry

        lax.fori_loop(0, half // size, body, 0)

    return [(odd, cost), (even, cost)]


def prologue(micro, up_ref, resid_ref, pair_ref, own_ref, kept_ref, pair_grad_ref):
    gains = (pair_ref[0:1], pair_ref[1:2])
    grad, gain_grad, shift_grad = norm_back(up_ref[micro].astype(wide), resid_ref[micro], gains)
    kept_ref[micro] = grad
    own_ref[micro] = grad.astype(low)
    if micro == 0:
        pair_grad_ref[0:1] = gain_grad
        pair_grad_ref[1:2] = shift_grad
    else:
        pair_grad_ref[0:1] += gain_grad
        pair_grad_ref[1:2] += shift_grad


class Task:
    def __init__(self, begin, arrive, compute, leave, drain, load=None, store=None):
        self.begin, self.arrive, self.compute = begin, arrive, compute
        self.leave, self.drain, self.load, self.store = leave, drain, load, store


class Waits:
    def __init__(self):
        self.time, self.queues = 0.0, []

    def add(self, steps):
        if steps:
            self.queues.append([list(steps), self.time + steps[0][1]])

    def take(self, entry):
        queue = entry[0]
        queue.pop(0)[0]()
        self.time += 0.4
        if queue:
            entry[1] = self.time + queue[0][1]
        else:
            self.queues.remove(entry)

    def run(self, step, cost):
        step()
        self.time += cost
        ready = [entry for entry in self.queues if entry[1] <= self.time]
        while ready:
            self.take(ready[0])
            ready = [entry for entry in self.queues if entry[1] <= self.time]

    def finish(self, steps):
        while any(entry[0] and entry[0][-1] is steps[-1] for entry in self.queues):
            entry = min(self.queues, key=lambda entry: entry[1])
            self.time = max(self.time, entry[1])
            self.take(entry)


def run_tasks(tasks, io, fill=(), fill_load=None, opening=None, closing=None):
    waits = Waits()
    for task in tasks[:2]:
        task.begin()
        waits.add(task.arrive)
    if opening is not None and len(tasks) <= 2:
        waits.add(opening())
    for index, task in enumerate(tasks):
        if task.arrive:
            waits.finish(task.arrive)
        io.load(task.load)
        for step, cost in task.compute:
            waits.run(step, cost)
        io.store(task.store)
        waits.add(task.leave)
        if index + 2 < len(tasks):
            tasks[index + 2].begin()
            waits.add(tasks[index + 2].arrive)
    if opening is not None and len(tasks) > 2:
        waits.add(opening())
    if closing is not None:
        waits.add(closing())
    if fill:
        io.load(fill_load)
        for step, cost in fill:
            waits.run(step, cost)
    while waits.queues:
        waits.take(min(waits.queues, key=lambda entry: entry[1]))
    for task in tasks:
        task.drain()
    io.close()


def make_task(micro, gathers, scatters, compute, finish, before=None, load=None, store=None):
    def begin():
        if before is not None:
            before(micro)
        for gather in gathers:
            gather.start(micro)

    def drain():
        for item in gathers + scatters:
            item.drain(micro)

    arrive = arrive_steps(gathers, micro)
    leave = leave_steps(scatters, finish, micro) if scatters else []
    return Task(begin, arrive, compute(micro), leave, drain, load, store)


class Operands:
    def __init__(self, ins, outs, in_sems, out_sems):
        self.ins, self.outs, self.in_sems, self.out_sems = ins, outs, in_sems, out_sems
        self.open = []

    def start(self):
        for index, (_, source, target) in enumerate(self.ins):
            pltpu.make_async_copy(source, target, self.in_sems.at[index]).start()

    def load(self, key):
        for index, (name, source, target) in enumerate(self.ins):
            if key is not None and name == key:
                pltpu.make_async_copy(source, target, self.in_sems.at[index]).wait()

    def copy_out(self, index, micro):
        _, source, target = self.outs[index]
        return pltpu.make_async_copy(
            source.at[micro], target.at[micro], self.out_sems.at[index, micro]
        )

    def store(self, key):
        if key is None:
            return
        name, micro = key
        for index, (group, _, _) in enumerate(self.outs):
            if group == name:
                self.copy_out(index, micro).start()
                self.open.append((index, micro))

    def close(self):
        for index, micro in self.open:
            self.copy_out(index, micro).wait()


def stage_call(kernel, name_id, outs, scratch, args, micros, lazy=None, early=None):
    lazy, early = lazy or {}, early or {}
    count, given, own = len(args), len(outs), len(scratch)
    lazy_places, early_places = sorted(lazy), sorted(early)
    parts = max([outs[place].shape[0] for place in early_places] + [1])

    def body(*refs):
        ins, results = list(refs[:count]), list(refs[count : count + given])
        own_scratch = refs[count + given : count + given + own]
        extra = refs[count + given + own :]
        loads, stores = [], []
        for index, place in enumerate(lazy_places):
            loads.append((lazy[place], ins[place], extra[index]))
            ins[place] = extra[index]
        for index, place in enumerate(early_places):
            buffer = extra[len(lazy_places) + index]
            stores.append((early[place], buffer, results[place]))
            results[place] = buffer
        io = Operands(loads, stores, extra[-2], extra[-1])
        io.start()
        kernel(io, *ins, *results, *own_scratch)

    held = [pltpu.VMEM(args[place].shape, args[place].dtype) for place in lazy_places]
    held += [pltpu.VMEM(outs[place].shape, outs[place].dtype) for place in early_places]
    sems = [
        pltpu.SemaphoreType.DMA((max(len(lazy_places), 1),)),
        pltpu.SemaphoreType.DMA((max(len(early_places), 1), parts)),
    ]
    near, far = pl.BlockSpec(memory_space=pltpu.VMEM), pl.BlockSpec(memory_space=pl.ANY)
    return pl.pallas_call(
        body,
        out_shape=tuple(outs),
        in_specs=[far if place in lazy else near for place in range(count)],
        out_specs=tuple(far if place in early else near for place in range(given)),
        scratch_shapes=list(scratch) + held + sems,
        compiler_params=pltpu.CompilerParams(
            collective_id=name_id, has_side_effects=True, vmem_limit_bytes=VMEM_LIMIT
        ),
        cost_estimate=pl.CostEstimate(
            flops=micros * 2_500_000_000, bytes_accessed=1 << 24, transcendentals=0
        ),
    )(*args)


def ffn_kernel(
    seq, io, own_ref, resid_ref, one_ref, two_ref, pair_ref, all_ref, before_ref, hidden_ref,
    sum_ref, norm_ref, low_ref, *scratch,
):
    links = Links(seq)
    micros, rows, _ = own_ref.shape
    length = all_ref.shape[1]
    gather = Gather(links, own_ref, all_ref, *scratch[:3])
    scatter = Scatter(links, rows, *scratch[3:8], scratch[8:])
    links.enter()

    def compute(micro):
        def chunk(start, size):
            place = pl.ds(start, size)
            before = dot(all_ref[micro, place], one_ref[...], 1, 1)
            before_ref[micro, place] = before
            after = gelu_exact(before).astype(low)
            hidden_ref[micro, place] = after
            return dot(after, two_ref[...], 1, 1)

        return half_steps(scatter, micro, length, chunk, 2.5)

    def finish(micro):
        total = resid_ref[micro] + scatter.total(micro)
        sum_ref[micro] = total
        value = layer_norm(total, (pair_ref[0:1], pair_ref[1:2]))
        norm_ref[micro] = value
        low_ref[micro] = value.astype(low)

    tasks = [
        make_task(
            micro, [gather], [scatter], compute, finish, None, 0 if micro == 0 else None, (0, micro)
        )
        for micro in range(micros)
    ]
    run_tasks(tasks, io)


def ffn_stage(seq, name_id, own, resid, one, two, pair):
    micros, rows, width = own.shape
    hidden = one.shape[0]
    length = rows * seq
    outs = (
        jax.ShapeDtypeStruct((micros, length, width), low),
        jax.ShapeDtypeStruct((micros, length, hidden), wide),
        jax.ShapeDtypeStruct((micros, length, hidden), low),
        jax.ShapeDtypeStruct((micros, rows, width), wide),
        jax.ShapeDtypeStruct((micros, rows, width), wide),
        jax.ShapeDtypeStruct((micros, rows, width), low),
    )
    scratch = gather_scratch(seq, micros) + scatter_scratch(seq, micros, rows, width)
    return stage_call(
        functools.partial(ffn_kernel, seq), name_id, outs, scratch,
        (own, resid, one, two, pair), 60, {1: 0, 2: 0, 3: 0, 4: 0}, {0: 0, 1: 0, 2: 0},
    )


def token_sum(left_ref, lanes, right_ref, micros):
    total = None
    for micro in range(micros):
        value = dot(left_ref[micro, :, lanes], right_ref[micro], 0, 0)
        total = value if total is None else total + value
    return total


def ffn_back_kernel(
    seq, ranks, hidden, io, up_ref, resid_ref, pair_ref, before_ref, one_ref, two_ref, rows_ref,
    hidden_ref, out_ref, pair_grad_ref, expand_ref, down_ref, two_terms_ref, all_ref, slope_ref,
    own_ref, kept_ref, *scratch,
):
    links = Links(seq)
    micros, rows, width = own_ref.shape
    length = all_ref.shape[1]
    adapt = down_ref.shape[0] * down_ref.shape[1]
    gather = Gather(links, own_ref, all_ref, *scratch[:3])
    scatter = Scatter(links, rows, *scratch[3:8], scratch[8:])
    links.enter()

    def before(micro):
        prologue(micro, up_ref, resid_ref, pair_ref, own_ref, kept_ref, pair_grad_ref)

    def compute(micro):
        def chunk(start, size):
            place = pl.ds(start, size)
            slope = dot(all_ref[micro, place], two_ref[...], 1, 0)
            slope = (slope * gelu_slope(before_ref[micro, place])).astype(low)
            slope_ref[micro, place] = slope
            return dot(slope, one_ref[...], 1, 0)

        return half_steps(scatter, micro, length, chunk, 2.5)

    def finish(micro):
        out_ref[micro] = kept_ref[micro] + scatter.total(micro)

    cut = hidden // ranks

    def one_tile(start):
        value = token_sum(slope_ref, slice(start, start + LANES), rows_ref, micros)
        if start < hidden:
            for part in range(0, LANES, cut):
                rank = (start + part) // cut
                expand_ref[rank] = value[part : part + cut].astype(low)
        else:
            down_ref[...] = value[:adapt].reshape(ranks, adapt // ranks, width).astype(low)

    def two_tile(start):
        value = token_sum(hidden_ref, slice(start, start + LANES), all_ref, micros).T
        value = value.reshape(seq, ranks, width // (seq * ranks), LANES)
        for rank in range(ranks):
            two_terms_ref[rank, :, :, start : start + LANES] = value[:, rank].astype(low)

    starts = range(0, slope_ref.shape[2], LANES)
    fill = [
        (functools.partial(tile, start), 1.2) for tile in (two_tile, one_tile) for start in starts
    ]
    tasks = [
        make_task(
            micro, [gather], [scatter], compute, finish, before, 0 if micro == 0 else None
        )
        for micro in range(micros)
    ]
    run_tasks(tasks, io, fill, 1)


def ffn_back_stage(seq, ranks, hidden, adapt, name_id, up, resid, pair, before, one, two, rows_all,
                   hidden_low):
    micros, rows, width = up.shape
    padded = one.shape[0]
    length = rows * seq
    outs = (
        jax.ShapeDtypeStruct((micros, rows, width), wide),
        jax.ShapeDtypeStruct((2, width), wide),
        jax.ShapeDtypeStruct((ranks, hidden // ranks, width), low),
        jax.ShapeDtypeStruct((ranks, adapt // ranks, width), low),
        jax.ShapeDtypeStruct((ranks, seq, width // (seq * ranks), padded), low),
    )
    scratch = (
        [pltpu.VMEM((micros, length, width), low), pltpu.VMEM((micros, length, padded), low)]
        + back_scratch(micros, rows, width)
        + gather_scratch(seq, micros)
        + scatter_scratch(seq, micros, rows, width)
    )
    return stage_call(
        functools.partial(ffn_back_kernel, seq, ranks, hidden), name_id, outs, scratch,
        (up, resid, pair, before, one, two, rows_all, hidden_low), 65,
        {3: 0, 4: 0, 5: 0, 6: 1, 7: 1},
    )


def opening_kernel(
    seq, ranks, io, source_ref, target_ref, out_ref, ffn_ref, small_ref, source_all, target_all,
    out_all, ffn_all, small_all, norm_all, *scratch,
):
    links = Links(seq)
    me, row = lax.axis_index("seq"), lax.axis_index("rows")
    gathers = [
        Gather(links, source_ref, source_all, *scratch[0:3]),
        Gather(links, target_ref, target_all, *scratch[3:6]),
    ]
    out_sems, ffn_sems, norm_sems, out_row_sems, small_row_sems, local_sems = scratch[6:]
    masks = range(1, seq)
    row_bits = bit_list(ranks)
    norm_rows = norm_all.shape[2]

    def remote(source, target, sems, index, device):
        return pltpu.make_async_remote_copy(
            src_ref=source,
            dst_ref=target,
            send_sem=sems.at[0, index],
            recv_sem=sems.at[1, index],
            device_id=device,
            device_id_type=pl.DeviceIdType.MESH,
        )

    def plane(mask):
        return {"seq": jnp.bitwise_xor(me, mask)}

    def other(mask):
        return jnp.bitwise_xor(me, mask)

    barrier = pltpu.get_barrier_semaphore()
    for mask in masks:
        pl.semaphore_signal(
            barrier, inc=1, device_id=plane(mask), device_id_type=pl.DeviceIdType.MESH
        )
    for bit in row_bits:
        pl.semaphore_signal(
            barrier,
            inc=1,
            device_id={"rows": jnp.bitwise_xor(row, bit)},
            device_id_type=pl.DeviceIdType.MESH,
        )
    pl.semaphore_wait(barrier, seq - 1 + len(row_bits))

    locals_ = [
        pltpu.make_async_copy(out_ref.at[me], out_all.at[row, me], local_sems.at[0]),
        pltpu.make_async_copy(ffn_ref.at[me], ffn_all.at[me], local_sems.at[1]),
        pltpu.make_async_copy(small_ref, small_all.at[row], local_sems.at[2]),
    ]
    for copy in locals_:
        copy.start()

    def out_send(mask):
        return remote(
            out_ref.at[other(mask)], out_all.at[row, me], out_sems, mask, plane(mask)
        )

    def out_wait(mask):
        return remote(
            out_ref.at[other(mask)], out_all.at[row, other(mask)], out_sems, mask, plane(mask)
        )

    def ffn_send(mask):
        return remote(ffn_ref.at[other(mask)], ffn_all.at[me], ffn_sems, mask, plane(mask))

    def ffn_wait(mask):
        return remote(
            ffn_ref.at[other(mask)], ffn_all.at[other(mask)], ffn_sems, mask, plane(mask)
        )

    def norm_send(mask):
        return remote(
            small_all.at[:, 0:norm_rows], norm_all.at[me], norm_sems, mask, plane(mask)
        )

    def norm_wait(mask):
        return remote(
            small_all.at[:, 0:norm_rows], norm_all.at[other(mask)], norm_sems, mask, plane(mask)
        )

    def row_copy(array, sems, mask, bit, there):
        at = jnp.bitwise_xor(row, mask)
        place = jnp.bitwise_xor(at, bit) if there else at
        return remote(
            array.at[at],
            array.at[place],
            sems,
            mask | bit,
            {"rows": jnp.bitwise_xor(row, bit)},
        )

    def row_phase(array, sems, phase):
        bit = row_bits[phase]
        for mask in span(row_bits[:phase]):
            row_copy(array, sems, mask, bit, False).start()

    def row_done(array, sems, phase):
        bit = row_bits[phase]
        for mask in span(row_bits[:phase]):
            row_copy(array, sems, mask, bit, True).wait_recv()

    for mask in masks:
        out_send(mask).start()
    tasks = [
        make_task(micro, [gather], [], lambda micro: [], None)
        for gather in gathers
        for micro in range(source_ref.shape[0])
    ]
    locals_[2].wait()
    row_phase(small_all, small_row_sems, 0)
    for task in tasks:
        task.begin()
    for mask in masks:
        ffn_send(mask).start()
    locals_[0].wait()
    for mask in masks:
        out_wait(mask).wait_recv()
    row_phase(out_all, out_row_sems, 0)
    steps = [
        functools.partial(task.arrive[phase][0])
        for phase in range(len(tasks[0].arrive))
        for task in tasks
    ]
    for phase in range(len(row_bits)):
        row_done(small_all, small_row_sems, phase)
        if phase + 1 < len(row_bits):
            row_phase(small_all, small_row_sems, phase + 1)
    norm_all[me] = small_all[:, 0:norm_rows]
    for mask in masks:
        norm_send(mask).start()
    cuts = [len(steps) * part // len(row_bits) for part in range(len(row_bits) + 1)]
    for phase in range(len(row_bits)):
        for step in steps[cuts[phase] : cuts[phase + 1]]:
            step()
        row_done(out_all, out_row_sems, phase)
        if phase + 1 < len(row_bits):
            row_phase(out_all, out_row_sems, phase + 1)
    for mask in masks:
        norm_wait(mask).wait_recv()
        ffn_wait(mask).wait_recv()
    locals_[1].wait()
    for mask in masks:
        out_send(mask).wait_send()
        ffn_send(mask).wait_send()
        norm_send(mask).wait_send()
    for phase, bit in enumerate(row_bits):
        for mask in span(row_bits[:phase]):
            row_copy(out_all, out_row_sems, mask, bit, False).wait_send()
            row_copy(small_all, small_row_sems, mask, bit, False).wait_send()
    for task in tasks:
        task.drain()


def opening_stage(seq, ranks, name_id, norm_rows, args):
    source, _, out_pieces, ffn_pieces, small = args
    micros, rows, width = source.shape
    whole = jax.ShapeDtypeStruct((micros, seq * rows, width), low)
    outs = (
        whole,
        whole,
        jax.ShapeDtypeStruct((ranks,) + out_pieces.shape, low),
        jax.ShapeDtypeStruct(ffn_pieces.shape, low),
        jax.ShapeDtypeStruct((ranks,) + small.shape, low),
        jax.ShapeDtypeStruct((seq, ranks, norm_rows, small.shape[1]), low),
    )
    scratch = gather_scratch(seq, micros) * 2 + [
        pltpu.SemaphoreType.DMA((2, seq)),
        pltpu.SemaphoreType.DMA((2, seq)),
        pltpu.SemaphoreType.DMA((2, seq)),
        pltpu.SemaphoreType.DMA((2, ranks)),
        pltpu.SemaphoreType.DMA((2, ranks)),
        pltpu.SemaphoreType.DMA((3,)),
    ]
    return stage_call(
        functools.partial(opening_kernel, seq, ranks), name_id, outs, scratch, args, 55
    )


class Attention:
    def __init__(self, q_ref, kv_ref, offsets, prefix_ref, ids, count, causal):
        self.q, self.kv, self.offsets, self.prefix = q_ref, kv_ref, offsets, prefix_ref
        self.key_ids, self.query_ids, self.key_places, self.query_places = ids
        self.count, self.causal = count, causal
        self.heads = prefix_ref.shape[2] // HEAD_DIM

    def load(self, micro, head, place):
        q_at, k_at, v_at = (at + head * HEAD_DIM for at in self.offsets)
        queries = self.q[micro, place, q_at : q_at + HEAD_DIM] * jnp.asarray(SCALING, low)
        keys = self.kv[micro, :, k_at : k_at + HEAD_DIM]
        values = self.kv[micro, :, v_at : v_at + HEAD_DIM]
        return queries, keys, values

    def scores(self, micro, keys, queries, lanes, place):
        scores = dot(keys, queries, 1, 1)
        allowed = self.key_ids[micro] == self.query_ids[micro, :, place]
        if self.causal:
            allowed = allowed & (self.key_places[...] <= self.query_places[:, place])
        scores = jnp.where(allowed, scores, MASKED)
        extra = dot(self.prefix[0, :, lanes], queries, 1, 1)
        rows = lax.broadcasted_iota(jnp.int32, extra.shape, 0)
        return scores, jnp.where(rows < self.count, extra, MASKED)

    def forward(self, micro, start, size, context_ref, logs_ref):
        place = pl.ds(start, size)
        for head in range(self.heads):
            lanes = slice(head * HEAD_DIM, (head + 1) * HEAD_DIM)
            queries, keys, values = self.load(micro, head, place)
            scores, extra = self.scores(micro, keys, queries, lanes, place)
            peak = jnp.maximum(
                jnp.max(scores, axis=0, keepdims=True), jnp.max(extra, axis=0, keepdims=True)
            )
            scores = jnp.exp(scores - peak)
            extra = jnp.exp(extra - peak)
            total = jnp.sum(scores, axis=0, keepdims=True) + jnp.sum(extra, axis=0, keepdims=True)
            context = dot(values, scores.astype(low), 0, 0)
            context = context + dot(self.prefix[1, :, lanes], extra.astype(low), 0, 0)
            context_ref[micro, place, lanes] = (context / total).T.astype(low)
            logs_ref[micro, head : head + 1, place] = peak + jnp.log(total)

    def backward(self, micro, start, size, up_ref, logs_ref, grad_ref, k_sum, v_sum, pre_ref):
        place = pl.ds(start, size)
        for head in range(self.heads):
            lanes = slice(head * HEAD_DIM, (head + 1) * HEAD_DIM)
            queries, keys, values = self.load(micro, head, place)
            scores, extra = self.scores(micro, keys, queries, lanes, place)
            logs = logs_ref[micro, head : head + 1, place]
            weights = jnp.exp(scores - logs)
            extra = jnp.exp(extra - logs)
            up = up_ref[:, lanes]
            dots = dot(values, up, 1, 1)
            extra_dots = dot(self.prefix[1, :, lanes], up, 1, 1)
            centre = jnp.sum(weights * dots, axis=0, keepdims=True) + jnp.sum(
                extra * extra_dots, axis=0, keepdims=True
            )
            slope = (weights * (dots - centre)).astype(low)
            extra_slope = (extra * (extra_dots - centre)).astype(low)
            query_grad = dot(keys, slope, 0, 0) + dot(self.prefix[0, :, lanes], extra_slope, 0, 0)
            grad_ref[micro, place, lanes] = (query_grad * SCALING).T.astype(low)
            k_sum[:, lanes] += dot(slope, queries, 1, 0)
            v_sum[:, lanes] += dot(weights.astype(low), up, 1, 0)
            pre_ref[0, :, lanes] += dot(extra_slope, queries, 1, 0)
            pre_ref[1, :, lanes] += dot(extra.astype(low), up, 1, 0)


def loop(first, count, size, body):
    def step(index, carry):
        body(pl.multiple_of(first + index * size, size), index)
        return carry

    lax.fori_loop(0, count, step, 0)


def project_steps(micro, rows_ref, weight_ref, out_ref):
    length = rows_ref.shape[1]
    size = min(CHUNK, length)

    def body(start, index):
        place = pl.ds(start, size)
        out_ref[micro, place] = dot(rows_ref[micro, place], weight_ref[...], 1, 1).astype(low)

    return [(lambda: loop(0, length // size, size, body), 1.3)]


def self_kernel(seq, count, io, *refs):
    kinds = 2
    scratch = refs[-kinds * 7 :]
    refs = refs[: -kinds * 7]
    places = refs[:2]
    links = Links(seq)
    links.enter()
    tasks = []
    for kind in range(kinds):
        (all_ref, own_ref, in_ref, out_ref, prefix_ref, kid_ref, qid_ref, pair_ref) = refs[
            2 + 8 * kind : 10 + 8 * kind
        ]
        (qkv_ref, context_ref, logs_ref, sum_ref, norm_ref, low_ref) = refs[
            2 + 8 * kinds + 6 * kind : 8 + 8 * kinds + 6 * kind
        ]
        micros, rows, _ = own_ref.shape
        length = all_ref.shape[1]
        head_width = prefix_ref.shape[2]
        piece = scratch[7 * kind : 7 * kind + 7]
        scatter = Scatter(links, rows, *piece[:5], piece[5:])
        ids = (kid_ref, qid_ref) + tuple(places)
        attention = Attention(
            qkv_ref, qkv_ref, (0, head_width, 2 * head_width), prefix_ref, ids, count, kind == 1
        )

        def compute(
            micro, attention=attention, context_ref=context_ref, logs_ref=logs_ref,
            out_ref=out_ref, all_ref=all_ref, in_ref=in_ref, qkv_ref=qkv_ref, scatter=scatter,
        ):
            def chunk(start, size):
                attention.forward(micro, start, size, context_ref, logs_ref)
                return dot(context_ref[micro, pl.ds(start, size)], out_ref[...], 1, 1)

            return project_steps(micro, all_ref, in_ref, qkv_ref) + half_steps(
                scatter, micro, length, chunk, 4.2
            )

        def finish(
            micro, own_ref=own_ref, scatter=scatter, sum_ref=sum_ref, norm_ref=norm_ref,
            low_ref=low_ref, pair_ref=pair_ref,
        ):
            total = own_ref[micro].astype(wide) + scatter.total(micro)
            sum_ref[micro] = total
            value = layer_norm(total, (pair_ref[0:1], pair_ref[1:2]))
            norm_ref[micro] = value
            low_ref[micro] = value.astype(low)

        for micro in range(micros):
            load = kind if micro == 0 else None
            tasks.append(
                make_task(micro, [], [scatter], compute, finish, None, load, (kind, micro))
            )
    run_tasks(tasks, io)


def self_stage(seq, name_id, count, places, sides):
    micros, rows, width = sides[0][1].shape
    length = rows * seq
    head_width = sides[0][4].shape[2]
    heads = head_width // HEAD_DIM
    side_outs = (
        jax.ShapeDtypeStruct((micros, length, 3 * head_width), low),
        jax.ShapeDtypeStruct((micros, length, head_width), low),
        jax.ShapeDtypeStruct((micros, heads, length), wide),
        jax.ShapeDtypeStruct((micros, rows, width), wide),
        jax.ShapeDtypeStruct((micros, rows, width), wide),
        jax.ShapeDtypeStruct((micros, rows, width), low),
    )
    scratch = scatter_scratch(seq, micros, rows, width) * 2
    args = tuple(places) + sides[0] + sides[1]
    outs = stage_call(
        functools.partial(self_kernel, seq, count), name_id, side_outs * 2, scratch, args, 75,
        {10: 1, 11: 1, 12: 1, 13: 1, 15: 1}, {0: 0, 1: 0, 6: 1, 7: 1},
    )
    return outs[:6], outs[6:]


def cross_kernel(
    seq, count, io, kpos_ref, qpos_ref, first_ref, first_low_ref, memory_ref, q_in_ref, kv_in_ref,
    out_ref, prefix_ref, kid_ref, qid_ref, pair_ref, first_all, memory_all, q_ref, kv_ref,
    context_ref, logs_ref, sum_ref, norm_ref, low_ref, *scratch,
):
    links = Links(seq)
    micros, rows, _ = first_ref.shape
    length = first_all.shape[1]
    head_width = prefix_ref.shape[2]
    gathers = [
        Gather(links, memory_ref, memory_all, *scratch[:3]),
        Gather(links, first_low_ref, first_all, *scratch[3:6]),
    ]
    scatter = Scatter(links, rows, *scratch[6:11], scratch[11:])
    ids = (kid_ref, qid_ref, kpos_ref, qpos_ref)
    attention = Attention(q_ref, kv_ref, (0, 0, head_width), prefix_ref, ids, count, False)
    links.enter()

    def compute(micro):
        def chunk(start, size):
            attention.forward(micro, start, size, context_ref, logs_ref)
            return dot(context_ref[micro, pl.ds(start, size)], out_ref[...], 1, 1)

        return (
            project_steps(micro, memory_all, kv_in_ref, kv_ref)
            + project_steps(micro, first_all, q_in_ref, q_ref)
            + half_steps(scatter, micro, length, chunk, 4.2)
        )

    def finish(micro):
        total = first_ref[micro] + scatter.total(micro)
        sum_ref[micro] = total
        value = layer_norm(total, (pair_ref[0:1], pair_ref[1:2]))
        norm_ref[micro] = value
        low_ref[micro] = value.astype(low)

    tasks = [
        make_task(
            micro, gathers, [scatter], compute, finish, None, 0 if micro == 0 else None, (0, micro)
        )
        for micro in range(micros)
    ]
    run_tasks(tasks, io)


def cross_stage(seq, name_id, count, places, args):
    micros, rows, width = args[0].shape
    length = rows * seq
    head_width = args[6].shape[2]
    heads = head_width // HEAD_DIM
    whole = jax.ShapeDtypeStruct((micros, length, width), low)
    outs = (
        whole,
        whole,
        jax.ShapeDtypeStruct((micros, length, head_width), low),
        jax.ShapeDtypeStruct((micros, length, 2 * head_width), low),
        jax.ShapeDtypeStruct((micros, length, head_width), low),
        jax.ShapeDtypeStruct((micros, heads, length), wide),
        jax.ShapeDtypeStruct((micros, rows, width), wide),
        jax.ShapeDtypeStruct((micros, rows, width), wide),
        jax.ShapeDtypeStruct((micros, rows, width), low),
    )
    scratch = gather_scratch(seq, micros) * 2 + scatter_scratch(seq, micros, rows, width)
    return stage_call(
        functools.partial(cross_kernel, seq, count), name_id, outs, scratch,
        tuple(places) + args, 85, {place: 0 for place in (2, 5, 6, 7, 8, 9, 10)},
        {place: 0 for place in range(5)},
    )


def attend_back_steps(
    attention, micro, length, up_all, out_ref, logs_ref, grad_ref, k_sum, v_sum, pre_ref, up_ref,
    emit=None,
):
    head_width = up_ref.shape[1]
    half = length // 2
    size = min(CHUNK, half)

    def run(first, zero):
        if zero:
            k_sum[...] = jnp.zeros_like(k_sum)
            v_sum[...] = jnp.zeros_like(v_sum)
            if micro == 0:
                pre_ref[...] = jnp.zeros_like(pre_ref)

        def body(start, index):
            place = pl.ds(start, size)
            up_ref[...] = dot(up_all[micro, place], out_ref[...], 1, 0).astype(low)
            attention.backward(
                micro, start, size, up_ref, logs_ref, grad_ref, k_sum, v_sum, pre_ref
            )
            if emit is not None:
                emit(start, index, size)

        loop(first, half // size, size, body)

    def keys():
        grad_ref[micro, :, head_width : 2 * head_width] = k_sum[...].astype(low)
        grad_ref[micro, :, 2 * head_width : 3 * head_width] = v_sum[...].astype(low)

    return [(lambda: run(half, True), 5.0), (lambda: run(0, False), 5.0), (keys, 0.5)]


def term_steps(context_ref, up_all, grad_ref, sources, terms_ref, seq, send=None):
    micros = grad_ref.shape[0]
    ranks, _, cols, width = terms_ref.shape
    head_width = context_ref.shape[2]

    def tile(part):
        if part == 3:
            value = token_sum(context_ref, slice(0, head_width), up_all, micros).T
            value = value.reshape(seq, ranks, cols, head_width)
            for owner in range(seq):
                lanes = slice(owner * head_width, (owner + 1) * head_width)
                terms_ref[:, 3, :, lanes] = value[owner].astype(low)
        else:
            lanes = slice(part * head_width, (part + 1) * head_width)
            value = token_sum(grad_ref, lanes, sources[part], micros)
            terms_ref[:, part] = value.reshape(ranks, cols, width).astype(low)
        if send is not None:
            send(part)

    return [(functools.partial(tile, part), 1.2) for part in (3, 0, 1, 2)]


def term_shape(seq, ranks, width):
    return jax.ShapeDtypeStruct((ranks, 4, width // (seq * ranks), width), low)


class RankSum:
    def __init__(self, ranks, terms_ref, recv_ref, total_ref, sems):
        self.ranks, self.terms, self.recv = ranks, terms_ref, recv_ref
        self.total, self.sems, self.row = total_ref, sems, lax.axis_index("rows")

    def greet(self, barrier):
        for mask in range(1, self.ranks):
            pl.semaphore_signal(
                barrier,
                inc=1,
                device_id={"rows": jnp.bitwise_xor(self.row, mask)},
                device_id_type=pl.DeviceIdType.MESH,
            )
        return self.ranks - 1

    def copy(self, part, mask):
        owner = jnp.bitwise_xor(self.row, mask)
        return pltpu.make_async_remote_copy(
            src_ref=self.terms.at[owner, part],
            dst_ref=self.recv.at[mask, part],
            send_sem=self.sems.at[0, mask, part],
            recv_sem=self.sems.at[1, mask, part],
            device_id={"rows": owner},
            device_id_type=pl.DeviceIdType.MESH,
        )

    def send(self, part):
        for mask in range(1, self.ranks):
            self.copy(part, mask).start()

    def finish(self):
        for part in (3, 0, 1, 2):
            value = self.terms[self.row, part].astype(wide)
            for mask in range(1, self.ranks):
                self.copy(part, mask).wait_recv()
                value = value + self.recv[mask, part].astype(wide)
            self.total[part] = value
        for part in range(4):
            for mask in range(1, self.ranks):
                self.copy(part, mask).wait_send()


class SmallSum:
    def __init__(self, hops, held_ref, recv_ref, sems):
        self.hops, self.held, self.recv, self.sems = hops, held_ref, recv_ref, sems

    def copy(self, hop):
        name, bit = self.hops[hop]
        return pltpu.make_async_remote_copy(
            src_ref=self.held.at[hop],
            dst_ref=self.recv.at[hop],
            send_sem=self.sems.at[0, hop],
            recv_sem=self.sems.at[1, hop],
            device_id={name: jnp.bitwise_xor(lax.axis_index(name), bit)},
            device_id_type=pl.DeviceIdType.MESH,
        )

    def step(self, hop):
        self.copy(hop).wait_recv()
        self.held[hop + 1] = self.held[hop] + self.recv[hop]
        if hop + 1 < len(self.hops):
            self.copy(hop + 1).start()

    def start(self, gap):
        self.copy(0).start()
        return [(functools.partial(self.step, hop), gap) for hop in range(len(self.hops))]

    def total(self):
        return self.held[len(self.hops)]

    def drain(self):
        for hop in range(len(self.hops)):
            self.copy(hop).wait_send()


def small_scratch(hops, shape):
    return [
        pltpu.VMEM((hops + 1,) + shape, wide),
        pltpu.VMEM((hops,) + shape, wide),
        pltpu.SemaphoreType.DMA((2, hops)),
    ]


def cross_back_kernel(
    seq, count, io, kpos_ref, qpos_ref, up_ref, resid_ref, pair_ref, q_ref, kv_ref, logs_ref,
    q_in_ref, kv_in_ref, out_ref, prefix_ref, kid_ref, qid_ref, first_all, memory_all, context_ref,
    pre_ref, first_out, memory_out, pair_grad_ref, terms_ref, up_all, grad_ref, own_ref, kept_ref, k_sum, v_sum, up_chunk, *scratch,
):
    links = Links(seq)
    micros, rows, _ = own_ref.shape
    length = up_all.shape[1]
    head_width = prefix_ref.shape[2]
    gather = Gather(links, own_ref, up_all, *scratch[:3])
    first_sum = Scatter(links, rows, *scratch[3:8], scratch[8:10])
    memory_sum = Scatter(links, rows, *scratch[10:15], scratch[15:17])
    ids = (kid_ref, qid_ref, kpos_ref, qpos_ref)
    attention = Attention(q_ref, kv_ref, (0, 0, head_width), prefix_ref, ids, count, False)
    links.enter()

    def before(micro):
        prologue(micro, up_ref, resid_ref, pair_ref, own_ref, kept_ref, pair_grad_ref)

    def compute(micro):
        def first_chunk(start, size):
            return dot(
                grad_ref[micro, pl.ds(start, size), 0:head_width], q_in_ref[...], 1, 0
            )

        def memory_chunk(start, size):
            return dot(
                grad_ref[micro, pl.ds(start, size), head_width : 3 * head_width],
                kv_in_ref[...],
                1,
                0,
            )

        attend = attend_back_steps(
            attention, micro, length, up_all, out_ref, logs_ref, grad_ref, k_sum, v_sum, pre_ref,
            up_chunk,
        )
        sums = half_steps(first_sum, micro, length, first_chunk, 0.6)
        return (
            [attend[0], sums[0], attend[1], sums[1], attend[2]]
            + half_steps(memory_sum, micro, length, memory_chunk, 0.8)
        )

    def finish(micro):
        first_out[micro] = kept_ref[micro] + first_sum.total(micro)
        memory_out[micro] = memory_sum.total(micro)

    tasks = [
        make_task(
            micro, [gather], [first_sum, memory_sum], compute, finish, before,
            0 if micro == 0 else None,
        )
        for micro in range(micros)
    ]
    fill = term_steps(
        context_ref, up_all, grad_ref, (first_all, memory_all, memory_all), terms_ref, seq
    )
    run_tasks(tasks, io, fill, 1)


def cross_back_stage(seq, ranks, name_id, count, places, args):
    micros, rows, width = args[0].shape
    length = rows * seq
    head_width = args[9].shape[2]
    own = jax.ShapeDtypeStruct((micros, rows, width), wide)
    outs = (
        jax.ShapeDtypeStruct((2, PAD_PREFIX, head_width), wide),
        own,
        own,
        jax.ShapeDtypeStruct((2, width), wide),
        term_shape(seq, ranks, width),
    )
    scratch = (
        [
            pltpu.VMEM((micros, length, width), low),
            pltpu.VMEM((micros, length, 3 * head_width), low),
        ]
        + back_scratch(micros, rows, width)
        + sum_scratch(length, head_width)
        + gather_scratch(seq, micros)
        + scatter_scratch(seq, micros, rows, width) * 2
    )
    lazy = {place: 0 for place in range(5, 14)}
    lazy.update({14: 1, 15: 1, 16: 1})
    return stage_call(
        functools.partial(cross_back_kernel, seq, count), name_id, outs, scratch,
        tuple(places) + args, 85, lazy,
    )


def back_scratch(micros, rows, width):
    return [pltpu.VMEM((micros, rows, width), low), pltpu.VMEM((micros, rows, width), wide)]


def sum_scratch(length, head_width):
    return [
        pltpu.VMEM((length, head_width), wide),
        pltpu.VMEM((length, head_width), wide),
        pltpu.VMEM((min(CHUNK, length // 2), head_width), low),
    ]


def self_back_kernel(
    seq, count, causal, reduce, io, kpos_ref, qpos_ref, up_ref, resid_ref, pair_ref, qkv_ref,
    logs_ref, in_ref, out_ref, prefix_ref, kid_ref, qid_ref, context_ref, rows_ref, *rest,
):
    if reduce:
        norm_in_ref, pre_in_ref, norm_out_ref, pre_out_ref, *rest = rest
    else:
        pre_ref, pair_grad_ref, *rest = rest
    grad_out, result_ref, up_all, grad_ref, own_ref, kept_ref, k_sum, v_sum, up_chunk, *scratch = rest
    links = Links(seq)
    micros, rows, _ = own_ref.shape
    length = up_all.shape[1]
    head_width = prefix_ref.shape[2]
    gather = Gather(links, own_ref, up_all, *scratch[:3])
    scatter = Scatter(links, rows, *scratch[3:8], scratch[8:10])
    terms_ref, rank_sum = result_ref, None
    if reduce:
        terms_ref, recv_ref, rank_sems, pre_ref, pair_grad_ref = scratch[10:15]
        row_hops = [("rows", bit) for bit in bit_list(terms_ref.shape[0])]
        norm_sum = SmallSum(
            [("seq", bit) for bit in bit_list(seq)] + row_hops, *scratch[15:18]
        )
        pre_sum = SmallSum(row_hops, *scratch[18:21])
        rank_sum = RankSum(terms_ref.shape[0], terms_ref, recv_ref, result_ref, rank_sems)
    ids = (kid_ref, qid_ref, kpos_ref, qpos_ref)
    attention = Attention(
        qkv_ref, qkv_ref, (0, head_width, 2 * head_width), prefix_ref, ids, count, causal
    )
    links.enter([rank_sum] if reduce else [])

    def before(micro):
        prologue(micro, up_ref, resid_ref, pair_ref, own_ref, kept_ref, pair_grad_ref)

    def compute(micro):
        def chunk(start, size):
            return dot(grad_ref[micro, pl.ds(start, size)], in_ref[...], 1, 0)

        return attend_back_steps(
            attention, micro, length, up_all, out_ref, logs_ref, grad_ref, k_sum, v_sum,
            pre_ref, up_chunk,
        ) + half_steps(scatter, micro, length, chunk, 0.9)

    def finish(micro):
        grad_out[micro] = kept_ref[micro] + scatter.total(micro)

    tasks = [
        make_task(
            micro, [gather], [scatter], compute, finish, before, 0 if micro == 0 else None
        )
        for micro in range(micros)
    ]
    fill = term_steps(
        context_ref, up_all, grad_ref, (rows_ref,) * 3, terms_ref, seq,
        rank_sum.send if reduce else None,
    )
    def opening():
        norm_sum.held[0] = norm_in_ref[...]
        norm_sum.held[0, 0:2] = pair_grad_ref[...]
        return norm_sum.start(9.0)

    def closing():
        pre_sum.held[0, 0:2] = pre_ref[...]
        pre_sum.held[0, 2:6] = pre_in_ref[...]
        return pre_sum.start(15.0)

    if reduce:
        run_tasks(tasks, io, fill, 1, opening, closing)
        rank_sum.finish()
        norm_out_ref[...] = norm_sum.total()
        pre_out_ref[...] = pre_sum.total()
        norm_sum.drain()
        pre_sum.drain()
    else:
        run_tasks(tasks, io, fill, 1)


def self_back_stage(seq, ranks, name_id, count, places, causal, reduce, side):
    micros, rows, width = side[0].shape
    length = rows * seq
    head_width = side[7].shape[2]
    terms = term_shape(seq, ranks, width)
    pre = jax.ShapeDtypeStruct((2, PAD_PREFIX, head_width), wide)
    outs = (pre, jax.ShapeDtypeStruct((2, width), wide))
    total = terms
    if reduce:
        outs = tuple(
            jax.ShapeDtypeStruct(shape, wide)
            for shape in (side[12].shape, (6, PAD_PREFIX, head_width))
        )
        total = jax.ShapeDtypeStruct(terms.shape[1:], wide)
    outs += (jax.ShapeDtypeStruct((micros, rows, width), wide), total)
    scratch = (
        [
            pltpu.VMEM((micros, length, width), low),
            pltpu.VMEM((micros, length, 3 * head_width), low),
        ]
        + back_scratch(micros, rows, width)
        + sum_scratch(length, head_width)
        + gather_scratch(seq, micros)
        + scatter_scratch(seq, micros, rows, width)
    )
    if reduce:
        scratch += [
            pltpu.VMEM(terms.shape, low),
            pltpu.VMEM(terms.shape, low),
            pltpu.SemaphoreType.DMA((2, ranks, 4)),
            pltpu.VMEM(pre.shape, wide),
            pltpu.VMEM((2, width), wide),
        ]
        row_hops, hops = len(bit_list(ranks)), len(bit_list(ranks)) + len(bit_list(seq))
        scratch += small_scratch(hops, side[12].shape)
        scratch += small_scratch(row_hops, (6, PAD_PREFIX, head_width))
    lazy = {place: 0 for place in range(5, 12)}
    lazy.update({12: 1, 13: 1})
    return stage_call(
        functools.partial(self_back_kernel, seq, count, causal, reduce), name_id, outs, scratch,
        tuple(places) + side, 75, lazy,
    )


def local(
    seq, ranks,
    source, target, source_segments, target_segments, cotangent,
    encoder_qkv, encoder_output, encoder_prefix, encoder_expand, encoder_contract, encoder_down,
    encoder_up, encoder_norms, decoder_qkv, decoder_output, decoder_prefix, cross_query, cross_kv,
    cross_output, cross_prefix, decoder_expand, decoder_contract, decoder_down, decoder_up,
    decoder_norms,
):
    micro_count, batch_rows, block, width = source.shape
    length = source_segments.shape[2]
    me = lax.axis_index("seq")
    stacked = micro_count * batch_rows
    head_width = width // seq
    slice_cols = encoder_output.shape[1]
    count = encoder_prefix.shape[1]
    hidden = encoder_contract.shape[0] // seq
    adapt = encoder_up.shape[0] // seq
    both = hidden + adapt
    padded = (both + LANES - 1) // LANES * LANES

    sources = source.reshape(stacked, block, width)
    targets = target.reshape(stacked, block, width)

    order = relative(jnp.arange(length, dtype=jnp.int32), seq, me)
    places = (order[:, None], order[None, :])

    def relative_ids(ids):
        rows = [relative(row, seq, me) for row in ids.reshape(stacked, length)]
        value = jnp.stack(rows)
        return value[:, :, None], value[:, None, :]

    source_keys, source_queries = relative_ids(source_segments)
    target_keys, target_queries = relative_ids(target_segments)

    def columns(weight):
        return jnp.swapaxes(weight, -1, -2)

    def gather_rows(value):
        return lax.all_gather(value, "rows", axis=0, tiled=False)

    def stack_columns(pieces):
        gathered = gather_rows(jnp.concatenate(pieces, axis=0))
        outs = []
        start = 0
        for piece in pieces:
            size = piece.shape[0]
            outs.append(gathered[:, start : start + size])
            start += size
        return outs

    def flat_columns(gathered, parts):
        value = gathered.reshape(ranks, parts, slice_cols, width)
        return jnp.swapaxes(value, 0, 1).reshape(parts * ranks * slice_cols, width)

    def split_rows(weight):
        return columns(weight).reshape(slice_cols, seq, -1)

    def ffn_rows(contract, up):
        pieces = [split_rows(contract), split_rows(up) * jnp.asarray(ADAPTER_SCALE, low)]
        if padded > both:
            pieces.append(jnp.zeros((slice_cols, seq, padded - both), low))
        return pieces

    def by_target(pieces):
        return jnp.swapaxes(jnp.concatenate(pieces, axis=2), 0, 1)

    out_pieces = by_target([split_rows(encoder_output), split_rows(decoder_output)])
    ffn_pieces = by_target(
        [split_rows(cross_output)]
        + ffn_rows(encoder_contract, encoder_up)
        + ffn_rows(decoder_contract, decoder_up)
    )
    qkv_parts = gather_rows(
        jnp.concatenate(
            [
                columns(encoder_qkv).reshape(-1, width),
                columns(decoder_qkv).reshape(-1, width),
            ]
        )
    )
    norm_count = encoder_norms.shape[0]
    norms = jnp.concatenate([encoder_norms, decoder_norms]).reshape(-1, slice_cols)
    prefixes = jnp.concatenate([encoder_prefix, decoder_prefix, cross_prefix])
    prefixes = prefixes.reshape(-1, slice_cols)
    norm_rows = (norms.shape[0] + 15) // 16 * 16
    small = jnp.concatenate(
        [jnp.pad(norms, ((0, norm_rows - norms.shape[0]), (0, 0))), prefixes]
    )
    small = jnp.pad(small, ((0, -small.shape[0] % 16), (0, 0)))
    source_all, target_all, front, row_pieces, small_all, norm_all = opening_stage(
        seq, ranks, 1, norm_rows, (sources, targets, out_pieces, ffn_pieces, small)
    )
    scales = norm_all[:, :, : norms.shape[0]].reshape(seq * ranks, -1, slice_cols)
    scales = jnp.moveaxis(scales, 0, 1).reshape(-1, 2, width).astype(wide)
    prefixes = small_all[:, norm_rows : norm_rows + 6 * count]
    prefixes = jnp.moveaxis(prefixes.reshape(ranks, 6, count, slice_cols), 0, 2)
    prefixes = prefixes.reshape(6, count, head_width)
    prefixes = jnp.pad(prefixes, ((0, 0), (0, PAD_PREFIX - count), (0, 0)))
    encoder_pre, decoder_pre, cross_pre = prefixes[0:2], prefixes[2:4], prefixes[4:6]

    late = [
        jnp.concatenate(
            [
                columns(encoder_expand),
                columns(encoder_down),
                columns(cross_query),
                columns(cross_kv).reshape(-1, width),
            ]
        ),
        row_pieces[:, :, : head_width + padded],
        jnp.concatenate([columns(decoder_expand), columns(decoder_down)]),
        row_pieces[:, :, head_width + padded :],
    ]
    source_all, late = lax.optimization_barrier((source_all, late))
    encoder_in = flat_columns(qkv_parts[:, : 3 * slice_cols], 3)
    decoder_in = flat_columns(qkv_parts[:, 3 * slice_cols :], 3)
    front_rows = jnp.swapaxes(front, 0, 1).reshape(width, -1)
    encoder_out = front_rows[:, :head_width]
    decoder_out = front_rows[:, head_width:]
    cut = encoder_expand.shape[1]

    def ffn_in(gathered):
        pieces = [gathered[:, :cut].reshape(-1, width), gathered[:, cut:].reshape(-1, width)]
        if padded > both:
            pieces.append(jnp.zeros((padded - both, width), low))
        return jnp.concatenate(pieces)

    def row_order(gathered):
        return jnp.swapaxes(gathered, 0, 1).reshape(width, -1)

    second_parts = gather_rows(late[0])
    rest = gather_rows(late[1])
    encoder_side, decoder_side = self_stage(
        seq, 2, count, places,
        (
            (
                source_all, sources, encoder_in, encoder_out, encoder_pre, source_keys,
                source_queries, scales[0],
            ),
            (
                target_all, targets, decoder_in, decoder_out, decoder_pre, target_keys,
                target_queries, scales[norm_count],
            ),
        ),
    )
    encoder_qkvs, encoder_ctx, encoder_logs, resid_one, middle, middle_low = encoder_side
    middle_low, second_parts, rest, last = lax.optimization_barrier(
        (middle_low, second_parts, rest, late[2:])
    )
    rest = row_order(rest)
    cross_out, encoder_two = rest[:, :head_width], rest[:, head_width:]
    ffn_cut = cut + encoder_down.shape[1]
    encoder_one = ffn_in(second_parts[:, :ffn_cut])
    cross_in = flat_columns(second_parts[:, ffn_cut:], 3)
    cross_q_in, cross_kv_in = cross_in[:head_width], cross_in[head_width:]
    decoder_qkvs, decoder_ctx, decoder_logs, resid_three, first, first_low = decoder_side
    middle_all, encoder_before, encoder_hidden, resid_two, _, memory_low = ffn_stage(
        seq, 3, middle_low, middle, encoder_one, encoder_two, scales[1]
    )
    memory_low, last = lax.optimization_barrier(
        (memory_low, [gather_rows(piece) for piece in last])
    )
    decoder_one, decoder_two = ffn_in(last[0]), row_order(last[1])
    (
        first_all, memory_all, cross_q, cross_kvs, cross_ctx, cross_logs, resid_four, second,
        second_low,
    ) = cross_stage(
        seq, 4, count, places,
        (
            first, first_low, memory_low, cross_q_in, cross_kv_in, cross_out, cross_pre,
            source_keys, target_queries, scales[norm_count + 1],
        ),
    )
    second_all, decoder_before, decoder_hidden, resid_five, _, result = ffn_stage(
        seq, 5, second_low, second, decoder_one, decoder_two, scales[norm_count + 2]
    )

    def scatter_ranks(value):
        return lax.psum_scatter(value, "rows", scatter_dimension=0, tiled=False)

    norm_grads = {}

    def ffn_back(name_id, index, up, resid, before, hidden_low, rows_all, one, two):
        out, pair, expand, down, two_terms = ffn_back_stage(
            seq, ranks, hidden, adapt, name_id, up, resid, scales[index], before, one, two,
            rows_all, hidden_low,
        )
        keep_pair(index, pair)
        return out, [two_terms, jnp.concatenate([expand, down], axis=1)]

    def hold(value, terms, sums):
        value, terms, sums = lax.optimization_barrier((value, terms, sums))
        return value, [scatter_ranks(term) for term in terms], sums

    def keep_pair(index, pair):
        norm_grads[index] = pair

    second_up, terms = ffn_back(
        6, norm_count + 2, cotangent.reshape(stacked, block, width), resid_five, decoder_before,
        decoder_hidden, second_all, decoder_one, decoder_two,
    )
    second_up, ffn_sums, _ = hold(second_up, terms, [])

    cross_pre_grad, first_up, memory_up, pair, terms = cross_back_stage(
        seq, ranks, 7, count, places,
        (
            second_up, resid_four, scales[norm_count + 1], cross_q, cross_kvs, cross_logs,
            cross_q_in, cross_kv_in, cross_out, cross_pre, source_keys, target_queries,
            first_all, memory_all, cross_ctx,
        ),
    )
    keep_pair(norm_count + 1, pair)
    first_up, cross_sums, ffn_sums = hold(first_up, [terms], ffn_sums)
    decoder_two_grad, decoder_one_grad = ffn_sums

    def self_back(name_id, index, causal, reduce, side, sums):
        held = self_back_stage(seq, ranks, name_id, count, places, causal, reduce, side)
        held, sums = lax.optimization_barrier((tuple(held), sums))
        return held + (sums,)

    def owner_parts(value):
        out_part = value[3].reshape(slice_cols, seq, head_width)
        return jnp.swapaxes(out_part, 0, 1), value[:3]

    decoder_pre_grad, pair, target_grad, self_terms, cross_sums = self_back(
        9, norm_count, True, False,
        (
            first_up, resid_three, scales[norm_count], decoder_qkvs, decoder_logs, decoder_in,
            decoder_out, decoder_pre, target_keys, target_queries, decoder_ctx, target_all,
        ),
        cross_sums,
    )
    keep_pair(norm_count, pair)
    memory_up, self_sums, _ = hold(memory_up, [self_terms], [])
    cross_out_grad, cross_in_grad = owner_parts(cross_sums[0])

    middle_up, terms = ffn_back(
        8, 1, memory_up, resid_two, encoder_before, encoder_hidden, middle_all,
        encoder_one, encoder_two,
    )
    middle_up, ffn_sums, self_sums = hold(middle_up, terms, self_sums)
    decoder_out_grad, decoder_in_grad = owner_parts(self_sums[0])

    def give_back(pieces):
        value = jnp.concatenate(pieces, axis=2) if len(pieces) > 1 else pieces[0]
        return lax.all_to_all(value, "seq", 0, 1, tiled=False)

    decoder_rows = give_back([decoder_two_grad, cross_out_grad, decoder_out_grad])

    pairs = [jnp.zeros((2, width), wide)] + [norm_grads[index] for index in sorted(norm_grads)]
    norm_in = jnp.concatenate(pairs)
    norm_in = jnp.pad(norm_in, ((0, -norm_in.shape[0] % 16), (0, 0)))
    norm_total, prefix_total, source_grad, self_terms, ffn_sums = self_back(
        10, 0, False, True,
        (
            middle_up, resid_one, scales[0], encoder_qkvs, encoder_logs, encoder_in,
            encoder_out, encoder_pre, source_keys, source_queries, encoder_ctx, source_all,
            norm_in, jnp.concatenate([decoder_pre_grad, cross_pre_grad]),
        ),
        ffn_sums,
    )
    encoder_two_grad, encoder_one_grad = ffn_sums
    encoder_out_grad, encoder_in_grad = owner_parts(self_terms)
    encoder_rows = give_back([encoder_two_grad, encoder_out_grad.astype(low)])

    def row_grad(value, start, size, scale=None):
        piece = value[:, :, start : start + size].astype(wide)
        if scale is not None:
            piece = piece * scale
        return piece.reshape(slice_cols, -1).T

    def column_grad(value):
        return jnp.swapaxes(value.astype(wide), -1, -2)

    row = lax.axis_index("rows")
    prefix_total = lax.dynamic_slice_in_dim(
        prefix_total[:, :count], row * slice_cols, slice_cols, 2
    )
    norm_total = lax.dynamic_slice_in_dim(
        norm_total[: 2 * len(pairs)], (me * ranks + row) * slice_cols, slice_cols, 1
    )
    norm_total = norm_total.reshape(-1, 2, slice_cols)

    shape_out = source.shape
    return (
        result.reshape(shape_out),
        source_grad.reshape(shape_out),
        target_grad.reshape(shape_out),
        column_grad(encoder_in_grad),
        row_grad(encoder_rows, padded, head_width),
        prefix_total[0:2],
        column_grad(encoder_one_grad[:cut]),
        row_grad(encoder_rows, 0, hidden),
        column_grad(encoder_one_grad[cut:]),
        row_grad(encoder_rows, hidden, adapt, ADAPTER_SCALE),
        norm_total[:norm_count],
        column_grad(decoder_in_grad),
        row_grad(decoder_rows, padded + head_width, head_width),
        prefix_total[2:4],
        column_grad(cross_in_grad[0]),
        column_grad(cross_in_grad[1:]),
        row_grad(decoder_rows, padded, head_width),
        prefix_total[4:6],
        column_grad(decoder_one_grad[:cut]),
        row_grad(decoder_rows, 0, hidden),
        column_grad(decoder_one_grad[cut:]),
        row_grad(decoder_rows, hidden, adapt, ADAPTER_SCALE),
        norm_total[norm_count:],
    )


def solution(mesh):
    rows = P(None, "rows", "seq", None)
    ids = P(None, "rows", None)
    flat = P(None, ("seq", "rows"))
    deep = P(None, None, ("seq", "rows"))
    weights = (
        deep, flat, deep, flat, flat, flat, flat, deep, deep, flat, deep, flat, deep, flat, deep,
        flat, flat, flat, flat, deep,
    )
    body = functools.partial(local, mesh.shape["seq"], mesh.shape["rows"])
    return jax.shard_map(
        body,
        mesh=mesh,
        in_specs=(rows, rows, ids, ids, rows) + weights,
        out_specs=(rows, rows, rows) + weights,
        check_vma=False,
    )
```

```python
import functools

import jax
import jax.numpy as jnp
from jax import lax
from jax.experimental import pallas as pl
from jax.experimental.layout import Layout, with_layout_constraint
from jax.experimental.pallas import tpu as pltpu
from jax.sharding import PartitionSpec as P

HEADS = 16
HEAD_DIM = 64
EPSILON = 1e-05
MASKED = -1e30
ADAPTER_SCALE = 4.0
SCALING = HEAD_DIM ** (-0.5)
PAD_PREFIX = 32
CHUNK = 256
LANES = 128
VMEM_LIMIT = 60 * 1024 * 1024
HALF_ROOT = 0.7071067811865476
DENSITY = 0.3989422804014327

low = jnp.bfloat16
wide = jnp.float32


def dot(left, right, left_axis, right_axis):
    return lax.dot_general(
        left, right, (((left_axis,), (right_axis,)), ((), ())), preferred_element_type=wide
    )


def bit_list(count):
    bits = []
    value = 1
    while value < count:
        bits.append(value)
        value *= 2
    return bits


def swap_pairs(count, bit):
    return [(index, index ^ bit) for index in range(count)]


def relative(places, seq, me):
    depth = len(bit_list(seq))
    value = places.reshape((2,) * depth + (-1,))
    for axis in range(depth):
        bit = 1 << (depth - 1 - axis)
        value = jnp.where((me & bit) != 0, jnp.flip(value, axis), value)
    return jnp.moveaxis(value, depth - 1, 0).reshape(-1)


def normalized(tensor):
    average = jnp.mean(tensor, axis=-1, keepdims=True)
    centered = tensor - average
    spread = jnp.mean(centered * centered, axis=-1, keepdims=True)
    inverse = lax.rsqrt(spread + EPSILON)
    return centered * inverse, inverse


def layer_norm(tensor, scales):
    return normalized(tensor)[0] * scales[0] + scales[1]


def norm_back(upstream, tensor, scales):
    unit, inverse = normalized(tensor)
    slope = upstream * scales[0]
    grad = inverse * (
        slope
        - jnp.mean(slope, axis=-1, keepdims=True)
        - unit * jnp.mean(slope * unit, axis=-1, keepdims=True)
    )
    return (
        grad,
        jnp.sum(upstream * unit, axis=0, keepdims=True),
        jnp.sum(upstream, axis=0, keepdims=True),
    )


def gelu_exact(tensor):
    return tensor * (0.5 + 0.5 * lax.erf(tensor * HALF_ROOT))


def gelu_slope(tensor):
    density = jnp.exp(-0.5 * tensor * tensor) * DENSITY
    return 0.5 + 0.5 * lax.erf(tensor * HALF_ROOT) + tensor * density


class Links:
    def __init__(self, seq):
        self.seq = seq
        self.far = [bit for bit in bit_list(seq) if bit > 1]
        self.orders = [self.far, self.far[::-1]]
        self.half = seq // 2
        self.me = lax.axis_index("seq")

    def place(self, mask):
        return (mask & 1) * self.half + (mask >> 1)

    def device(self, bit):
        return {"seq": jnp.bitwise_xor(self.me, bit)}

    def enter(self, others=()):
        barrier = pltpu.get_barrier_semaphore()
        bits = bit_list(self.seq)
        for bit in bits:
            pl.semaphore_signal(
                barrier, inc=1, device_id=self.device(bit), device_id_type=pl.DeviceIdType.MESH
            )
        count = len(bits)
        for other in others:
            count += other.greet(barrier)
        pl.semaphore_wait(barrier, count)

    def copy(self, source, target, send_sem, recv_sem, bit):
        return pltpu.make_async_remote_copy(
            src_ref=source,
            dst_ref=target,
            send_sem=send_sem,
            recv_sem=recv_sem,
            device_id=self.device(bit),
            device_id_type=pl.DeviceIdType.MESH,
        )


def span(bits):
    masks = [0]
    for bit in bits:
        masks = masks + [mask | bit for mask in masks]
    return masks


class Gather:
    def __init__(self, links, own_ref, all_ref, sends, recvs, local_sem):
        self.links, self.own, self.all = links, own_ref, all_ref
        self.sends, self.recvs, self.local = sends, recvs, local_sem
        self.rows = own_ref.shape[1]
        self.cut = self.rows // 2

    def at(self, micro, mask, part):
        start = self.links.place(mask) * self.rows + part * self.cut
        return self.all.at[micro, start : start + self.cut]

    def piece(self, micro, mask, part):
        if mask & 1:
            return 1
        seen = 0
        for bit in self.links.orders[part]:
            if mask & bit:
                seen = bit
        return seen

    def send(self, micro, mask, part, bit):
        there = mask ^ bit
        source = self.at(micro, mask, part)
        if mask == 0:
            source = self.own.at[micro, part * self.cut : (part + 1) * self.cut]
        self.links.copy(
            source,
            self.at(micro, there, part),
            self.sends.at[micro, self.links.place(there), part],
            self.recvs.at[micro, self.links.place(there), part],
            bit,
        ).start()

    def descriptor(self, micro, mask, part):
        bit = self.piece(micro, mask, part)
        source = self.at(micro, mask ^ bit, part)
        if mask ^ bit == 0:
            source = self.own.at[micro, part * self.cut : (part + 1) * self.cut]
        place = self.links.place(mask)
        return self.links.copy(
            source,
            self.at(micro, mask, part),
            self.sends.at[micro, place, part],
            self.recvs.at[micro, place, part],
            bit,
        )

    def keep_own(self, micro):
        return pltpu.make_async_copy(
            self.own.at[micro], self.all.at[micro, 0 : self.rows], self.local.at[micro]
        )

    def start(self, micro):
        for part in range(2):
            self.send(micro, 0, part, self.links.orders[part][0])
        for part in range(2):
            self.send(micro, 0, part, 1)
        self.keep_own(micro).start()

    def advance(self, micro, phase):
        count = len(self.links.far)
        for part in range(2):
            order = self.links.orders[part]
            fresh = [mask | order[phase] for mask in span(order[:phase])]
            for mask in fresh:
                self.descriptor(micro, mask, part).wait_recv()
            if phase + 1 < count:
                for mask in span(order[: phase + 1]):
                    self.send(micro, mask, part, order[phase + 1])
            for mask in fresh:
                self.send(micro, mask, part, 1)

    def phases(self):
        return len(self.links.far)

    def near(self, micro):
        for part in range(2):
            for mask in span(self.links.far):
                self.descriptor(micro, mask | 1, part).wait_recv()
        self.keep_own(micro).wait()

    def drain(self, micro):
        for part in range(2):
            for mask in range(1, self.links.seq):
                self.descriptor(micro, mask, part).wait_send()


class Scatter:
    def __init__(self, links, rows, sum_ref, near_send, near_recv, far_send, far_recv, sems):
        self.links, self.rows, self.cut = links, rows, rows // 2
        self.sum, self.near_send, self.near_recv = sum_ref, near_send, near_recv
        self.far_send, self.far_recv = far_send, far_recv
        self.near_sems, self.far_sems = sems

    def near_copy(self, micro, index):
        view = slice(index * self.rows, (index + 1) * self.rows)
        return self.links.copy(
            self.near_send.at[micro, view],
            self.near_recv.at[micro, view],
            self.near_sems.at[0, micro, index],
            self.near_sems.at[1, micro, index],
            1,
        )

    def start(self, micro, indexes):
        for index in indexes:
            self.near_copy(micro, index).start()

    def far_view(self, index, part):
        start = index * self.rows + part * self.cut
        return slice(start, start + self.cut)

    def bit_of(self, index, part):
        last = 0
        for bit in self.links.orders[part]:
            if (index * 2) & bit:
                last = bit
        return last

    def far_copy(self, micro, index, part):
        view = self.far_view(index, part)
        return self.links.copy(
            self.far_send.at[micro, view],
            self.far_recv.at[micro, view],
            self.far_sems.at[0, micro, index, part],
            self.far_sems.at[1, micro, index, part],
            self.bit_of(index, part),
        )

    def send_far(self, micro, index, part, value):
        self.far_send[micro, self.far_view(index, part)] = value.astype(low)
        self.far_copy(micro, index, part).start()

    def near_sum(self, micro):
        count = len(self.links.far)
        first = {}
        for part in range(2):
            bit = self.links.orders[part][count - 1]
            first[part] = [mask | bit for mask in span(self.links.orders[part][: count - 1])]
        ordered = sorted(range(self.links.half), key=lambda index: index == 0)
        for index in ordered:
            self.near_copy(micro, index).wait_recv()
            for part in range(2):
                view = self.far_view(index, part)
                value = self.sum[micro, view] + self.near_recv[micro, view].astype(wide)
                if index * 2 in first[part]:
                    self.send_far(micro, index, part, value)
                else:
                    self.sum[micro, view] = value

    def far_sum(self, micro, phase):
        count = len(self.links.far)
        for part in range(2):
            order = self.links.orders[part]
            bit = order[count - 1 - phase]
            remain = span(order[: count - 1 - phase])
            following = order[count - 2 - phase] if phase + 1 < count else 0
            for mask in sorted(remain, key=lambda mask: (mask & following) == 0):
                index, came = mask // 2, (mask | bit) // 2
                self.far_copy(micro, came, part).wait_recv()
                view = self.far_view(index, part)
                value = self.sum[micro, view] + self.far_recv[
                    micro, self.far_view(came, part)
                ].astype(wide)
                if mask & following:
                    self.send_far(micro, index, part, value)
                else:
                    self.sum[micro, view] = value

    def total(self, micro):
        return self.sum[micro, 0 : self.rows]

    def phases(self):
        return len(self.links.far)

    def drain(self, micro):
        for index in range(self.links.half):
            self.near_copy(micro, index).wait_send()
        for part in range(2):
            for index in range(1, self.links.half):
                self.far_copy(micro, index, part).wait_send()


def gather_scratch(seq, micros):
    return [
        pltpu.SemaphoreType.DMA((micros, seq, 2)),
        pltpu.SemaphoreType.DMA((micros, seq, 2)),
        pltpu.SemaphoreType.DMA((micros,)),
    ]


def scatter_scratch(seq, micros, rows, width):
    half = seq // 2
    part = pltpu.VMEM((micros, half * rows, width), low)
    return [
        pltpu.VMEM((micros, half * rows, width), wide),
        part,
        part,
        part,
        part,
        pltpu.SemaphoreType.DMA((2, micros, half)),
        pltpu.SemaphoreType.DMA((2, micros, half, 2)),
    ]


NEAR_GAP, FAR_GAP, SHORT_GAP = 3.0, 6.0, 0.1


def arrive_steps(gathers, micro):
    steps = []
    for phase in range(gathers[0].phases() if gathers else 0):
        for index, gather in enumerate(gathers):
            gap = SHORT_GAP if index else FAR_GAP
            steps.append((functools.partial(gather.advance, micro, phase), gap))
    for index, gather in enumerate(gathers):
        gap = SHORT_GAP if index else NEAR_GAP
        steps.append((functools.partial(gather.near, micro), gap))
    return steps


def leave_steps(scatters, finish, micro):
    steps = []
    for index, scatter in enumerate(scatters):
        gap = SHORT_GAP if index else NEAR_GAP
        steps.append((functools.partial(scatter.near_sum, micro), gap))
    for phase in range(scatters[0].phases()):
        for index, scatter in enumerate(scatters):
            gap = SHORT_GAP if index else FAR_GAP
            steps.append((functools.partial(scatter.far_sum, micro, phase), gap))
    return steps + [(functools.partial(finish, micro), SHORT_GAP)]


def half_steps(scatter, micro, length, chunk, cost):
    half = length // 2
    size = min(CHUNK, half)

    def odd():
        def body(index, carry):
            start = pl.multiple_of(half + index * size, size)
            place = pl.ds(pl.multiple_of(index * size, size), size)
            scatter.near_send[micro, place] = chunk(start, size).astype(low)
            return carry

        lax.fori_loop(0, half // size, body, 0)
        scatter.start(micro, range(scatter.links.half))

    def even():
        def body(index, carry):
            start = pl.multiple_of(index * size, size)
            scatter.sum[micro, pl.ds(start, size)] = chunk(start, size)
            return carry

        lax.fori_loop(0, half // size, body, 0)

    return [(odd, cost), (even, cost)]


def prologue(micro, up_ref, resid_ref, pair_ref, own_ref, kept_ref, pair_grad_ref):
    gains = (pair_ref[0:1], pair_ref[1:2])
    grad, gain_grad, shift_grad = norm_back(up_ref[micro].astype(wide), resid_ref[micro], gains)
    kept_ref[micro] = grad
    own_ref[micro] = grad.astype(low)
    if micro == 0:
        pair_grad_ref[0:1] = gain_grad
        pair_grad_ref[1:2] = shift_grad
    else:
        pair_grad_ref[0:1] += gain_grad
        pair_grad_ref[1:2] += shift_grad


class Task:
    def __init__(self, begin, arrive, compute, leave, drain, load=None, store=None):
        self.begin, self.arrive, self.compute = begin, arrive, compute
        self.leave, self.drain, self.load, self.store = leave, drain, load, store


class Waits:
    def __init__(self):
        self.time, self.queues = 0.0, []

    def add(self, steps):
        if steps:
            self.queues.append([list(steps), self.time + steps[0][1]])

    def take(self, entry):
        queue = entry[0]
        queue.pop(0)[0]()
        self.time += 0.4
        if queue:
            entry[1] = self.time + queue[0][1]
        else:
            self.queues.remove(entry)

    def run(self, step, cost):
        step()
        self.time += cost
        ready = [entry for entry in self.queues if entry[1] <= self.time]
        while ready:
            self.take(ready[0])
            ready = [entry for entry in self.queues if entry[1] <= self.time]

    def finish(self, steps):
        while any(entry[0] and entry[0][-1] is steps[-1] for entry in self.queues):
            entry = min(self.queues, key=lambda entry: entry[1])
            self.time = max(self.time, entry[1])
            self.take(entry)


def run_tasks(tasks, io, fill=(), fill_load=None, opening=None, closing=None, ahead=2):
    waits = Waits()
    for task in tasks[:ahead]:
        task.begin()
        waits.add(task.arrive)
    if opening is not None and len(tasks) <= 2:
        waits.add(opening())
    for index, task in enumerate(tasks):
        if task.arrive:
            waits.finish(task.arrive)
        io.load(task.load)
        for step, cost in task.compute:
            waits.run(step, cost)
        io.store(task.store)
        waits.add(task.leave)
        if index + ahead < len(tasks):
            tasks[index + ahead].begin()
            waits.add(tasks[index + ahead].arrive)
    if opening is not None and len(tasks) > 2:
        waits.add(opening())
    if closing is not None:
        waits.add(closing())
    if fill:
        io.load(fill_load)
        for step, cost in fill:
            waits.run(step, cost)
    while waits.queues:
        waits.take(min(waits.queues, key=lambda entry: entry[1]))
    for task in tasks:
        task.drain()
    io.close()


def make_task(micro, gathers, scatters, compute, finish, before=None, load=None, store=None):
    def begin():
        if before is not None:
            before(micro)
        for gather in gathers:
            gather.start(micro)

    def drain():
        for item in gathers + scatters:
            item.drain(micro)

    arrive = arrive_steps(gathers, micro)
    leave = leave_steps(scatters, finish, micro) if scatters else []
    return Task(begin, arrive, compute(micro), leave, drain, load, store)


class Operands:
    def __init__(self, ins, outs, in_sems, out_sems):
        self.ins, self.outs, self.in_sems, self.out_sems = ins, outs, in_sems, out_sems
        self.open = []

    def start(self):
        for index, (_, source, target) in enumerate(self.ins):
            pltpu.make_async_copy(source, target, self.in_sems.at[index]).start()

    def load(self, key):
        for index, (name, source, target) in enumerate(self.ins):
            if key is not None and name == key:
                pltpu.make_async_copy(source, target, self.in_sems.at[index]).wait()

    def copy_out(self, index, micro):
        _, source, target = self.outs[index]
        return pltpu.make_async_copy(
            source.at[micro], target.at[micro], self.out_sems.at[index, micro]
        )

    def store(self, key):
        if key is None:
            return
        name, micro = key
        for index, (group, _, _) in enumerate(self.outs):
            if group == name:
                self.copy_out(index, micro).start()
                self.open.append((index, micro))

    def close(self):
        for index, micro in self.open:
            self.copy_out(index, micro).wait()


def stage_call(kernel, name_id, outs, scratch, args, micros, lazy=None, early=None):
    lazy, early = lazy or {}, early or {}
    count, given, own = len(args), len(outs), len(scratch)
    lazy_places, early_places = sorted(lazy), sorted(early)
    parts = max([outs[place].shape[0] for place in early_places] + [1])

    def body(*refs):
        ins, results = list(refs[:count]), list(refs[count : count + given])
        own_scratch = refs[count + given : count + given + own]
        extra = refs[count + given + own :]
        loads, stores = [], []
        for index, place in enumerate(lazy_places):
            loads.append((lazy[place], ins[place], extra[index]))
            ins[place] = extra[index]
        for index, place in enumerate(early_places):
            buffer = extra[len(lazy_places) + index]
            stores.append((early[place], buffer, results[place]))
            results[place] = buffer
        io = Operands(loads, stores, extra[-2], extra[-1])
        io.start()
        kernel(io, *ins, *results, *own_scratch)

    held = [pltpu.VMEM(args[place].shape, args[place].dtype) for place in lazy_places]
    held += [pltpu.VMEM(outs[place].shape, outs[place].dtype) for place in early_places]
    sems = [
        pltpu.SemaphoreType.DMA((max(len(lazy_places), 1),)),
        pltpu.SemaphoreType.DMA((max(len(early_places), 1), parts)),
    ]
    near, far = pl.BlockSpec(memory_space=pltpu.VMEM), pl.BlockSpec(memory_space=pl.ANY)
    return pl.pallas_call(
        body,
        out_shape=tuple(outs),
        in_specs=[far if place in lazy else near for place in range(count)],
        out_specs=tuple(far if place in early else near for place in range(given)),
        scratch_shapes=list(scratch) + held + sems,
        compiler_params=pltpu.CompilerParams(
            collective_id=name_id, has_side_effects=True, vmem_limit_bytes=VMEM_LIMIT
        ),
        cost_estimate=pl.CostEstimate(
            flops=micros * 2_500_000_000, bytes_accessed=1 << 24, transcendentals=0
        ),
    )(*args)


def ffn_kernel(
    seq, io, own_ref, resid_ref, one_ref, two_ref, pair_ref, all_ref, before_ref, hidden_ref,
    sum_ref, norm_ref, low_ref, *scratch,
):
    links = Links(seq)
    micros, rows, _ = own_ref.shape
    length = all_ref.shape[1]
    gather = Gather(links, own_ref, all_ref, *scratch[:3])
    scatter = Scatter(links, rows, *scratch[3:8], scratch[8:])
    links.enter()

    def compute(micro):
        def chunk(start, size):
            place = pl.ds(start, size)
            before = dot(all_ref[micro, place], one_ref[...], 1, 1)
            before_ref[micro, place] = before
            after = gelu_exact(before).astype(low)
            hidden_ref[micro, place] = after
            return dot(after, two_ref[...], 1, 1)

        return half_steps(scatter, micro, length, chunk, 2.5)

    def finish(micro):
        total = resid_ref[micro] + scatter.total(micro)
        sum_ref[micro] = total
        value = layer_norm(total, (pair_ref[0:1], pair_ref[1:2]))
        norm_ref[micro] = value
        low_ref[micro] = value.astype(low)

    tasks = [
        make_task(
            micro, [gather], [scatter], compute, finish, None, 0 if micro == 0 else None, (0, micro)
        )
        for micro in range(micros)
    ]
    run_tasks(tasks, io)


def ffn_stage(seq, name_id, own, resid, one, two, pair):
    micros, rows, width = own.shape
    hidden = one.shape[0]
    length = rows * seq
    outs = (
        jax.ShapeDtypeStruct((micros, length, width), low),
        jax.ShapeDtypeStruct((micros, length, hidden), wide),
        jax.ShapeDtypeStruct((micros, length, hidden), low),
        jax.ShapeDtypeStruct((micros, rows, width), wide),
        jax.ShapeDtypeStruct((micros, rows, width), wide),
        jax.ShapeDtypeStruct((micros, rows, width), low),
    )
    scratch = gather_scratch(seq, micros) + scatter_scratch(seq, micros, rows, width)
    return stage_call(
        functools.partial(ffn_kernel, seq), name_id, outs, scratch,
        (own, resid, one, two, pair), 60, {1: 0, 2: 0, 3: 0, 4: 0}, {0: 0, 1: 0, 2: 0},
    )


def token_sum(left_ref, lanes, right_ref, micros):
    total = None
    for micro in range(micros):
        value = dot(left_ref[micro, :, lanes], right_ref[micro], 0, 0)
        total = value if total is None else total + value
    return total


def ffn_back_kernel(
    seq, ranks, hidden, io, up_ref, resid_ref, pair_ref, before_ref, one_ref, two_ref, rows_ref,
    hidden_ref, out_ref, pair_grad_ref, expand_ref, down_ref, two_terms_ref, all_ref, slope_ref,
    own_ref, kept_ref, *scratch,
):
    links = Links(seq)
    micros, rows, width = own_ref.shape
    length = all_ref.shape[1]
    adapt = down_ref.shape[0] * down_ref.shape[1]
    gather = Gather(links, own_ref, all_ref, *scratch[:3])
    scatter = Scatter(links, rows, *scratch[3:8], scratch[8:])
    links.enter()

    def before(micro):
        prologue(micro, up_ref, resid_ref, pair_ref, own_ref, kept_ref, pair_grad_ref)

    def compute(micro):
        def chunk(start, size):
            place = pl.ds(start, size)
            slope = dot(all_ref[micro, place], two_ref[...], 1, 0)
            slope = (slope * gelu_slope(before_ref[micro, place])).astype(low)
            slope_ref[micro, place] = slope
            return dot(slope, one_ref[...], 1, 0)

        return half_steps(scatter, micro, length, chunk, 2.5)

    def finish(micro):
        out_ref[micro] = kept_ref[micro] + scatter.total(micro)

    cut = hidden // ranks

    def one_tile(start):
        value = token_sum(slope_ref, slice(start, start + LANES), rows_ref, micros)
        if start < hidden:
            for part in range(0, LANES, cut):
                rank = (start + part) // cut
                expand_ref[rank] = value[part : part + cut].astype(low)
        else:
            down_ref[...] = value[:adapt].reshape(ranks, adapt // ranks, width).astype(low)

    def two_tile(start):
        value = token_sum(hidden_ref, slice(start, start + LANES), all_ref, micros).T
        value = value.reshape(seq, ranks, width // (seq * ranks), LANES)
        for rank in range(ranks):
            two_terms_ref[rank, :, :, start : start + LANES] = value[:, rank].astype(low)

    starts = range(0, slope_ref.shape[2], LANES)
    fill = [
        (functools.partial(tile, start), 1.2) for tile in (two_tile, one_tile) for start in starts
    ]
    tasks = [
        make_task(
            micro, [gather], [scatter], compute, finish, before, 0 if micro == 0 else None
        )
        for micro in range(micros)
    ]
    run_tasks(tasks, io, fill, 1)


def ffn_back_stage(seq, ranks, hidden, adapt, name_id, up, resid, pair, before, one, two, rows_all,
                   hidden_low):
    micros, rows, width = up.shape
    padded = one.shape[0]
    length = rows * seq
    outs = (
        jax.ShapeDtypeStruct((micros, rows, width), wide),
        jax.ShapeDtypeStruct((2, width), wide),
        jax.ShapeDtypeStruct((ranks, hidden // ranks, width), low),
        jax.ShapeDtypeStruct((ranks, adapt // ranks, width), low),
        jax.ShapeDtypeStruct((ranks, seq, width // (seq * ranks), padded), low),
    )
    scratch = (
        [pltpu.VMEM((micros, length, width), low), pltpu.VMEM((micros, length, padded), low)]
        + back_scratch(micros, rows, width)
        + gather_scratch(seq, micros)
        + scatter_scratch(seq, micros, rows, width)
    )
    return stage_call(
        functools.partial(ffn_back_kernel, seq, ranks, hidden), name_id, outs, scratch,
        (up, resid, pair, before, one, two, rows_all, hidden_low), 65,
        {3: 0, 4: 0, 5: 0, 6: 1, 7: 1},
    )


def opening_kernel(
    seq, ranks, io, source_ref, out_ref, ffn_ref, small_ref, source_all, out_all, ffn_all,
    small_all, norm_all, *scratch,
):
    links = Links(seq)
    me, row = lax.axis_index("seq"), lax.axis_index("rows")
    gathers = [Gather(links, source_ref, source_all, *scratch[0:3])]
    out_sems, ffn_sems, norm_sems, out_row_sems, small_row_sems, local_sems = scratch[3:]
    masks = range(1, seq)
    row_bits = bit_list(ranks)
    norm_rows = norm_all.shape[2]

    def remote(source, target, sems, index, device):
        return pltpu.make_async_remote_copy(
            src_ref=source,
            dst_ref=target,
            send_sem=sems.at[0, index],
            recv_sem=sems.at[1, index],
            device_id=device,
            device_id_type=pl.DeviceIdType.MESH,
        )

    def plane(mask):
        return {"seq": jnp.bitwise_xor(me, mask)}

    def other(mask):
        return jnp.bitwise_xor(me, mask)

    barrier = pltpu.get_barrier_semaphore()
    for mask in masks:
        pl.semaphore_signal(
            barrier, inc=1, device_id=plane(mask), device_id_type=pl.DeviceIdType.MESH
        )
    for bit in row_bits:
        pl.semaphore_signal(
            barrier,
            inc=1,
            device_id={"rows": jnp.bitwise_xor(row, bit)},
            device_id_type=pl.DeviceIdType.MESH,
        )
    pl.semaphore_wait(barrier, seq - 1 + len(row_bits))

    locals_ = [
        pltpu.make_async_copy(out_ref.at[me], out_all.at[row, me], local_sems.at[0]),
        pltpu.make_async_copy(ffn_ref.at[me], ffn_all.at[me], local_sems.at[1]),
        pltpu.make_async_copy(small_ref, small_all.at[row], local_sems.at[2]),
    ]
    for copy in locals_:
        copy.start()

    def out_send(mask):
        return remote(
            out_ref.at[other(mask)], out_all.at[row, me], out_sems, mask, plane(mask)
        )

    def out_wait(mask):
        return remote(
            out_ref.at[other(mask)], out_all.at[row, other(mask)], out_sems, mask, plane(mask)
        )

    def ffn_send(mask):
        return remote(ffn_ref.at[other(mask)], ffn_all.at[me], ffn_sems, mask, plane(mask))

    def ffn_wait(mask):
        return remote(
            ffn_ref.at[other(mask)], ffn_all.at[other(mask)], ffn_sems, mask, plane(mask)
        )

    def norm_send(mask):
        return remote(
            small_all.at[:, 0:norm_rows], norm_all.at[me], norm_sems, mask, plane(mask)
        )

    def norm_wait(mask):
        return remote(
            small_all.at[:, 0:norm_rows], norm_all.at[other(mask)], norm_sems, mask, plane(mask)
        )

    def row_copy(array, sems, mask, bit, there):
        at = jnp.bitwise_xor(row, mask)
        place = jnp.bitwise_xor(at, bit) if there else at
        return remote(
            array.at[at],
            array.at[place],
            sems,
            mask | bit,
            {"rows": jnp.bitwise_xor(row, bit)},
        )

    def row_phase(array, sems, phase):
        bit = row_bits[phase]
        for mask in span(row_bits[:phase]):
            row_copy(array, sems, mask, bit, False).start()

    def row_done(array, sems, phase):
        bit = row_bits[phase]
        for mask in span(row_bits[:phase]):
            row_copy(array, sems, mask, bit, True).wait_recv()

    for mask in masks:
        out_send(mask).start()
    tasks = [
        make_task(micro, [gather], [], lambda micro: [], None)
        for gather in gathers
        for micro in range(source_ref.shape[0])
    ]
    locals_[2].wait()
    row_phase(small_all, small_row_sems, 0)
    for task in tasks:
        task.begin()
    for mask in masks:
        ffn_send(mask).start()
    locals_[0].wait()
    for mask in masks:
        out_wait(mask).wait_recv()
    row_phase(out_all, out_row_sems, 0)
    steps = [
        functools.partial(task.arrive[phase][0])
        for phase in range(len(tasks[0].arrive))
        for task in tasks
    ]
    for phase in range(len(row_bits)):
        row_done(small_all, small_row_sems, phase)
        if phase + 1 < len(row_bits):
            row_phase(small_all, small_row_sems, phase + 1)
    norm_all[me] = small_all[:, 0:norm_rows]
    for mask in masks:
        norm_send(mask).start()
    cuts = [len(steps) * part // len(row_bits) for part in range(len(row_bits) + 1)]
    for phase in range(len(row_bits)):
        for step in steps[cuts[phase] : cuts[phase + 1]]:
            step()
        row_done(out_all, out_row_sems, phase)
        if phase + 1 < len(row_bits):
            row_phase(out_all, out_row_sems, phase + 1)
    for mask in masks:
        norm_wait(mask).wait_recv()
        ffn_wait(mask).wait_recv()
    locals_[1].wait()
    for mask in masks:
        out_send(mask).wait_send()
        ffn_send(mask).wait_send()
        norm_send(mask).wait_send()
    for phase, bit in enumerate(row_bits):
        for mask in span(row_bits[:phase]):
            row_copy(out_all, out_row_sems, mask, bit, False).wait_send()
            row_copy(small_all, small_row_sems, mask, bit, False).wait_send()
    for task in tasks:
        task.drain()


def opening_stage(seq, ranks, name_id, norm_rows, args):
    source, out_pieces, ffn_pieces, small = args
    micros, rows, width = source.shape
    whole = jax.ShapeDtypeStruct((micros, seq * rows, width), low)
    outs = (
        whole,
        jax.ShapeDtypeStruct((ranks,) + out_pieces.shape, low),
        jax.ShapeDtypeStruct(ffn_pieces.shape, low),
        jax.ShapeDtypeStruct((ranks,) + small.shape, low),
        jax.ShapeDtypeStruct((seq, ranks, norm_rows, small.shape[1]), low),
    )
    scratch = gather_scratch(seq, micros) + [
        pltpu.SemaphoreType.DMA((2, seq)),
        pltpu.SemaphoreType.DMA((2, seq)),
        pltpu.SemaphoreType.DMA((2, seq)),
        pltpu.SemaphoreType.DMA((2, ranks)),
        pltpu.SemaphoreType.DMA((2, ranks)),
        pltpu.SemaphoreType.DMA((3,)),
    ]
    return stage_call(
        functools.partial(opening_kernel, seq, ranks), name_id, outs, scratch, args, 40
    )


class Attention:
    def __init__(self, q_ref, kv_ref, offsets, prefix_ref, ids, count, causal):
        self.q, self.kv, self.offsets, self.prefix = q_ref, kv_ref, offsets, prefix_ref
        self.key_ids, self.query_ids, self.key_places, self.query_places = ids
        self.count, self.causal = count, causal
        self.heads = prefix_ref.shape[2] // HEAD_DIM

    def load(self, micro, head, place):
        q_at, k_at, v_at = (at + head * HEAD_DIM for at in self.offsets)
        queries = self.q[micro, place, q_at : q_at + HEAD_DIM] * jnp.asarray(SCALING, low)
        keys = self.kv[micro, :, k_at : k_at + HEAD_DIM]
        values = self.kv[micro, :, v_at : v_at + HEAD_DIM]
        return queries, keys, values

    def scores(self, micro, keys, queries, lanes, place):
        scores = dot(keys, queries, 1, 1)
        allowed = self.key_ids[micro] == self.query_ids[micro, :, place]
        if self.causal:
            allowed = allowed & (self.key_places[...] <= self.query_places[:, place])
        scores = jnp.where(allowed, scores, MASKED)
        extra = dot(self.prefix[0, :, lanes], queries, 1, 1)
        rows = lax.broadcasted_iota(jnp.int32, extra.shape, 0)
        return scores, jnp.where(rows < self.count, extra, MASKED)

    def forward(self, micro, start, size, context_ref, logs_ref):
        place = pl.ds(start, size)
        for head in range(self.heads):
            lanes = slice(head * HEAD_DIM, (head + 1) * HEAD_DIM)
            queries, keys, values = self.load(micro, head, place)
            scores, extra = self.scores(micro, keys, queries, lanes, place)
            peak = jnp.maximum(
                jnp.max(scores, axis=0, keepdims=True), jnp.max(extra, axis=0, keepdims=True)
            )
            scores = jnp.exp(scores - peak)
            extra = jnp.exp(extra - peak)
            total = jnp.sum(scores, axis=0, keepdims=True) + jnp.sum(extra, axis=0, keepdims=True)
            context = dot(values, scores.astype(low), 0, 0)
            context = context + dot(self.prefix[1, :, lanes], extra.astype(low), 0, 0)
            context_ref[micro, place, lanes] = (context / total).T.astype(low)
            logs_ref[micro, head : head + 1, place] = peak + jnp.log(total)

    def backward(self, micro, start, size, up_ref, logs_ref, grad_ref, k_sum, v_sum, pre_ref):
        place = pl.ds(start, size)
        for head in range(self.heads):
            lanes = slice(head * HEAD_DIM, (head + 1) * HEAD_DIM)
            queries, keys, values = self.load(micro, head, place)
            scores, extra = self.scores(micro, keys, queries, lanes, place)
            logs = logs_ref[micro, head : head + 1, place]
            weights = jnp.exp(scores - logs)
            extra = jnp.exp(extra - logs)
            up = up_ref[:, lanes]
            dots = dot(values, up, 1, 1)
            extra_dots = dot(self.prefix[1, :, lanes], up, 1, 1)
            centre = jnp.sum(weights * dots, axis=0, keepdims=True) + jnp.sum(
                extra * extra_dots, axis=0, keepdims=True
            )
            slope = (weights * (dots - centre)).astype(low)
            extra_slope = (extra * (extra_dots - centre)).astype(low)
            query_grad = dot(keys, slope, 0, 0) + dot(self.prefix[0, :, lanes], extra_slope, 0, 0)
            grad_ref[micro, place, lanes] = (query_grad * SCALING).T.astype(low)
            k_sum[:, lanes] += dot(slope, queries, 1, 0)
            v_sum[:, lanes] += dot(weights.astype(low), up, 1, 0)
            pre_ref[0, :, lanes] += dot(extra_slope, queries, 1, 0)
            pre_ref[1, :, lanes] += dot(extra.astype(low), up, 1, 0)


def loop(first, count, size, body):
    def step(index, carry):
        body(pl.multiple_of(first + index * size, size), index)
        return carry

    lax.fori_loop(0, count, step, 0)


def project_steps(micro, rows_ref, weight_ref, out_ref):
    length = rows_ref.shape[1]
    size = min(CHUNK, length)

    def body(start, index):
        place = pl.ds(start, size)
        out_ref[micro, place] = dot(rows_ref[micro, place], weight_ref[...], 1, 1).astype(low)

    return [(lambda: loop(0, length // size, size, body), 1.3)]


def self_kernel(seq, count, io, *refs):
    kinds = 2
    scratch = refs[-kinds * 7 - 3 :]
    refs = refs[: -kinds * 7 - 3]
    target_all = refs[-1]
    places = refs[:2]
    links = Links(seq)
    links.enter()
    tasks = []
    for kind in range(kinds):
        own_ref, in_ref, out_ref, prefix_ref, kid_ref, qid_ref, pair_ref = refs[
            3 + 7 * kind : 10 + 7 * kind
        ]
        (qkv_ref, context_ref, logs_ref, sum_ref, norm_ref, low_ref) = refs[
            3 + 7 * kinds + 6 * kind : 9 + 7 * kinds + 6 * kind
        ]
        all_ref = target_all if kind else refs[2]
        gathers = [Gather(links, own_ref, all_ref, *scratch[-3:])] if kind else []
        micros, rows, _ = own_ref.shape
        length = all_ref.shape[1]
        head_width = prefix_ref.shape[2]
        piece = scratch[7 * kind : 7 * kind + 7]
        scatter = Scatter(links, rows, *piece[:5], piece[5:])
        ids = (kid_ref, qid_ref) + tuple(places)
        attention = Attention(
            qkv_ref, qkv_ref, (0, head_width, 2 * head_width), prefix_ref, ids, count, kind == 1
        )

        def compute(
            micro, attention=attention, context_ref=context_ref, logs_ref=logs_ref,
            out_ref=out_ref, all_ref=all_ref, in_ref=in_ref, qkv_ref=qkv_ref, scatter=scatter,
        ):
            def chunk(start, size):
                attention.forward(micro, start, size, context_ref, logs_ref)
                return dot(context_ref[micro, pl.ds(start, size)], out_ref[...], 1, 1)

            return project_steps(micro, all_ref, in_ref, qkv_ref) + half_steps(
                scatter, micro, length, chunk, 4.2
            )

        def finish(
            micro, own_ref=own_ref, scatter=scatter, sum_ref=sum_ref, norm_ref=norm_ref,
            low_ref=low_ref, pair_ref=pair_ref,
        ):
            total = own_ref[micro].astype(wide) + scatter.total(micro)
            sum_ref[micro] = total
            value = layer_norm(total, (pair_ref[0:1], pair_ref[1:2]))
            norm_ref[micro] = value
            low_ref[micro] = value.astype(low)

        for micro in range(micros):
            load = kind if micro == 0 else None
            tasks.append(
                make_task(micro, gathers, [scatter], compute, finish, None, load, (kind, micro))
            )
    run_tasks(tasks, io, ahead=len(tasks))


def self_stage(seq, name_id, count, places, source_all, sides):
    micros, rows, width = sides[0][0].shape
    length = rows * seq
    head_width = sides[0][3].shape[2]
    heads = head_width // HEAD_DIM
    side_outs = (
        jax.ShapeDtypeStruct((micros, length, 3 * head_width), low),
        jax.ShapeDtypeStruct((micros, length, head_width), low),
        jax.ShapeDtypeStruct((micros, heads, length), wide),
        jax.ShapeDtypeStruct((micros, rows, width), wide),
        jax.ShapeDtypeStruct((micros, rows, width), wide),
        jax.ShapeDtypeStruct((micros, rows, width), low),
    )
    scratch = scatter_scratch(seq, micros, rows, width) * 2 + gather_scratch(seq, micros)
    args = tuple(places) + (source_all,) + sides[0] + sides[1]
    gathered = jax.ShapeDtypeStruct((micros, length, width), low)
    outs = stage_call(
        functools.partial(self_kernel, seq, count), name_id, side_outs * 2 + (gathered,), scratch,
        args, 75,
        {11: 1, 12: 1, 14: 1}, {0: 0, 1: 0, 6: 1, 7: 1, 12: 1},
    )
    return outs[:6], outs[6:12], outs[12]


def cross_kernel(
    seq, count, io, kpos_ref, qpos_ref, first_ref, first_low_ref, memory_ref, q_in_ref, kv_in_ref,
    out_ref, prefix_ref, kid_ref, qid_ref, pair_ref, first_all, memory_all, q_ref, kv_ref,
    context_ref, logs_ref, sum_ref, norm_ref, low_ref, *scratch,
):
    links = Links(seq)
    micros, rows, _ = first_ref.shape
    length = first_all.shape[1]
    head_width = prefix_ref.shape[2]
    gathers = [
        Gather(links, memory_ref, memory_all, *scratch[:3]),
        Gather(links, first_low_ref, first_all, *scratch[3:6]),
    ]
    scatter = Scatter(links, rows, *scratch[6:11], scratch[11:])
    ids = (kid_ref, qid_ref, kpos_ref, qpos_ref)
    attention = Attention(q_ref, kv_ref, (0, 0, head_width), prefix_ref, ids, count, False)
    links.enter()

    def compute(micro):
        def chunk(start, size):
            attention.forward(micro, start, size, context_ref, logs_ref)
            return dot(context_ref[micro, pl.ds(start, size)], out_ref[...], 1, 1)

        return (
            project_steps(micro, memory_all, kv_in_ref, kv_ref)
            + project_steps(micro, first_all, q_in_ref, q_ref)
            + half_steps(scatter, micro, length, chunk, 4.2)
        )

    def finish(micro):
        total = first_ref[micro] + scatter.total(micro)
        sum_ref[micro] = total
        value = layer_norm(total, (pair_ref[0:1], pair_ref[1:2]))
        norm_ref[micro] = value
        low_ref[micro] = value.astype(low)

    tasks = [
        make_task(
            micro, gathers, [scatter], compute, finish, None, 0 if micro == 0 else None, (0, micro)
        )
        for micro in range(micros)
    ]
    run_tasks(tasks, io)


def cross_stage(seq, name_id, count, places, args):
    micros, rows, width = args[0].shape
    length = rows * seq
    head_width = args[6].shape[2]
    heads = head_width // HEAD_DIM
    whole = jax.ShapeDtypeStruct((micros, length, width), low)
    outs = (
        whole,
        whole,
        jax.ShapeDtypeStruct((micros, length, head_width), low),
        jax.ShapeDtypeStruct((micros, length, 2 * head_width), low),
        jax.ShapeDtypeStruct((micros, length, head_width), low),
        jax.ShapeDtypeStruct((micros, heads, length), wide),
        jax.ShapeDtypeStruct((micros, rows, width), wide),
        jax.ShapeDtypeStruct((micros, rows, width), wide),
        jax.ShapeDtypeStruct((micros, rows, width), low),
    )
    scratch = gather_scratch(seq, micros) * 2 + scatter_scratch(seq, micros, rows, width)
    return stage_call(
        functools.partial(cross_kernel, seq, count), name_id, outs, scratch,
        tuple(places) + args, 85, {place: 0 for place in (2, 5, 6, 7, 8, 9, 10)},
        {place: 0 for place in range(5)},
    )


def attend_back_steps(
    attention, micro, length, up_all, out_ref, logs_ref, grad_ref, k_sum, v_sum, pre_ref, up_ref,
    emit=None,
):
    head_width = up_ref.shape[1]
    half = length // 2
    size = min(CHUNK, half)

    def run(first, zero):
        if zero:
            k_sum[...] = jnp.zeros_like(k_sum)
            v_sum[...] = jnp.zeros_like(v_sum)
            if micro == 0:
                pre_ref[...] = jnp.zeros_like(pre_ref)

        def body(start, index):
            place = pl.ds(start, size)
            up_ref[...] = dot(up_all[micro, place], out_ref[...], 1, 0).astype(low)
            attention.backward(
                micro, start, size, up_ref, logs_ref, grad_ref, k_sum, v_sum, pre_ref
            )
            if emit is not None:
                emit(start, index, size)

        loop(first, half // size, size, body)

    def keys():
        grad_ref[micro, :, head_width : 2 * head_width] = k_sum[...].astype(low)
        grad_ref[micro, :, 2 * head_width : 3 * head_width] = v_sum[...].astype(low)

    return [(lambda: run(half, True), 5.0), (lambda: run(0, False), 5.0), (keys, 0.5)]


def term_steps(context_ref, up_all, grad_ref, sources, terms_ref, seq, send=None):
    micros = grad_ref.shape[0]
    ranks, _, cols, width = terms_ref.shape
    head_width = context_ref.shape[2]

    def tile(part):
        if part == 3:
            value = token_sum(context_ref, slice(0, head_width), up_all, micros).T
            value = value.reshape(seq, ranks, cols, head_width)
            for owner in range(seq):
                lanes = slice(owner * head_width, (owner + 1) * head_width)
                terms_ref[:, 3, :, lanes] = value[owner].astype(low)
        else:
            lanes = slice(part * head_width, (part + 1) * head_width)
            value = token_sum(grad_ref, lanes, sources[part], micros)
            terms_ref[:, part] = value.reshape(ranks, cols, width).astype(low)
        if send is not None:
            send(part)

    return [(functools.partial(tile, part), 1.2) for part in (3, 0, 1, 2)]


def term_shape(seq, ranks, width):
    return jax.ShapeDtypeStruct((ranks, 4, width // (seq * ranks), width), low)


class RankSum:
    def __init__(self, ranks, terms_ref, recv_ref, total_ref, sems):
        self.ranks, self.terms, self.recv = ranks, terms_ref, recv_ref
        self.total, self.sems, self.row = total_ref, sems, lax.axis_index("rows")

    def greet(self, barrier):
        for mask in range(1, self.ranks):
            pl.semaphore_signal(
                barrier,
                inc=1,
                device_id={"rows": jnp.bitwise_xor(self.row, mask)},
                device_id_type=pl.DeviceIdType.MESH,
            )
        return self.ranks - 1

    def copy(self, part, mask):
        owner = jnp.bitwise_xor(self.row, mask)
        return pltpu.make_async_remote_copy(
            src_ref=self.terms.at[owner, part],
            dst_ref=self.recv.at[mask, part],
            send_sem=self.sems.at[0, mask, part],
            recv_sem=self.sems.at[1, mask, part],
            device_id={"rows": owner},
            device_id_type=pl.DeviceIdType.MESH,
        )

    def send(self, part):
        for mask in range(1, self.ranks):
            self.copy(part, mask).start()

    def finish(self):
        for part in (3, 0, 1, 2):
            value = self.terms[self.row, part].astype(wide)
            for mask in range(1, self.ranks):
                self.copy(part, mask).wait_recv()
                value = value + self.recv[mask, part].astype(wide)
            self.total[part] = value
        for part in range(4):
            for mask in range(1, self.ranks):
                self.copy(part, mask).wait_send()


class SmallSum:
    def __init__(self, hops, held_ref, recv_ref, sems):
        self.hops, self.held, self.recv, self.sems = hops, held_ref, recv_ref, sems

    def copy(self, hop):
        name, bit = self.hops[hop]
        return pltpu.make_async_remote_copy(
            src_ref=self.held.at[hop],
            dst_ref=self.recv.at[hop],
            send_sem=self.sems.at[0, hop],
            recv_sem=self.sems.at[1, hop],
            device_id={name: jnp.bitwise_xor(lax.axis_index(name), bit)},
            device_id_type=pl.DeviceIdType.MESH,
        )

    def step(self, hop):
        self.copy(hop).wait_recv()
        self.held[hop + 1] = self.held[hop] + self.recv[hop]
        if hop + 1 < len(self.hops):
            self.copy(hop + 1).start()

    def start(self, gap):
        self.copy(0).start()
        return [(functools.partial(self.step, hop), gap) for hop in range(len(self.hops))]

    def total(self):
        return self.held[len(self.hops)]

    def drain(self):
        for hop in range(len(self.hops)):
            self.copy(hop).wait_send()


def small_scratch(hops, shape):
    return [
        pltpu.VMEM((hops + 1,) + shape, wide),
        pltpu.VMEM((hops,) + shape, wide),
        pltpu.SemaphoreType.DMA((2, hops)),
    ]


def cross_back_kernel(
    seq, count, io, kpos_ref, qpos_ref, up_ref, resid_ref, pair_ref, q_ref, kv_ref, logs_ref,
    q_in_ref, kv_in_ref, out_ref, prefix_ref, kid_ref, qid_ref, first_all, memory_all, context_ref,
    pre_ref, first_out, memory_out, pair_grad_ref, terms_ref, up_all, grad_ref, own_ref, kept_ref, k_sum, v_sum, up_chunk, *scratch,
):
    links = Links(seq)
    micros, rows, _ = own_ref.shape
    length = up_all.shape[1]
    head_width = prefix_ref.shape[2]
    gather = Gather(links, own_ref, up_all, *scratch[:3])
    first_sum = Scatter(links, rows, *scratch[3:8], scratch[8:10])
    memory_sum = Scatter(links, rows, *scratch[10:15], scratch[15:17])
    ids = (kid_ref, qid_ref, kpos_ref, qpos_ref)
    attention = Attention(q_ref, kv_ref, (0, 0, head_width), prefix_ref, ids, count, False)
    links.enter()

    def before(micro):
        prologue(micro, up_ref, resid_ref, pair_ref, own_ref, kept_ref, pair_grad_ref)

    def compute(micro):
        def first_chunk(start, size):
            return dot(
                grad_ref[micro, pl.ds(start, size), 0:head_width], q_in_ref[...], 1, 0
            )

        def memory_chunk(start, size):
            return dot(
                grad_ref[micro, pl.ds(start, size), head_width : 3 * head_width],
                kv_in_ref[...],
                1,
                0,
            )

        attend = attend_back_steps(
            attention, micro, length, up_all, out_ref, logs_ref, grad_ref, k_sum, v_sum, pre_ref,
            up_chunk,
        )
        sums = half_steps(first_sum, micro, length, first_chunk, 0.6)
        return (
            [attend[0], sums[0], attend[1], sums[1], attend[2]]
            + half_steps(memory_sum, micro, length, memory_chunk, 0.8)
        )

    def finish(micro):
        first_out[micro] = kept_ref[micro] + first_sum.total(micro)
        memory_out[micro] = memory_sum.total(micro)

    tasks = [
        make_task(
            micro, [gather], [first_sum, memory_sum], compute, finish, before,
            0 if micro == 0 else None,
        )
        for micro in range(micros)
    ]
    fill = term_steps(
        context_ref, up_all, grad_ref, (first_all, memory_all, memory_all), terms_ref, seq
    )
    run_tasks(tasks, io, fill, 1)


def cross_back_stage(seq, ranks, name_id, count, places, args):
    micros, rows, width = args[0].shape
    length = rows * seq
    head_width = args[9].shape[2]
    own = jax.ShapeDtypeStruct((micros, rows, width), wide)
    outs = (
        jax.ShapeDtypeStruct((2, PAD_PREFIX, head_width), wide),
        own,
        own,
        jax.ShapeDtypeStruct((2, width), wide),
        term_shape(seq, ranks, width),
    )
    scratch = (
        [
            pltpu.VMEM((micros, length, width), low),
            pltpu.VMEM((micros, length, 3 * head_width), low),
        ]
        + back_scratch(micros, rows, width)
        + sum_scratch(length, head_width)
        + gather_scratch(seq, micros)
        + scatter_scratch(seq, micros, rows, width) * 2
    )
    lazy = {place: 0 for place in range(5, 14)}
    lazy.update({14: 1, 15: 1, 16: 1})
    return stage_call(
        functools.partial(cross_back_kernel, seq, count), name_id, outs, scratch,
        tuple(places) + args, 85, lazy,
    )


def back_scratch(micros, rows, width):
    return [pltpu.VMEM((micros, rows, width), low), pltpu.VMEM((micros, rows, width), wide)]


def sum_scratch(length, head_width):
    return [
        pltpu.VMEM((length, head_width), wide),
        pltpu.VMEM((length, head_width), wide),
        pltpu.VMEM((min(CHUNK, length // 2), head_width), low),
    ]


def self_back_kernel(
    seq, count, causal, reduce, io, kpos_ref, qpos_ref, up_ref, resid_ref, pair_ref, qkv_ref,
    logs_ref, in_ref, out_ref, prefix_ref, kid_ref, qid_ref, context_ref, rows_ref, *rest,
):
    if reduce:
        norm_in_ref, pre_in_ref, norm_out_ref, pre_out_ref, *rest = rest
    else:
        pre_ref, pair_grad_ref, *rest = rest
    grad_out, result_ref, up_all, grad_ref, own_ref, kept_ref, k_sum, v_sum, up_chunk, *scratch = rest
    links = Links(seq)
    micros, rows, _ = own_ref.shape
    length = up_all.shape[1]
    head_width = prefix_ref.shape[2]
    gather = Gather(links, own_ref, up_all, *scratch[:3])
    scatter = Scatter(links, rows, *scratch[3:8], scratch[8:10])
    terms_ref, rank_sum = result_ref, None
    if reduce:
        terms_ref, recv_ref, rank_sems, pre_ref, pair_grad_ref = scratch[10:15]
        row_hops = [("rows", bit) for bit in bit_list(terms_ref.shape[0])]
        norm_sum = SmallSum(
            [("seq", bit) for bit in bit_list(seq)] + row_hops, *scratch[15:18]
        )
        pre_sum = SmallSum(row_hops, *scratch[18:21])
        rank_sum = RankSum(terms_ref.shape[0], terms_ref, recv_ref, result_ref, rank_sems)
    ids = (kid_ref, qid_ref, kpos_ref, qpos_ref)
    attention = Attention(
        qkv_ref, qkv_ref, (0, head_width, 2 * head_width), prefix_ref, ids, count, causal
    )
    links.enter([rank_sum] if reduce else [])

    def before(micro):
        prologue(micro, up_ref, resid_ref, pair_ref, own_ref, kept_ref, pair_grad_ref)

    def compute(micro):
        def chunk(start, size):
            return dot(grad_ref[micro, pl.ds(start, size)], in_ref[...], 1, 0)

        return attend_back_steps(
            attention, micro, length, up_all, out_ref, logs_ref, grad_ref, k_sum, v_sum,
            pre_ref, up_chunk,
        ) + half_steps(scatter, micro, length, chunk, 0.9)

    def finish(micro):
        grad_out[micro] = kept_ref[micro] + scatter.total(micro)

    tasks = [
        make_task(
            micro, [gather], [scatter], compute, finish, before, 0 if micro == 0 else None
        )
        for micro in range(micros)
    ]
    fill = term_steps(
        context_ref, up_all, grad_ref, (rows_ref,) * 3, terms_ref, seq,
        rank_sum.send if reduce else None,
    )
    def opening():
        norm_sum.held[0] = norm_in_ref[...]
        norm_sum.held[0, 0:2] = pair_grad_ref[...]
        return norm_sum.start(9.0)

    def closing():
        pre_sum.held[0, 0:2] = pre_ref[...]
        pre_sum.held[0, 2:6] = pre_in_ref[...]
        return pre_sum.start(15.0)

    if reduce:
        tasks[-1].compute = [(lambda: io.load(1), 0.1), fill[0]] + tasks[-1].compute
        run_tasks(tasks, io, fill[1:], None, opening, closing)
        rank_sum.finish()
        norm_out_ref[...] = norm_sum.total()
        pre_out_ref[...] = pre_sum.total()
        norm_sum.drain()
        pre_sum.drain()
    else:
        run_tasks(tasks, io, fill, 1)


def self_back_stage(seq, ranks, name_id, count, places, causal, reduce, side):
    micros, rows, width = side[0].shape
    length = rows * seq
    head_width = side[7].shape[2]
    terms = term_shape(seq, ranks, width)
    pre = jax.ShapeDtypeStruct((2, PAD_PREFIX, head_width), wide)
    outs = (pre, jax.ShapeDtypeStruct((2, width), wide))
    total = terms
    if reduce:
        outs = tuple(
            jax.ShapeDtypeStruct(shape, wide)
            for shape in (side[12].shape, (6, PAD_PREFIX, head_width))
        )
        total = jax.ShapeDtypeStruct(terms.shape[1:], wide)
    outs += (jax.ShapeDtypeStruct((micros, rows, width), wide), total)
    scratch = (
        [
            pltpu.VMEM((micros, length, width), low),
            pltpu.VMEM((micros, length, 3 * head_width), low),
        ]
        + back_scratch(micros, rows, width)
        + sum_scratch(length, head_width)
        + gather_scratch(seq, micros)
        + scatter_scratch(seq, micros, rows, width)
    )
    if reduce:
        scratch += [
            pltpu.VMEM(terms.shape, low),
            pltpu.VMEM(terms.shape, low),
            pltpu.SemaphoreType.DMA((2, ranks, 4)),
            pltpu.VMEM(pre.shape, wide),
            pltpu.VMEM((2, width), wide),
        ]
        row_hops, hops = len(bit_list(ranks)), len(bit_list(ranks)) + len(bit_list(seq))
        scratch += small_scratch(hops, side[12].shape)
        scratch += small_scratch(row_hops, (6, PAD_PREFIX, head_width))
    lazy = {place: 0 for place in range(5, 12)}
    lazy.update({12: 1, 13: 1})
    return stage_call(
        functools.partial(self_back_kernel, seq, count, causal, reduce), name_id, outs, scratch,
        tuple(places) + side, 75, lazy,
    )


def local(
    seq, ranks,
    source, target, source_segments, target_segments, cotangent,
    encoder_qkv, encoder_output, encoder_prefix, encoder_expand, encoder_contract, encoder_down,
    encoder_up, encoder_norms, decoder_qkv, decoder_output, decoder_prefix, cross_query, cross_kv,
    cross_output, cross_prefix, decoder_expand, decoder_contract, decoder_down, decoder_up,
    decoder_norms,
):
    micro_count, batch_rows, block, width = source.shape
    length = source_segments.shape[2]
    me = lax.axis_index("seq")
    stacked = micro_count * batch_rows
    head_width = width // seq
    slice_cols = encoder_output.shape[1]
    count = encoder_prefix.shape[1]
    hidden = encoder_contract.shape[0] // seq
    adapt = encoder_up.shape[0] // seq
    both = hidden + adapt
    padded = (both + LANES - 1) // LANES * LANES

    sources = source.reshape(stacked, block, width)
    targets = target.reshape(stacked, block, width)

    order = relative(jnp.arange(length, dtype=jnp.int32), seq, me)
    places = (order[:, None], order[None, :])

    def relative_ids(ids):
        rows = [relative(row, seq, me) for row in ids.reshape(stacked, length)]
        value = jnp.stack(rows)
        return value[:, :, None], value[:, None, :]

    source_keys, source_queries = relative_ids(source_segments)
    target_keys, target_queries = relative_ids(target_segments)

    def columns(weight):
        return jnp.swapaxes(weight, -1, -2)

    def gather_rows(value):
        return lax.all_gather(value, "rows", axis=0, tiled=False)

    def stack_columns(pieces):
        gathered = gather_rows(jnp.concatenate(pieces, axis=0))
        outs = []
        start = 0
        for piece in pieces:
            size = piece.shape[0]
            outs.append(gathered[:, start : start + size])
            start += size
        return outs

    def flat_columns(gathered, parts):
        value = gathered.reshape(ranks, parts, slice_cols, width)
        return jnp.swapaxes(value, 0, 1).reshape(parts * ranks * slice_cols, width)

    def split_rows(weight):
        return columns(weight).reshape(slice_cols, seq, -1)

    def ffn_rows(contract, up):
        pieces = [split_rows(contract), split_rows(up) * jnp.asarray(ADAPTER_SCALE, low)]
        if padded > both:
            pieces.append(jnp.zeros((slice_cols, seq, padded - both), low))
        return pieces

    def by_target(pieces):
        return jnp.swapaxes(jnp.concatenate(pieces, axis=2), 0, 1)

    out_pieces = by_target([split_rows(encoder_output), split_rows(decoder_output)])
    ffn_pieces = by_target(
        [split_rows(cross_output)]
        + ffn_rows(encoder_contract, encoder_up)
        + ffn_rows(decoder_contract, decoder_up)
    )
    qkv_parts = gather_rows(
        jnp.concatenate(
            [
                columns(encoder_qkv).reshape(-1, width),
                columns(decoder_qkv).reshape(-1, width),
            ]
        )
    )
    norm_count = encoder_norms.shape[0]
    norms = jnp.concatenate([encoder_norms, decoder_norms]).reshape(-1, slice_cols)
    prefixes = jnp.concatenate([encoder_prefix, decoder_prefix, cross_prefix])
    prefixes = prefixes.reshape(-1, slice_cols)
    norm_rows = (norms.shape[0] + 15) // 16 * 16
    small = jnp.concatenate(
        [jnp.pad(norms, ((0, norm_rows - norms.shape[0]), (0, 0))), prefixes]
    )
    small = jnp.pad(small, ((0, -small.shape[0] % 16), (0, 0)))
    source_all, front, row_pieces, small_all, norm_all = opening_stage(
        seq, ranks, 1, norm_rows, (sources, out_pieces, ffn_pieces, small)
    )
    scales = norm_all[:, :, : norms.shape[0]].reshape(seq * ranks, -1, slice_cols)
    scales = jnp.moveaxis(scales, 0, 1).reshape(-1, 2, width).astype(wide)
    prefixes = small_all[:, norm_rows : norm_rows + 6 * count]
    prefixes = jnp.moveaxis(prefixes.reshape(ranks, 6, count, slice_cols), 0, 2)
    prefixes = prefixes.reshape(6, count, head_width)
    prefixes = jnp.pad(prefixes, ((0, 0), (0, PAD_PREFIX - count), (0, 0)))
    encoder_pre, decoder_pre, cross_pre = prefixes[0:2], prefixes[2:4], prefixes[4:6]

    late = [
        jnp.concatenate(
            [
                columns(encoder_expand),
                columns(encoder_down),
                columns(cross_query),
                columns(cross_kv).reshape(-1, width),
            ]
        ),
        row_pieces[:, :, : head_width + padded],
        jnp.concatenate([columns(decoder_expand), columns(decoder_down)]),
        row_pieces[:, :, head_width + padded :],
    ]
    source_all, late = lax.optimization_barrier((source_all, late))
    encoder_in = flat_columns(qkv_parts[:, : 3 * slice_cols], 3)
    decoder_in = flat_columns(qkv_parts[:, 3 * slice_cols :], 3)
    front_rows = jnp.swapaxes(front, 0, 1).reshape(width, -1)
    encoder_out = front_rows[:, :head_width]
    decoder_out = front_rows[:, head_width:]
    cut = encoder_expand.shape[1]

    def ffn_in(gathered):
        pieces = [gathered[:, :cut].reshape(-1, width), gathered[:, cut:].reshape(-1, width)]
        if padded > both:
            pieces.append(jnp.zeros((padded - both, width), low))
        return jnp.concatenate(pieces)

    def row_order(gathered):
        return jnp.swapaxes(gathered, 0, 1).reshape(width, -1)

    second_parts = gather_rows(late[0])
    rest = gather_rows(late[1])
    encoder_side, decoder_side, target_all = self_stage(
        seq, 2, count, places, source_all,
        (
            (
                sources, encoder_in, encoder_out, encoder_pre, source_keys, source_queries,
                scales[0],
            ),
            (
                targets, decoder_in, decoder_out, decoder_pre, target_keys, target_queries,
                scales[norm_count],
            ),
        ),
    )
    encoder_qkvs, encoder_ctx, encoder_logs, resid_one, middle, middle_low = encoder_side
    middle_low, second_parts, rest, last = lax.optimization_barrier(
        (middle_low, second_parts, rest, late[2:])
    )
    rest = row_order(rest)
    cross_out, encoder_two = rest[:, :head_width], rest[:, head_width:]
    ffn_cut = cut + encoder_down.shape[1]
    encoder_one = ffn_in(second_parts[:, :ffn_cut])
    cross_in = flat_columns(second_parts[:, ffn_cut:], 3)
    cross_q_in, cross_kv_in = cross_in[:head_width], cross_in[head_width:]
    decoder_qkvs, decoder_ctx, decoder_logs, resid_three, first, first_low = decoder_side
    middle_all, encoder_before, encoder_hidden, resid_two, _, memory_low = ffn_stage(
        seq, 3, middle_low, middle, encoder_one, encoder_two, scales[1]
    )
    memory_low, last = lax.optimization_barrier(
        (memory_low, [gather_rows(piece) for piece in last])
    )
    decoder_one, decoder_two = ffn_in(last[0]), row_order(last[1])
    (
        first_all, memory_all, cross_q, cross_kvs, cross_ctx, cross_logs, resid_four, second,
        second_low,
    ) = cross_stage(
        seq, 4, count, places,
        (
            first, first_low, memory_low, cross_q_in, cross_kv_in, cross_out, cross_pre,
            source_keys, target_queries, scales[norm_count + 1],
        ),
    )
    second_all, decoder_before, decoder_hidden, resid_five, _, result = ffn_stage(
        seq, 5, second_low, second, decoder_one, decoder_two, scales[norm_count + 2]
    )

    def scatter_ranks(value):
        return lax.psum_scatter(value, "rows", scatter_dimension=0, tiled=False)

    norm_grads = {}

    def ffn_back(name_id, index, up, resid, before, hidden_low, rows_all, one, two):
        out, pair, expand, down, two_terms = ffn_back_stage(
            seq, ranks, hidden, adapt, name_id, up, resid, scales[index], before, one, two,
            rows_all, hidden_low,
        )
        keep_pair(index, pair)
        return out, [two_terms, jnp.concatenate([expand, down], axis=1)]

    def hold(value, terms, sums):
        value, terms, sums = lax.optimization_barrier((value, terms, sums))
        return value, [scatter_ranks(term) for term in terms], sums

    def keep_pair(index, pair):
        norm_grads[index] = pair

    second_up, terms = ffn_back(
        6, norm_count + 2, cotangent.reshape(stacked, block, width), resid_five, decoder_before,
        decoder_hidden, second_all, decoder_one, decoder_two,
    )
    second_up, ffn_sums, _ = hold(second_up, terms, [])

    cross_pre_grad, first_up, memory_up, pair, terms = cross_back_stage(
        seq, ranks, 7, count, places,
        (
            second_up, resid_four, scales[norm_count + 1], cross_q, cross_kvs, cross_logs,
            cross_q_in, cross_kv_in, cross_out, cross_pre, source_keys, target_queries,
            first_all, memory_all, cross_ctx,
        ),
    )
    keep_pair(norm_count + 1, pair)
    first_up, cross_sums, ffn_sums = hold(first_up, [terms], ffn_sums)
    decoder_two_grad, decoder_one_grad = ffn_sums

    def self_back(name_id, index, causal, reduce, side, sums):
        held = self_back_stage(seq, ranks, name_id, count, places, causal, reduce, side)
        held, sums = lax.optimization_barrier((tuple(held), sums))
        return held + (sums,)

    def owner_parts(value):
        out_part = value[3].reshape(slice_cols, seq, head_width)
        return jnp.swapaxes(out_part, 0, 1), value[:3]

    decoder_pre_grad, pair, target_grad, self_terms, cross_sums = self_back(
        9, norm_count, True, False,
        (
            first_up, resid_three, scales[norm_count], decoder_qkvs, decoder_logs, decoder_in,
            decoder_out, decoder_pre, target_keys, target_queries, decoder_ctx, target_all,
        ),
        cross_sums,
    )
    keep_pair(norm_count, pair)
    memory_up, self_sums, _ = hold(memory_up, [self_terms], [])
    cross_out_grad, cross_in_grad = owner_parts(cross_sums[0])

    middle_up, terms = ffn_back(
        8, 1, memory_up, resid_two, encoder_before, encoder_hidden, middle_all,
        encoder_one, encoder_two,
    )
    middle_up, ffn_sums, self_sums = hold(middle_up, terms, self_sums)
    decoder_out_grad, decoder_in_grad = owner_parts(self_sums[0])

    def give_back(pieces):
        value = jnp.concatenate(pieces, axis=2) if len(pieces) > 1 else pieces[0]
        return lax.all_to_all(value, "seq", 0, 1, tiled=False)

    decoder_rows = give_back([decoder_two_grad, cross_out_grad, decoder_out_grad])

    pairs = [jnp.zeros((2, width), wide)] + [norm_grads[index] for index in sorted(norm_grads)]
    norm_in = jnp.concatenate(pairs)
    norm_in = jnp.pad(norm_in, ((0, -norm_in.shape[0] % 16), (0, 0)))
    norm_total, prefix_total, source_grad, self_terms, ffn_sums = self_back(
        10, 0, False, True,
        (
            middle_up, resid_one, scales[0], encoder_qkvs, encoder_logs, encoder_in,
            encoder_out, encoder_pre, source_keys, source_queries, encoder_ctx, source_all,
            norm_in, jnp.concatenate([decoder_pre_grad, cross_pre_grad]),
        ),
        ffn_sums,
    )
    encoder_two_grad, encoder_one_grad = ffn_sums
    encoder_out_grad, encoder_in_grad = owner_parts(self_terms)
    encoder_rows = give_back([encoder_two_grad, encoder_out_grad.astype(low)])

    def row_grad(value, start, size, scale=None):
        piece = value[:, :, start : start + size].astype(wide)
        if scale is not None:
            piece = piece * scale
        return piece.reshape(slice_cols, -1).T

    def column_grad(value):
        return jnp.swapaxes(value.astype(wide), -1, -2)

    row = lax.axis_index("rows")
    prefix_total = lax.dynamic_slice_in_dim(
        prefix_total[:, :count], row * slice_cols, slice_cols, 2
    )
    norm_total = lax.dynamic_slice_in_dim(
        norm_total[: 2 * len(pairs)], (me * ranks + row) * slice_cols, slice_cols, 1
    )
    norm_total = norm_total.reshape(-1, 2, slice_cols)

    shape_out = source.shape
    return (
        result.reshape(shape_out),
        source_grad.reshape(shape_out),
        target_grad.reshape(shape_out),
        column_grad(encoder_in_grad),
        row_grad(encoder_rows, padded, head_width),
        prefix_total[0:2],
        column_grad(encoder_one_grad[:cut]),
        row_grad(encoder_rows, 0, hidden),
        column_grad(encoder_one_grad[cut:]),
        row_grad(encoder_rows, hidden, adapt, ADAPTER_SCALE),
        norm_total[:norm_count],
        column_grad(decoder_in_grad),
        row_grad(decoder_rows, padded + head_width, head_width),
        prefix_total[2:4],
        column_grad(cross_in_grad[0]),
        column_grad(cross_in_grad[1:]),
        row_grad(decoder_rows, padded, head_width),
        prefix_total[4:6],
        column_grad(decoder_one_grad[:cut]),
        row_grad(decoder_rows, 0, hidden),
        column_grad(decoder_one_grad[cut:]),
        row_grad(decoder_rows, hidden, adapt, ADAPTER_SCALE),
        norm_total[norm_count:],
    )


def solution(mesh):
    rows = P(None, "rows", "seq", None)
    ids = P(None, "rows", None)
    flat = P(None, ("seq", "rows"))
    deep = P(None, None, ("seq", "rows"))
    weights = (
        deep, flat, deep, flat, flat, flat, flat, deep, deep, flat, deep, flat, deep, flat, deep,
        flat, flat, flat, flat, deep,
    )
    body = functools.partial(local, mesh.shape["seq"], mesh.shape["rows"])
    return jax.shard_map(
        body,
        mesh=mesh,
        in_specs=(rows, rows, ids, ids, rows) + weights,
        out_specs=(rows, rows, rows) + weights,
        check_vma=False,
    )
```

```python
import functools

import jax
import jax.numpy as jnp
from jax import lax
from jax.experimental import pallas as pl
from jax.experimental.layout import Layout, with_layout_constraint
from jax.experimental.pallas import tpu as pltpu
from jax.sharding import PartitionSpec as P

HEADS = 16
HEAD_DIM = 64
EPSILON = 1e-05
MASKED = -1e30
ADAPTER_SCALE = 4.0
SCALING = HEAD_DIM ** (-0.5)
PAD_PREFIX = 32
CHUNK = 256
LANES = 128
VMEM_LIMIT = 60 * 1024 * 1024
HALF_ROOT = 0.7071067811865476
DENSITY = 0.3989422804014327

low = jnp.bfloat16
wide = jnp.float32


def dot(left, right, left_axis, right_axis):
    return lax.dot_general(
        left, right, (((left_axis,), (right_axis,)), ((), ())), preferred_element_type=wide
    )


def bit_list(count):
    bits = []
    value = 1
    while value < count:
        bits.append(value)
        value *= 2
    return bits


def swap_pairs(count, bit):
    return [(index, index ^ bit) for index in range(count)]


def relative(places, seq, me):
    depth = len(bit_list(seq))
    value = places.reshape((2,) * depth + (-1,))
    for axis in range(depth):
        bit = 1 << (depth - 1 - axis)
        value = jnp.where((me & bit) != 0, jnp.flip(value, axis), value)
    return jnp.moveaxis(value, depth - 1, 0).reshape(-1)


def normalized(tensor):
    average = jnp.mean(tensor, axis=-1, keepdims=True)
    centered = tensor - average
    spread = jnp.mean(centered * centered, axis=-1, keepdims=True)
    inverse = lax.rsqrt(spread + EPSILON)
    return centered * inverse, inverse


def layer_norm(tensor, scales):
    return normalized(tensor)[0] * scales[0] + scales[1]


def norm_back(upstream, tensor, scales):
    unit, inverse = normalized(tensor)
    slope = upstream * scales[0]
    grad = inverse * (
        slope
        - jnp.mean(slope, axis=-1, keepdims=True)
        - unit * jnp.mean(slope * unit, axis=-1, keepdims=True)
    )
    return (
        grad,
        jnp.sum(upstream * unit, axis=0, keepdims=True),
        jnp.sum(upstream, axis=0, keepdims=True),
    )


def gelu_exact(tensor):
    return tensor * (0.5 + 0.5 * lax.erf(tensor * HALF_ROOT))


def gelu_slope(tensor):
    density = jnp.exp(-0.5 * tensor * tensor) * DENSITY
    return 0.5 + 0.5 * lax.erf(tensor * HALF_ROOT) + tensor * density


class Links:
    def __init__(self, seq):
        self.seq = seq
        self.far = [bit for bit in bit_list(seq) if bit > 1]
        self.orders = [self.far, self.far[::-1]]
        self.half = seq // 2
        self.me = lax.axis_index("seq")

    def place(self, mask):
        return (mask & 1) * self.half + (mask >> 1)

    def device(self, bit):
        return {"seq": jnp.bitwise_xor(self.me, bit)}

    def enter(self, others=()):
        barrier = pltpu.get_barrier_semaphore()
        bits = bit_list(self.seq)
        for bit in bits:
            pl.semaphore_signal(
                barrier, inc=1, device_id=self.device(bit), device_id_type=pl.DeviceIdType.MESH
            )
        count = len(bits)
        for other in others:
            count += other.greet(barrier)
        pl.semaphore_wait(barrier, count)

    def copy(self, source, target, send_sem, recv_sem, bit):
        return pltpu.make_async_remote_copy(
            src_ref=source,
            dst_ref=target,
            send_sem=send_sem,
            recv_sem=recv_sem,
            device_id=self.device(bit),
            device_id_type=pl.DeviceIdType.MESH,
        )


def span(bits):
    masks = [0]
    for bit in bits:
        masks = masks + [mask | bit for mask in masks]
    return masks


class Gather:
    def __init__(self, links, own_ref, all_ref, sends, recvs, local_sem):
        self.links, self.own, self.all = links, own_ref, all_ref
        self.sends, self.recvs, self.local = sends, recvs, local_sem
        self.rows = own_ref.shape[1]
        self.cut = self.rows // 2

    def at(self, micro, mask, part):
        start = self.links.place(mask) * self.rows + part * self.cut
        return self.all.at[micro, start : start + self.cut]

    def piece(self, micro, mask, part):
        if mask & 1:
            return 1
        seen = 0
        for bit in self.links.orders[part]:
            if mask & bit:
                seen = bit
        return seen

    def send(self, micro, mask, part, bit):
        there = mask ^ bit
        source = self.at(micro, mask, part)
        if mask == 0:
            source = self.own.at[micro, part * self.cut : (part + 1) * self.cut]
        self.links.copy(
            source,
            self.at(micro, there, part),
            self.sends.at[micro, self.links.place(there), part],
            self.recvs.at[micro, self.links.place(there), part],
            bit,
        ).start()

    def descriptor(self, micro, mask, part):
        bit = self.piece(micro, mask, part)
        source = self.at(micro, mask ^ bit, part)
        if mask ^ bit == 0:
            source = self.own.at[micro, part * self.cut : (part + 1) * self.cut]
        place = self.links.place(mask)
        return self.links.copy(
            source,
            self.at(micro, mask, part),
            self.sends.at[micro, place, part],
            self.recvs.at[micro, place, part],
            bit,
        )

    def keep_own(self, micro):
        return pltpu.make_async_copy(
            self.own.at[micro], self.all.at[micro, 0 : self.rows], self.local.at[micro]
        )

    def start(self, micro):
        for part in range(2):
            self.send(micro, 0, part, self.links.orders[part][0])
        for part in range(2):
            self.send(micro, 0, part, 1)
        self.keep_own(micro).start()

    def advance(self, micro, phase):
        count = len(self.links.far)
        for part in range(2):
            order = self.links.orders[part]
            fresh = [mask | order[phase] for mask in span(order[:phase])]
            for mask in fresh:
                self.descriptor(micro, mask, part).wait_recv()
            if phase + 1 < count:
                for mask in span(order[: phase + 1]):
                    self.send(micro, mask, part, order[phase + 1])
            for mask in fresh:
                self.send(micro, mask, part, 1)

    def phases(self):
        return len(self.links.far)

    def near(self, micro):
        for part in range(2):
            for mask in span(self.links.far):
                self.descriptor(micro, mask | 1, part).wait_recv()
        self.keep_own(micro).wait()

    def drain(self, micro):
        for part in range(2):
            for mask in range(1, self.links.seq):
                self.descriptor(micro, mask, part).wait_send()


class Scatter:
    def __init__(self, links, rows, sum_ref, near_send, near_recv, far_send, far_recv, sems):
        self.links, self.rows, self.cut = links, rows, rows // 2
        self.sum, self.near_send, self.near_recv = sum_ref, near_send, near_recv
        self.far_send, self.far_recv = far_send, far_recv
        self.near_sems, self.far_sems = sems

    def near_copy(self, micro, index):
        view = slice(index * self.rows, (index + 1) * self.rows)
        return self.links.copy(
            self.near_send.at[micro, view],
            self.near_recv.at[micro, view],
            self.near_sems.at[0, micro, index],
            self.near_sems.at[1, micro, index],
            1,
        )

    def start(self, micro, indexes):
        for index in indexes:
            self.near_copy(micro, index).start()

    def far_view(self, index, part):
        start = index * self.rows + part * self.cut
        return slice(start, start + self.cut)

    def bit_of(self, index, part):
        last = 0
        for bit in self.links.orders[part]:
            if (index * 2) & bit:
                last = bit
        return last

    def far_copy(self, micro, index, part):
        view = self.far_view(index, part)
        return self.links.copy(
            self.far_send.at[micro, view],
            self.far_recv.at[micro, view],
            self.far_sems.at[0, micro, index, part],
            self.far_sems.at[1, micro, index, part],
            self.bit_of(index, part),
        )

    def send_far(self, micro, index, part, value):
        self.far_send[micro, self.far_view(index, part)] = value.astype(low)
        self.far_copy(micro, index, part).start()

    def near_sum(self, micro):
        count = len(self.links.far)
        first = {}
        for part in range(2):
            bit = self.links.orders[part][count - 1]
            first[part] = [mask | bit for mask in span(self.links.orders[part][: count - 1])]
        ordered = sorted(range(self.links.half), key=lambda index: index == 0)
        for index in ordered:
            self.near_copy(micro, index).wait_recv()
            for part in range(2):
                view = self.far_view(index, part)
                value = self.sum[micro, view] + self.near_recv[micro, view].astype(wide)
                if index * 2 in first[part]:
                    self.send_far(micro, index, part, value)
                else:
                    self.sum[micro, view] = value

    def far_sum(self, micro, phase):
        count = len(self.links.far)
        for part in range(2):
            order = self.links.orders[part]
            bit = order[count - 1 - phase]
            remain = span(order[: count - 1 - phase])
            following = order[count - 2 - phase] if phase + 1 < count else 0
            for mask in sorted(remain, key=lambda mask: (mask & following) == 0):
                index, came = mask // 2, (mask | bit) // 2
                self.far_copy(micro, came, part).wait_recv()
                view = self.far_view(index, part)
                value = self.sum[micro, view] + self.far_recv[
                    micro, self.far_view(came, part)
                ].astype(wide)
                if mask & following:
                    self.send_far(micro, index, part, value)
                else:
                    self.sum[micro, view] = value

    def total(self, micro):
        return self.sum[micro, 0 : self.rows]

    def phases(self):
        return len(self.links.far)

    def drain(self, micro):
        for index in range(self.links.half):
            self.near_copy(micro, index).wait_send()
        for part in range(2):
            for index in range(1, self.links.half):
                self.far_copy(micro, index, part).wait_send()


def gather_scratch(seq, micros):
    return [
        pltpu.SemaphoreType.DMA((micros, seq, 2)),
        pltpu.SemaphoreType.DMA((micros, seq, 2)),
        pltpu.SemaphoreType.DMA((micros,)),
    ]


def scatter_scratch(seq, micros, rows, width):
    half = seq // 2
    part = pltpu.VMEM((micros, half * rows, width), low)
    return [
        pltpu.VMEM((micros, half * rows, width), wide),
        part,
        part,
        part,
        part,
        pltpu.SemaphoreType.DMA((2, micros, half)),
        pltpu.SemaphoreType.DMA((2, micros, half, 2)),
    ]


NEAR_GAP, FAR_GAP, SHORT_GAP = 2.5, 4.5, 0.1


def arrive_steps(gathers, micro):
    steps = []
    for phase in range(gathers[0].phases() if gathers else 0):
        for index, gather in enumerate(gathers):
            gap = SHORT_GAP if index else FAR_GAP
            steps.append((functools.partial(gather.advance, micro, phase), gap))
    for index, gather in enumerate(gathers):
        gap = SHORT_GAP if index else NEAR_GAP
        steps.append((functools.partial(gather.near, micro), gap))
    return steps


def leave_steps(scatters, finish, micro):
    steps = []
    for index, scatter in enumerate(scatters):
        gap = SHORT_GAP if index else NEAR_GAP
        steps.append((functools.partial(scatter.near_sum, micro), gap))
    for phase in range(scatters[0].phases()):
        for index, scatter in enumerate(scatters):
            gap = SHORT_GAP if index else FAR_GAP
            steps.append((functools.partial(scatter.far_sum, micro, phase), gap))
    return steps + [(functools.partial(finish, micro), SHORT_GAP)]


def half_steps(scatter, micro, length, chunk, cost):
    half = length // 2
    size = min(CHUNK, half)

    def odd():
        def body(index, carry):
            start = pl.multiple_of(half + index * size, size)
            place = pl.ds(pl.multiple_of(index * size, size), size)
            scatter.near_send[micro, place] = chunk(start, size).astype(low)
            return carry

        lax.fori_loop(0, half // size, body, 0)
        scatter.start(micro, range(scatter.links.half))

    def even():
        def body(index, carry):
            start = pl.multiple_of(index * size, size)
            scatter.sum[micro, pl.ds(start, size)] = chunk(start, size)
            return carry

        lax.fori_loop(0, half // size, body, 0)

    return [(odd, cost), (even, cost)]


def prologue(micro, up_ref, resid_ref, pair_ref, own_ref, kept_ref, pair_grad_ref):
    gains = (pair_ref[0:1], pair_ref[1:2])
    grad, gain_grad, shift_grad = norm_back(up_ref[micro].astype(wide), resid_ref[micro], gains)
    kept_ref[micro] = grad
    own_ref[micro] = grad.astype(low)
    if micro == 0:
        pair_grad_ref[0:1] = gain_grad
        pair_grad_ref[1:2] = shift_grad
    else:
        pair_grad_ref[0:1] += gain_grad
        pair_grad_ref[1:2] += shift_grad


class Task:
    def __init__(self, begin, arrive, compute, leave, drain, load=None, store=None):
        self.begin, self.arrive, self.compute = begin, arrive, compute
        self.leave, self.drain, self.load, self.store = leave, drain, load, store


class Waits:
    def __init__(self):
        self.time, self.queues = 0.0, []

    def add(self, steps):
        if steps:
            self.queues.append([list(steps), self.time + steps[0][1]])

    def take(self, entry):
        queue = entry[0]
        queue.pop(0)[0]()
        self.time += 0.4
        if queue:
            entry[1] = self.time + queue[0][1]
        else:
            self.queues.remove(entry)

    def run(self, step, cost):
        step()
        self.time += cost
        ready = [entry for entry in self.queues if entry[1] <= self.time]
        while ready:
            self.take(ready[0])
            ready = [entry for entry in self.queues if entry[1] <= self.time]

    def finish(self, steps):
        while any(entry[0] and entry[0][-1] is steps[-1] for entry in self.queues):
            entry = min(self.queues, key=lambda entry: entry[1])
            self.time = max(self.time, entry[1])
            self.take(entry)


def run_tasks(tasks, io, fill=(), fill_load=None, opening=None, closing=None, ahead=2):
    waits = Waits()
    for task in tasks[:ahead]:
        task.begin()
        waits.add(task.arrive)
    if opening is not None and len(tasks) <= 2:
        waits.add(opening())
    for index, task in enumerate(tasks):
        if task.arrive:
            waits.finish(task.arrive)
        io.load(task.load)
        for step, cost in task.compute:
            waits.run(step, cost)
        io.store(task.store)
        waits.add(task.leave)
        if index + ahead < len(tasks):
            tasks[index + ahead].begin()
            waits.add(tasks[index + ahead].arrive)
    if opening is not None and len(tasks) > 2:
        waits.add(opening())
    if closing is not None:
        waits.add(closing())
    if fill:
        io.load(fill_load)
        for step, cost in fill:
            waits.run(step, cost)
    while waits.queues:
        waits.take(min(waits.queues, key=lambda entry: entry[1]))
    for task in tasks:
        task.drain()
    io.close()


def make_task(micro, gathers, scatters, compute, finish, before=None, load=None, store=None):
    def begin():
        if before is not None:
            before(micro)
        for gather in gathers:
            gather.start(micro)

    def drain():
        for item in gathers + scatters:
            item.drain(micro)

    arrive = arrive_steps(gathers, micro)
    leave = leave_steps(scatters, finish, micro) if scatters else []
    return Task(begin, arrive, compute(micro), leave, drain, load, store)


class Operands:
    def __init__(self, ins, outs, in_sems, out_sems):
        self.ins, self.outs, self.in_sems, self.out_sems = ins, outs, in_sems, out_sems
        self.open = []

    def start(self):
        for index, (_, source, target) in enumerate(self.ins):
            pltpu.make_async_copy(source, target, self.in_sems.at[index]).start()

    def load(self, key):
        for index, (name, source, target) in enumerate(self.ins):
            if key is not None and name == key:
                pltpu.make_async_copy(source, target, self.in_sems.at[index]).wait()

    def copy_out(self, index, micro):
        _, source, target = self.outs[index]
        return pltpu.make_async_copy(
            source.at[micro], target.at[micro], self.out_sems.at[index, micro]
        )

    def store(self, key):
        if key is None:
            return
        name, micro = key
        for index, (group, _, _) in enumerate(self.outs):
            if group == name:
                self.copy_out(index, micro).start()
                self.open.append((index, micro))

    def close(self):
        for index, micro in self.open:
            self.copy_out(index, micro).wait()


def stage_call(kernel, name_id, outs, scratch, args, micros, lazy=None, early=None):
    lazy, early = lazy or {}, early or {}
    count, given, own = len(args), len(outs), len(scratch)
    lazy_places, early_places = sorted(lazy), sorted(early)
    parts = max([outs[place].shape[0] for place in early_places] + [1])

    def body(*refs):
        ins, results = list(refs[:count]), list(refs[count : count + given])
        own_scratch = refs[count + given : count + given + own]
        extra = refs[count + given + own :]
        loads, stores = [], []
        for index, place in enumerate(lazy_places):
            loads.append((lazy[place], ins[place], extra[index]))
            ins[place] = extra[index]
        for index, place in enumerate(early_places):
            buffer = extra[len(lazy_places) + index]
            stores.append((early[place], buffer, results[place]))
            results[place] = buffer
        io = Operands(loads, stores, extra[-2], extra[-1])
        io.start()
        kernel(io, *ins, *results, *own_scratch)

    held = [pltpu.VMEM(args[place].shape, args[place].dtype) for place in lazy_places]
    held += [pltpu.VMEM(outs[place].shape, outs[place].dtype) for place in early_places]
    sems = [
        pltpu.SemaphoreType.DMA((max(len(lazy_places), 1),)),
        pltpu.SemaphoreType.DMA((max(len(early_places), 1), parts)),
    ]
    near, far = pl.BlockSpec(memory_space=pltpu.VMEM), pl.BlockSpec(memory_space=pl.ANY)
    return pl.pallas_call(
        body,
        out_shape=tuple(outs),
        in_specs=[far if place in lazy else near for place in range(count)],
        out_specs=tuple(far if place in early else near for place in range(given)),
        scratch_shapes=list(scratch) + held + sems,
        compiler_params=pltpu.CompilerParams(
            collective_id=name_id, has_side_effects=True, vmem_limit_bytes=VMEM_LIMIT
        ),
        cost_estimate=pl.CostEstimate(
            flops=micros * 2_500_000_000, bytes_accessed=1 << 24, transcendentals=0
        ),
    )(*args)


def ffn_kernel(
    seq, io, own_ref, resid_ref, one_ref, two_ref, pair_ref, all_ref, before_ref, hidden_ref,
    sum_ref, norm_ref, low_ref, *scratch,
):
    links = Links(seq)
    micros, rows, _ = own_ref.shape
    length = all_ref.shape[1]
    gather = Gather(links, own_ref, all_ref, *scratch[:3])
    scatter = Scatter(links, rows, *scratch[3:8], scratch[8:])
    links.enter()

    def compute(micro):
        def chunk(start, size):
            place = pl.ds(start, size)
            before = dot(all_ref[micro, place], one_ref[...], 1, 1)
            before_ref[micro, place] = before
            after = gelu_exact(before).astype(low)
            hidden_ref[micro, place] = after
            return dot(after, two_ref[...], 1, 1)

        return half_steps(scatter, micro, length, chunk, 2.5)

    def finish(micro):
        total = resid_ref[micro] + scatter.total(micro)
        sum_ref[micro] = total
        value = layer_norm(total, (pair_ref[0:1], pair_ref[1:2]))
        norm_ref[micro] = value
        low_ref[micro] = value.astype(low)

    tasks = [
        make_task(
            micro, [gather], [scatter], compute, finish, None, 0 if micro == 0 else None, (0, micro)
        )
        for micro in range(micros)
    ]
    run_tasks(tasks, io)


def ffn_stage(seq, name_id, own, resid, one, two, pair):
    micros, rows, width = own.shape
    hidden = one.shape[0]
    length = rows * seq
    outs = (
        jax.ShapeDtypeStruct((micros, length, width), low),
        jax.ShapeDtypeStruct((micros, length, hidden), wide),
        jax.ShapeDtypeStruct((micros, length, hidden), low),
        jax.ShapeDtypeStruct((micros, rows, width), wide),
        jax.ShapeDtypeStruct((micros, rows, width), wide),
        jax.ShapeDtypeStruct((micros, rows, width), low),
    )
    scratch = gather_scratch(seq, micros) + scatter_scratch(seq, micros, rows, width)
    return stage_call(
        functools.partial(ffn_kernel, seq), name_id, outs, scratch,
        (own, resid, one, two, pair), 60, {1: 0, 2: 0, 3: 0, 4: 0}, {0: 0, 1: 0, 2: 0},
    )


def token_sum(left_ref, lanes, right_ref, micros):
    total = None
    for micro in range(micros):
        value = dot(left_ref[micro, :, lanes], right_ref[micro], 0, 0)
        total = value if total is None else total + value
    return total


def ffn_back_kernel(
    seq, ranks, hidden, io, up_ref, resid_ref, pair_ref, before_ref, one_ref, two_ref, rows_ref,
    hidden_ref, out_ref, pair_grad_ref, expand_ref, down_ref, two_terms_ref, all_ref, slope_ref,
    own_ref, kept_ref, *scratch,
):
    links = Links(seq)
    micros, rows, width = own_ref.shape
    length = all_ref.shape[1]
    adapt = down_ref.shape[0] * down_ref.shape[1]
    gather = Gather(links, own_ref, all_ref, *scratch[:3])
    scatter = Scatter(links, rows, *scratch[3:8], scratch[8:])
    links.enter()

    def before(micro):
        prologue(micro, up_ref, resid_ref, pair_ref, own_ref, kept_ref, pair_grad_ref)

    def compute(micro):
        def chunk(start, size):
            place = pl.ds(start, size)
            slope = dot(all_ref[micro, place], two_ref[...], 1, 0)
            slope = (slope * gelu_slope(before_ref[micro, place])).astype(low)
            slope_ref[micro, place] = slope
            return dot(slope, one_ref[...], 1, 0)

        return half_steps(scatter, micro, length, chunk, 2.5)

    def finish(micro):
        out_ref[micro] = kept_ref[micro] + scatter.total(micro)

    cut = hidden // ranks

    def one_tile(start):
        value = token_sum(slope_ref, slice(start, start + LANES), rows_ref, micros)
        if start < hidden:
            for part in range(0, LANES, cut):
                rank = (start + part) // cut
                expand_ref[rank] = value[part : part + cut].astype(low)
        else:
            down_ref[...] = value[:adapt].reshape(ranks, adapt // ranks, width).astype(low)

    def two_tile(start):
        value = token_sum(hidden_ref, slice(start, start + LANES), all_ref, micros).T
        value = value.reshape(seq, ranks, width // (seq * ranks), LANES)
        for rank in range(ranks):
            two_terms_ref[rank, :, :, start : start + LANES] = value[:, rank].astype(low)

    starts = range(0, slope_ref.shape[2], LANES)
    fill = [
        (functools.partial(tile, start), 1.2) for tile in (two_tile, one_tile) for start in starts
    ]
    tasks = [
        make_task(
            micro, [gather], [scatter], compute, finish, before, 0 if micro == 0 else None
        )
        for micro in range(micros)
    ]
    run_tasks(tasks, io, fill, 1)


def ffn_back_stage(seq, ranks, hidden, adapt, name_id, up, resid, pair, before, one, two, rows_all,
                   hidden_low):
    micros, rows, width = up.shape
    padded = one.shape[0]
    length = rows * seq
    outs = (
        jax.ShapeDtypeStruct((micros, rows, width), wide),
        jax.ShapeDtypeStruct((2, width), wide),
        jax.ShapeDtypeStruct((ranks, hidden // ranks, width), low),
        jax.ShapeDtypeStruct((ranks, adapt // ranks, width), low),
        jax.ShapeDtypeStruct((ranks, seq, width // (seq * ranks), padded), low),
    )
    scratch = (
        [pltpu.VMEM((micros, length, width), low), pltpu.VMEM((micros, length, padded), low)]
        + back_scratch(micros, rows, width)
        + gather_scratch(seq, micros)
        + scatter_scratch(seq, micros, rows, width)
    )
    return stage_call(
        functools.partial(ffn_back_kernel, seq, ranks, hidden), name_id, outs, scratch,
        (up, resid, pair, before, one, two, rows_all, hidden_low), 65,
        {3: 0, 4: 0, 5: 0, 6: 1, 7: 1},
    )


def opening_kernel(
    seq, ranks, io, source_ref, out_ref, ffn_ref, small_ref, source_all, out_all, ffn_all,
    small_all, norm_all, *scratch,
):
    links = Links(seq)
    me, row = lax.axis_index("seq"), lax.axis_index("rows")
    gathers = [Gather(links, source_ref, source_all, *scratch[0:3])]
    out_sems, ffn_sems, norm_sems, out_row_sems, small_row_sems, local_sems = scratch[3:]
    masks = range(1, seq)
    row_bits = bit_list(ranks)
    norm_rows = norm_all.shape[2]

    def remote(source, target, sems, index, device):
        return pltpu.make_async_remote_copy(
            src_ref=source,
            dst_ref=target,
            send_sem=sems.at[0, index],
            recv_sem=sems.at[1, index],
            device_id=device,
            device_id_type=pl.DeviceIdType.MESH,
        )

    def plane(mask):
        return {"seq": jnp.bitwise_xor(me, mask)}

    def other(mask):
        return jnp.bitwise_xor(me, mask)

    barrier = pltpu.get_barrier_semaphore()
    for mask in masks:
        pl.semaphore_signal(
            barrier, inc=1, device_id=plane(mask), device_id_type=pl.DeviceIdType.MESH
        )
    for bit in row_bits:
        pl.semaphore_signal(
            barrier,
            inc=1,
            device_id={"rows": jnp.bitwise_xor(row, bit)},
            device_id_type=pl.DeviceIdType.MESH,
        )
    pl.semaphore_wait(barrier, seq - 1 + len(row_bits))

    locals_ = [
        pltpu.make_async_copy(out_ref.at[me], out_all.at[row, me], local_sems.at[0]),
        pltpu.make_async_copy(ffn_ref.at[me], ffn_all.at[me], local_sems.at[1]),
        pltpu.make_async_copy(small_ref, small_all.at[row], local_sems.at[2]),
    ]
    for copy in locals_:
        copy.start()

    def out_send(mask):
        return remote(
            out_ref.at[other(mask)], out_all.at[row, me], out_sems, mask, plane(mask)
        )

    def out_wait(mask):
        return remote(
            out_ref.at[other(mask)], out_all.at[row, other(mask)], out_sems, mask, plane(mask)
        )

    def ffn_send(mask):
        return remote(ffn_ref.at[other(mask)], ffn_all.at[me], ffn_sems, mask, plane(mask))

    def ffn_wait(mask):
        return remote(
            ffn_ref.at[other(mask)], ffn_all.at[other(mask)], ffn_sems, mask, plane(mask)
        )

    def norm_send(mask):
        return remote(
            small_all.at[:, 0:norm_rows], norm_all.at[me], norm_sems, mask, plane(mask)
        )

    def norm_wait(mask):
        return remote(
            small_all.at[:, 0:norm_rows], norm_all.at[other(mask)], norm_sems, mask, plane(mask)
        )

    def row_copy(array, sems, mask, bit, there):
        at = jnp.bitwise_xor(row, mask)
        place = jnp.bitwise_xor(at, bit) if there else at
        return remote(
            array.at[at],
            array.at[place],
            sems,
            mask | bit,
            {"rows": jnp.bitwise_xor(row, bit)},
        )

    def row_phase(array, sems, phase):
        bit = row_bits[phase]
        for mask in span(row_bits[:phase]):
            row_copy(array, sems, mask, bit, False).start()

    def row_done(array, sems, phase):
        bit = row_bits[phase]
        for mask in span(row_bits[:phase]):
            row_copy(array, sems, mask, bit, True).wait_recv()

    for mask in masks:
        out_send(mask).start()
    tasks = [
        make_task(micro, [gather], [], lambda micro: [], None)
        for gather in gathers
        for micro in range(source_ref.shape[0])
    ]
    locals_[2].wait()
    row_phase(small_all, small_row_sems, 0)
    for task in tasks:
        task.begin()
    for mask in masks:
        ffn_send(mask).start()
    locals_[0].wait()
    for mask in masks:
        out_wait(mask).wait_recv()
    row_phase(out_all, out_row_sems, 0)
    steps = [
        functools.partial(task.arrive[phase][0])
        for phase in range(len(tasks[0].arrive))
        for task in tasks
    ]
    for phase in range(len(row_bits)):
        row_done(small_all, small_row_sems, phase)
        if phase + 1 < len(row_bits):
            row_phase(small_all, small_row_sems, phase + 1)
    norm_all[me] = small_all[:, 0:norm_rows]
    for mask in masks:
        norm_send(mask).start()
    cuts = [len(steps) * part // len(row_bits) for part in range(len(row_bits) + 1)]
    for phase in range(len(row_bits)):
        for step in steps[cuts[phase] : cuts[phase + 1]]:
            step()
        row_done(out_all, out_row_sems, phase)
        if phase + 1 < len(row_bits):
            row_phase(out_all, out_row_sems, phase + 1)
    for mask in masks:
        norm_wait(mask).wait_recv()
        ffn_wait(mask).wait_recv()
    locals_[1].wait()
    for mask in masks:
        out_send(mask).wait_send()
        ffn_send(mask).wait_send()
        norm_send(mask).wait_send()
    for phase, bit in enumerate(row_bits):
        for mask in span(row_bits[:phase]):
            row_copy(out_all, out_row_sems, mask, bit, False).wait_send()
            row_copy(small_all, small_row_sems, mask, bit, False).wait_send()
    for task in tasks:
        task.drain()


def opening_stage(seq, ranks, name_id, norm_rows, args):
    source, out_pieces, ffn_pieces, small = args
    micros, rows, width = source.shape
    whole = jax.ShapeDtypeStruct((micros, seq * rows, width), low)
    outs = (
        whole,
        jax.ShapeDtypeStruct((ranks,) + out_pieces.shape, low),
        jax.ShapeDtypeStruct(ffn_pieces.shape, low),
        jax.ShapeDtypeStruct((ranks,) + small.shape, low),
        jax.ShapeDtypeStruct((seq, ranks, norm_rows, small.shape[1]), low),
    )
    scratch = gather_scratch(seq, micros) + [
        pltpu.SemaphoreType.DMA((2, seq)),
        pltpu.SemaphoreType.DMA((2, seq)),
        pltpu.SemaphoreType.DMA((2, seq)),
        pltpu.SemaphoreType.DMA((2, ranks)),
        pltpu.SemaphoreType.DMA((2, ranks)),
        pltpu.SemaphoreType.DMA((3,)),
    ]
    return stage_call(
        functools.partial(opening_kernel, seq, ranks), name_id, outs, scratch, args, 40
    )


class Attention:
    def __init__(self, q_ref, kv_ref, offsets, prefix_ref, ids, count, causal):
        self.q, self.kv, self.offsets, self.prefix = q_ref, kv_ref, offsets, prefix_ref
        self.key_ids, self.query_ids, self.key_places, self.query_places = ids
        self.count, self.causal = count, causal
        self.heads = prefix_ref.shape[2] // HEAD_DIM

    def load(self, micro, head, place):
        q_at, k_at, v_at = (at + head * HEAD_DIM for at in self.offsets)
        queries = self.q[micro, place, q_at : q_at + HEAD_DIM] * jnp.asarray(SCALING, low)
        keys = self.kv[micro, :, k_at : k_at + HEAD_DIM]
        values = self.kv[micro, :, v_at : v_at + HEAD_DIM]
        return queries, keys, values

    def scores(self, micro, keys, queries, lanes, place):
        scores = dot(keys, queries, 1, 1)
        allowed = self.key_ids[micro] == self.query_ids[micro, :, place]
        if self.causal:
            allowed = allowed & (self.key_places[...] <= self.query_places[:, place])
        scores = jnp.where(allowed, scores, MASKED)
        extra = dot(self.prefix[0, :, lanes], queries, 1, 1)
        rows = lax.broadcasted_iota(jnp.int32, extra.shape, 0)
        return scores, jnp.where(rows < self.count, extra, MASKED)

    def forward(self, micro, start, size, context_ref, logs_ref):
        place = pl.ds(start, size)
        for head in range(self.heads):
            lanes = slice(head * HEAD_DIM, (head + 1) * HEAD_DIM)
            queries, keys, values = self.load(micro, head, place)
            scores, extra = self.scores(micro, keys, queries, lanes, place)
            peak = jnp.maximum(
                jnp.max(scores, axis=0, keepdims=True), jnp.max(extra, axis=0, keepdims=True)
            )
            scores = jnp.exp(scores - peak)
            extra = jnp.exp(extra - peak)
            total = jnp.sum(scores, axis=0, keepdims=True) + jnp.sum(extra, axis=0, keepdims=True)
            context = dot(values, scores.astype(low), 0, 0)
            context = context + dot(self.prefix[1, :, lanes], extra.astype(low), 0, 0)
            context_ref[micro, place, lanes] = (context / total).T.astype(low)
            logs_ref[micro, head : head + 1, place] = peak + jnp.log(total)

    def backward(self, micro, start, size, up_ref, logs_ref, grad_ref, k_sum, v_sum, pre_ref):
        place = pl.ds(start, size)
        for head in range(self.heads):
            lanes = slice(head * HEAD_DIM, (head + 1) * HEAD_DIM)
            queries, keys, values = self.load(micro, head, place)
            scores, extra = self.scores(micro, keys, queries, lanes, place)
            logs = logs_ref[micro, head : head + 1, place]
            weights = jnp.exp(scores - logs)
            extra = jnp.exp(extra - logs)
            up = up_ref[:, lanes]
            dots = dot(values, up, 1, 1)
            extra_dots = dot(self.prefix[1, :, lanes], up, 1, 1)
            centre = jnp.sum(weights * dots, axis=0, keepdims=True) + jnp.sum(
                extra * extra_dots, axis=0, keepdims=True
            )
            slope = (weights * (dots - centre)).astype(low)
            extra_slope = (extra * (extra_dots - centre)).astype(low)
            query_grad = dot(keys, slope, 0, 0) + dot(self.prefix[0, :, lanes], extra_slope, 0, 0)
            grad_ref[micro, place, lanes] = (query_grad * SCALING).T.astype(low)
            k_sum[:, lanes] += dot(slope, queries, 1, 0)
            v_sum[:, lanes] += dot(weights.astype(low), up, 1, 0)
            pre_ref[0, :, lanes] += dot(extra_slope, queries, 1, 0)
            pre_ref[1, :, lanes] += dot(extra.astype(low), up, 1, 0)


def loop(first, count, size, body):
    def step(index, carry):
        body(pl.multiple_of(first + index * size, size), index)
        return carry

    lax.fori_loop(0, count, step, 0)


def project_steps(micro, rows_ref, weight_ref, out_ref):
    length = rows_ref.shape[1]
    size = min(CHUNK, length)

    def body(start, index):
        place = pl.ds(start, size)
        out_ref[micro, place] = dot(rows_ref[micro, place], weight_ref[...], 1, 1).astype(low)

    return [(lambda: loop(0, length // size, size, body), 1.3)]


def self_kernel(seq, count, io, *refs):
    kinds = 2
    scratch = refs[-kinds * 7 - 3 :]
    refs = refs[: -kinds * 7 - 3]
    target_all = refs[-1]
    places = refs[:2]
    links = Links(seq)
    links.enter()
    tasks = []
    for kind in range(kinds):
        own_ref, in_ref, out_ref, prefix_ref, kid_ref, qid_ref, pair_ref = refs[
            3 + 7 * kind : 10 + 7 * kind
        ]
        (qkv_ref, context_ref, logs_ref, sum_ref, norm_ref, low_ref) = refs[
            3 + 7 * kinds + 6 * kind : 9 + 7 * kinds + 6 * kind
        ]
        all_ref = target_all if kind else refs[2]
        gathers = [Gather(links, own_ref, all_ref, *scratch[-3:])] if kind else []
        micros, rows, _ = own_ref.shape
        length = all_ref.shape[1]
        head_width = prefix_ref.shape[2]
        piece = scratch[7 * kind : 7 * kind + 7]
        scatter = Scatter(links, rows, *piece[:5], piece[5:])
        ids = (kid_ref, qid_ref) + tuple(places)
        attention = Attention(
            qkv_ref, qkv_ref, (0, head_width, 2 * head_width), prefix_ref, ids, count, kind == 1
        )

        def compute(
            micro, attention=attention, context_ref=context_ref, logs_ref=logs_ref,
            out_ref=out_ref, all_ref=all_ref, in_ref=in_ref, qkv_ref=qkv_ref, scatter=scatter,
        ):
            def chunk(start, size):
                attention.forward(micro, start, size, context_ref, logs_ref)
                return dot(context_ref[micro, pl.ds(start, size)], out_ref[...], 1, 1)

            return project_steps(micro, all_ref, in_ref, qkv_ref) + half_steps(
                scatter, micro, length, chunk, 4.2
            )

        def finish(
            micro, own_ref=own_ref, scatter=scatter, sum_ref=sum_ref, norm_ref=norm_ref,
            low_ref=low_ref, pair_ref=pair_ref,
        ):
            total = own_ref[micro].astype(wide) + scatter.total(micro)
            sum_ref[micro] = total
            value = layer_norm(total, (pair_ref[0:1], pair_ref[1:2]))
            norm_ref[micro] = value
            low_ref[micro] = value.astype(low)

        for micro in range(micros):
            load = kind if micro == 0 else None
            tasks.append(
                make_task(micro, gathers, [scatter], compute, finish, None, load, (kind, micro))
            )
    run_tasks(tasks, io, ahead=len(tasks))


def self_stage(seq, name_id, count, places, source_all, sides):
    micros, rows, width = sides[0][0].shape
    length = rows * seq
    head_width = sides[0][3].shape[2]
    heads = head_width // HEAD_DIM
    side_outs = (
        jax.ShapeDtypeStruct((micros, length, 3 * head_width), low),
        jax.ShapeDtypeStruct((micros, length, head_width), low),
        jax.ShapeDtypeStruct((micros, heads, length), wide),
        jax.ShapeDtypeStruct((micros, rows, width), wide),
        jax.ShapeDtypeStruct((micros, rows, width), wide),
        jax.ShapeDtypeStruct((micros, rows, width), low),
    )
    scratch = scatter_scratch(seq, micros, rows, width) * 2 + gather_scratch(seq, micros)
    args = tuple(places) + (source_all,) + sides[0] + sides[1]
    gathered = jax.ShapeDtypeStruct((micros, length, width), low)
    outs = stage_call(
        functools.partial(self_kernel, seq, count), name_id, side_outs * 2 + (gathered,), scratch,
        args, 75,
        {11: 1, 12: 1, 14: 1}, {0: 0, 1: 0, 6: 1, 7: 1, 12: 1},
    )
    return outs[:6], outs[6:12], outs[12]


def cross_kernel(
    seq, count, io, kpos_ref, qpos_ref, first_ref, first_low_ref, memory_ref, q_in_ref, kv_in_ref,
    out_ref, prefix_ref, kid_ref, qid_ref, pair_ref, first_all, memory_all, q_ref, kv_ref,
    context_ref, logs_ref, sum_ref, norm_ref, low_ref, *scratch,
):
    links = Links(seq)
    micros, rows, _ = first_ref.shape
    length = first_all.shape[1]
    head_width = prefix_ref.shape[2]
    gathers = [
        Gather(links, memory_ref, memory_all, *scratch[:3]),
        Gather(links, first_low_ref, first_all, *scratch[3:6]),
    ]
    scatter = Scatter(links, rows, *scratch[6:11], scratch[11:])
    ids = (kid_ref, qid_ref, kpos_ref, qpos_ref)
    attention = Attention(q_ref, kv_ref, (0, 0, head_width), prefix_ref, ids, count, False)
    links.enter()

    def compute(micro):
        def chunk(start, size):
            attention.forward(micro, start, size, context_ref, logs_ref)
            return dot(context_ref[micro, pl.ds(start, size)], out_ref[...], 1, 1)

        return (
            project_steps(micro, memory_all, kv_in_ref, kv_ref)
            + project_steps(micro, first_all, q_in_ref, q_ref)
            + half_steps(scatter, micro, length, chunk, 4.2)
        )

    def finish(micro):
        total = first_ref[micro] + scatter.total(micro)
        sum_ref[micro] = total
        value = layer_norm(total, (pair_ref[0:1], pair_ref[1:2]))
        norm_ref[micro] = value
        low_ref[micro] = value.astype(low)

    tasks = [
        make_task(
            micro, gathers, [scatter], compute, finish, None, 0 if micro == 0 else None, (0, micro)
        )
        for micro in range(micros)
    ]
    run_tasks(tasks, io)


def cross_stage(seq, name_id, count, places, args):
    micros, rows, width = args[0].shape
    length = rows * seq
    head_width = args[6].shape[2]
    heads = head_width // HEAD_DIM
    whole = jax.ShapeDtypeStruct((micros, length, width), low)
    outs = (
        whole,
        whole,
        jax.ShapeDtypeStruct((micros, length, head_width), low),
        jax.ShapeDtypeStruct((micros, length, 2 * head_width), low),
        jax.ShapeDtypeStruct((micros, length, head_width), low),
        jax.ShapeDtypeStruct((micros, heads, length), wide),
        jax.ShapeDtypeStruct((micros, rows, width), wide),
        jax.ShapeDtypeStruct((micros, rows, width), wide),
        jax.ShapeDtypeStruct((micros, rows, width), low),
    )
    scratch = gather_scratch(seq, micros) * 2 + scatter_scratch(seq, micros, rows, width)
    return stage_call(
        functools.partial(cross_kernel, seq, count), name_id, outs, scratch,
        tuple(places) + args, 85, {place: 0 for place in (2, 5, 6, 7, 8, 9, 10)},
        {place: 0 for place in range(5)},
    )


def attend_back_steps(
    attention, micro, length, up_all, out_ref, logs_ref, grad_ref, k_sum, v_sum, pre_ref, up_ref,
    emit=None,
):
    head_width = up_ref.shape[1]
    half = length // 2
    size = min(CHUNK, half)

    def run(first, zero):
        if zero:
            k_sum[...] = jnp.zeros_like(k_sum)
            v_sum[...] = jnp.zeros_like(v_sum)
            if micro == 0:
                pre_ref[...] = jnp.zeros_like(pre_ref)

        def body(start, index):
            place = pl.ds(start, size)
            up_ref[...] = dot(up_all[micro, place], out_ref[...], 1, 0).astype(low)
            attention.backward(
                micro, start, size, up_ref, logs_ref, grad_ref, k_sum, v_sum, pre_ref
            )
            if emit is not None:
                emit(start, index, size)

        loop(first, half // size, size, body)

    def keys():
        grad_ref[micro, :, head_width : 2 * head_width] = k_sum[...].astype(low)
        grad_ref[micro, :, 2 * head_width : 3 * head_width] = v_sum[...].astype(low)

    return [(lambda: run(half, True), 5.0), (lambda: run(0, False), 5.0), (keys, 0.5)]


def term_steps(context_ref, up_all, grad_ref, sources, terms_ref, seq, send=None):
    micros = grad_ref.shape[0]
    ranks, _, cols, width = terms_ref.shape
    head_width = context_ref.shape[2]

    def tile(part):
        if part == 3:
            value = token_sum(context_ref, slice(0, head_width), up_all, micros).T
            value = value.reshape(seq, ranks, cols, head_width)
            for owner in range(seq):
                lanes = slice(owner * head_width, (owner + 1) * head_width)
                terms_ref[:, 3, :, lanes] = value[owner].astype(low)
        else:
            lanes = slice(part * head_width, (part + 1) * head_width)
            value = token_sum(grad_ref, lanes, sources[part], micros)
            terms_ref[:, part] = value.reshape(ranks, cols, width).astype(low)
        if send is not None:
            send(part)

    return [(functools.partial(tile, part), 1.2) for part in (3, 0, 1, 2)]


def term_shape(seq, ranks, width):
    return jax.ShapeDtypeStruct((ranks, 4, width // (seq * ranks), width), low)


class RankSum:
    def __init__(self, ranks, terms_ref, recv_ref, total_ref, sems):
        self.ranks, self.terms, self.recv = ranks, terms_ref, recv_ref
        self.total, self.sems, self.row = total_ref, sems, lax.axis_index("rows")

    def greet(self, barrier):
        for mask in range(1, self.ranks):
            pl.semaphore_signal(
                barrier,
                inc=1,
                device_id={"rows": jnp.bitwise_xor(self.row, mask)},
                device_id_type=pl.DeviceIdType.MESH,
            )
        return self.ranks - 1

    def copy(self, part, mask):
        owner = jnp.bitwise_xor(self.row, mask)
        return pltpu.make_async_remote_copy(
            src_ref=self.terms.at[owner, part],
            dst_ref=self.recv.at[mask, part],
            send_sem=self.sems.at[0, mask, part],
            recv_sem=self.sems.at[1, mask, part],
            device_id={"rows": owner},
            device_id_type=pl.DeviceIdType.MESH,
        )

    def send(self, part):
        for mask in range(1, self.ranks):
            self.copy(part, mask).start()

    def finish(self):
        for part in (3, 0, 1, 2):
            value = self.terms[self.row, part].astype(wide)
            for mask in range(1, self.ranks):
                self.copy(part, mask).wait_recv()
                value = value + self.recv[mask, part].astype(wide)
            self.total[part] = value
        for part in range(4):
            for mask in range(1, self.ranks):
                self.copy(part, mask).wait_send()


class SmallSum:
    def __init__(self, hops, held_ref, recv_ref, sems):
        self.hops, self.held, self.recv, self.sems = hops, held_ref, recv_ref, sems

    def copy(self, hop):
        name, bit = self.hops[hop]
        return pltpu.make_async_remote_copy(
            src_ref=self.held.at[hop],
            dst_ref=self.recv.at[hop],
            send_sem=self.sems.at[0, hop],
            recv_sem=self.sems.at[1, hop],
            device_id={name: jnp.bitwise_xor(lax.axis_index(name), bit)},
            device_id_type=pl.DeviceIdType.MESH,
        )

    def step(self, hop):
        self.copy(hop).wait_recv()
        self.held[hop + 1] = self.held[hop] + self.recv[hop]
        if hop + 1 < len(self.hops):
            self.copy(hop + 1).start()

    def start(self, gap):
        self.copy(0).start()
        return [(functools.partial(self.step, hop), gap) for hop in range(len(self.hops))]

    def total(self):
        return self.held[len(self.hops)]

    def drain(self):
        for hop in range(len(self.hops)):
            self.copy(hop).wait_send()


def small_scratch(hops, shape):
    return [
        pltpu.VMEM((hops + 1,) + shape, wide),
        pltpu.VMEM((hops,) + shape, wide),
        pltpu.SemaphoreType.DMA((2, hops)),
    ]


def cross_back_kernel(
    seq, count, io, kpos_ref, qpos_ref, up_ref, resid_ref, pair_ref, q_ref, kv_ref, logs_ref,
    q_in_ref, kv_in_ref, out_ref, prefix_ref, kid_ref, qid_ref, first_all, memory_all, context_ref,
    pre_ref, first_out, memory_out, pair_grad_ref, terms_ref, up_all, grad_ref, own_ref, kept_ref, k_sum, v_sum, up_chunk, *scratch,
):
    links = Links(seq)
    micros, rows, _ = own_ref.shape
    length = up_all.shape[1]
    head_width = prefix_ref.shape[2]
    gather = Gather(links, own_ref, up_all, *scratch[:3])
    first_sum = Scatter(links, rows, *scratch[3:8], scratch[8:10])
    memory_sum = Scatter(links, rows, *scratch[10:15], scratch[15:17])
    ids = (kid_ref, qid_ref, kpos_ref, qpos_ref)
    attention = Attention(q_ref, kv_ref, (0, 0, head_width), prefix_ref, ids, count, False)
    links.enter()

    def before(micro):
        prologue(micro, up_ref, resid_ref, pair_ref, own_ref, kept_ref, pair_grad_ref)

    def compute(micro):
        def first_chunk(start, size):
            return dot(
                grad_ref[micro, pl.ds(start, size), 0:head_width], q_in_ref[...], 1, 0
            )

        def memory_chunk(start, size):
            return dot(
                grad_ref[micro, pl.ds(start, size), head_width : 3 * head_width],
                kv_in_ref[...],
                1,
                0,
            )

        attend = attend_back_steps(
            attention, micro, length, up_all, out_ref, logs_ref, grad_ref, k_sum, v_sum, pre_ref,
            up_chunk,
        )
        sums = half_steps(first_sum, micro, length, first_chunk, 0.6)
        return (
            [attend[0], sums[0], attend[1], sums[1], attend[2]]
            + half_steps(memory_sum, micro, length, memory_chunk, 0.8)
        )

    def finish(micro):
        first_out[micro] = kept_ref[micro] + first_sum.total(micro)
        memory_out[micro] = memory_sum.total(micro)

    tasks = [
        make_task(
            micro, [gather], [first_sum, memory_sum], compute, finish, before,
            0 if micro == 0 else None,
        )
        for micro in range(micros)
    ]
    fill = term_steps(
        context_ref, up_all, grad_ref, (first_all, memory_all, memory_all), terms_ref, seq
    )
    run_tasks(tasks, io, fill, 1)


def cross_back_stage(seq, ranks, name_id, count, places, args):
    micros, rows, width = args[0].shape
    length = rows * seq
    head_width = args[9].shape[2]
    own = jax.ShapeDtypeStruct((micros, rows, width), wide)
    outs = (
        jax.ShapeDtypeStruct((2, PAD_PREFIX, head_width), wide),
        own,
        own,
        jax.ShapeDtypeStruct((2, width), wide),
        term_shape(seq, ranks, width),
    )
    scratch = (
        [
            pltpu.VMEM((micros, length, width), low),
            pltpu.VMEM((micros, length, 3 * head_width), low),
        ]
        + back_scratch(micros, rows, width)
        + sum_scratch(length, head_width)
        + gather_scratch(seq, micros)
        + scatter_scratch(seq, micros, rows, width) * 2
    )
    lazy = {place: 0 for place in range(5, 14)}
    lazy.update({14: 1, 15: 1, 16: 1})
    return stage_call(
        functools.partial(cross_back_kernel, seq, count), name_id, outs, scratch,
        tuple(places) + args, 85, lazy,
    )


def back_scratch(micros, rows, width):
    return [pltpu.VMEM((micros, rows, width), low), pltpu.VMEM((micros, rows, width), wide)]


def sum_scratch(length, head_width):
    return [
        pltpu.VMEM((length, head_width), wide),
        pltpu.VMEM((length, head_width), wide),
        pltpu.VMEM((min(CHUNK, length // 2), head_width), low),
    ]


def self_back_kernel(
    seq, count, causal, reduce, io, kpos_ref, qpos_ref, up_ref, resid_ref, pair_ref, qkv_ref,
    logs_ref, in_ref, out_ref, prefix_ref, kid_ref, qid_ref, context_ref, rows_ref, *rest,
):
    if reduce:
        norm_in_ref, pre_in_ref, norm_out_ref, pre_out_ref, *rest = rest
    else:
        pre_ref, pair_grad_ref, *rest = rest
    grad_out, result_ref, up_all, grad_ref, own_ref, kept_ref, k_sum, v_sum, up_chunk, *scratch = rest
    links = Links(seq)
    micros, rows, _ = own_ref.shape
    length = up_all.shape[1]
    head_width = prefix_ref.shape[2]
    gather = Gather(links, own_ref, up_all, *scratch[:3])
    scatter = Scatter(links, rows, *scratch[3:8], scratch[8:10])
    terms_ref, rank_sum = result_ref, None
    if reduce:
        terms_ref, recv_ref, rank_sems, pre_ref, pair_grad_ref = scratch[10:15]
        row_hops = [("rows", bit) for bit in bit_list(terms_ref.shape[0])]
        norm_sum = SmallSum(
            [("seq", bit) for bit in bit_list(seq)] + row_hops, *scratch[15:18]
        )
        pre_sum = SmallSum(row_hops, *scratch[18:21])
        rank_sum = RankSum(terms_ref.shape[0], terms_ref, recv_ref, result_ref, rank_sems)
    ids = (kid_ref, qid_ref, kpos_ref, qpos_ref)
    attention = Attention(
        qkv_ref, qkv_ref, (0, head_width, 2 * head_width), prefix_ref, ids, count, causal
    )
    links.enter([rank_sum] if reduce else [])

    def before(micro):
        prologue(micro, up_ref, resid_ref, pair_ref, own_ref, kept_ref, pair_grad_ref)

    def compute(micro):
        def chunk(start, size):
            return dot(grad_ref[micro, pl.ds(start, size)], in_ref[...], 1, 0)

        return attend_back_steps(
            attention, micro, length, up_all, out_ref, logs_ref, grad_ref, k_sum, v_sum,
            pre_ref, up_chunk,
        ) + half_steps(scatter, micro, length, chunk, 0.9)

    def finish(micro):
        grad_out[micro] = kept_ref[micro] + scatter.total(micro)

    tasks = [
        make_task(
            micro, [gather], [scatter], compute, finish, before, 0 if micro == 0 else None
        )
        for micro in range(micros)
    ]
    fill = term_steps(
        context_ref, up_all, grad_ref, (rows_ref,) * 3, terms_ref, seq,
        rank_sum.send if reduce else None,
    )
    def opening():
        norm_sum.held[0] = norm_in_ref[...]
        norm_sum.held[0, 0:2] = pair_grad_ref[...]
        return norm_sum.start(9.0)

    def closing():
        pre_sum.held[0, 0:2] = pre_ref[...]
        pre_sum.held[0, 2:6] = pre_in_ref[...]
        return pre_sum.start(15.0)

    if reduce:
        tasks[-1].compute = [(lambda: io.load(1), 0.1), fill[0]] + tasks[-1].compute
        run_tasks(tasks, io, fill[1:], None, opening, closing)
        rank_sum.finish()
        norm_out_ref[...] = norm_sum.total()
        pre_out_ref[...] = pre_sum.total()
        norm_sum.drain()
        pre_sum.drain()
    else:
        run_tasks(tasks, io, fill, 1)


def self_back_stage(seq, ranks, name_id, count, places, causal, reduce, side):
    micros, rows, width = side[0].shape
    length = rows * seq
    head_width = side[7].shape[2]
    terms = term_shape(seq, ranks, width)
    pre = jax.ShapeDtypeStruct((2, PAD_PREFIX, head_width), wide)
    outs = (pre, jax.ShapeDtypeStruct((2, width), wide))
    total = terms
    if reduce:
        outs = tuple(
            jax.ShapeDtypeStruct(shape, wide)
            for shape in (side[12].shape, (6, PAD_PREFIX, head_width))
        )
        total = jax.ShapeDtypeStruct(terms.shape[1:], wide)
    outs += (jax.ShapeDtypeStruct((micros, rows, width), wide), total)
    scratch = (
        [
            pltpu.VMEM((micros, length, width), low),
            pltpu.VMEM((micros, length, 3 * head_width), low),
        ]
        + back_scratch(micros, rows, width)
        + sum_scratch(length, head_width)
        + gather_scratch(seq, micros)
        + scatter_scratch(seq, micros, rows, width)
    )
    if reduce:
        scratch += [
            pltpu.VMEM(terms.shape, low),
            pltpu.VMEM(terms.shape, low),
            pltpu.SemaphoreType.DMA((2, ranks, 4)),
            pltpu.VMEM(pre.shape, wide),
            pltpu.VMEM((2, width), wide),
        ]
        row_hops, hops = len(bit_list(ranks)), len(bit_list(ranks)) + len(bit_list(seq))
        scratch += small_scratch(hops, side[12].shape)
        scratch += small_scratch(row_hops, (6, PAD_PREFIX, head_width))
    lazy = {place: 0 for place in range(5, 12)}
    lazy.update({12: 1, 13: 1})
    return stage_call(
        functools.partial(self_back_kernel, seq, count, causal, reduce), name_id, outs, scratch,
        tuple(places) + side, 75, lazy,
    )


def local(
    seq, ranks,
    source, target, source_segments, target_segments, cotangent,
    encoder_qkv, encoder_output, encoder_prefix, encoder_expand, encoder_contract, encoder_down,
    encoder_up, encoder_norms, decoder_qkv, decoder_output, decoder_prefix, cross_query, cross_kv,
    cross_output, cross_prefix, decoder_expand, decoder_contract, decoder_down, decoder_up,
    decoder_norms,
):
    micro_count, batch_rows, block, width = source.shape
    length = source_segments.shape[2]
    me = lax.axis_index("seq")
    stacked = micro_count * batch_rows
    head_width = width // seq
    slice_cols = encoder_output.shape[1]
    count = encoder_prefix.shape[1]
    hidden = encoder_contract.shape[0] // seq
    adapt = encoder_up.shape[0] // seq
    both = hidden + adapt
    padded = (both + LANES - 1) // LANES * LANES

    sources = source.reshape(stacked, block, width)
    targets = target.reshape(stacked, block, width)

    order = relative(jnp.arange(length, dtype=jnp.int32), seq, me)
    places = (order[:, None], order[None, :])

    def relative_ids(ids):
        rows = [relative(row, seq, me) for row in ids.reshape(stacked, length)]
        value = jnp.stack(rows)
        return value[:, :, None], value[:, None, :]

    source_keys, source_queries = relative_ids(source_segments)
    target_keys, target_queries = relative_ids(target_segments)

    def columns(weight):
        return jnp.swapaxes(weight, -1, -2)

    def gather_rows(value):
        return lax.all_gather(value, "rows", axis=0, tiled=False)

    def stack_columns(pieces):
        gathered = gather_rows(jnp.concatenate(pieces, axis=0))
        outs = []
        start = 0
        for piece in pieces:
            size = piece.shape[0]
            outs.append(gathered[:, start : start + size])
            start += size
        return outs

    def flat_columns(gathered, parts):
        value = gathered.reshape(ranks, parts, slice_cols, width)
        return jnp.swapaxes(value, 0, 1).reshape(parts * ranks * slice_cols, width)

    def split_rows(weight):
        return columns(weight).reshape(slice_cols, seq, -1)

    def ffn_rows(contract, up):
        pieces = [split_rows(contract), split_rows(up) * jnp.asarray(ADAPTER_SCALE, low)]
        if padded > both:
            pieces.append(jnp.zeros((slice_cols, seq, padded - both), low))
        return pieces

    def by_target(pieces):
        return jnp.swapaxes(jnp.concatenate(pieces, axis=2), 0, 1)

    out_pieces = by_target([split_rows(encoder_output), split_rows(decoder_output)])
    ffn_pieces = by_target(
        [split_rows(cross_output)]
        + ffn_rows(encoder_contract, encoder_up)
        + ffn_rows(decoder_contract, decoder_up)
    )
    qkv_parts = gather_rows(
        jnp.concatenate(
            [
                columns(encoder_qkv).reshape(-1, width),
                columns(decoder_qkv).reshape(-1, width),
            ]
        )
    )
    norm_count = encoder_norms.shape[0]
    norms = jnp.concatenate([encoder_norms, decoder_norms]).reshape(-1, slice_cols)
    prefixes = jnp.concatenate([encoder_prefix, decoder_prefix, cross_prefix])
    prefixes = prefixes.reshape(-1, slice_cols)
    norm_rows = (norms.shape[0] + 15) // 16 * 16
    small = jnp.concatenate(
        [jnp.pad(norms, ((0, norm_rows - norms.shape[0]), (0, 0))), prefixes]
    )
    small = jnp.pad(small, ((0, -small.shape[0] % 16), (0, 0)))
    source_all, front, row_pieces, small_all, norm_all = opening_stage(
        seq, ranks, 1, norm_rows, (sources, out_pieces, ffn_pieces, small)
    )
    scales = norm_all[:, :, : norms.shape[0]].reshape(seq * ranks, -1, slice_cols)
    scales = jnp.moveaxis(scales, 0, 1).reshape(-1, 2, width).astype(wide)
    prefixes = small_all[:, norm_rows : norm_rows + 6 * count]
    prefixes = jnp.moveaxis(prefixes.reshape(ranks, 6, count, slice_cols), 0, 2)
    prefixes = prefixes.reshape(6, count, head_width)
    prefixes = jnp.pad(prefixes, ((0, 0), (0, PAD_PREFIX - count), (0, 0)))
    encoder_pre, decoder_pre, cross_pre = prefixes[0:2], prefixes[2:4], prefixes[4:6]

    late = [
        jnp.concatenate(
            [
                columns(encoder_expand),
                columns(encoder_down),
                columns(cross_query),
                columns(cross_kv).reshape(-1, width),
            ]
        ),
        row_pieces[:, :, : head_width + padded],
        jnp.concatenate([columns(decoder_expand), columns(decoder_down)]),
        row_pieces[:, :, head_width + padded :],
    ]
    source_all, late = lax.optimization_barrier((source_all, late))
    encoder_in = flat_columns(qkv_parts[:, : 3 * slice_cols], 3)
    decoder_in = flat_columns(qkv_parts[:, 3 * slice_cols :], 3)
    front_rows = jnp.swapaxes(front, 0, 1).reshape(width, -1)
    encoder_out = front_rows[:, :head_width]
    decoder_out = front_rows[:, head_width:]
    cut = encoder_expand.shape[1]

    def ffn_in(gathered):
        pieces = [gathered[:, :cut].reshape(-1, width), gathered[:, cut:].reshape(-1, width)]
        if padded > both:
            pieces.append(jnp.zeros((padded - both, width), low))
        return jnp.concatenate(pieces)

    def row_order(gathered):
        return jnp.swapaxes(gathered, 0, 1).reshape(width, -1)

    second_parts = gather_rows(late[0])
    rest = gather_rows(late[1])
    encoder_side, decoder_side, target_all = self_stage(
        seq, 2, count, places, source_all,
        (
            (
                sources, encoder_in, encoder_out, encoder_pre, source_keys, source_queries,
                scales[0],
            ),
            (
                targets, decoder_in, decoder_out, decoder_pre, target_keys, target_queries,
                scales[norm_count],
            ),
        ),
    )
    encoder_qkvs, encoder_ctx, encoder_logs, resid_one, middle, middle_low = encoder_side
    middle_low, second_parts, rest, last = lax.optimization_barrier(
        (middle_low, second_parts, rest, late[2:])
    )
    rest = row_order(rest)
    cross_out, encoder_two = rest[:, :head_width], rest[:, head_width:]
    ffn_cut = cut + encoder_down.shape[1]
    encoder_one = ffn_in(second_parts[:, :ffn_cut])
    cross_in = flat_columns(second_parts[:, ffn_cut:], 3)
    cross_q_in, cross_kv_in = cross_in[:head_width], cross_in[head_width:]
    decoder_qkvs, decoder_ctx, decoder_logs, resid_three, first, first_low = decoder_side
    middle_all, encoder_before, encoder_hidden, resid_two, _, memory_low = ffn_stage(
        seq, 3, middle_low, middle, encoder_one, encoder_two, scales[1]
    )
    memory_low, last = lax.optimization_barrier(
        (memory_low, [gather_rows(piece) for piece in last])
    )
    decoder_one, decoder_two = ffn_in(last[0]), row_order(last[1])
    (
        first_all, memory_all, cross_q, cross_kvs, cross_ctx, cross_logs, resid_four, second,
        second_low,
    ) = cross_stage(
        seq, 4, count, places,
        (
            first, first_low, memory_low, cross_q_in, cross_kv_in, cross_out, cross_pre,
            source_keys, target_queries, scales[norm_count + 1],
        ),
    )
    second_all, decoder_before, decoder_hidden, resid_five, _, result = ffn_stage(
        seq, 5, second_low, second, decoder_one, decoder_two, scales[norm_count + 2]
    )

    def scatter_ranks(value):
        return lax.psum_scatter(value, "rows", scatter_dimension=0, tiled=False)

    norm_grads = {}

    def ffn_back(name_id, index, up, resid, before, hidden_low, rows_all, one, two):
        out, pair, expand, down, two_terms = ffn_back_stage(
            seq, ranks, hidden, adapt, name_id, up, resid, scales[index], before, one, two,
            rows_all, hidden_low,
        )
        keep_pair(index, pair)
        return out, [two_terms, jnp.concatenate([expand, down], axis=1)]

    def hold(value, terms, sums):
        value, terms, sums = lax.optimization_barrier((value, terms, sums))
        return value, [scatter_ranks(term) for term in terms], sums

    def keep_pair(index, pair):
        norm_grads[index] = pair

    second_up, terms = ffn_back(
        6, norm_count + 2, cotangent.reshape(stacked, block, width), resid_five, decoder_before,
        decoder_hidden, second_all, decoder_one, decoder_two,
    )
    second_up, ffn_sums, _ = hold(second_up, terms, [])

    cross_pre_grad, first_up, memory_up, pair, terms = cross_back_stage(
        seq, ranks, 7, count, places,
        (
            second_up, resid_four, scales[norm_count + 1], cross_q, cross_kvs, cross_logs,
            cross_q_in, cross_kv_in, cross_out, cross_pre, source_keys, target_queries,
            first_all, memory_all, cross_ctx,
        ),
    )
    keep_pair(norm_count + 1, pair)
    first_up, cross_sums, ffn_sums = hold(first_up, [terms], ffn_sums)
    decoder_two_grad, decoder_one_grad = ffn_sums

    def self_back(name_id, index, causal, reduce, side, sums):
        held = self_back_stage(seq, ranks, name_id, count, places, causal, reduce, side)
        held, sums = lax.optimization_barrier((tuple(held), sums))
        return held + (sums,)

    def owner_parts(value):
        out_part = value[3].reshape(slice_cols, seq, head_width)
        return jnp.swapaxes(out_part, 0, 1), value[:3]

    decoder_pre_grad, pair, target_grad, self_terms, cross_sums = self_back(
        9, norm_count, True, False,
        (
            first_up, resid_three, scales[norm_count], decoder_qkvs, decoder_logs, decoder_in,
            decoder_out, decoder_pre, target_keys, target_queries, decoder_ctx, target_all,
        ),
        cross_sums,
    )
    keep_pair(norm_count, pair)
    memory_up, self_sums, _ = hold(memory_up, [self_terms], [])
    cross_out_grad, cross_in_grad = owner_parts(cross_sums[0])

    middle_up, terms = ffn_back(
        8, 1, memory_up, resid_two, encoder_before, encoder_hidden, middle_all,
        encoder_one, encoder_two,
    )
    middle_up, ffn_sums, self_sums = hold(middle_up, terms, self_sums)
    decoder_out_grad, decoder_in_grad = owner_parts(self_sums[0])

    def give_back(pieces):
        value = jnp.concatenate(pieces, axis=2) if len(pieces) > 1 else pieces[0]
        return lax.all_to_all(value, "seq", 0, 1, tiled=False)

    decoder_rows = give_back([decoder_two_grad, cross_out_grad, decoder_out_grad])

    pairs = [jnp.zeros((2, width), wide)] + [norm_grads[index] for index in sorted(norm_grads)]
    norm_in = jnp.concatenate(pairs)
    norm_in = jnp.pad(norm_in, ((0, -norm_in.shape[0] % 16), (0, 0)))
    norm_total, prefix_total, source_grad, self_terms, ffn_sums = self_back(
        10, 0, False, True,
        (
            middle_up, resid_one, scales[0], encoder_qkvs, encoder_logs, encoder_in,
            encoder_out, encoder_pre, source_keys, source_queries, encoder_ctx, source_all,
            norm_in, jnp.concatenate([decoder_pre_grad, cross_pre_grad]),
        ),
        ffn_sums,
    )
    encoder_two_grad, encoder_one_grad = ffn_sums
    encoder_out_grad, encoder_in_grad = owner_parts(self_terms)
    encoder_rows = give_back([encoder_two_grad, encoder_out_grad.astype(low)])

    def row_grad(value, start, size, scale=None):
        piece = value[:, :, start : start + size].astype(wide)
        if scale is not None:
            piece = piece * scale
        return piece.reshape(slice_cols, -1).T

    def column_grad(value):
        return jnp.swapaxes(value.astype(wide), -1, -2)

    row = lax.axis_index("rows")
    prefix_total = lax.dynamic_slice_in_dim(
        prefix_total[:, :count], row * slice_cols, slice_cols, 2
    )
    norm_total = lax.dynamic_slice_in_dim(
        norm_total[: 2 * len(pairs)], (me * ranks + row) * slice_cols, slice_cols, 1
    )
    norm_total = norm_total.reshape(-1, 2, slice_cols)

    shape_out = source.shape
    return (
        result.reshape(shape_out),
        source_grad.reshape(shape_out),
        target_grad.reshape(shape_out),
        column_grad(encoder_in_grad),
        row_grad(encoder_rows, padded, head_width),
        prefix_total[0:2],
        column_grad(encoder_one_grad[:cut]),
        row_grad(encoder_rows, 0, hidden),
        column_grad(encoder_one_grad[cut:]),
        row_grad(encoder_rows, hidden, adapt, ADAPTER_SCALE),
        norm_total[:norm_count],
        column_grad(decoder_in_grad),
        row_grad(decoder_rows, padded + head_width, head_width),
        prefix_total[2:4],
        column_grad(cross_in_grad[0]),
        column_grad(cross_in_grad[1:]),
        row_grad(decoder_rows, padded, head_width),
        prefix_total[4:6],
        column_grad(decoder_one_grad[:cut]),
        row_grad(decoder_rows, 0, hidden),
        column_grad(decoder_one_grad[cut:]),
        row_grad(decoder_rows, hidden, adapt, ADAPTER_SCALE),
        norm_total[norm_count:],
    )


def solution(mesh):
    rows = P(None, "rows", "seq", None)
    ids = P(None, "rows", None)
    flat = P(None, ("seq", "rows"))
    deep = P(None, None, ("seq", "rows"))
    weights = (
        deep, flat, deep, flat, flat, flat, flat, deep, deep, flat, deep, flat, deep, flat, deep,
        flat, flat, flat, flat, deep,
    )
    body = functools.partial(local, mesh.shape["seq"], mesh.shape["rows"])
    return jax.shard_map(
        body,
        mesh=mesh,
        in_specs=(rows, rows, ids, ids, rows) + weights,
        out_specs=(rows, rows, rows) + weights,
        check_vma=False,
    )
```
